32 devices in a mesh: dom: 8 (over z, x), sub: 4 (over y, core).
Axes of the slice: x: 2, y: 2, z: 4, core: 2. Of those that a mesh axis runs over, the one named last changes fastest.
Arguments:
- fine_residual: float32 [35, 5, 8192], P(None, None, ('dom', 'sub')), may hold values from -6 to 6
- fine_basis: float32 [64, 35], replicated, may hold values from -1 to 1
- coarse_basis: float32 [64, 10, 8192], P(None, None, ('dom', 'sub')), may hold values from -0.75 to 0.75
- donor_cells: int32 [8192, 4], P(('dom', 'sub')), may hold values from 0 to 4095, as said below
- point_counts: int32 [8192, 4], P(('dom', 'sub')), may hold values from 1 to 32, 64 in all within a row
- solver_pos: int32 [4096], P(('dom', 'sub')), may hold values from 0 to 4095, as said below
- block_inverse: float32 [50, 50, 4096], P(None, None, ('dom', 'sub')), may hold values from -0.25 to 1.65
- face_jacobian: float32 [4, 5, 5, 4096], P(None, None, None, ('dom', 'sub')), may hold values from -0.5 to 0.5
- face_lift: float32 [4, 10, 10], replicated, may hold values from -2 to 2
- face_offset: int32 [4, 4096], P(None, ('dom', 'sub')), may hold values from -32 to 32, as said below
Outputs:
- coarse_residual: float32 [50, 4096], P(None, ('dom', 'sub'))
- correction: float32 [50, 4096], P(None, ('dom', 'sub'))
The draws below stay inside these ranges and needn't reach their ends.
Inputs may be any that keep to these rules, and one draw needn't show every extreme that they name: `donor_cells`: among the 4 donors of the 256 fine elements of one device, at most 64 lie in any one block of 128 consecutive coarse elements; in 1 group of 4 consecutive blocks every block receives exactly 64 from every device. `solver_pos`: A permutation; all 128 elements of one block go to one block of 128 solver positions in the same group of 4 consecutive blocks, distinct blocks to distinct ones. `face_offset`: 0 marks a boundary face, and so does a neighbour position outside 0 to 4095.
All inputs are finite; a program needn't handle non-finite values.
Results may differ from the reference program's by a relative error of at most 0.0003.
Values sent between devices are 32-bit elements; how exact they have to be, the bound alone decides.
No kernel may reach another device: no remote copies, remote signals or barrier semaphores. Data moves between devices by JAX's collectives and lax.ppermute only.
A program may use at most 64 MiB of HBM per device.

```python
import math
import jax
import jax.numpy as jnp
import numpy as np
from jax import lax

MF = 35
MC = 10
NVAR = 5
NB = 50
Q = 64
K = 4
F_DEV = 256
C_DEV = 128
OWNERS = 32
NF = 8192
NC = 4096
CAP = 64
BUSYG = 1
REACH = 32
N_DOM = 8
N_SUB = 4


def draw_donor_cells(key, part):
    slot_total = OWNERS * CAP
    slot_owner = jnp.arange(slot_total, dtype=jnp.int32) // CAP
    group_pick = jax.random.permutation(jax.random.fold_in(key, 1), N_DOM)[:BUSYG]
    busy_group = jnp.zeros((N_DOM,), jnp.int32).at[group_pick].set(1)
    busy_slot = busy_group[slot_owner // N_SUB]

    def one_block(block_index):
        block_key = jax.random.fold_in(jax.random.fold_in(key, 2), block_index)
        random_score = jax.random.randint(jax.random.fold_in(block_key, 0), (slot_total,), 0, 2 ** 20)
        slot_score = random_score + (1 - busy_slot) * 2 ** 20
        chosen = jnp.argsort(slot_score, stable=True)[:F_DEV * K]
        shuffled = jax.random.permutation(jax.random.fold_in(block_key, 1), chosen)
        owner_block = slot_owner[shuffled]
        local_seat = jax.random.randint(jax.random.fold_in(block_key, 2), (F_DEV * K,), 0, C_DEV)
        return (owner_block * C_DEV + local_seat).reshape(F_DEV, K)
    return jax.vmap(one_block)(jnp.arange(OWNERS)).reshape(NF, K).astype(jnp.int32)


def draw_solver_pos(key, part):
    base_key = jax.random.fold_in(key, 11)

    def one_group(group_index):
        group_key = jax.random.fold_in(base_key, group_index)
        sub_order = jax.random.permutation(jax.random.fold_in(group_key, 0), N_SUB)
        inner_order = jax.vmap(lambda sub_index: jax.random.permutation(jax.random.fold_in(group_key, sub_index + 1), C_DEV))(jnp.arange(N_SUB))
        return ((group_index * N_SUB + sub_order)[:, None] * C_DEV + inner_order).reshape(N_SUB * C_DEV)
    return jax.vmap(one_group)(jnp.arange(N_DOM)).reshape(NC).astype(jnp.int32)


def draw_face_offset(key, part):
    base_key = jax.random.fold_in(key, 21)
    reach_size = jax.random.randint(jax.random.fold_in(base_key, 0), (4, NC), 1, REACH + 1)
    sign_choice = jax.random.randint(jax.random.fold_in(base_key, 1), (4, NC), 0, 2) * 2 - 1
    is_wall = jax.random.randint(jax.random.fold_in(base_key, 2), (4, NC), 0, 10) == 0
    return jnp.where(is_wall, 0, reach_size * sign_choice).astype(jnp.int32)


def draw_block_inverse(key, part):
    base_key = jax.random.fold_in(key, 31)
    identity = (jnp.arange(NB)[:, None] == jnp.arange(NB)[None, :]).astype(jnp.float32)[:, :, None]
    diagonal = jax.random.uniform(jax.random.fold_in(base_key, 0), (NB, 1, NC), jnp.float32, 0.6, 1.4)
    off_diagonal = jnp.clip(0.05 * jax.random.normal(jax.random.fold_in(base_key, 1), (NB, NB, NC), jnp.float32), -0.25, 0.25)
    return (identity * diagonal + off_diagonal).astype(jnp.float32)


def levels(stream_key, extent, shards, low, high):
    factor_of = 1.0
    for dim, blocks in shards:
        heights = jax.random.uniform(jax.random.fold_in(jax.random.fold_in(stream_key, 6), dim), (blocks,), jnp.float32, low / len(shards), high / len(shards))
        factor_of = factor_of * jnp.repeat(jnp.exp(heights), extent[dim] // blocks).reshape((-1,) + (1,) * (len(extent) - 1 - dim))
    return factor_of


def profile(number_of, total, limit, lean):
    weights = [(1 << 20) // math.isqrt(rank ** lean) + 1 for rank in range(2, number_of + 1)]
    spare, given = total - limit - (number_of - 1), [1] * (number_of - 1)
    while spare > 0:
        candidates = [i for i in range(number_of - 1) if given[i] < limit]
        mass, budget = sum([weights[i] for i in candidates]), spare
        for i in candidates:
            more = min(limit - given[i], max(1, budget * weights[i] // mass), spare)
            given[i] = given[i] + more
            spare = spare - more
    return np.array([limit] + given)


def ragged(rng, amount, total, reach, lean):
    if amount == 2:
        one = jax.random.randint(rng, (), max(1, total - reach), min(reach, total - 1) + 1)
        return jnp.stack([one, total - one])
    tallies = jnp.asarray(profile(amount, total, reach, lean), jnp.int32)
    twos = (amount - 1) // 2
    giver, taker = tallies[1:1 + 2 * twos:2], tallies[2:2 + 2 * twos:2]
    slack = jnp.minimum(giver - 1, reach - taker)
    shifted = jax.random.randint(jax.random.fold_in(rng, 1), (twos,), 0, 1 << 20) % (slack + 1)
    tallies = tallies.at[1:1 + 2 * twos:2].set(giver - shifted).at[2:2 + 2 * twos:2].set(taker + shifted)
    return tallies[jax.random.permutation(jax.random.fold_in(rng, 2), amount)]


def gaussian(own_key, extent, deviation, most, shards=(), kind=jnp.bfloat16):
    entries = jax.random.normal(own_key, extent, jnp.float32) * deviation
    if len(shards) > 0:
        entries = levels(own_key, extent, shards, -0.22, 0.18) * entries
    return jnp.clip(entries, min=-most, max=most).astype(kind)


def setup_inputs(seed: int = 0) -> dict:
    splits = jax.random.split(jax.random.key(seed), 11)
    return {
        "fine_residual": gaussian(splits[0], (MF, NVAR, NF), 1.0, 6.0, ((2, 32),), jnp.float32),
        "fine_basis": gaussian(splits[1], (Q, MF), MF ** -0.5, 1.0, (), jnp.float32),
        "coarse_basis": gaussian(splits[2], (Q, MC, NF), Q ** -0.5, 0.75, ((2, 32),), jnp.float32),
        "donor_cells": draw_donor_cells(jax.random.fold_in(splits[10], 71), 0),
        "point_counts": jax.vmap(lambda own: ragged(own, K, Q, Q // 2, 1))(jax.random.split(splits[4], NF)).reshape((NF, K)).astype(jnp.int32),
        "solver_pos": draw_solver_pos(jax.random.fold_in(splits[10], 71), 0),
        "block_inverse": draw_block_inverse(jax.random.fold_in(splits[10], 71), 0),
        "face_jacobian": gaussian(splits[7], (4, NVAR, NVAR, NC), 0.08, 0.5, ((3, 32),), jnp.float32),
        "face_lift": gaussian(splits[8], (4, MC, MC), MC ** -0.5, 2.0, (), jnp.float32),
        "face_offset": draw_face_offset(jax.random.fold_in(splits[10], 71), 0),
    }


def pair_terms(residual, fine_basis, coarse_basis, counts):
    mode_count, variables, fine_count = residual.shape
    point_total = fine_basis.shape[0]
    values = jnp.dot(fine_basis, residual.reshape(mode_count, variables * fine_count), precision=lax.Precision.HIGHEST, preferred_element_type=jnp.float32)
    values = values.reshape(point_total, variables, fine_count)
    upper_point = jnp.cumsum(counts, axis=1)
    lower_point = upper_point - counts
    points = jnp.arange(point_total, dtype=jnp.int32)[:, None]
    slot_terms = []
    for slot_index in range(counts.shape[1]):
        inside = (points >= lower_point[:, slot_index][None, :]) & (points < upper_point[:, slot_index][None, :])
        masked = jnp.where(inside[:, None, :], coarse_basis, jnp.float32(0.0))
        slot_terms.append(jnp.einsum("qae,qve->eav", masked, values, precision=lax.Precision.HIGHEST))
    stacked = jnp.stack(slot_terms, axis=1)
    return stacked.reshape(fine_count * counts.shape[1], -1)


def couple(coarse_field, face_jacobian, face_lift, face_offset):
    element_total = coarse_field.shape[1]
    own_index = jnp.arange(element_total, dtype=jnp.int32)
    result = jnp.zeros((MC, NVAR, element_total), jnp.float32)
    for face_index in range(4):
        offset_row = face_offset[face_index]
        neighbour = own_index + offset_row
        inside = (offset_row != 0) & (neighbour >= 0) & (neighbour < element_total)
        picked = jnp.where(inside[None, :], coarse_field[:, jnp.clip(neighbour, 0, element_total - 1)], jnp.float32(0.0))
        picked = picked.reshape(MC, NVAR, element_total)
        lifted = jnp.einsum("ab,bvp->avp", face_lift[face_index], picked, precision=lax.Precision.HIGHEST)
        result = result + jnp.einsum("avp,wvp->awp", lifted, face_jacobian[face_index], precision=lax.Precision.HIGHEST)
    return result.reshape(MC * NVAR, element_total)


def apply_inverse(block_inverse, coarse_field):
    return jnp.einsum("ijp,jp->ip", block_inverse, coarse_field, precision=lax.Precision.HIGHEST)


def reference(fine_residual, fine_basis, coarse_basis, donor_cells, point_counts, solver_pos, block_inverse, face_jacobian, face_lift, face_offset):
    blocks = fine_residual.shape[2] // F_DEV
    element_total = solver_pos.shape[0]
    residual_blocks = jnp.moveaxis(fine_residual.reshape(MF, NVAR, blocks, F_DEV), 2, 0)
    basis_blocks = jnp.moveaxis(coarse_basis.reshape(Q, MC, blocks, F_DEV), 2, 0)
    donor_blocks = donor_cells.reshape(blocks, F_DEV * K)
    count_blocks = point_counts.reshape(blocks, F_DEV, K)

    def accumulate(restricted, block_items):
        residual, basis, donors, counts = block_items
        pair_values = pair_terms(residual, fine_basis, basis, counts)
        return restricted.at[donors].add(pair_values), None

    restricted, unused = lax.scan(accumulate, jnp.zeros((element_total, MC * NVAR), jnp.float32), (residual_blocks, basis_blocks, donor_blocks, count_blocks))
    coarse_residual = jnp.zeros((element_total, MC * NVAR), jnp.float32).at[solver_pos].set(restricted).T
    first_sweep = apply_inverse(block_inverse, coarse_residual)
    second = apply_inverse(block_inverse, coarse_residual - couple(first_sweep, face_jacobian, face_lift, face_offset))
    third_sweep = apply_inverse(block_inverse, coarse_residual - couple(second, face_jacobian, face_lift, face_offset))
    return coarse_residual, third_sweep
```

```python
import functools
import jax
import jax.numpy as jnp
from jax import lax
from jax.experimental import pallas as pl
from jax.experimental.pallas import tpu as pltpu
from jax.sharding import PartitionSpec as P

F32 = jnp.float32
BF16 = jnp.bfloat16
AXES = ("dom", "sub")
VMEM = pl.BlockSpec(memory_space=pltpu.VMEM)


def split(x):
    high = x.astype(BF16)
    return high, (x - high.astype(F32)).astype(BF16)


def mm(a, b, ca=1, cb=0, precision=None):
    return lax.dot_general(
        a, b, (((ca,), (cb,)), ((), ())), precision=precision, preferred_element_type=F32
    )


def rows_of(iota_shape, dim):
    return lax.broadcasted_iota(jnp.int32, iota_shape, dim)


def pair_kernel(res_ref, basis_ref, coarse_ref, counts_ref, out_ref):
    variables, _, fine = res_ref.shape
    modes, points, _ = coarse_ref.shape
    donors = counts_ref.shape[0]
    basis_high, basis_low = split(basis_ref[...])
    res_high, res_low = split(jnp.concatenate([res_ref[v] for v in range(variables)], axis=1))
    values = mm(basis_high, res_high, 0, 0)
    values += mm(basis_high, res_low, 0, 0) + mm(basis_low, res_high, 0, 0)
    used = modes * variables
    out_ref[used:, :] = jnp.zeros((out_ref.shape[0] - used, out_ref.shape[1]), F32)
    width = 128
    point = rows_of((points, width), 0)
    for at in range(0, fine, width):
        upper = jnp.zeros((1, width), jnp.int32)
        inside = []
        for k in range(donors):
            lower = upper
            upper = lower + counts_ref[k : k + 1, at : at + width]
            inside.append((point >= lower) & (point < upper))
        for v in range(variables):
            column = v * fine + at
            value = values[:, column : column + width]
            masked = [jnp.where(inside[k], value, 0.0) for k in range(donors)]
            for a in range(modes):
                coarse = coarse_ref[a, :, at : at + width]
                row = a * variables + v
                for k in range(donors):
                    out_ref[row : row + 1, k * fine + at : k * fine + at + width] = jnp.sum(
                        coarse * masked[k], axis=0, keepdims=True
                    )


def scatter_kernel(pair_ref, donors_ref, table_ref, out_ref, pair_scratch, place_scratch):
    owners, block = table_ref.shape
    chunk, used, _ = out_ref.shape
    donors, fine = donors_ref.shape
    depth = pair_ref.shape[0]

    @pl.when(pl.program_id(0) == 0)
    def _():
        high, low = split(pair_ref[...])
        pair_scratch[:depth, :] = high
        pair_scratch[depth:, :] = low
        table = table_ref[...].astype(F32)
        for k in range(donors):
            cell = donors_ref[k : k + 1, :]
            owner = cell // block
            seat = cell % block
            own = (rows_of((owners, fine), 0) == owner).astype(F32)
            found = mm(table, own, 0, 0, lax.Precision.HIGHEST)
            place = jnp.sum(
                jnp.where(rows_of((block, fine), 0) == seat, found, 0.0), axis=0, keepdims=True
            )
            place_scratch[k * fine : (k + 1) * fine, :] = jnp.broadcast_to(place, (block, fine)).T

    first = pl.program_id(0) * (chunk * block)
    lane = rows_of((donors * fine, block), 1) + first
    place = place_scratch[...]
    chooser = jnp.concatenate(
        [(place == (lane + j * block).astype(F32)).astype(F32).astype(BF16) for j in range(chunk)],
        axis=1,
    )
    total = mm(pair_scratch[...], chooser)
    total = total[:depth] + total[depth:]
    for j in range(chunk):
        out_ref[j] = total[:used, j * block : (j + 1) * block]


def prepare_kernel(offset_ref, lift_ref, chooser_ref, lift_out_ref, *, variables, slab):
    faces, block = offset_ref.shape
    modes = lift_ref.shape[0]
    own = rows_of((1, block), 1)
    row = rows_of((2 * block, block), 0)
    for f in range(faces):
        offset = offset_ref[f : f + 1, :]
        there = own + offset
        source = jnp.where(there < 0, there + 2 * block, there)
        source = jnp.where(offset != 0, source, -1)
        chooser_ref[:, f * block : (f + 1) * block] = (row == source).astype(F32).astype(BF16)
    width = variables * faces * slab
    column = rows_of((modes, width), 1)
    mode = rows_of((modes, width), 0)
    spread = jnp.zeros((modes, width), F32)
    for f in range(faces):
        put = (column % slab == mode) & ((column // slab) % faces == f)
        spread += mm(lift_ref[:, f, :], put.astype(F32), 1, 0, lax.Precision.HIGHEST)
    full = modes * variables
    expand = (rows_of((full, modes), 0) // variables == rows_of((full, modes), 1)).astype(F32)
    lifted = mm(expand, spread, 1, 0, lax.Precision.HIGHEST)
    keep = rows_of((full, width), 1) // (slab * faces) == rows_of((full, width), 0) % variables
    lift_out_ref[...] = jnp.where(keep, lifted, 0.0)


def apply_inverse(inverse_ref, field, out_ref, variables, slab):
    full = inverse_ref.shape[0]
    modes = full // variables
    if slab:
        out_ref[...] = jnp.zeros(out_ref.shape, F32)
    for i in range(full):
        row = (i % variables) * slab + i // variables if slab else i
        out_ref[row : row + 1, :] = jnp.sum(inverse_ref[i] * field, axis=0, keepdims=True)


def first_kernel(inverse_ref, residual_ref, out_ref, *, variables, slab):
    apply_inverse(inverse_ref, residual_ref[...], out_ref, variables, slab)


def sweep_kernel(
    inverse_ref, residual_ref, x_ref, low_ref, high_ref, chooser_ref, lift_ref, jacobian_ref, out_ref,
    z_high, z_low, *, variables, slab, last
):
    block = residual_ref.shape[1]
    faces = jacobian_ref.shape[2]
    lane = rows_of(x_ref.shape, 1)
    beside = jnp.where(lane < block // 2, high_ref[...], low_ref[...])
    x_high, x_low = split(jnp.concatenate([x_ref[...], beside], axis=1))
    rows = x_ref.shape[0]
    picked = mm(jnp.concatenate([x_high, x_low], axis=0), chooser_ref[...])
    picked = picked[:rows] + picked[rows:]
    for f in range(faces):
        part = [
            picked[v * slab : (v + 1) * slab, f * block : (f + 1) * block] for v in range(variables)
        ]
        for w in range(variables):
            z = part[0] * jacobian_ref[w, 0, f : f + 1, :]
            for v in range(1, variables):
                z += part[v] * jacobian_ref[w, v, f : f + 1, :]
            at = (w * faces + f) * slab
            z_high[at : at + slab, :], z_low[at : at + slab, :] = split(z)
    lift_high, lift_low = split(lift_ref[...])
    coupled = mm(lift_high, z_high[...]) + mm(lift_high, z_low[...]) + mm(lift_low, z_high[...])
    apply_inverse(inverse_ref, residual_ref[...] - coupled, out_ref, variables, 0 if last else slab)


def per_device(
    fine_residual,
    fine_basis,
    coarse_basis,
    donor_cells,
    point_counts,
    solver_pos,
    block_inverse,
    face_jacobian,
    face_lift,
    face_offset,
):
    owners = lax.axis_size("dom") * lax.axis_size("sub")
    _, variables, fine = fine_residual.shape
    modes = coarse_basis.shape[1]
    donors = donor_cells.shape[1]
    block = solver_pos.shape[0]
    faces = face_offset.shape[0]
    full = modes * variables
    slab = -(-modes // 16) * 16
    depth = -(-full // 16) * 16

    table = lax.all_gather(solver_pos, AXES, axis=0, tiled=True).reshape(owners, block)
    pair = pl.pallas_call(
        pair_kernel,
        out_shape=jax.ShapeDtypeStruct((depth, donors * fine), F32),
        in_specs=[VMEM] * 4,
        out_specs=VMEM,
        name="donor_sums",
    )(
        fine_residual.transpose(1, 0, 2),
        fine_basis.T,
        coarse_basis.transpose(1, 0, 2),
        point_counts.T,
    )
    chunk = 8
    dense = pl.pallas_call(
        scatter_kernel,
        grid=(owners // chunk,),
        out_shape=jax.ShapeDtypeStruct((owners, full, block), F32),
        in_specs=[VMEM] * 3,
        out_specs=pl.BlockSpec((chunk, full, block), lambda i: (i, 0, 0)),
        scratch_shapes=[
            pltpu.VMEM((2 * depth, donors * fine), BF16),
            pltpu.VMEM((donors * fine, block), F32),
        ],
        compiler_params=pltpu.CompilerParams(vmem_limit_bytes=32 * 2**20),
        name="scatter_rows",
    )(pair, donor_cells.T, table)
    coarse_residual = lax.psum_scatter(dense, AXES, scatter_dimension=0, tiled=True)[0]

    chooser, lift = pl.pallas_call(
        functools.partial(prepare_kernel, variables=variables, slab=slab),
        out_shape=(
            jax.ShapeDtypeStruct((2 * block, faces * block), BF16),
            jax.ShapeDtypeStruct((full, variables * faces * slab), F32),
        ),
        in_specs=[VMEM] * 2,
        out_specs=(VMEM, VMEM),
        name="prepare",
    )(face_offset, face_lift.transpose(1, 0, 2))
    jacobian = face_jacobian.transpose(1, 2, 0, 3)

    forward = [(i, i + 1) for i in range(owners - 1)]
    backward = [(j, i) for i, j in forward]
    x = pl.pallas_call(
        functools.partial(first_kernel, variables=variables, slab=slab),
        out_shape=jax.ShapeDtypeStruct((variables * slab, block), F32),
        in_specs=[VMEM] * 2,
        out_specs=VMEM,
        name="first",
    )(block_inverse, coarse_residual)
    for last in (False, True):
        low = lax.ppermute(x, AXES, forward)
        high = lax.ppermute(x, AXES, backward)
        shape = (full, block) if last else (variables * slab, block)
        x = pl.pallas_call(
            functools.partial(sweep_kernel, variables=variables, slab=slab, last=last),
            out_shape=jax.ShapeDtypeStruct(shape, F32),
            in_specs=[VMEM] * 8,
            out_specs=VMEM,
            scratch_shapes=[pltpu.VMEM((variables * faces * slab, block), BF16)] * 2,
            name="correction" if last else "second",
        )(block_inverse, coarse_residual, x, low, high, chooser, lift, jacobian)
    return coarse_residual, x


def solution(mesh):
    in_specs = (
        P(None, None, AXES),
        P(),
        P(None, None, AXES),
        P(AXES, None),
        P(AXES, None),
        P(AXES),
        P(None, None, AXES),
        P(None, None, None, AXES),
        P(),
        P(None, AXES),
    )
    return jax.shard_map(
        per_device,
        mesh=mesh,
        in_specs=in_specs,
        out_specs=(P(None, AXES), P(None, AXES)),
        check_vma=False,
    )
```

```python
import functools
import jax
import jax.numpy as jnp
from jax import lax
from jax.experimental import pallas as pl
from jax.experimental.pallas import tpu as pltpu
from jax.sharding import PartitionSpec as P

F32 = jnp.float32
BF16 = jnp.bfloat16
PLANE = ("low", "sub")
WHOLE = ("high", "low", "sub")
VMEM = pl.BlockSpec(memory_space=pltpu.VMEM)


def split(x):
    high = x.astype(BF16)
    return high, (x - high.astype(F32)).astype(BF16)


def mm(a, b, ca=1, cb=0, precision=None):
    return lax.dot_general(
        a, b, (((ca,), (cb,)), ((), ())), precision=precision, preferred_element_type=F32
    )


def rows_of(iota_shape, dim):
    return lax.broadcasted_iota(jnp.int32, iota_shape, dim)


def pair_kernel(res_ref, basis_ref, coarse_ref, counts_ref, out_ref):
    variables, _, fine = res_ref.shape
    modes, points, _ = coarse_ref.shape
    donors = counts_ref.shape[0]
    basis_high, basis_low = split(basis_ref[...])
    res_high, res_low = split(jnp.concatenate([res_ref[v] for v in range(variables)], axis=1))
    values = mm(basis_high, res_high, 0, 0)
    values += mm(basis_high, res_low, 0, 0) + mm(basis_low, res_high, 0, 0)
    used = modes * variables
    out_ref[used:, :] = jnp.zeros((out_ref.shape[0] - used, out_ref.shape[1]), F32)
    width = 128
    point = rows_of((points, width), 0)
    for at in range(0, fine, width):
        upper = jnp.zeros((1, width), jnp.int32)
        inside = []
        for k in range(donors):
            lower = upper
            upper = lower + counts_ref[k : k + 1, at : at + width]
            inside.append((point >= lower) & (point < upper))
        for v in range(variables):
            column = v * fine + at
            value = values[:, column : column + width]
            masked = [jnp.where(inside[k], value, 0.0) for k in range(donors)]
            for a in range(modes):
                coarse = coarse_ref[a, :, at : at + width]
                row = a * variables + v
                for k in range(donors):
                    out_ref[row : row + 1, k * fine + at : k * fine + at + width] = jnp.sum(
                        coarse * masked[k], axis=0, keepdims=True
                    )


def place_kernel(pair_ref, donors_ref, table_ref, out_ref, *, passing, capacity):
    owners, block = table_ref.shape
    chunks, used, width = out_ref.shape
    donors, fine = donors_ref.shape
    total = donors * fine
    depth = pair_ref.shape[0]
    table = table_ref[...].astype(F32)
    places = []
    for k in range(donors):
        cell = donors_ref[k : k + 1, :]
        own = (rows_of((owners, fine), 0) == cell // block).astype(F32)
        found = mm(table, own, 0, 0, lax.Precision.HIGHEST)
        at_seat = rows_of((block, fine), 0) == cell % block
        places.append(jnp.sum(jnp.where(at_seat, found, 0.0), axis=0, keepdims=True))
    place = jnp.concatenate(places, axis=1).astype(jnp.int32)
    owner = place // block
    seat = (place % block).astype(F32)
    lanes = 128
    parts = total // lanes
    mine = (rows_of((owners, total), 0) == owner).astype(F32)
    stacked = jnp.concatenate([mine[:, j * lanes : (j + 1) * lanes] for j in range(parts)], axis=0)
    earlier = (rows_of((lanes, lanes), 0) < rows_of((lanes, lanes), 1)).astype(F32)
    counter = jnp.concatenate([earlier, jnp.ones((lanes, lanes), F32)], axis=1)
    counted = mm(stacked.astype(BF16), counter.astype(BF16))
    before = jnp.zeros((owners, lanes), F32)
    ranks = []
    for j in range(parts):
        own = mine[:, j * lanes : (j + 1) * lanes]
        part = counted[j * owners : (j + 1) * owners]
        ranks.append(jnp.sum(own * (before + part[:, :lanes]), axis=0, keepdims=True))
        before += part[:, lanes:]
    rank = jnp.concatenate(ranks, axis=1).astype(jnp.int32)
    slot = (owner % passing) * width + (owner // passing) * capacity + rank
    slot = jnp.broadcast_to(slot.astype(F32), (lanes, total)).T
    rows = pair_ref[...]
    rows = jnp.where(rows_of(rows.shape, 0) == used - 1, seat, rows)
    both = jnp.concatenate(split(rows), axis=0)
    lane = rows_of((total, lanes), 1)
    for c in range(chunks):
        chooser = jnp.concatenate(
            [
                (slot == (lane + (c * width + j)).astype(F32)).astype(F32).astype(BF16)
                for j in range(0, width, lanes)
            ],
            axis=1,
        )
        placed = mm(both, chooser)
        out_ref[c] = placed[:used] + placed[depth : depth + used]


def seat_kernel(columns_ref, out_ref, *, capacity):
    sources, _, _ = columns_ref.shape
    blocks, full, block = out_ref.shape
    for h in range(blocks):
        got = jnp.concatenate(
            [columns_ref[s, :, h * capacity : (h + 1) * capacity] for s in range(sources)], axis=1
        )
        seat = got[full : full + 1, :]
        chooser = (rows_of((block, got.shape[1]), 0).astype(F32) == seat).astype(F32).astype(BF16)
        high, low = split(got)
        out_ref[h] = (mm(high, chooser, 1, 1) + mm(low, chooser, 1, 1))[:full]


def prepare_kernel(offset_ref, lift_ref, chooser_ref, lift_out_ref, *, variables, slab):
    faces, block = offset_ref.shape
    modes = lift_ref.shape[0]
    own = rows_of((1, block), 1)
    row = rows_of((2 * block, block), 0)
    for f in range(faces):
        offset = offset_ref[f : f + 1, :]
        there = own + offset
        source = jnp.where(there < 0, there + 2 * block, there)
        source = jnp.where(offset != 0, source, -1)
        chooser_ref[:, f * block : (f + 1) * block] = (row == source).astype(F32).astype(BF16)
    width = variables * faces * slab
    column = rows_of((modes, width), 1)
    mode = rows_of((modes, width), 0)
    spread = jnp.zeros((modes, width), F32)
    for f in range(faces):
        put = (column % slab == mode) & ((column // slab) % faces == f)
        spread += mm(lift_ref[:, f, :], put.astype(F32), 1, 0, lax.Precision.HIGHEST)
    full = modes * variables
    expand = (rows_of((full, modes), 0) // variables == rows_of((full, modes), 1)).astype(F32)
    lifted = mm(expand, spread, 1, 0, lax.Precision.HIGHEST)
    keep = rows_of((full, width), 1) // (slab * faces) == rows_of((full, width), 0) % variables
    lift_out_ref[...] = jnp.where(keep, lifted, 0.0)


def apply_inverse(inverse_ref, field, out_ref, parts, variables, slab):
    full, _, block = inverse_ref.shape
    for i in range(full):
        product = inverse_ref[i] * field
        partial = product[0:8]
        for j in range(8, full - 7, 8):
            partial += product[j : j + 8]
        rest = full % 8
        if rest:
            partial = jnp.concatenate([partial[:rest] + product[full - rest :], partial[rest:]], axis=0)
        parts[i * 8 : i * 8 + 8, :] = partial
    row = rows_of((out_ref.shape[0], 8 * full), 0)
    source = rows_of((out_ref.shape[0], 8 * full), 1) // 8
    target = (source % variables) * slab + source // variables if slab else source
    adder = (row == target).astype(F32).astype(BF16)
    high, low = split(parts[...])
    out_ref[...] = mm(adder, high) + mm(adder, low)


def first_kernel(inverse_ref, residual_ref, out_ref, total_ref, parts, *, variables, slab):
    residual = residual_ref[0]
    for h in range(1, residual_ref.shape[0]):
        residual += residual_ref[h]
    total_ref[...] = residual
    apply_inverse(inverse_ref, residual, out_ref, parts, variables, slab)


def sweep_kernel(
    inverse_ref, residual_ref, x_ref, low_ref, high_ref, chooser_ref, lift_ref, jacobian_ref, out_ref,
    z_high, z_low, parts, *, variables, slab, last
):
    block = residual_ref.shape[1]
    faces = jacobian_ref.shape[2]
    lane = rows_of(x_ref.shape, 1)
    beside = jnp.where(lane < block // 2, high_ref[...], low_ref[...])
    x_high, x_low = split(jnp.concatenate([x_ref[...], beside], axis=1))
    rows = x_ref.shape[0]
    picked = mm(jnp.concatenate([x_high, x_low], axis=0), chooser_ref[...])
    picked = picked[:rows] + picked[rows:]
    for f in range(faces):
        part = [
            picked[v * slab : (v + 1) * slab, f * block : (f + 1) * block] for v in range(variables)
        ]
        for w in range(variables):
            z = part[0] * jacobian_ref[w, 0, f : f + 1, :]
            for v in range(1, variables):
                z += part[v] * jacobian_ref[w, v, f : f + 1, :]
            at = (w * faces + f) * slab
            z_high[at : at + slab, :], z_low[at : at + slab, :] = split(z)
    lift_high, lift_low = split(lift_ref[...])
    coupled = mm(lift_high, z_high[...]) + mm(lift_high, z_low[...]) + mm(lift_low, z_high[...])
    apply_inverse(
        inverse_ref, residual_ref[...] - coupled, out_ref, parts, variables, 0 if last else slab
    )


def per_device(
    fine_residual,
    fine_basis,
    coarse_basis,
    donor_cells,
    point_counts,
    solver_pos,
    block_inverse,
    face_jacobian,
    face_lift,
    face_offset,
):
    high_count = lax.axis_size("high")
    passing = lax.axis_size("low") * lax.axis_size("sub")
    owners = high_count * passing
    _, variables, fine = fine_residual.shape
    modes = coarse_basis.shape[1]
    donors = donor_cells.shape[1]
    block = solver_pos.shape[0]
    faces = face_offset.shape[0]
    full = modes * variables
    slab = -(-modes // 16) * 16
    depth = -(-full // 16) * 16

    capacity = max(2, 2 * fine * donors // owners)
    table = lax.all_to_all(
        jnp.broadcast_to(solver_pos[None, :], (owners, block)), WHOLE, 0, 0, tiled=True
    )
    pair = pl.pallas_call(
        pair_kernel,
        out_shape=jax.ShapeDtypeStruct((depth, donors * fine), F32),
        in_specs=[VMEM] * 4,
        out_specs=VMEM,
        name="donor_sums",
    )(
        fine_residual.transpose(1, 0, 2),
        fine_basis.T,
        coarse_basis.transpose(1, 0, 2),
        point_counts.T,
    )
    columns = pl.pallas_call(
        functools.partial(place_kernel, passing=passing, capacity=capacity),
        out_shape=jax.ShapeDtypeStruct((passing, full + 1, high_count * capacity), F32),
        in_specs=[VMEM] * 3,
        out_specs=VMEM,
        compiler_params=pltpu.CompilerParams(vmem_limit_bytes=32 * 2**20),
        name="place_columns",
    )(pair, donor_cells.T, table)
    columns = lax.all_to_all(columns, PLANE, 0, 0, tiled=True)
    blocks = pl.pallas_call(
        functools.partial(seat_kernel, capacity=capacity),
        out_shape=jax.ShapeDtypeStruct((high_count, full, block), F32),
        in_specs=[VMEM],
        out_specs=VMEM,
        compiler_params=pltpu.CompilerParams(vmem_limit_bytes=32 * 2**20),
        name="seat_columns",
    )(columns)
    blocks = lax.all_to_all(blocks, "high", 0, 0, tiled=True)

    chooser, lift = pl.pallas_call(
        functools.partial(prepare_kernel, variables=variables, slab=slab),
        out_shape=(
            jax.ShapeDtypeStruct((2 * block, faces * block), BF16),
            jax.ShapeDtypeStruct((full, variables * faces * slab), F32),
        ),
        in_specs=[VMEM] * 2,
        out_specs=(VMEM, VMEM),
        name="prepare",
    )(face_offset, face_lift.transpose(1, 0, 2))
    jacobian = face_jacobian.transpose(1, 2, 0, 3)

    forward = [(i, i + 1) for i in range(owners - 1)]
    backward = [(j, i) for i, j in forward]
    x, coarse_residual = pl.pallas_call(
        functools.partial(first_kernel, variables=variables, slab=slab),
        out_shape=(
            jax.ShapeDtypeStruct((variables * slab, block), F32),
            jax.ShapeDtypeStruct((full, block), F32),
        ),
        in_specs=[VMEM] * 2,
        out_specs=(VMEM, VMEM),
        scratch_shapes=[pltpu.VMEM((8 * full, block), F32)],
        name="first",
    )(block_inverse, blocks)
    for last in (False, True):
        low = lax.ppermute(x, WHOLE, forward)
        high = lax.ppermute(x, WHOLE, backward)
        shape = (full, block) if last else (variables * slab, block)
        x = pl.pallas_call(
            functools.partial(sweep_kernel, variables=variables, slab=slab, last=last),
            out_shape=jax.ShapeDtypeStruct(shape, F32),
            in_specs=[VMEM] * 8,
            out_specs=VMEM,
            scratch_shapes=[pltpu.VMEM((variables * faces * slab, block), BF16)] * 2
            + [pltpu.VMEM((8 * full, block), F32)],
            name="correction" if last else "second",
        )(block_inverse, coarse_residual, x, low, high, chooser, lift, jacobian)
    return coarse_residual, x


def solution(mesh):
    dom, sub = mesh.devices.shape
    low = 2 if dom % 2 == 0 else 1
    split_mesh = jax.sharding.Mesh(mesh.devices.reshape(dom // low, low, sub), WHOLE)
    in_specs = (
        P(None, None, WHOLE),
        P(),
        P(None, None, WHOLE),
        P(WHOLE, None),
        P(WHOLE, None),
        P(WHOLE),
        P(None, None, WHOLE),
        P(None, None, None, WHOLE),
        P(),
        P(None, WHOLE),
    )
    return jax.shard_map(
        per_device,
        mesh=split_mesh,
        in_specs=in_specs,
        out_specs=(P(None, WHOLE), P(None, WHOLE)),
        check_vma=False,
    )
```

```python
import functools
import jax
import jax.numpy as jnp
from jax import lax
from jax.experimental import pallas as pl
from jax.experimental.pallas import tpu as pltpu
from jax.sharding import PartitionSpec as P

F32 = jnp.float32
BF16 = jnp.bfloat16
PLANE = ("low", "sub")
WHOLE = ("high", "low", "sub")
VMEM = pl.BlockSpec(memory_space=pltpu.VMEM)


def split(x):
    high = x.astype(BF16)
    return high, (x - high.astype(F32)).astype(BF16)


def mm(a, b, ca=1, cb=0, precision=None):
    return lax.dot_general(
        a, b, (((ca,), (cb,)), ((), ())), precision=precision, preferred_element_type=F32
    )


def rows_of(iota_shape, dim):
    return lax.broadcasted_iota(jnp.int32, iota_shape, dim)


def call(kernel, name, shapes, args, scratch=(), megabytes=8):
    single = not isinstance(shapes, list)
    out = [jax.ShapeDtypeStruct(*shape) for shape in ([shapes] if single else shapes)]
    result = pl.pallas_call(
        kernel,
        out_shape=out,
        in_specs=[VMEM] * len(args),
        out_specs=[VMEM] * len(out),
        scratch_shapes=list(scratch),
        compiler_params=pltpu.CompilerParams(vmem_limit_bytes=megabytes * 2**20),
        name=name,
    )(*args)
    return result[0] if single else result


def rotate(blocks, axis):
    count = len(blocks)
    return [blocks[0]] + [
        lax.ppermute(blocks[d], axis, [(i, (i + d) % count) for i in range(count)])
        for d in range(1, count)
    ]


def pair_kernel(res_ref, basis_ref, coarse_ref, counts_ref, out_ref):
    variables, _, fine = res_ref.shape
    modes, points, _ = coarse_ref.shape
    donors = counts_ref.shape[0]
    basis_high, basis_low = split(basis_ref[...])
    res_high, res_low = split(jnp.concatenate([res_ref[v] for v in range(variables)], axis=1))
    values = mm(basis_high, res_high, 0, 0)
    values += mm(basis_high, res_low, 0, 0) + mm(basis_low, res_high, 0, 0)
    used = modes * variables
    out_ref[used:, :] = jnp.zeros((out_ref.shape[0] - used, out_ref.shape[1]), F32)
    width = 128
    point = rows_of((points, width), 0)
    for at in range(0, fine, width):
        upper = jnp.zeros((1, width), jnp.int32)
        inside = []
        for k in range(donors):
            lower = upper
            upper = lower + counts_ref[k : k + 1, at : at + width]
            inside.append((point >= lower) & (point < upper))
        for v in range(variables):
            column = v * fine + at
            value = values[:, column : column + width]
            masked = [jnp.where(inside[k], value, 0.0) for k in range(donors)]
            for a in range(modes):
                coarse = coarse_ref[a, :, at : at + width]
                row = a * variables + v
                for k in range(donors):
                    out_ref[row : row + 1, k * fine + at : k * fine + at + width] = jnp.sum(
                        coarse * masked[k], axis=0, keepdims=True
                    )


def place_kernel(pair_ref, donors_ref, out_ref, *, owners, block, passing, capacity):
    chunks, used, width = out_ref.shape
    donors, fine = donors_ref.shape
    total = donors * fine
    depth = pair_ref.shape[0]
    cell = jnp.concatenate([donors_ref[k : k + 1, :] for k in range(donors)], axis=1)
    owner = cell // block
    seat = (cell % block).astype(F32)
    lanes = 128
    parts = total // lanes
    mine = (rows_of((owners, total), 0) == owner).astype(F32)
    stacked = jnp.concatenate([mine[:, j * lanes : (j + 1) * lanes] for j in range(parts)], axis=0)
    earlier = (rows_of((lanes, lanes), 0) < rows_of((lanes, lanes), 1)).astype(F32)
    counter = jnp.concatenate([earlier, jnp.ones((lanes, lanes), F32)], axis=1)
    counted = mm(stacked.astype(BF16), counter.astype(BF16))
    before = jnp.zeros((owners, lanes), F32)
    ranks = []
    for j in range(parts):
        own = mine[:, j * lanes : (j + 1) * lanes]
        part = counted[j * owners : (j + 1) * owners]
        ranks.append(jnp.sum(own * (before + part[:, :lanes]), axis=0, keepdims=True))
        before += part[:, lanes:]
    rank = jnp.concatenate(ranks, axis=1).astype(jnp.int32)
    slot = (owner % passing) * width + (owner // passing) * capacity + rank
    slot = jnp.broadcast_to(slot.astype(F32), (lanes, total)).T
    rows = pair_ref[...]
    rows = jnp.where(rows_of(rows.shape, 0) == used - 1, seat, rows)
    both = jnp.concatenate(split(rows), axis=0)
    lane = rows_of((total, lanes), 1)
    for c in range(chunks):
        chooser = jnp.concatenate(
            [
                (slot == (lane + (c * width + j)).astype(F32)).astype(F32).astype(BF16)
                for j in range(0, width, lanes)
            ],
            axis=1,
        )
        placed = mm(both, chooser)
        out_ref[c] = placed[:used] + placed[depth : depth + used]


def seat_kernel(columns_ref, *refs, capacity):
    out_refs, scratch = refs[:-1], refs[-1]
    sources, _, _ = columns_ref.shape
    count, full, block = scratch.shape
    for h in range(count):
        got = jnp.concatenate(
            [columns_ref[s, :, h * capacity : (h + 1) * capacity] for s in range(sources)], axis=1
        )
        seat = got[full : full + 1, :]
        chooser = (rows_of((block, got.shape[1]), 0).astype(F32) == seat).astype(F32).astype(BF16)
        high, low = split(got)
        scratch[h] = (mm(high, chooser, 1, 1) + mm(low, chooser, 1, 1))[:full]
    if len(out_refs) == 1:
        out_refs[0][...] = scratch[...]
    else:
        here = lax.axis_index("high")
        for d in range(count):
            out_refs[d][...] = scratch[lax.rem(here + d, count)]


def renumber_kernel(place_ref, *refs):
    block_refs, out_ref = refs[:-1], refs[-1]
    block = place_ref.shape[1]
    if len(block_refs) == 1:
        total = block_refs[0][0]
        for h in range(1, block_refs[0].shape[0]):
            total += block_refs[0][h]
    else:
        total = block_refs[0][...]
        for ref in block_refs[1:]:
            total += ref[...]
    full = total.shape[0]
    place = place_ref[...]
    chooser = (rows_of((block, block), 0) == place % block).astype(F32).astype(BF16)
    high, low = split(total)
    out_ref[:full, :] = mm(high, chooser, 1, 1) + mm(low, chooser, 1, 1)
    out_ref[full:, :] = (place // block).astype(F32)


def prepare_kernel(offset_ref, lift_ref, chooser_ref, lift_out_ref, *, variables, slab):
    faces, block = offset_ref.shape
    modes = lift_ref.shape[0]
    own = rows_of((1, block), 1)
    row = rows_of((2 * block, block), 0)
    for f in range(faces):
        offset = offset_ref[f : f + 1, :]
        there = own + offset
        source = jnp.where(there < 0, there + 2 * block, there)
        source = jnp.where(offset != 0, source, -1)
        chooser_ref[:, f * block : (f + 1) * block] = (row == source).astype(F32).astype(BF16)
    width = variables * faces * slab
    column = rows_of((modes, width), 1)
    mode = rows_of((modes, width), 0)
    spread = jnp.zeros((modes, width), F32)
    for f in range(faces):
        put = (column % slab == mode) & ((column // slab) % faces == f)
        spread += mm(lift_ref[:, f, :], put.astype(F32), 1, 0, lax.Precision.HIGHEST)
    full = modes * variables
    expand = (rows_of((full, modes), 0) // variables == rows_of((full, modes), 1)).astype(F32)
    lifted = mm(expand, spread, 1, 0, lax.Precision.HIGHEST)
    keep = rows_of((full, width), 1) // (slab * faces) == rows_of((full, width), 0) % variables
    lift_out_ref[...] = jnp.where(keep, lifted, 0.0)


def apply_inverse(inverse_ref, field, out_ref, parts, variables, slab):
    full, _, block = inverse_ref.shape
    for i in range(full):
        product = inverse_ref[i] * field
        partial = product[0:8]
        for j in range(8, full - 7, 8):
            partial += product[j : j + 8]
        rest = full % 8
        if rest:
            partial = jnp.concatenate([partial[:rest] + product[full - rest :], partial[rest:]], axis=0)
        parts[i * 8 : i * 8 + 8, :] = partial
    row = rows_of((out_ref.shape[0], 8 * full), 0)
    source = rows_of((out_ref.shape[0], 8 * full), 1) // 8
    target = (source % variables) * slab + source // variables if slab else source
    adder = (row == target).astype(F32).astype(BF16)
    high, low = split(parts[...])
    out_ref[...] = mm(adder, high) + mm(adder, low)


def first_kernel(inverse_ref, *refs, variables, slab, subs):
    block_refs, (out_ref, total_ref, parts) = refs[:-3], refs[-3:]
    full = total_ref.shape[0]
    owner = lax.axis_index("high") * lax.axis_size("low") + lax.axis_index("low")
    owner = (owner * subs + lax.axis_index("sub")).astype(F32)
    residual = jnp.zeros(total_ref.shape, F32)
    for ref in block_refs:
        residual += jnp.where(ref[full:, :] == owner, ref[:full, :], 0.0)
    total_ref[...] = residual
    apply_inverse(inverse_ref, residual, out_ref, parts, variables, slab)


def sweep_kernel(
    inverse_ref, residual_ref, x_ref, low_ref, high_ref, chooser_ref, lift_ref, jacobian_ref, out_ref,
    z_high, z_low, parts, *, variables, slab, last
):
    block = residual_ref.shape[1]
    faces = jacobian_ref.shape[2]
    lane = rows_of(x_ref.shape, 1)
    beside = jnp.where(lane < block // 2, high_ref[...], low_ref[...])
    x_high, x_low = split(jnp.concatenate([x_ref[...], beside], axis=1))
    rows = x_ref.shape[0]
    picked = mm(jnp.concatenate([x_high, x_low], axis=0), chooser_ref[...])
    picked = picked[:rows] + picked[rows:]
    for f in range(faces):
        part = [
            picked[v * slab : (v + 1) * slab, f * block : (f + 1) * block] for v in range(variables)
        ]
        for w in range(variables):
            z = part[0] * jacobian_ref[w, 0, f : f + 1, :]
            for v in range(1, variables):
                z += part[v] * jacobian_ref[w, v, f : f + 1, :]
            at = (w * faces + f) * slab
            z_high[at : at + slab, :], z_low[at : at + slab, :] = split(z)
    lift_high, lift_low = split(lift_ref[...])
    coupled = mm(lift_high, z_high[...]) + mm(lift_high, z_low[...]) + mm(lift_low, z_high[...])
    apply_inverse(
        inverse_ref, residual_ref[...] - coupled, out_ref, parts, variables, 0 if last else slab
    )


def per_device(
    fine_residual,
    fine_basis,
    coarse_basis,
    donor_cells,
    point_counts,
    solver_pos,
    block_inverse,
    face_jacobian,
    face_lift,
    face_offset,
):
    high_count = lax.axis_size("high")
    passing = lax.axis_size("low") * lax.axis_size("sub")
    owners = high_count * passing
    _, variables, fine = fine_residual.shape
    modes = coarse_basis.shape[1]
    donors = donor_cells.shape[1]
    block = solver_pos.shape[0]
    faces = face_offset.shape[0]
    full = modes * variables
    slab = -(-modes // 16) * 16
    depth = -(-full // 16) * 16

    capacity = max(2, 2 * fine * donors // owners)
    subs = lax.axis_size("sub")
    pair = call(
        pair_kernel,
        "donor_sums",
        ((depth, donors * fine), F32),
        (
            fine_residual.transpose(1, 0, 2),
            fine_basis.T,
            coarse_basis.transpose(1, 0, 2),
            point_counts.T,
        ),
    )
    columns = call(
        functools.partial(
            place_kernel, owners=owners, block=block, passing=passing, capacity=capacity
        ),
        "place_columns",
        ((passing, full + 1, high_count * capacity), F32),
        (pair, donor_cells.T),
        megabytes=24,
    )
    columns = lax.all_to_all(columns, PLANE, 0, 0, tiled=True)
    few = high_count <= 8
    blocks = call(
        functools.partial(seat_kernel, capacity=capacity),
        "seat_columns",
        [((full, block), F32)] * high_count if few else [((high_count, full, block), F32)],
        (columns,),
        [pltpu.VMEM((high_count, full, block), F32)],
        megabytes=24,
    )
    if few:
        blocks = rotate(blocks, "high")
    else:
        blocks = [lax.all_to_all(blocks[0], "high", 0, 0, tiled=True)]
    whole = call(
        renumber_kernel, "renumber", ((full + 1, block), F32), (solver_pos[None, :], *blocks)
    )
    blocks = rotate([whole] * subs, "sub")

    chooser, lift = call(
        functools.partial(prepare_kernel, variables=variables, slab=slab),
        "prepare",
        [((2 * block, faces * block), BF16), ((full, variables * faces * slab), F32)],
        (face_offset, face_lift.transpose(1, 0, 2)),
    )
    jacobian = face_jacobian.transpose(1, 2, 0, 3)

    forward = [(i, i + 1) for i in range(owners - 1)]
    backward = [(j, i) for i, j in forward]
    parts = pltpu.VMEM((8 * full, block), F32)
    x, coarse_residual = call(
        functools.partial(first_kernel, variables=variables, slab=slab, subs=subs),
        "first",
        [((variables * slab, block), F32), ((full, block), F32)],
        (block_inverse, *blocks),
        [parts],
    )
    for last in (False, True):
        low = lax.ppermute(x, WHOLE, forward)
        high = lax.ppermute(x, WHOLE, backward)
        x = call(
            functools.partial(sweep_kernel, variables=variables, slab=slab, last=last),
            "correction" if last else "second",
            ((full, block) if last else (variables * slab, block), F32),
            (block_inverse, coarse_residual, x, low, high, chooser, lift, jacobian),
            [pltpu.VMEM((variables * faces * slab, block), BF16)] * 2 + [parts],
        )
    return coarse_residual, x


def solution(mesh):
    dom, sub = mesh.devices.shape
    low = 2 if dom % 2 == 0 else 1
    split_mesh = jax.sharding.Mesh(mesh.devices.reshape(dom // low, low, sub), WHOLE)
    in_specs = (
        P(None, None, WHOLE),
        P(),
        P(None, None, WHOLE),
        P(WHOLE, None),
        P(WHOLE, None),
        P(WHOLE),
        P(None, None, WHOLE),
        P(None, None, None, WHOLE),
        P(),
        P(None, WHOLE),
    )
    return jax.shard_map(
        per_device,
        mesh=split_mesh,
        in_specs=in_specs,
        out_specs=(P(None, WHOLE), P(None, WHOLE)),
        check_vma=False,
    )
```

```python
import functools
import jax
import jax.numpy as jnp
from jax import lax
from jax.experimental import pallas as pl
from jax.experimental.pallas import tpu as pltpu
from jax.sharding import PartitionSpec as P

F32 = jnp.float32
BF16 = jnp.bfloat16
PLANE = ("low", "sub")
WHOLE = ("high", "low", "sub")
VMEM = pl.BlockSpec(memory_space=pltpu.VMEM)


def split(x):
    high = x.astype(BF16)
    return high, (x - high.astype(F32)).astype(BF16)


def mm(a, b, ca=1, cb=0, precision=None):
    return lax.dot_general(
        a, b, (((ca,), (cb,)), ((), ())), precision=precision, preferred_element_type=F32
    )


def rows_of(iota_shape, dim):
    return lax.broadcasted_iota(jnp.int32, iota_shape, dim)


def call(kernel, name, shapes, args, scratch=(), megabytes=8):
    single = not isinstance(shapes, list)
    out = [jax.ShapeDtypeStruct(*shape) for shape in ([shapes] if single else shapes)]
    result = pl.pallas_call(
        kernel,
        out_shape=out,
        in_specs=[VMEM] * len(args),
        out_specs=[VMEM] * len(out),
        scratch_shapes=list(scratch),
        compiler_params=pltpu.CompilerParams(vmem_limit_bytes=megabytes * 2**20),
        name=name,
    )(*args)
    return result[0] if single else result


def rotate(blocks, axis):
    count = len(blocks)
    return [blocks[0]] + [
        lax.ppermute(blocks[d], axis, [(i, (i + d) % count) for i in range(count)])
        for d in range(1, count)
    ]


def pair_kernel(res_ref, basis_ref, coarse_ref, counts_ref, out_ref):
    variables, _, fine = res_ref.shape
    modes, points, _ = coarse_ref.shape
    donors = counts_ref.shape[0]
    basis_high, basis_low = split(basis_ref[...])
    res_high, res_low = split(jnp.concatenate([res_ref[v] for v in range(variables)], axis=1))
    values = mm(basis_high, res_high, 0, 0)
    values += mm(basis_high, res_low, 0, 0) + mm(basis_low, res_high, 0, 0)
    used = modes * variables
    out_ref[used:, :] = jnp.zeros((out_ref.shape[0] - used, out_ref.shape[1]), F32)
    width = 128
    point = rows_of((points, width), 0)
    for at in range(0, fine, width):
        upper = jnp.zeros((1, width), jnp.int32)
        inside = []
        for k in range(donors):
            lower = upper
            upper = lower + counts_ref[k : k + 1, at : at + width]
            inside.append((point >= lower) & (point < upper))
        for v in range(variables):
            column = v * fine + at
            value = values[:, column : column + width]
            masked = [jnp.where(inside[k], value, 0.0) for k in range(donors)]
            for a in range(modes):
                coarse = coarse_ref[a, :, at : at + width]
                row = a * variables + v
                for k in range(donors):
                    out_ref[row : row + 1, k * fine + at : k * fine + at + width] = jnp.sum(
                        coarse * masked[k], axis=0, keepdims=True
                    )


def place_kernel(pair_ref, donors_ref, out_ref, *, owners, block, passing, capacity):
    chunks, used, width = out_ref.shape
    donors, fine = donors_ref.shape
    total = donors * fine
    depth = pair_ref.shape[0]
    cell = jnp.concatenate([donors_ref[k : k + 1, :] for k in range(donors)], axis=1)
    owner = cell // block
    seat = (cell % block).astype(F32)
    lanes = 128
    parts = total // lanes
    mine = (rows_of((owners, total), 0) == owner).astype(F32)
    stacked = jnp.concatenate([mine[:, j * lanes : (j + 1) * lanes] for j in range(parts)], axis=0)
    earlier = (rows_of((lanes, lanes), 0) < rows_of((lanes, lanes), 1)).astype(F32)
    counter = jnp.concatenate([earlier, jnp.ones((lanes, lanes), F32)], axis=1)
    counted = mm(stacked.astype(BF16), counter.astype(BF16))
    before = jnp.zeros((owners, lanes), F32)
    ranks = []
    for j in range(parts):
        own = mine[:, j * lanes : (j + 1) * lanes]
        part = counted[j * owners : (j + 1) * owners]
        ranks.append(jnp.sum(own * (before + part[:, :lanes]), axis=0, keepdims=True))
        before += part[:, lanes:]
    rank = jnp.concatenate(ranks, axis=1).astype(jnp.int32)
    slot = (owner % passing) * width + (owner // passing) * capacity + rank
    slot = jnp.broadcast_to(slot.astype(F32), (lanes, total)).T
    rows = pair_ref[...]
    rows = jnp.where(rows_of(rows.shape, 0) == used - 1, seat, rows)
    both = jnp.concatenate(split(rows), axis=0)
    lane = rows_of((total, lanes), 1)
    for c in range(chunks):
        chooser = jnp.concatenate(
            [
                (slot == (lane + (c * width + j)).astype(F32)).astype(F32).astype(BF16)
                for j in range(0, width, lanes)
            ],
            axis=1,
        )
        placed = mm(both, chooser)
        out_ref[c] = placed[:used] + placed[depth : depth + used]


def seat_kernel(columns_ref, *refs, capacity):
    out_refs, scratch = refs[:-1], refs[-1]
    sources, _, _ = columns_ref.shape
    count, full, block = scratch.shape
    for h in range(count):
        got = jnp.concatenate(
            [columns_ref[s, :, h * capacity : (h + 1) * capacity] for s in range(sources)], axis=1
        )
        seat = got[full : full + 1, :]
        chooser = (rows_of((block, got.shape[1]), 0).astype(F32) == seat).astype(F32).astype(BF16)
        high, low = split(got)
        scratch[h] = (mm(high, chooser, 1, 1) + mm(low, chooser, 1, 1))[:full]
    if len(out_refs) == 1:
        out_refs[0][...] = scratch[...]
    else:
        here = lax.axis_index("high")
        for d in range(count):
            out_refs[d][...] = scratch[lax.rem(here + d, count)]


def renumber_kernel(place_ref, *refs):
    block_refs, out_ref = refs[:-1], refs[-1]
    block = place_ref.shape[1]
    if len(block_refs) == 1:
        total = block_refs[0][0]
        for h in range(1, block_refs[0].shape[0]):
            total += block_refs[0][h]
    else:
        total = block_refs[0][...]
        for ref in block_refs[1:]:
            total += ref[...]
    full = total.shape[0]
    place = place_ref[...]
    chooser = (rows_of((block, block), 0) == place % block).astype(F32).astype(BF16)
    high, low = split(total)
    out_ref[:full, :] = mm(high, chooser, 1, 1) + mm(low, chooser, 1, 1)
    out_ref[full:, :] = (place // block).astype(F32)


def pack_kernel(inverse_ref, jacobian_ref, offset_ref, right_ref, left_ref, scratch):
    full, _, block = inverse_ref.shape
    variables, _, faces, _ = jacobian_ref.shape
    half = full // 2
    lower = rows_of((full, block), 1) < block // 2

    def put(index, first, second):
        turned = pltpu.roll(second, block // 2, 1)
        right_ref[index] = jnp.where(lower, turned, first)
        left_ref[index] = jnp.where(lower, first, turned)

    for i in range(half):
        put(i, inverse_ref[i], inverse_ref[i + half])
    for w in range(variables):
        for v in range(variables):
            at = (w * variables + v) * faces
            scratch[at : at + faces, :] = jacobian_ref[w, v]
    rows = scratch.shape[0] // 2
    put(half, scratch[:rows, :], scratch[rows:, :])
    offset = offset_ref[...].astype(F32)
    for ref in (right_ref, left_ref):
        ref[half + 1] = jnp.zeros((full, block), F32)
        ref[half + 1, :faces, :] = offset


def prepare_kernel(
    offset_ref, lift_ref, low_ref, high_ref, chooser_ref, lift_out_ref, inverse_ref, jacobian_ref,
    *, variables, slab
):
    faces, block = offset_ref.shape
    modes = lift_ref.shape[0]
    full = modes * variables
    half = full // 2
    lower = rows_of((full, block), 1) < block // 2

    def take(index):
        first = jnp.where(lower, high_ref[index], low_ref[index])
        second = jnp.where(lower, low_ref[index], high_ref[index])
        return first, pltpu.roll(second, block // 2, 1)

    for i in range(half):
        inverse_ref[i], inverse_ref[i + half] = take(i)
    rows = jacobian_ref.shape[0] // 2
    jacobian_ref[:rows, :], jacobian_ref[rows:, :] = take(half)
    beside = jnp.where(lower, high_ref[half + 1], low_ref[half + 1])[:faces].astype(jnp.int32)
    lane = rows_of((1, block), 1)
    row = rows_of((2 * block, block), 0)
    for t, offsets in enumerate((offset_ref[...], beside)):
        for f in range(faces):
            offset = offsets[f : f + 1, :]
            source = jnp.where(offset != 0, (lane + (t * block) + offset) & (2 * block - 1), -1)
            at = (t * faces + f) * block
            chooser_ref[:, at : at + block] = (row == source).astype(F32).astype(BF16)
    width = variables * faces * slab
    column = rows_of((modes, width), 1)
    mode = rows_of((modes, width), 0)
    spread = jnp.zeros((modes, width), F32)
    for f in range(faces):
        put = (column % slab == mode) & ((column // slab) % faces == f)
        spread += mm(lift_ref[:, f, :], put.astype(F32), 1, 0, lax.Precision.HIGHEST)
    expand = (rows_of((full, modes), 0) // variables == rows_of((full, modes), 1)).astype(F32)
    lifted = mm(expand, spread, 1, 0, lax.Precision.HIGHEST)
    keep = rows_of((full, width), 1) // (slab * faces) == rows_of((full, width), 0) % variables
    lift_out_ref[...] = jnp.where(keep, lifted, 0.0)


def apply_inverse(inverse_ref, field, parts, variables, slab):
    full, _, block = inverse_ref.shape
    for i in range(full):
        product = inverse_ref[i] * field
        partial = product[0:8]
        for j in range(8, full - 7, 8):
            partial += product[j : j + 8]
        rest = full % 8
        if rest:
            partial = jnp.concatenate([partial[:rest] + product[full - rest :], partial[rest:]], axis=0)
        parts[i * 8 : i * 8 + 8, :] = partial
    depth = variables * slab if slab else full
    row = rows_of((depth, 8 * full), 0)
    source = rows_of((depth, 8 * full), 1) // 8
    target = (source % variables) * slab + source // variables if slab else source
    adder = (row == target).astype(F32).astype(BF16)
    high, low = split(parts[...])
    return mm(adder, high) + mm(adder, low)


def pick_kernel(*refs, subs):
    block_refs, (own_ref, beside_ref) = refs[:-2], refs[-2:]
    full, block = own_ref.shape
    owner = lax.axis_index("high") * lax.axis_size("low") + lax.axis_index("low")
    owner = (owner * subs + lax.axis_index("sub")).astype(F32)
    near = owner + jnp.where(rows_of((1, block), 1) < block // 2, 1.0, -1.0)
    own = jnp.zeros((full, block), F32)
    beside = jnp.zeros((full, block), F32)
    for ref in block_refs:
        whose = ref[full:, :]
        own += jnp.where(whose == owner, ref[:full, :], 0.0)
        beside += jnp.where(whose == near, ref[:full, :], 0.0)
    own_ref[...] = own
    beside_ref[...] = beside


def first_kernel(inverse_ref, residual_ref, out_ref, parts, *, variables, slab):
    out_ref[...] = apply_inverse(inverse_ref, residual_ref[...], parts, variables, slab)


def sweep_kernel(
    inverse_ref, inverse_beside_ref, jacobian_ref, jacobian_beside_ref, chooser_ref, lift_ref,
    residual_ref, beside_ref, swapped_ref, first_ref, out_ref, z_high, z_low, parts,
    *, variables, slab
):
    full, block = residual_ref.shape
    faces = jacobian_ref.shape[2]
    lift_high, lift_low = split(lift_ref[...])
    sub = lax.axis_index("sub")
    lower = rows_of((1, block), 1) < block // 2
    mine = (lower & (sub == lax.axis_size("sub") - 1)) | (~lower & (sub == 0))
    residual_beside = jnp.where(mine, swapped_ref[...], beside_ref[...])
    rows = variables * slab

    def coupled(x, tiles):
        x = jnp.concatenate(split(x), axis=0)
        picked = mm(x, chooser_ref[:, : tiles * faces * block])
        picked = picked[:rows] + picked[rows:]
        for t in range(tiles):
            for f in range(faces):
                at = (t * faces + f) * block
                part = [picked[v * slab : (v + 1) * slab, at : at + block] for v in range(variables)]
                for w in range(variables):
                    z = jnp.zeros((slab, block), F32)
                    for v in range(variables):
                        if t:
                            line = (w * variables + v) * faces + f
                            weight = jacobian_beside_ref[line : line + 1, :]
                        else:
                            weight = jacobian_ref[w, v, f : f + 1, :]
                        z += part[v] * weight
                    line, column = (w * faces + f) * slab, t * block
                    z_high[line : line + slab, column : column + block], z_low[
                        line : line + slab, column : column + block
                    ] = split(z)
        width = tiles * block
        high, low = z_high[:, :width], z_low[:, :width]
        return mm(lift_high, high) + mm(lift_high, low) + mm(lift_low, high)

    first_beside = apply_inverse(inverse_beside_ref, residual_beside, parts, variables, slab)
    taken = coupled(jnp.concatenate([first_ref[...], first_beside], axis=1), 2)
    second = [
        apply_inverse(inverses, residual - taken[:, t * block : (t + 1) * block], parts, variables, slab)
        for t, (inverses, residual) in enumerate(
            ((inverse_ref, residual_ref[...]), (inverse_beside_ref, residual_beside))
        )
    ]
    taken = coupled(jnp.concatenate(second, axis=1), 1)
    out_ref[...] = apply_inverse(inverse_ref, residual_ref[...] - taken, parts, variables, 0)


def per_device(
    fine_residual,
    fine_basis,
    coarse_basis,
    donor_cells,
    point_counts,
    solver_pos,
    block_inverse,
    face_jacobian,
    face_lift,
    face_offset,
):
    high_count = lax.axis_size("high")
    passing = lax.axis_size("low") * lax.axis_size("sub")
    owners = high_count * passing
    _, variables, fine = fine_residual.shape
    modes = coarse_basis.shape[1]
    donors = donor_cells.shape[1]
    block = solver_pos.shape[0]
    faces = face_offset.shape[0]
    full = modes * variables
    slab = -(-modes // 16) * 16
    depth = -(-full // 16) * 16

    capacity = max(2, 2 * fine * donors // owners)
    subs = lax.axis_size("sub")
    pair = call(
        pair_kernel,
        "donor_sums",
        ((depth, donors * fine), F32),
        (
            fine_residual.transpose(1, 0, 2),
            fine_basis.T,
            coarse_basis.transpose(1, 0, 2),
            point_counts.T,
        ),
    )
    columns = call(
        functools.partial(
            place_kernel, owners=owners, block=block, passing=passing, capacity=capacity
        ),
        "place_columns",
        ((passing, full + 1, high_count * capacity), F32),
        (pair, donor_cells.T),
        megabytes=24,
    )
    columns = lax.all_to_all(columns, PLANE, 0, 0, tiled=True)
    few = high_count <= 8
    blocks = call(
        functools.partial(seat_kernel, capacity=capacity),
        "seat_columns",
        [((full, block), F32)] * high_count if few else [((high_count, full, block), F32)],
        (columns,),
        [pltpu.VMEM((high_count, full, block), F32)],
        megabytes=24,
    )
    if few:
        blocks = rotate(blocks, "high")
    else:
        blocks = [lax.all_to_all(blocks[0], "high", 0, 0, tiled=True)]
    whole = call(
        renumber_kernel, "renumber", ((full + 1, block), F32), (solver_pos[None, :], *blocks)
    )
    blocks = rotate([whole] * subs, "sub")

    forward = [(i, i + 1) for i in range(owners - 1)]
    backward = [(j, i) for i, j in forward]
    jacobian = face_jacobian.transpose(1, 2, 0, 3)
    lines = variables * variables * faces
    packed = ((full // 2 + 2, full, block), F32)
    to_right, to_left = call(
        pack_kernel,
        "pack",
        [packed, packed],
        (block_inverse, jacobian, face_offset),
        [pltpu.VMEM((lines, block), F32)],
    )
    low = lax.ppermute(to_right, WHOLE, forward)
    high = lax.ppermute(to_left, WHOLE, backward)
    chooser, lift, inverse_beside, jacobian_beside = call(
        functools.partial(prepare_kernel, variables=variables, slab=slab),
        "prepare",
        [
            ((2 * block, 2 * faces * block), BF16),
            ((full, variables * faces * slab), F32),
            ((full, full, block), F32),
            ((lines, block), F32),
        ],
        (face_offset, face_lift.transpose(1, 0, 2), low, high),
    )

    coarse_residual, beside = call(
        functools.partial(pick_kernel, subs=subs),
        "pick",
        [((full, block), F32)] * 2,
        blocks,
    )
    ends = [(i, i + 1) for i in range(subs - 1, owners - 1, subs)]
    swapped = lax.ppermute(coarse_residual, WHOLE, ends + [(j, i) for i, j in ends])
    parts = pltpu.VMEM((8 * full, block), F32)
    first = call(
        functools.partial(first_kernel, variables=variables, slab=slab),
        "first",
        ((variables * slab, block), F32),
        (block_inverse, coarse_residual),
        [parts],
    )
    x = call(
        functools.partial(sweep_kernel, variables=variables, slab=slab),
        "sweeps",
        ((full, block), F32),
        (
            block_inverse,
            inverse_beside,
            jacobian,
            jacobian_beside,
            chooser,
            lift,
            coarse_residual,
            beside,
            swapped,
            first,
        ),
        [pltpu.VMEM((variables * faces * slab, 2 * block), BF16)] * 2 + [parts],
    )
    return coarse_residual, x


def solution(mesh):
    dom, sub = mesh.devices.shape
    low = 2 if dom % 2 == 0 else 1
    split_mesh = jax.sharding.Mesh(mesh.devices.reshape(dom // low, low, sub), WHOLE)
    in_specs = (
        P(None, None, WHOLE),
        P(),
        P(None, None, WHOLE),
        P(WHOLE, None),
        P(WHOLE, None),
        P(WHOLE),
        P(None, None, WHOLE),
        P(None, None, None, WHOLE),
        P(),
        P(None, WHOLE),
    )
    return jax.shard_map(
        per_device,
        mesh=split_mesh,
        in_specs=in_specs,
        out_specs=(P(None, WHOLE), P(None, WHOLE)),
        check_vma=False,
    )
```

```python
import functools
import jax
import jax.numpy as jnp
from jax import lax
from jax.experimental import pallas as pl
from jax.experimental.pallas import tpu as pltpu
from jax.sharding import PartitionSpec as P

F32 = jnp.float32
BF16 = jnp.bfloat16
PLANE = ("low", "sub")
WHOLE = ("high", "low", "sub")
VMEM = pl.BlockSpec(memory_space=pltpu.VMEM)


def split(x):
    high = x.astype(BF16)
    return high, (x - high.astype(F32)).astype(BF16)


def mm(a, b, ca=1, cb=0, precision=None):
    return lax.dot_general(
        a, b, (((ca,), (cb,)), ((), ())), precision=precision, preferred_element_type=F32
    )


def rows_of(iota_shape, dim):
    return lax.broadcasted_iota(jnp.int32, iota_shape, dim)


def call(kernel, name, shapes, args, scratch=(), megabytes=8, spec=VMEM):
    single = not isinstance(shapes, list)
    out = [jax.ShapeDtypeStruct(*shape) for shape in ([shapes] if single else shapes)]
    result = pl.pallas_call(
        kernel,
        out_shape=out,
        in_specs=[spec] * len(args),
        out_specs=[VMEM] * len(out),
        scratch_shapes=list(scratch),
        compiler_params=pltpu.CompilerParams(vmem_limit_bytes=megabytes * 2**20),
        name=name,
    )(*args)
    return result[0] if single else result


def swap_all(blocks, axis):
    count = len(blocks)
    return [blocks[0]] + [
        lax.ppermute(blocks[d], axis, [(i, i ^ d) for i in range(count)]) for d in range(1, count)
    ]


def free_columns(owner, owners, passing, capacity, width):
    lanes = 128
    total = owner.shape[1]
    parts = total // lanes
    mine = (rows_of((owners, total), 0) == owner).astype(F32)
    stacked = jnp.concatenate([mine[:, j * lanes : (j + 1) * lanes] for j in range(parts)], axis=0)
    earlier = (rows_of((lanes, lanes), 0) < rows_of((lanes, lanes), 1)).astype(F32)
    counter = jnp.concatenate([earlier, jnp.ones((lanes, lanes), F32)], axis=1)
    counted = mm(stacked.astype(BF16), counter.astype(BF16))
    before = jnp.zeros((owners, lanes), F32)
    ranks = []
    for j in range(parts):
        own = mine[:, j * lanes : (j + 1) * lanes]
        part = counted[j * owners : (j + 1) * owners]
        ranks.append(jnp.sum(own * (before + part[:, :lanes]), axis=0, keepdims=True))
        before += part[:, lanes:]
    rank = jnp.concatenate(ranks, axis=1).astype(jnp.int32)
    return (owner % passing) * width + (owner // passing) * capacity + rank


def restrict_kernel(
    res_hbm, basis_hbm, coarse_hbm, counts_hbm, donors_hbm, out_ref,
    res_ref, basis_ref, coarse_ref, counts_ref, donors_ref, pair_ref, sems,
    *, owners, block, passing, capacity
):
    variables, _, fine = res_ref.shape
    modes, points, _ = coarse_ref.shape
    donors = counts_ref.shape[0]
    chunks, used, width = out_ref.shape
    full = modes * variables
    depth = pair_ref.shape[0]
    total = donors * fine
    lanes = 128

    steps = range(0, fine, lanes)
    small = [(donors_hbm, donors_ref), (basis_hbm, basis_ref), (res_hbm, res_ref), (counts_hbm, counts_ref)]
    large = [
        (coarse_hbm.at[:, :, at : at + lanes], coarse_ref.at[:, :, at : at + lanes]) for at in steps
    ]
    copies = [
        pltpu.make_async_copy(source, target, sems.at[i])
        for i, (source, target) in enumerate(small + large)
    ]
    for copy in copies:
        copy.start()

    copies[0].wait()
    cell = jnp.concatenate([donors_ref[k : k + 1, :] for k in range(donors)], axis=1)
    pair_ref[full:, :] = jnp.zeros((depth - full, total), F32)
    pair_ref[full : full + 1, :] = (cell % block).astype(F32)
    slot = free_columns(cell // block, owners, passing, capacity, width)
    slot = jnp.broadcast_to(slot.astype(F32), (lanes, total)).T

    copies[1].wait()
    copies[2].wait()
    basis_high, basis_low = split(basis_ref[...])
    res_high, res_low = split(jnp.concatenate([res_ref[v] for v in range(variables)], axis=1))
    values = mm(basis_high, res_high, 0, 0)
    values += mm(basis_high, res_low, 0, 0) + mm(basis_low, res_high, 0, 0)

    copies[3].wait()
    point = rows_of((points, lanes), 0)
    for i, at in enumerate(steps):
        copies[4 + i].wait()
        upper = jnp.zeros((1, lanes), jnp.int32)
        inside = []
        for k in range(donors):
            lower = upper
            upper = lower + counts_ref[k : k + 1, at : at + lanes]
            inside.append((point >= lower) & (point < upper))
        for v in range(variables):
            column = v * fine + at
            value = values[:, column : column + lanes]
            masked = [jnp.where(inside[k], value, 0.0) for k in range(donors)]
            for a in range(modes):
                coarse = coarse_ref[a, :, at : at + lanes]
                row = a * variables + v
                for k in range(donors):
                    pair_ref[row : row + 1, k * fine + at : k * fine + at + lanes] = jnp.sum(
                        coarse * masked[k], axis=0, keepdims=True
                    )

    both = jnp.concatenate(split(pair_ref[...]), axis=0)
    lane = rows_of((total, lanes), 1)
    for c in range(chunks):
        chooser = jnp.concatenate(
            [
                (slot == (lane + (c * width + j)).astype(F32)).astype(F32).astype(BF16)
                for j in range(0, width, lanes)
            ],
            axis=1,
        )
        placed = mm(both, chooser)
        out_ref[c] = placed[:used] + placed[depth : depth + used]


def seat_kernel(columns_ref, *refs, capacity):
    out_refs, scratch = refs[:-1], refs[-1]
    sources, _, _ = columns_ref.shape
    count, full, block = scratch.shape
    for h in range(count):
        got = jnp.concatenate(
            [columns_ref[s, :, h * capacity : (h + 1) * capacity] for s in range(sources)], axis=1
        )
        seat = got[full : full + 1, :]
        chooser = (rows_of((block, got.shape[1]), 0).astype(F32) == seat).astype(F32).astype(BF16)
        high, low = split(got)
        scratch[h] = (mm(high, chooser, 1, 1) + mm(low, chooser, 1, 1))[:full]
    if len(out_refs) == 1:
        out_refs[0][...] = scratch[...]
    else:
        here = lax.axis_index("high")
        for d in range(count):
            out_refs[d][...] = scratch[here ^ d]


def renumber_kernel(place_ref, *refs):
    block_refs, out_ref = refs[:-1], refs[-1]
    block = place_ref.shape[1]
    if len(block_refs) == 1:
        total = block_refs[0][0]
        for h in range(1, block_refs[0].shape[0]):
            total += block_refs[0][h]
    else:
        total = block_refs[0][...]
        for ref in block_refs[1:]:
            total += ref[...]
    full = total.shape[0]
    place = place_ref[...]
    chooser = (rows_of((block, block), 0) == place % block).astype(F32).astype(BF16)
    high, low = split(total)
    out_ref[:full, :] = mm(high, chooser, 1, 1) + mm(low, chooser, 1, 1)
    out_ref[full:, :] = (place // block).astype(F32)


def inner_is_left():
    return lax.axis_index("sub") % 2 == 1


def pack_kernel(after_ref, inverse_ref, jacobian_ref, offset_ref, inner_ref, outer_ref, scratch):
    del after_ref
    full, _, block = inverse_ref.shape
    variables, _, faces, _ = jacobian_ref.shape
    half = full // 2
    kept = (rows_of((full, block), 1) < block // 2) == inner_is_left()

    def put(index, first, second):
        turned = pltpu.roll(second, block // 2, 1)
        inner_ref[index] = jnp.where(kept, first, turned)
        outer_ref[index] = jnp.where(kept, turned, first)

    for i in range(half):
        put(i, inverse_ref[i], inverse_ref[i + half])
    for w in range(variables):
        for v in range(variables):
            at = (w * variables + v) * faces
            scratch[at : at + faces, :] = jacobian_ref[w, v]
    rows = scratch.shape[0] // 2
    put(half, scratch[:rows, :], scratch[rows:, :])
    offset = offset_ref[...].astype(F32)
    for ref in (inner_ref, outer_ref):
        ref[half + 1] = jnp.zeros((full, block), F32)
        ref[half + 1, :faces, :] = offset


def prepare_kernel(
    offset_ref, lift_ref, inner_ref, outer_ref, chooser_ref, lift_out_ref, inverse_ref, jacobian_ref,
    *, variables, slab
):
    faces, block = offset_ref.shape
    modes = lift_ref.shape[0]
    full = modes * variables
    half = full // 2
    from_inner = (rows_of((full, block), 1) >= block // 2) == inner_is_left()

    def take(index):
        first = jnp.where(from_inner, inner_ref[index], outer_ref[index])
        second = jnp.where(from_inner, outer_ref[index], inner_ref[index])
        return first, pltpu.roll(second, block // 2, 1)

    for i in range(half):
        inverse_ref[i], inverse_ref[i + half] = take(i)
    rows = jacobian_ref.shape[0] // 2
    jacobian_ref[:rows, :], jacobian_ref[rows:, :] = take(half)
    beside = jnp.where(from_inner, inner_ref[half + 1], outer_ref[half + 1])
    beside = beside[:faces].astype(jnp.int32)
    lane = rows_of((1, block), 1)
    row = rows_of((2 * block, block), 0)
    for t, offsets in enumerate((offset_ref[...], beside)):
        for f in range(faces):
            offset = offsets[f : f + 1, :]
            source = jnp.where(offset != 0, (lane + (t * block) + offset) & (2 * block - 1), -1)
            at = (t * faces + f) * block
            chooser_ref[:, at : at + block] = (row == source).astype(F32).astype(BF16)
    width = variables * faces * slab
    column = rows_of((modes, width), 1)
    mode = rows_of((modes, width), 0)
    spread = jnp.zeros((modes, width), F32)
    for f in range(faces):
        put = (column % slab == mode) & ((column // slab) % faces == f)
        spread += mm(lift_ref[:, f, :], put.astype(F32), 1, 0, lax.Precision.HIGHEST)
    expand = (rows_of((full, modes), 0) // variables == rows_of((full, modes), 1)).astype(F32)
    lifted = mm(expand, spread, 1, 0, lax.Precision.HIGHEST)
    keep = rows_of((full, width), 1) // (slab * faces) == rows_of((full, width), 0) % variables
    lift_out_ref[...] = jnp.where(keep, lifted, 0.0)


def apply_inverse(inverse_ref, field, parts, variables, slab):
    full, _, block = inverse_ref.shape
    for i in range(full):
        product = inverse_ref[i] * field
        partial = product[0:8]
        for j in range(8, full - 7, 8):
            partial += product[j : j + 8]
        rest = full % 8
        if rest:
            partial = jnp.concatenate([partial[:rest] + product[full - rest :], partial[rest:]], axis=0)
        parts[i * 8 : i * 8 + 8, :] = partial
    depth = variables * slab if slab else full
    row = rows_of((depth, 8 * full), 0)
    source = rows_of((depth, 8 * full), 1) // 8
    target = (source % variables) * slab + source // variables if slab else source
    adder = (row == target).astype(F32).astype(BF16)
    high, low = split(parts[...])
    return mm(adder, high) + mm(adder, low)


def pick_kernel(*refs, subs):
    block_refs, (own_ref, beside_ref) = refs[:-2], refs[-2:]
    full, block = own_ref.shape
    owner = lax.axis_index("high") * lax.axis_size("low") + lax.axis_index("low")
    owner = (owner * subs + lax.axis_index("sub")).astype(F32)
    near = owner + jnp.where(rows_of((1, block), 1) < block // 2, 1.0, -1.0)
    own = jnp.zeros((full, block), F32)
    beside = jnp.zeros((full, block), F32)
    for ref in block_refs:
        whose = ref[full:, :]
        own += jnp.where(whose == owner, ref[:full, :], 0.0)
        beside += jnp.where(whose == near, ref[:full, :], 0.0)
    own_ref[...] = own
    beside_ref[...] = beside


def first_kernel(inverse_ref, residual_ref, out_ref, parts, *, variables, slab):
    out_ref[...] = apply_inverse(inverse_ref, residual_ref[...], parts, variables, slab)


def sweep_kernel(
    inverse_ref, inverse_beside_ref, jacobian_ref, jacobian_beside_ref, chooser_ref, lift_ref,
    residual_ref, beside_ref, swapped_ref, first_ref, total_ref, out_ref, z_high, z_low, parts,
    *, variables, slab
):
    full, block = residual_ref.shape
    faces = jacobian_ref.shape[2]
    total_ref[...] = residual_ref[...]
    lift_high, lift_low = split(lift_ref[...])
    sub = lax.axis_index("sub")
    lower = rows_of((1, block), 1) < block // 2
    mine = (lower & (sub == lax.axis_size("sub") - 1)) | (~lower & (sub == 0))
    residual_beside = jnp.where(mine, swapped_ref[...], beside_ref[...])
    rows = variables * slab

    def coupled(x, tiles):
        x = jnp.concatenate(split(x), axis=0)
        picked = mm(x, chooser_ref[:, : tiles * faces * block])
        picked = picked[:rows] + picked[rows:]
        for t in range(tiles):
            for f in range(faces):
                at = (t * faces + f) * block
                part = [picked[v * slab : (v + 1) * slab, at : at + block] for v in range(variables)]
                for w in range(variables):
                    z = jnp.zeros((slab, block), F32)
                    for v in range(variables):
                        if t:
                            line = (w * variables + v) * faces + f
                            weight = jacobian_beside_ref[line : line + 1, :]
                        else:
                            weight = jacobian_ref[w, v, f : f + 1, :]
                        z += part[v] * weight
                    line, column = (w * faces + f) * slab, t * block
                    z_high[line : line + slab, column : column + block], z_low[
                        line : line + slab, column : column + block
                    ] = split(z)
        width = tiles * block
        high, low = z_high[:, :width], z_low[:, :width]
        return mm(lift_high, high) + mm(lift_high, low) + mm(lift_low, high)

    first_beside = apply_inverse(inverse_beside_ref, residual_beside, parts, variables, slab)
    taken = coupled(jnp.concatenate([first_ref[...], first_beside], axis=1), 2)
    second = [
        apply_inverse(inverses, residual - taken[:, t * block : (t + 1) * block], parts, variables, slab)
        for t, (inverses, residual) in enumerate(
            ((inverse_ref, residual_ref[...]), (inverse_beside_ref, residual_beside))
        )
    ]
    taken = coupled(jnp.concatenate(second, axis=1), 1)
    out_ref[...] = apply_inverse(inverse_ref, residual_ref[...] - taken, parts, variables, 0)


def per_device(
    fine_residual,
    fine_basis,
    coarse_basis,
    donor_cells,
    point_counts,
    solver_pos,
    block_inverse,
    face_jacobian,
    face_lift,
    face_offset,
):
    high_count = lax.axis_size("high")
    passing = lax.axis_size("low") * lax.axis_size("sub")
    owners = high_count * passing
    _, variables, fine = fine_residual.shape
    modes = coarse_basis.shape[1]
    donors = donor_cells.shape[1]
    block = solver_pos.shape[0]
    faces = face_offset.shape[0]
    full = modes * variables
    slab = -(-modes // 16) * 16
    depth = -(-full // 16) * 16

    capacity = max(2, 2 * fine * donors // owners)
    subs = lax.axis_size("sub")
    inputs = (
        fine_residual.transpose(1, 0, 2),
        fine_basis.T,
        coarse_basis.transpose(1, 0, 2),
        point_counts.T,
        donor_cells.T,
    )
    columns = call(
        functools.partial(
            restrict_kernel, owners=owners, block=block, passing=passing, capacity=capacity
        ),
        "restrict",
        ((passing, full + 1, high_count * capacity), F32),
        inputs,
        [pltpu.VMEM(x.shape, x.dtype) for x in inputs]
        + [
            pltpu.VMEM((depth, donors * fine), F32),
            pltpu.SemaphoreType.DMA((len(inputs) - 1 + fine // 128,)),
        ],
        megabytes=48,
        spec=pl.BlockSpec(memory_space=pl.ANY),
    )
    columns = lax.all_to_all(columns, PLANE, 0, 0, tiled=True)
    few = high_count <= 8
    blocks = call(
        functools.partial(seat_kernel, capacity=capacity),
        "seat_columns",
        [((full, block), F32)] * high_count if few else [((high_count, full, block), F32)],
        (columns,),
        [pltpu.VMEM((high_count, full, block), F32)],
        megabytes=24,
    )
    after = blocks[0]
    if few:
        blocks = swap_all(blocks, "high")
    else:
        blocks = [lax.all_to_all(blocks[0], "high", 0, 0, tiled=True)]
    whole = call(
        renumber_kernel, "renumber", ((full + 1, block), F32), (solver_pos[None, :], *blocks)
    )
    blocks = swap_all([whole] * subs, "sub")

    jacobian = face_jacobian.transpose(1, 2, 0, 3)
    lines = variables * variables * faces
    packed = ((full // 2 + 2, full, block), F32)
    to_inner, to_outer = call(
        pack_kernel,
        "pack",
        [packed, packed],
        (after, block_inverse, jacobian, face_offset),
        [pltpu.VMEM((lines, block), F32)],
    )
    inner = [(i, i ^ 1) for i in range(owners)]
    outer = [(i, i + 1) for i in range(1, owners - 1, 2)]
    outer += [(j, i) for i, j in outer]
    inner = lax.ppermute(to_inner, WHOLE, inner)
    outer = lax.ppermute(to_outer, WHOLE, outer)
    chooser, lift, inverse_beside, jacobian_beside = call(
        functools.partial(prepare_kernel, variables=variables, slab=slab),
        "prepare",
        [
            ((2 * block, 2 * faces * block), BF16),
            ((full, variables * faces * slab), F32),
            ((full, full, block), F32),
            ((lines, block), F32),
        ],
        (face_offset, face_lift.transpose(1, 0, 2), inner, outer),
    )

    residual, beside = call(
        functools.partial(pick_kernel, subs=subs),
        "pick",
        [((full, block), F32)] * 2,
        blocks,
    )
    ends = [(i, i + 1) for i in range(subs - 1, owners - 1, subs)]
    swapped = lax.ppermute(residual, WHOLE, ends + [(j, i) for i, j in ends])
    parts = pltpu.VMEM((8 * full, block), F32)
    first = call(
        functools.partial(first_kernel, variables=variables, slab=slab),
        "first",
        ((variables * slab, block), F32),
        (block_inverse, residual),
        [parts],
    )
    coarse_residual, x = call(
        functools.partial(sweep_kernel, variables=variables, slab=slab),
        "sweeps",
        [((full, block), F32)] * 2,
        (
            block_inverse,
            inverse_beside,
            jacobian,
            jacobian_beside,
            chooser,
            lift,
            residual,
            beside,
            swapped,
            first,
        ),
        [pltpu.VMEM((variables * faces * slab, 2 * block), BF16)] * 2 + [parts],
    )
    return coarse_residual, x


def solution(mesh):
    dom, sub = mesh.devices.shape
    low = 2 if dom % 2 == 0 else 1
    split_mesh = jax.sharding.Mesh(mesh.devices.reshape(dom // low, low, sub), WHOLE)
    in_specs = (
        P(None, None, WHOLE),
        P(),
        P(None, None, WHOLE),
        P(WHOLE, None),
        P(WHOLE, None),
        P(WHOLE),
        P(None, None, WHOLE),
        P(None, None, None, WHOLE),
        P(),
        P(None, WHOLE),
    )
    return jax.shard_map(
        per_device,
        mesh=split_mesh,
        in_specs=in_specs,
        out_specs=(P(None, WHOLE), P(None, WHOLE)),
        check_vma=False,
    )
```

```python
import functools
import jax
import jax.numpy as jnp
from jax import lax
from jax.experimental import pallas as pl
from jax.experimental.pallas import tpu as pltpu
from jax.sharding import PartitionSpec as P

F32 = jnp.float32
BF16 = jnp.bfloat16
PLANE = ("low", "sub")
WHOLE = ("high", "low", "sub")
VMEM = pl.BlockSpec(memory_space=pltpu.VMEM)


def split(x):
    high = x.astype(BF16)
    return high, (x - high.astype(F32)).astype(BF16)


def mm(a, b, ca=1, cb=0, precision=None):
    return lax.dot_general(
        a, b, (((ca,), (cb,)), ((), ())), precision=precision, preferred_element_type=F32
    )


def rows_of(iota_shape, dim):
    return lax.broadcasted_iota(jnp.int32, iota_shape, dim)


def call(kernel, name, shapes, args, scratch=(), megabytes=8, spec=VMEM):
    single = not isinstance(shapes, list)
    out = [jax.ShapeDtypeStruct(*shape) for shape in ([shapes] if single else shapes)]
    result = pl.pallas_call(
        kernel,
        out_shape=out,
        in_specs=[spec] * len(args),
        out_specs=[VMEM] * len(out),
        scratch_shapes=list(scratch),
        compiler_params=pltpu.CompilerParams(
            vmem_limit_bytes=megabytes * 2**20 if megabytes else None
        ),
        name=name,
    )(*args)
    return result[0] if single else result


def swap_all(blocks, axis):
    count = len(blocks)
    return [blocks[0]] + [
        lax.ppermute(blocks[d], axis, [(i, i ^ d) for i in range(count)]) for d in range(1, count)
    ]


def free_columns(owner, owners, passing, capacity, width):
    lanes = 128
    total = owner.shape[1]
    parts = total // lanes
    mine = (rows_of((owners, total), 0) == owner).astype(F32)
    stacked = jnp.concatenate([mine[:, j * lanes : (j + 1) * lanes] for j in range(parts)], axis=0)
    earlier = (rows_of((lanes, lanes), 0) < rows_of((lanes, lanes), 1)).astype(F32)
    counter = jnp.concatenate([earlier, jnp.ones((lanes, lanes), F32)], axis=1)
    counted = mm(stacked.astype(BF16), counter.astype(BF16))
    before = jnp.zeros((owners, lanes), F32)
    ranks = []
    for j in range(parts):
        own = mine[:, j * lanes : (j + 1) * lanes]
        part = counted[j * owners : (j + 1) * owners]
        ranks.append(jnp.sum(own * (before + part[:, :lanes]), axis=0, keepdims=True))
        before += part[:, lanes:]
    rank = jnp.concatenate(ranks, axis=1).astype(jnp.int32)
    return (owner % passing) * width + (owner // passing) * capacity + rank


def restrict_kernel(
    res_hbm, basis_hbm, coarse_hbm, counts_hbm, donors_hbm, out_ref,
    res_ref, basis_ref, coarse_ref, counts_ref, donors_ref, pair_ref, sems,
    *, owners, block, passing, capacity
):
    variables, _, fine = res_ref.shape
    modes, points, _ = coarse_ref.shape
    donors = counts_ref.shape[0]
    chunks, used, width = out_ref.shape
    full = modes * variables
    depth = pair_ref.shape[0]
    total = donors * fine
    lanes = 128

    steps = range(0, fine, lanes)
    small = [(donors_hbm, donors_ref), (basis_hbm, basis_ref), (res_hbm, res_ref), (counts_hbm, counts_ref)]
    large = [
        (coarse_hbm.at[:, :, at : at + lanes], coarse_ref.at[:, :, at : at + lanes]) for at in steps
    ]
    copies = [
        pltpu.make_async_copy(source, target, sems.at[i])
        for i, (source, target) in enumerate(small + large)
    ]
    for copy in copies:
        copy.start()

    copies[0].wait()
    cell = jnp.concatenate([donors_ref[k : k + 1, :] for k in range(donors)], axis=1)
    pair_ref[full:, :] = jnp.zeros((depth - full, total), F32)
    pair_ref[full : full + 1, :] = (cell % block).astype(F32)
    slot = free_columns(cell // block, owners, passing, capacity, width)
    slot = jnp.broadcast_to(slot.astype(F32), (lanes, total)).T

    copies[1].wait()
    copies[2].wait()
    basis_high, basis_low = split(basis_ref[...])
    res_high, res_low = split(jnp.concatenate([res_ref[v] for v in range(variables)], axis=1))
    values = mm(basis_high, res_high, 0, 0)
    values += mm(basis_high, res_low, 0, 0) + mm(basis_low, res_high, 0, 0)

    copies[3].wait()
    point = rows_of((points, lanes), 0)
    for i, at in enumerate(steps):
        copies[4 + i].wait()
        upper = jnp.zeros((1, lanes), jnp.int32)
        inside = []
        for k in range(donors):
            lower = upper
            upper = lower + counts_ref[k : k + 1, at : at + lanes]
            inside.append((point >= lower) & (point < upper))
        for v in range(variables):
            column = v * fine + at
            value = values[:, column : column + lanes]
            masked = [jnp.where(inside[k], value, 0.0) for k in range(donors)]
            for a in range(modes):
                coarse = coarse_ref[a, :, at : at + lanes]
                row = a * variables + v
                for k in range(donors):
                    pair_ref[row : row + 1, k * fine + at : k * fine + at + lanes] = jnp.sum(
                        coarse * masked[k], axis=0, keepdims=True
                    )

    both = jnp.concatenate(split(pair_ref[...]), axis=0)
    lane = rows_of((total, lanes), 1)
    for c in range(chunks):
        chooser = jnp.concatenate(
            [
                (slot == (lane + (c * width + j)).astype(F32)).astype(F32).astype(BF16)
                for j in range(0, width, lanes)
            ],
            axis=1,
        )
        placed = mm(both, chooser)
        out_ref[c] = placed[:used] + placed[depth : depth + used]


def seat_kernel(columns_ref, *refs, capacity):
    out_refs, scratch = refs[:-1], refs[-1]
    sources, _, _ = columns_ref.shape
    count, full, block = scratch.shape
    for h in range(count):
        got = jnp.concatenate(
            [columns_ref[s, :, h * capacity : (h + 1) * capacity] for s in range(sources)], axis=1
        )
        seat = got[full : full + 1, :]
        chooser = (rows_of((block, got.shape[1]), 0).astype(F32) == seat).astype(F32).astype(BF16)
        high, low = split(got)
        scratch[h] = (mm(high, chooser, 1, 1) + mm(low, chooser, 1, 1))[:full]
    if len(out_refs) == 1:
        out_refs[0][...] = scratch[...]
    else:
        here = lax.axis_index("high")
        for d in range(count):
            out_refs[d][...] = scratch[here ^ d]


def renumber_kernel(place_ref, *refs):
    block_refs, out_ref = refs[:-1], refs[-1]
    block = place_ref.shape[1]
    if len(block_refs) == 1:
        total = block_refs[0][0]
        for h in range(1, block_refs[0].shape[0]):
            total += block_refs[0][h]
    else:
        total = block_refs[0][...]
        for ref in block_refs[1:]:
            total += ref[...]
    full = total.shape[0]
    place = place_ref[...]
    chooser = (rows_of((block, block), 0) == place % block).astype(F32).astype(BF16)
    high, low = split(total)
    out_ref[:full, :] = mm(high, chooser, 1, 1) + mm(low, chooser, 1, 1)
    out_ref[full:, :] = (place // block).astype(F32)


def inner_is_left():
    return lax.axis_index("sub") % 2 == 1


def prepare_kernel(offset_ref, lift_ref, chooser_ref, lift_out_ref, *, variables, slab):
    faces, block = offset_ref.shape
    modes = lift_ref.shape[0]
    full = modes * variables
    lane = rows_of((1, block), 1)
    row = rows_of((2 * block, block), 0)
    for f in range(faces):
        offset = offset_ref[f : f + 1, :]
        source = jnp.where(offset != 0, (lane + offset) & (2 * block - 1), -1)
        chooser_ref[:, f * block : (f + 1) * block] = (row == source).astype(F32).astype(BF16)
    width = variables * faces * slab
    column = rows_of((modes, width), 1)
    mode = rows_of((modes, width), 0)
    spread = jnp.zeros((modes, width), F32)
    for f in range(faces):
        put = (column % slab == mode) & ((column // slab) % faces == f)
        spread += mm(lift_ref[:, f, :], put.astype(F32), 1, 0, lax.Precision.HIGHEST)
    expand = (rows_of((full, modes), 0) // variables == rows_of((full, modes), 1)).astype(F32)
    lifted = mm(expand, spread, 1, 0, lax.Precision.HIGHEST)
    keep = rows_of((full, width), 1) // (slab * faces) == rows_of((full, width), 0) % variables
    lift_out_ref[...] = jnp.where(keep, lifted, 0.0)


def apply_inverse(inverse_ref, field, parts, variables, slab):
    full, _, block = inverse_ref.shape
    for i in range(full):
        product = inverse_ref[i] * field
        partial = product[0:8]
        for j in range(8, full - 7, 8):
            partial += product[j : j + 8]
        rest = full % 8
        if rest:
            partial = jnp.concatenate([partial[:rest] + product[full - rest :], partial[rest:]], axis=0)
        parts[i * 8 : i * 8 + 8, :] = partial
    depth = variables * slab if slab else full
    row = rows_of((depth, 8 * full), 0)
    source = rows_of((depth, 8 * full), 1) // 8
    target = (source % variables) * slab + source // variables if slab else source
    adder = (row == target).astype(F32).astype(BF16)
    high, low = split(parts[...])
    return mm(adder, high) + mm(adder, low)


def first_kernel(inverse_ref, *refs, variables, slab, subs):
    block_refs, (total_ref, out_ref, parts) = refs[:-3], refs[-3:]
    full = total_ref.shape[0]
    owner = lax.axis_index("high") * lax.axis_size("low") + lax.axis_index("low")
    owner = (owner * subs + lax.axis_index("sub")).astype(F32)
    residual = jnp.zeros(total_ref.shape, F32)
    for ref in block_refs:
        residual += jnp.where(ref[full:, :] == owner, ref[:full, :], 0.0)
    total_ref[...] = residual
    out_ref[...] = apply_inverse(inverse_ref, residual, parts, variables, slab)


def sweep_kernel(
    inverse_ref, residual_ref, x_ref, inner_ref, outer_ref, chooser_ref, lift_ref, jacobian_ref, *refs,
    variables, slab, last
):
    *total_ref, out_ref, z_high, z_low, parts = refs
    if last:
        total_ref[0][...] = residual_ref[...]
    rows, block = x_ref.shape
    faces = jacobian_ref.shape[2]
    inner_is_left = lax.axis_index("sub") % 2 == 1
    from_inner = (rows_of((rows, block), 1) >= block // 2) == inner_is_left
    beside = jnp.where(from_inner, inner_ref[...], outer_ref[...])
    x = jnp.concatenate(split(jnp.concatenate([x_ref[...], beside], axis=1)), axis=0)
    picked = mm(x, chooser_ref[...])
    picked = picked[:rows] + picked[rows:]
    for f in range(faces):
        at = f * block
        part = [picked[v * slab : (v + 1) * slab, at : at + block] for v in range(variables)]
        for w in range(variables):
            z = part[0] * jacobian_ref[w, 0, f : f + 1, :]
            for v in range(1, variables):
                z += part[v] * jacobian_ref[w, v, f : f + 1, :]
            line = (w * faces + f) * slab
            z_high[line : line + slab, :], z_low[line : line + slab, :] = split(z)
    lift_high, lift_low = split(lift_ref[...])
    high, low = z_high[...], z_low[...]
    coupled = mm(lift_high, high) + mm(lift_high, low) + mm(lift_low, high)
    out_ref[...] = apply_inverse(
        inverse_ref, residual_ref[...] - coupled, parts, variables, 0 if last else slab
    )


def per_device(
    fine_residual,
    fine_basis,
    coarse_basis,
    donor_cells,
    point_counts,
    solver_pos,
    block_inverse,
    face_jacobian,
    face_lift,
    face_offset,
):
    high_count = lax.axis_size("high")
    passing = lax.axis_size("low") * lax.axis_size("sub")
    owners = high_count * passing
    _, variables, fine = fine_residual.shape
    modes = coarse_basis.shape[1]
    donors = donor_cells.shape[1]
    block = solver_pos.shape[0]
    faces = face_offset.shape[0]
    full = modes * variables
    slab = -(-modes // 16) * 16
    depth = -(-full // 16) * 16

    capacity = max(2, 2 * fine * donors // owners)
    subs = lax.axis_size("sub")
    inputs = (
        fine_residual.transpose(1, 0, 2),
        fine_basis.T,
        coarse_basis.transpose(1, 0, 2),
        point_counts.T,
        donor_cells.T,
    )
    columns = call(
        functools.partial(
            restrict_kernel, owners=owners, block=block, passing=passing, capacity=capacity
        ),
        "restrict",
        ((passing, full + 1, high_count * capacity), F32),
        inputs,
        [pltpu.VMEM(x.shape, x.dtype) for x in inputs]
        + [
            pltpu.VMEM((depth, donors * fine), F32),
            pltpu.SemaphoreType.DMA((len(inputs) - 1 + fine // 128,)),
        ],
        megabytes=None,
        spec=pl.BlockSpec(memory_space=pl.ANY),
    )
    columns = lax.all_to_all(columns, PLANE, 0, 0, tiled=True)
    few = high_count <= 8
    blocks = call(
        functools.partial(seat_kernel, capacity=capacity),
        "seat_columns",
        [((full, block), F32)] * high_count if few else [((high_count, full, block), F32)],
        (columns,),
        [pltpu.VMEM((high_count, full, block), F32)],
        megabytes=24,
    )
    if few:
        blocks = swap_all(blocks, "high")
    else:
        blocks = [lax.all_to_all(blocks[0], "high", 0, 0, tiled=True)]
    whole = call(
        renumber_kernel, "renumber", ((full + 1, block), F32), (solver_pos[None, :], *blocks)
    )
    blocks = swap_all([whole] * subs, "sub")

    jacobian = face_jacobian.transpose(1, 2, 0, 3)
    chooser, lift = call(
        functools.partial(prepare_kernel, variables=variables, slab=slab),
        "prepare",
        [((2 * block, faces * block), BF16), ((full, variables * faces * slab), F32)],
        (face_offset, face_lift.transpose(1, 0, 2)),
    )
    outer_pairs = [(i, i + 1) for i in range(1, owners - 1, 2)]
    outer_pairs += [(j, i) for i, j in outer_pairs]
    inner_pairs = [(i, i ^ 1) for i in range(owners)]
    parts = pltpu.VMEM((8 * full, block), F32)
    plain, sweep = ((full, block), F32), ((variables * slab, block), F32)
    residual, x = call(
        functools.partial(first_kernel, variables=variables, slab=slab, subs=subs),
        "first",
        [plain, sweep],
        (block_inverse, *blocks),
        [parts],
    )
    for last in (False, True):
        outer = lax.ppermute(x, WHOLE, outer_pairs)
        inner = lax.ppermute(x, WHOLE, inner_pairs)
        x = call(
            functools.partial(sweep_kernel, variables=variables, slab=slab, last=last),
            "correction" if last else "second",
            [plain, plain] if last else sweep,
            (block_inverse, residual, x, inner, outer, chooser, lift, jacobian),
            [pltpu.VMEM((variables * faces * slab, block), BF16)] * 2 + [parts],
        )
    return tuple(x)


def solution(mesh):
    dom, sub = mesh.devices.shape
    low = 2 if dom % 2 == 0 else 1
    split_mesh = jax.sharding.Mesh(mesh.devices.reshape(dom // low, low, sub), WHOLE)
    in_specs = (
        P(None, None, WHOLE),
        P(),
        P(None, None, WHOLE),
        P(WHOLE, None),
        P(WHOLE, None),
        P(WHOLE),
        P(None, None, WHOLE),
        P(None, None, None, WHOLE),
        P(),
        P(None, WHOLE),
    )
    return jax.shard_map(
        per_device,
        mesh=split_mesh,
        in_specs=in_specs,
        out_specs=(P(None, WHOLE), P(None, WHOLE)),
        check_vma=False,
    )
```

```python
import functools
import jax
import jax.numpy as jnp
from jax import lax
from jax.experimental import pallas as pl
from jax.experimental.pallas import tpu as pltpu
from jax.sharding import PartitionSpec as P

F32 = jnp.float32
BF16 = jnp.bfloat16
PLANE = ("low", "sub")
WHOLE = ("high", "low", "sub")
VMEM = pl.BlockSpec(memory_space=pltpu.VMEM)


def split(x):
    high = x.astype(BF16)
    return high, (x - high.astype(F32)).astype(BF16)


def mm(a, b, ca=1, cb=0, precision=None):
    return lax.dot_general(
        a, b, (((ca,), (cb,)), ((), ())), precision=precision, preferred_element_type=F32
    )


def rows_of(iota_shape, dim):
    return lax.broadcasted_iota(jnp.int32, iota_shape, dim)


def call(kernel, name, shapes, args, scratch=(), megabytes=8, spec=VMEM):
    single = not isinstance(shapes, list)
    out = [jax.ShapeDtypeStruct(*shape) for shape in ([shapes] if single else shapes)]
    result = pl.pallas_call(
        kernel,
        out_shape=out,
        in_specs=[spec] * len(args),
        out_specs=[VMEM] * len(out),
        scratch_shapes=list(scratch),
        compiler_params=pltpu.CompilerParams(
            vmem_limit_bytes=megabytes * 2**20 if megabytes else None
        ),
        name=name,
    )(*args)
    return result[0] if single else result


def swap_all(blocks, axis):
    count = len(blocks)
    return [blocks[0]] + [
        lax.ppermute(blocks[d], axis, [(i, i ^ d) for i in range(count)]) for d in range(1, count)
    ]


def free_columns(owner, owners, passing, capacity, width):
    lanes = 128
    total = owner.shape[1]
    parts = total // lanes
    mine = (rows_of((owners, total), 0) == owner).astype(F32)
    stacked = jnp.concatenate([mine[:, j * lanes : (j + 1) * lanes] for j in range(parts)], axis=0)
    earlier = (rows_of((lanes, lanes), 0) < rows_of((lanes, lanes), 1)).astype(F32)
    counter = jnp.concatenate([earlier, jnp.ones((lanes, lanes), F32)], axis=1)
    counted = mm(stacked.astype(BF16), counter.astype(BF16))
    before = jnp.zeros((owners, lanes), F32)
    ranks = []
    for j in range(parts):
        own = mine[:, j * lanes : (j + 1) * lanes]
        part = counted[j * owners : (j + 1) * owners]
        ranks.append(jnp.sum(own * (before + part[:, :lanes]), axis=0, keepdims=True))
        before += part[:, lanes:]
    rank = jnp.concatenate(ranks, axis=1).astype(jnp.int32)
    return (owner % passing) * width + (owner // passing) * capacity + rank


def restrict_kernel(
    res_hbm, basis_hbm, coarse_hbm, counts_hbm, donors_hbm, out_ref,
    res_ref, basis_ref, coarse_ref, counts_ref, donors_ref, masked_ref, pair_ref, sems,
    *, owners, block, passing, capacity, joint
):
    variables, _, fine = res_ref.shape
    modes, points, _ = coarse_ref.shape
    donors = counts_ref.shape[0]
    full = modes * variables
    depth = pair_ref.shape[0]
    total = donors * fine
    lanes = 128

    small = [(donors_hbm, donors_ref), (basis_hbm, basis_ref), (res_hbm, res_ref), (counts_hbm, counts_ref)]
    large = [(coarse_hbm.at[a], coarse_ref.at[a]) for a in range(modes)]
    copies = [
        pltpu.make_async_copy(source, target, sems.at[i])
        for i, (source, target) in enumerate(small + large)
    ]
    for copy in copies:
        copy.start()

    copies[0].wait()
    cell = jnp.concatenate([donors_ref[k : k + 1, :] for k in range(donors)], axis=1)
    pair_ref[full:, :] = jnp.zeros((depth - full, total), F32)
    pair_ref[full : full + 1, :] = (cell % block).astype(F32)
    width = capacity if joint else out_ref.shape[2]
    slot = free_columns(cell // block, owners, owners if joint else passing, capacity, width)
    slot = jnp.broadcast_to(slot.astype(F32), (lanes, total)).T

    copies[1].wait()
    copies[2].wait()
    basis_high, basis_low = split(basis_ref[...])
    res_high, res_low = split(jnp.concatenate([res_ref[v] for v in range(variables)], axis=1))
    values = mm(basis_high, res_high, 0, 0)
    values += mm(basis_high, res_low, 0, 0) + mm(basis_low, res_high, 0, 0)

    copies[3].wait()
    point = rows_of((points, fine), 0)
    upper = jnp.zeros((1, fine), jnp.int32)
    for k in range(donors):
        lower = upper
        upper = lower + counts_ref[k : k + 1, :]
        inside = (point >= lower) & (point < upper)
        for v in range(variables):
            masked_ref[v, k] = jnp.where(inside, values[:, v * fine : (v + 1) * fine], 0.0)

    for a in range(modes):
        copies[4 + a].wait()
        for at in range(0, fine, lanes):
            coarse = coarse_ref[a, :, at : at + lanes]
            for v in range(variables):
                row = a * variables + v
                for k in range(donors):
                    pair_ref[row : row + 1, k * fine + at : k * fine + at + lanes] = jnp.sum(
                        coarse * masked_ref[v, k, :, at : at + lanes], axis=0, keepdims=True
                    )

    both = jnp.concatenate(split(pair_ref[...]), axis=0)
    lane = rows_of((total, lanes), 1)

    def placed(first, columns):
        chooser = jnp.concatenate(
            [
                (slot == (lane + (first + j)).astype(F32)).astype(F32).astype(BF16)
                for j in range(0, columns, lanes)
            ],
            axis=1,
        )
        result = mm(both, chooser)
        return result[:depth] + result[depth:]

    if joint:
        half = depth // 2
        left = rows_of((half, lanes), 1) < capacity
        for first in range(0, owners * capacity, 2 * lanes):
            result = placed(first, 2 * lanes)
            for j in range(0, 2 * lanes, lanes):
                tile = result[:, j : j + lanes]
                turned = pltpu.roll(tile, capacity, 1)
                c = (first + j) // capacity
                out_ref[c] = jnp.where(left, tile[:half], turned[half:])
                out_ref[c + 1] = jnp.where(left, turned[:half], tile[half:])
    else:
        for c in range(out_ref.shape[0]):
            out_ref[c] = placed(c * width, width)[: out_ref.shape[1]]


def collect_kernel(place_ref, columns_ref, out_ref):
    sources, half, block = columns_ref.shape
    left = rows_of((half, block), 1) < block // 2
    upper, lower = [], []
    for s in range(0, sources, 2):
        one, two = columns_ref[s], columns_ref[s + 1]
        upper.append(jnp.where(left, one, pltpu.roll(two, block // 2, 1)))
        lower.append(jnp.where(left, pltpu.roll(one, block // 2, 1), two))
    upper, lower = jnp.concatenate(upper, axis=1), jnp.concatenate(lower, axis=1)
    full = out_ref.shape[0] - 1
    seat = lower[full - half : full - half + 1, :]
    chooser = (rows_of((block, seat.shape[1]), 0).astype(F32) == seat).astype(F32).astype(BF16)
    both = jnp.concatenate([*split(upper), *split(lower)], axis=0)
    total = mm(both, chooser, 1, 1)
    upper, lower = total[:half] + total[half : 2 * half], total[2 * half : 3 * half] + total[3 * half :]
    renumber(place_ref, jnp.concatenate([upper, lower], axis=0)[:full], out_ref)


def renumber(place_ref, total, out_ref):
    full, block = total.shape
    place = place_ref[...]
    chooser = (rows_of((block, block), 0) == place % block).astype(F32).astype(BF16)
    high, low = split(total)
    out_ref[:full, :] = mm(high, chooser, 1, 1) + mm(low, chooser, 1, 1)
    out_ref[full:, :] = (place // block).astype(F32)


def seat_kernel(columns_ref, out_ref, *, capacity):
    sources, _, _ = columns_ref.shape
    count, full, block = out_ref.shape
    for h in range(count):
        got = jnp.concatenate(
            [columns_ref[s, :, h * capacity : (h + 1) * capacity] for s in range(sources)], axis=1
        )
        seat = got[full : full + 1, :]
        chooser = (rows_of((block, got.shape[1]), 0).astype(F32) == seat).astype(F32).astype(BF16)
        high, low = split(got)
        out_ref[h] = (mm(high, chooser, 1, 1) + mm(low, chooser, 1, 1))[:full]


def renumber_kernel(place_ref, parts_ref, out_ref):
    total = parts_ref[0]
    for h in range(1, parts_ref.shape[0]):
        total += parts_ref[h]
    renumber(place_ref, total, out_ref)


def prepare_kernel(offset_ref, lift_ref, chooser_ref, lift_out_ref, *, variables, slab):
    faces, block = offset_ref.shape
    modes = lift_ref.shape[0]
    full = modes * variables
    lane = rows_of((1, block), 1)
    row = rows_of((2 * block, block), 0)
    for f in range(faces):
        offset = offset_ref[f : f + 1, :]
        source = jnp.where(offset != 0, (lane + offset) & (2 * block - 1), -1)
        chooser_ref[:, f * block : (f + 1) * block] = (row == source).astype(F32).astype(BF16)
    width = variables * faces * slab
    column = rows_of((modes, width), 1)
    mode = rows_of((modes, width), 0)
    spread = jnp.zeros((modes, width), F32)
    for f in range(faces):
        put = (column % slab == mode) & ((column // slab) % faces == f)
        spread += mm(lift_ref[:, f, :], put.astype(F32), 1, 0, lax.Precision.HIGHEST)
    expand = (rows_of((full, modes), 0) // variables == rows_of((full, modes), 1)).astype(F32)
    lifted = mm(expand, spread, 1, 0, lax.Precision.HIGHEST)
    keep = rows_of((full, width), 1) // (slab * faces) == rows_of((full, width), 0) % variables
    lift_out_ref[...] = jnp.where(keep, lifted, 0.0)


def apply_inverse(inverse_ref, field, parts, variables, slab):
    full, _, block = inverse_ref.shape
    for i in range(full):
        product = inverse_ref[i] * field
        partial = product[0:8]
        for j in range(8, full - 7, 8):
            partial += product[j : j + 8]
        rest = full % 8
        if rest:
            partial = jnp.concatenate([partial[:rest] + product[full - rest :], partial[rest:]], axis=0)
        parts[i * 8 : i * 8 + 8, :] = partial
    depth = variables * slab if slab else full
    row = rows_of((depth, 8 * full), 0)
    source = rows_of((depth, 8 * full), 1) // 8
    target = (source % variables) * slab + source // variables if slab else source
    adder = (row == target).astype(F32).astype(BF16)
    high, low = split(parts[...])
    return mm(adder, high) + mm(adder, low)


def first_kernel(inverse_ref, *refs, variables, slab, subs):
    block_refs, (total_ref, out_ref, parts) = refs[:-3], refs[-3:]
    full = total_ref.shape[0]
    owner = lax.axis_index("high") * lax.axis_size("low") + lax.axis_index("low")
    owner = (owner * subs + lax.axis_index("sub")).astype(F32)
    residual = jnp.zeros(total_ref.shape, F32)
    for ref in block_refs:
        residual += jnp.where(ref[full:, :] == owner, ref[:full, :], 0.0)
    total_ref[...] = residual
    out_ref[...] = apply_inverse(inverse_ref, residual, parts, variables, slab)


def sweep_kernel(
    inverse_ref, residual_ref, x_ref, inner_ref, outer_ref, chooser_ref, lift_ref, jacobian_ref, *refs,
    variables, slab, last
):
    *total_ref, out_ref, z_high, z_low, parts = refs
    if last:
        total_ref[0][...] = residual_ref[...]
    rows, block = x_ref.shape
    faces = jacobian_ref.shape[2]
    inner_is_left = lax.axis_index("sub") % 2 == 1
    from_inner = (rows_of((rows, block), 1) >= block // 2) == inner_is_left
    beside = jnp.where(from_inner, inner_ref[...], outer_ref[...])
    x = jnp.concatenate(split(jnp.concatenate([x_ref[...], beside], axis=1)), axis=0)
    picked = mm(x, chooser_ref[...])
    picked = picked[:rows] + picked[rows:]
    for f in range(faces):
        at = f * block
        part = [picked[v * slab : (v + 1) * slab, at : at + block] for v in range(variables)]
        for w in range(variables):
            z = part[0] * jacobian_ref[w, 0, f : f + 1, :]
            for v in range(1, variables):
                z += part[v] * jacobian_ref[w, v, f : f + 1, :]
            line = (w * faces + f) * slab
            z_high[line : line + slab, :], z_low[line : line + slab, :] = split(z)
    lift_high, lift_low = split(lift_ref[...])
    high, low = z_high[...], z_low[...]
    coupled = mm(lift_high, high) + mm(lift_high, low) + mm(lift_low, high)
    out_ref[...] = apply_inverse(
        inverse_ref, residual_ref[...] - coupled, parts, variables, 0 if last else slab
    )


def per_device(
    fine_residual,
    fine_basis,
    coarse_basis,
    donor_cells,
    point_counts,
    solver_pos,
    block_inverse,
    face_jacobian,
    face_lift,
    face_offset,
):
    high_count = lax.axis_size("high")
    passing = lax.axis_size("low") * lax.axis_size("sub")
    owners = high_count * passing
    _, variables, fine = fine_residual.shape
    modes = coarse_basis.shape[1]
    donors = donor_cells.shape[1]
    block = solver_pos.shape[0]
    faces = face_offset.shape[0]
    full = modes * variables
    slab = -(-modes // 16) * 16
    depth = -(-full // 16) * 16

    capacity = max(2, 2 * fine * donors // owners)
    subs = lax.axis_size("sub")
    inputs = (
        fine_residual.transpose(1, 0, 2),
        fine_basis.T,
        coarse_basis.transpose(1, 0, 2),
        point_counts.T,
        donor_cells.T,
    )
    joint = 2 * capacity == block and owners % 4 == 0
    columns = call(
        functools.partial(
            restrict_kernel,
            owners=owners,
            block=block,
            passing=passing,
            capacity=capacity,
            joint=joint,
        ),
        "restrict",
        ((owners, depth // 2, block) if joint else (passing, full + 1, high_count * capacity), F32),
        inputs,
        [pltpu.VMEM(x.shape, x.dtype) for x in inputs]
        + [
            pltpu.VMEM((variables, donors, fine_basis.shape[0], fine), F32),
            pltpu.VMEM((depth, donors * fine), F32),
            pltpu.SemaphoreType.DMA((len(inputs) - 1 + modes,)),
        ],
        megabytes=None,
        spec=pl.BlockSpec(memory_space=pl.ANY),
    )
    place = solver_pos[None, :]
    if joint:
        columns = lax.all_to_all(columns, WHOLE, 0, 0, tiled=True)
        whole = call(collect_kernel, "collect", ((full + 1, block), F32), (place, columns), megabytes=24)
    else:
        columns = lax.all_to_all(columns, PLANE, 0, 0, tiled=True)
        blocks = call(
            functools.partial(seat_kernel, capacity=capacity),
            "seat_columns",
            ((high_count, full, block), F32),
            (columns,),
            megabytes=24,
        )
        blocks = lax.all_to_all(blocks, "high", 0, 0, tiled=True)
        whole = call(renumber_kernel, "renumber", ((full + 1, block), F32), (place, blocks))
    blocks = swap_all([whole] * subs, "sub")

    jacobian = face_jacobian.transpose(1, 2, 0, 3)
    chooser, lift = call(
        functools.partial(prepare_kernel, variables=variables, slab=slab),
        "prepare",
        [((2 * block, faces * block), BF16), ((full, variables * faces * slab), F32)],
        (face_offset, face_lift.transpose(1, 0, 2)),
    )
    outer_pairs = [(i, i + 1) for i in range(1, owners - 1, 2)]
    outer_pairs += [(j, i) for i, j in outer_pairs]
    inner_pairs = [(i, i ^ 1) for i in range(owners)]
    parts = pltpu.VMEM((8 * full, block), F32)
    plain, sweep = ((full, block), F32), ((variables * slab, block), F32)
    residual, x = call(
        functools.partial(first_kernel, variables=variables, slab=slab, subs=subs),
        "first",
        [plain, sweep],
        (block_inverse, *blocks),
        [parts],
    )
    for last in (False, True):
        outer = lax.ppermute(x, WHOLE, outer_pairs)
        inner = lax.ppermute(x, WHOLE, inner_pairs)
        x = call(
            functools.partial(sweep_kernel, variables=variables, slab=slab, last=last),
            "correction" if last else "second",
            [plain, plain] if last else sweep,
            (block_inverse, residual, x, inner, outer, chooser, lift, jacobian),
            [pltpu.VMEM((variables * faces * slab, block), BF16)] * 2 + [parts],
        )
    return tuple(x)


def solution(mesh):
    dom, sub = mesh.devices.shape
    low = 2 if dom % 2 == 0 else 1
    split_mesh = jax.sharding.Mesh(mesh.devices.reshape(dom // low, low, sub), WHOLE)
    in_specs = (
        P(None, None, WHOLE),
        P(),
        P(None, None, WHOLE),
        P(WHOLE, None),
        P(WHOLE, None),
        P(WHOLE),
        P(None, None, WHOLE),
        P(None, None, None, WHOLE),
        P(),
        P(None, WHOLE),
    )
    return jax.shard_map(
        per_device,
        mesh=split_mesh,
        in_specs=in_specs,
        out_specs=(P(None, WHOLE), P(None, WHOLE)),
        check_vma=False,
    )
```

```python
import functools
import jax
import jax.numpy as jnp
from jax import lax
from jax.experimental import pallas as pl
from jax.experimental.pallas import tpu as pltpu
from jax.sharding import PartitionSpec as P

F32 = jnp.float32
BF16 = jnp.bfloat16
PLANE = ("low", "sub")
WHOLE = ("high", "low", "sub")
VMEM = pl.BlockSpec(memory_space=pltpu.VMEM)


def split(x):
    high = x.astype(BF16)
    return high, (x - high.astype(F32)).astype(BF16)


def mm(a, b, ca=1, cb=0, precision=None):
    return lax.dot_general(
        a, b, (((ca,), (cb,)), ((), ())), precision=precision, preferred_element_type=F32
    )


def rows_of(iota_shape, dim):
    return lax.broadcasted_iota(jnp.int32, iota_shape, dim)


def call(kernel, name, shapes, args, scratch=(), megabytes=8, spec=VMEM, out_spec=VMEM):
    single = not isinstance(shapes, list)
    out = [jax.ShapeDtypeStruct(*shape) for shape in ([shapes] if single else shapes)]
    result = pl.pallas_call(
        kernel,
        out_shape=out,
        in_specs=[spec] * len(args),
        out_specs=[out_spec] * len(out),
        scratch_shapes=list(scratch),
        compiler_params=pltpu.CompilerParams(
            vmem_limit_bytes=megabytes * 2**20 if megabytes else None
        ),
        name=name,
    )(*args)
    return result[0] if single else result


def swap_all(blocks, axis):
    count = len(blocks)
    return [blocks[0]] + [
        lax.ppermute(blocks[d], axis, [(i, i ^ d) for i in range(count)])
        for d in range(count - 1, 0, -1)
    ]


def free_columns(owner, owners, passing, capacity, width):
    lanes = 128
    total = owner.shape[1]
    parts = total // lanes
    mine = (rows_of((owners, total), 0) == owner).astype(F32)
    stacked = jnp.concatenate([mine[:, j * lanes : (j + 1) * lanes] for j in range(parts)], axis=0)
    earlier = (rows_of((lanes, lanes), 0) < rows_of((lanes, lanes), 1)).astype(F32)
    counter = jnp.concatenate([earlier, jnp.ones((lanes, lanes), F32)], axis=1)
    counted = mm(stacked.astype(BF16), counter.astype(BF16))
    before = jnp.zeros((owners, lanes), F32)
    ranks = []
    for j in range(parts):
        own = mine[:, j * lanes : (j + 1) * lanes]
        part = counted[j * owners : (j + 1) * owners]
        ranks.append(jnp.sum(own * (before + part[:, :lanes]), axis=0, keepdims=True))
        before += part[:, lanes:]
    rank = jnp.concatenate(ranks, axis=1).astype(jnp.int32)
    return (owner % passing) * width + (owner // passing) * capacity + rank


def restrict_kernel(
    res_hbm, basis_hbm, coarse_hbm, counts_hbm, donors_hbm, out_hbm,
    res_ref, basis_ref, coarse_ref, counts_ref, donors_ref, pair_ref, chunk_ref, sems, out_sems,
    *, owners, block, passing, capacity
):
    variables, _, fine = res_ref.shape
    modes, points, _ = coarse_ref.shape
    donors = counts_ref.shape[0]
    chunks, used, width = chunk_ref.shape
    full = modes * variables
    depth = pair_ref.shape[0]
    total = donors * fine
    lanes = 128

    steps = [
        (at, a, min(a + 5, modes)) for at in range(0, fine, lanes) for a in range(0, modes, 5)
    ]
    small = [(donors_hbm, donors_ref), (basis_hbm, basis_ref), (res_hbm, res_ref), (counts_hbm, counts_ref)]
    large = [
        (coarse_hbm.at[a:end, :, at : at + lanes], coarse_ref.at[a:end, :, at : at + lanes])
        for at, a, end in steps
    ]
    copies = [
        pltpu.make_async_copy(source, target, sems.at[i])
        for i, (source, target) in enumerate(small + large)
    ]
    for copy in copies:
        copy.start()

    copies[0].wait()
    cell = jnp.concatenate([donors_ref[k : k + 1, :] for k in range(donors)], axis=1)
    pair_ref[full:, :] = jnp.zeros((depth - full, total), F32)
    pair_ref[full : full + 1, :] = (cell % block).astype(F32)
    slot = free_columns(cell // block, owners, passing, capacity, width)
    slot = jnp.broadcast_to(slot.astype(F32), (lanes, total)).T.astype(jnp.int32).astype(jnp.int16)

    copies[1].wait()
    copies[2].wait()
    basis_high, basis_low = split(basis_ref[...])
    res_high, res_low = split(jnp.concatenate([res_ref[v] for v in range(variables)], axis=1))
    values = mm(basis_high, res_high, 0, 0)
    values += mm(basis_high, res_low, 0, 0) + mm(basis_low, res_high, 0, 0)

    copies[3].wait()
    point = rows_of((points, lanes), 0)
    for i, (at, begin, end) in enumerate(steps):
        copies[4 + i].wait()
        upper = jnp.zeros((1, lanes), jnp.int32)
        inside = []
        for k in range(donors):
            lower = upper
            upper = lower + counts_ref[k : k + 1, at : at + lanes]
            inside.append((point >= lower) & (point < upper))
        for v in range(variables):
            column = v * fine + at
            value = values[:, column : column + lanes]
            masked = [jnp.where(inside[k], value, 0.0) for k in range(donors)]
            for a in range(begin, end):
                coarse = coarse_ref[a, :, at : at + lanes]
                row = a * variables + v
                for k in range(donors):
                    pair_ref[row : row + 1, k * fine + at : k * fine + at + lanes] = jnp.sum(
                        coarse * masked[k], axis=0, keepdims=True
                    )

    both = jnp.concatenate(split(pair_ref[...]), axis=0)
    lane = rows_of((total, lanes), 1).astype(jnp.int16)
    one, zero = jnp.ones((total, lanes), BF16), jnp.zeros((total, lanes), BF16)
    for c in range(chunks):
        chooser = jnp.concatenate(
            [
                jnp.where(slot == lane + jnp.int16(c * width + j), one, zero)
                for j in range(0, width, lanes)
            ],
            axis=1,
        )
        placed = mm(both, chooser)
        chunk_ref[c] = placed[:used] + placed[depth : depth + used]
        pltpu.make_async_copy(chunk_ref.at[c], out_hbm.at[c], out_sems.at[c]).start()
    for c in range(chunks):
        pltpu.make_async_copy(chunk_ref.at[c], out_hbm.at[c], out_sems.at[c]).wait()


def seat_kernel(columns_ref, *refs, capacity):
    out_refs, scratch = refs[:-1], refs[-1]
    sources, _, _ = columns_ref.shape
    count, full, block = scratch.shape
    for h in range(count):
        got = jnp.concatenate(
            [columns_ref[s, :, h * capacity : (h + 1) * capacity] for s in range(sources)], axis=1
        )
        seat = got[full : full + 1, :]
        chooser = (rows_of((block, got.shape[1]), 0).astype(F32) == seat).astype(F32).astype(BF16)
        high, low = split(got)
        scratch[h] = (mm(high, chooser, 1, 1) + mm(low, chooser, 1, 1))[:full]
    if len(out_refs) == 1:
        out_refs[0][...] = scratch[...]
    else:
        here = lax.axis_index("high")
        for d in range(count):
            out_refs[d][...] = scratch[here ^ d]


def renumber_kernel(place_ref, *refs):
    block_refs, out_ref = refs[:-1], refs[-1]
    block = place_ref.shape[1]
    if len(block_refs) == 1:
        total = block_refs[0][0]
        for h in range(1, block_refs[0].shape[0]):
            total += block_refs[0][h]
    else:
        total = block_refs[0][...]
        for ref in block_refs[1:]:
            total += ref[...]
    full = total.shape[0]
    place = place_ref[...]
    chooser = (rows_of((block, block), 0) == place % block).astype(F32).astype(BF16)
    high, low = split(total)
    out_ref[:full, :] = mm(high, chooser, 1, 1) + mm(low, chooser, 1, 1)
    out_ref[full:, :] = (place // block).astype(F32)


def inner_is_left():
    return lax.axis_index("sub") % 2 == 1


def prepare_kernel(offset_ref, lift_ref, chooser_ref, lift_out_ref, *, variables, slab):
    faces, block = offset_ref.shape
    modes = lift_ref.shape[0]
    full = modes * variables
    lane = rows_of((1, block), 1)
    row = rows_of((2 * block, block), 0)
    for f in range(faces):
        offset = offset_ref[f : f + 1, :]
        source = jnp.where(offset != 0, (lane + offset) & (2 * block - 1), -1)
        chooser_ref[:, f * block : (f + 1) * block] = (row == source).astype(F32).astype(BF16)
    width = variables * faces * slab
    column = rows_of((modes, width), 1)
    mode = rows_of((modes, width), 0)
    spread = jnp.zeros((modes, width), F32)
    for f in range(faces):
        put = (column % slab == mode) & ((column // slab) % faces == f)
        spread += mm(lift_ref[:, f, :], put.astype(F32), 1, 0, lax.Precision.HIGHEST)
    expand = (rows_of((full, modes), 0) // variables == rows_of((full, modes), 1)).astype(F32)
    lifted = mm(expand, spread, 1, 0, lax.Precision.HIGHEST)
    keep = rows_of((full, width), 1) // (slab * faces) == rows_of((full, width), 0) % variables
    lift_out_ref[...] = jnp.where(keep, lifted, 0.0)


def apply_inverse(inverse_ref, field, parts, variables, depth=None):
    full, _, block = inverse_ref.shape
    for i in range(full):
        product = inverse_ref[i] * field
        partial = product[0:8]
        for j in range(8, full - 7, 8):
            partial += product[j : j + 8]
        rest = full % 8
        if rest:
            partial = jnp.concatenate([partial[:rest] + product[full - rest :], partial[rest:]], axis=0)
        parts[i * 8 : i * 8 + 8, :] = partial
    row = rows_of((depth or full, 8 * full), 0)
    source = rows_of((depth or full, 8 * full), 1) // 8
    target = (source % variables) * (full // variables) + source // variables if depth else source
    adder = (row == target).astype(F32).astype(BF16)
    high, low = split(parts[...])
    return mm(adder, high) + mm(adder, low)


def inner_is_left():
    return lax.axis_index("sub") % 2 == 1


def put_edges(x, inner_ref, outer_ref):
    rows, block = x.shape
    reach, group = block // 4, rows // 4
    lane = rows_of((group, block), 1) // reach

    def packed(start):
        result = jnp.zeros((group, block), F32)
        for g in range(4):
            turned = x[g * group : (g + 1) * group]
            if (g * reach - start) % block:
                turned = pltpu.roll(turned, (g * reach - start) % block, 1)
            result = jnp.where(lane == g, turned, result)
        return result

    first, final = packed(0), packed(block - reach)
    inner_ref[...] = jnp.where(inner_is_left(), first, final)
    outer_ref[...] = jnp.where(inner_is_left(), final, first)


def take_edges(inner, outer):
    group, block = inner.shape
    reach = block // 4
    right = jnp.where(inner_is_left(), outer, inner)
    left = jnp.where(inner_is_left(), inner, outer)
    lower = rows_of((group, block), 1) < block // 2
    rows = []
    for g in range(4):
        after = pltpu.roll(right, block - g * reach, 1) if g else right
        before = pltpu.roll(left, (3 - g) * reach, 1) if g < 3 else left
        rows.append(jnp.where(lower, after, before))
    return jnp.concatenate(rows, axis=0)


def first_kernel(inverse_ref, *refs, variables, subs):
    block_refs, (total_ref, out_ref, inner_ref, outer_ref, parts) = refs[:-5], refs[-5:]
    full = total_ref.shape[0]
    owner = lax.axis_index("high") * lax.axis_size("low") + lax.axis_index("low")
    owner = (owner * subs + lax.axis_index("sub")).astype(F32)
    residual = jnp.zeros(total_ref.shape, F32)
    for ref in block_refs:
        residual += jnp.where(ref[full:, :] == owner, ref[:full, :], 0.0)
    total_ref[...] = residual
    x = apply_inverse(inverse_ref, residual, parts, variables, out_ref.shape[0])
    out_ref[...] = x
    put_edges(x, inner_ref, outer_ref)


def sweep_kernel(
    inverse_ref, residual_ref, x_ref, outer_ref, inner_ref, chooser_ref, lift_ref, jacobian_ref, *refs,
    variables, slab
):
    *out_refs, picked_ref, z_high, z_low, parts = refs
    rows, block = x_ref.shape
    modes = inverse_ref.shape[0] // variables
    faces = jacobian_ref.shape[2]
    beside = take_edges(inner_ref[...], outer_ref[...])
    x = jnp.concatenate(split(jnp.concatenate([x_ref[...], beside], axis=1)), axis=0)
    picked = mm(x, chooser_ref[...])
    picked_ref[...] = picked[:rows] + picked[rows:]
    for f in range(faces):
        at = f * block
        part = [
            picked_ref[v * modes : v * modes + slab, at : at + block] for v in range(variables)
        ]
        for w in range(variables):
            z = part[0] * jacobian_ref[w, 0, f : f + 1, :]
            for v in range(1, variables):
                z += part[v] * jacobian_ref[w, v, f : f + 1, :]
            line = (w * faces + f) * slab
            z_high[line : line + slab, :], z_low[line : line + slab, :] = split(z)
    lift_high, lift_low = split(lift_ref[...])
    high, low = z_high[...], z_low[...]
    coupled = mm(lift_high, high) + mm(lift_high, low) + mm(lift_low, high)
    field = residual_ref[...] - coupled
    if len(out_refs) == 2:
        total_ref, out_ref = out_refs
        total_ref[...] = residual_ref[...]
        out_ref[...] = apply_inverse(inverse_ref, field, parts, variables)
    else:
        x = apply_inverse(inverse_ref, field, parts, variables, rows)
        out_refs[0][...] = x
        put_edges(x, *out_refs[1:])


def per_device(
    fine_residual,
    fine_basis,
    coarse_basis,
    donor_cells,
    point_counts,
    solver_pos,
    block_inverse,
    face_jacobian,
    face_lift,
    face_offset,
):
    high_count = lax.axis_size("high")
    passing = lax.axis_size("low") * lax.axis_size("sub")
    owners = high_count * passing
    _, variables, fine = fine_residual.shape
    modes = coarse_basis.shape[1]
    donors = donor_cells.shape[1]
    block = solver_pos.shape[0]
    faces = face_offset.shape[0]
    full = modes * variables
    slab = -(-modes // 16) * 16
    depth = -(-full // 16) * 16

    capacity = max(2, 2 * fine * donors // owners)
    subs = lax.axis_size("sub")
    inputs = (
        fine_residual.transpose(1, 0, 2),
        fine_basis.T,
        coarse_basis.transpose(1, 0, 2),
        point_counts.T,
        donor_cells.T,
    )
    columns = call(
        functools.partial(
            restrict_kernel, owners=owners, block=block, passing=passing, capacity=capacity
        ),
        "restrict",
        ((passing, full + 1, high_count * capacity), F32),
        inputs,
        [pltpu.VMEM(x.shape, x.dtype) for x in inputs]
        + [
            pltpu.VMEM((depth, donors * fine), F32),
            pltpu.VMEM((passing, full + 1, high_count * capacity), F32),
            pltpu.SemaphoreType.DMA((len(inputs) - 1 + fine // 128 * -(-modes // 5),)),
            pltpu.SemaphoreType.DMA((passing,)),
        ],
        megabytes=None,
        spec=pl.BlockSpec(memory_space=pl.ANY),
        out_spec=pl.BlockSpec(memory_space=pl.ANY),
    )
    columns = lax.all_to_all(columns, PLANE, 0, 0, tiled=True)
    few = high_count <= 8
    blocks = call(
        functools.partial(seat_kernel, capacity=capacity),
        "seat_columns",
        [((full, block), F32)] * high_count if few else [((high_count, full, block), F32)],
        (columns,),
        [pltpu.VMEM((high_count, full, block), F32)],
        megabytes=24,
    )
    if few:
        blocks = swap_all(blocks, "high")
    else:
        blocks = [lax.all_to_all(blocks[0], "high", 0, 0, tiled=True)]
    whole = call(
        renumber_kernel, "renumber", ((full + 1, block), F32), (solver_pos[None, :], *blocks)
    )
    blocks = swap_all([whole] * subs, "sub")

    jacobian = face_jacobian.transpose(1, 2, 0, 3)
    chooser, lift = call(
        functools.partial(prepare_kernel, variables=variables, slab=slab),
        "prepare",
        [((2 * block, faces * block), BF16), ((full, variables * faces * slab), F32)],
        (face_offset, face_lift.transpose(1, 0, 2)),
    )
    outer_pairs = [(i, i + 1) for i in range(1, owners - 1, 2)]
    outer_pairs += [(j, i) for i, j in outer_pairs]
    inner_pairs = [(i, i ^ 1) for i in range(owners)]
    parts = pltpu.VMEM((8 * full, block), F32)
    plain, edge = ((full, block), F32), ((depth // 4, block), F32)
    sweep = [((depth, block), F32), edge, edge]
    residual, *x = call(
        functools.partial(first_kernel, variables=variables, subs=subs),
        "first",
        [plain] + sweep,
        (block_inverse, *blocks),
        [parts],
    )
    for last in (False, True):
        own, inner, outer = x
        outer = lax.ppermute(outer, WHOLE, outer_pairs)
        inner = lax.ppermute(inner, WHOLE, inner_pairs)
        x = call(
            functools.partial(sweep_kernel, variables=variables, slab=slab),
            "correction" if last else "second",
            [plain, plain] if last else sweep,
            (block_inverse, residual, own, outer, inner, chooser, lift, jacobian),
            [pltpu.VMEM((depth, faces * block), F32)]
            + [pltpu.VMEM((variables * faces * slab, block), BF16)] * 2
            + [parts],
        )
    return tuple(x)


def solution(mesh):
    dom, sub = mesh.devices.shape
    low = 2 if dom % 2 == 0 else 1
    split_mesh = jax.sharding.Mesh(mesh.devices.reshape(dom // low, low, sub), WHOLE)
    in_specs = (
        P(None, None, WHOLE),
        P(),
        P(None, None, WHOLE),
        P(WHOLE, None),
        P(WHOLE, None),
        P(WHOLE),
        P(None, None, WHOLE),
        P(None, None, None, WHOLE),
        P(),
        P(None, WHOLE),
    )
    return jax.shard_map(
        per_device,
        mesh=split_mesh,
        in_specs=in_specs,
        out_specs=(P(None, WHOLE), P(None, WHOLE)),
        check_vma=False,
    )
```

```python
import functools
import jax
import jax.numpy as jnp
from jax import lax
from jax.experimental import pallas as pl
from jax.experimental.pallas import tpu as pltpu
from jax.sharding import PartitionSpec as P

F32 = jnp.float32
BF16 = jnp.bfloat16
PLANE = ("low", "sub")
WHOLE = ("high", "low", "sub")
VMEM = pl.BlockSpec(memory_space=pltpu.VMEM)


def split(x):
    high = x.astype(BF16)
    return high, (x - high.astype(F32)).astype(BF16)


def mm(a, b, ca=1, cb=0, precision=None):
    return lax.dot_general(
        a, b, (((ca,), (cb,)), ((), ())), precision=precision, preferred_element_type=F32
    )


def rows_of(iota_shape, dim):
    return lax.broadcasted_iota(jnp.int32, iota_shape, dim)


def call(kernel, name, shapes, args, scratch=(), megabytes=8, cost=None):
    single = not isinstance(shapes, list)
    out = [jax.ShapeDtypeStruct(*shape) for shape in ([shapes] if single else shapes)]
    result = pl.pallas_call(
        kernel,
        out_shape=out,
        in_specs=[VMEM] * len(args),
        out_specs=[VMEM] * len(out),
        scratch_shapes=list(scratch),
        compiler_params=pltpu.CompilerParams(vmem_limit_bytes=megabytes * 2**20),
        cost_estimate=cost,
        name=name,
    )(*args)
    return result[0] if single else result


def swap_all(blocks, axis):
    count = len(blocks)
    return [blocks[0]] + [
        lax.ppermute(blocks[d], axis, [(i, i ^ d) for i in range(count)])
        for d in range(count - 1, 0, -1)
    ]


def constants_kernel(counter_ref, sweep_adder_ref, adder_ref, *, variables):
    lanes = counter_ref.shape[0]
    earlier = (rows_of((lanes, lanes), 0) < rows_of((lanes, lanes), 1)).astype(F32)
    counter = jnp.concatenate([earlier, jnp.ones((lanes, lanes), F32)], axis=1)
    counter_ref[...] = counter.astype(BF16)
    full = adder_ref.shape[0]
    for ref in (sweep_adder_ref, adder_ref):
        row, source = rows_of(ref.shape, 0), rows_of(ref.shape, 1) // 8
        if ref is sweep_adder_ref:
            source = (source % variables) * (full // variables) + source // variables
        ref[...] = (row == source).astype(F32).astype(BF16)


def free_columns(owner, counter, owners, passing, capacity, width):
    lanes = 128
    total = owner.shape[1]
    parts = total // lanes
    mine = (rows_of((owners, total), 0) == owner).astype(F32)
    stacked = jnp.concatenate([mine[:, j * lanes : (j + 1) * lanes] for j in range(parts)], axis=0)
    counted = mm(stacked.astype(BF16), counter)
    before = jnp.zeros((owners, lanes), F32)
    ranks = []
    for j in range(parts):
        own = mine[:, j * lanes : (j + 1) * lanes]
        part = counted[j * owners : (j + 1) * owners]
        ranks.append(jnp.sum(own * (before + part[:, :lanes]), axis=0, keepdims=True))
        before += part[:, lanes:]
    rank = jnp.concatenate(ranks, axis=1).astype(jnp.int32)
    return (owner % passing) * width + (owner // passing) * capacity + rank


def restrict_kernel(
    counter_ref, res_ref, basis_ref, coarse_ref, counts_ref, donors_ref, out_ref, pair_ref,
    *, owners, block, passing, capacity
):
    variables, _, fine = res_ref.shape
    modes, points, _ = coarse_ref.shape
    donors = counts_ref.shape[0]
    chunks = out_ref.shape[0]
    full = modes * variables
    depth = pair_ref.shape[0]
    total = donors * fine
    lanes = 128
    width = owners // passing * capacity

    cell = jnp.concatenate([donors_ref[k : k + 1, :] for k in range(donors)], axis=1)
    pair_ref[full:, :] = jnp.zeros((depth - full, total), F32)
    pair_ref[full : full + 1, :] = (cell % block).astype(F32)
    slot = free_columns(cell // block, counter_ref[...], owners, passing, capacity, width)
    slot = jnp.broadcast_to(slot.astype(F32), (lanes, total)).T.astype(jnp.int32).astype(jnp.int16)

    basis_high, basis_low = split(basis_ref[...])
    res_high, res_low = split(jnp.concatenate([res_ref[v] for v in range(variables)], axis=1))
    values = mm(basis_high, res_high, 0, 0)
    values += mm(basis_high, res_low, 0, 0) + mm(basis_low, res_high, 0, 0)

    point = rows_of((points, lanes), 0)
    for at in range(0, fine, lanes):
        upper = jnp.zeros((1, lanes), jnp.int32)
        inside = []
        for k in range(donors):
            lower = upper
            upper = lower + counts_ref[k : k + 1, at : at + lanes]
            inside.append((point >= lower) & (point < upper))
        for v in range(variables):
            column = v * fine + at
            value = values[:, column : column + lanes]
            masked = [jnp.where(inside[k], value, 0.0) for k in range(donors)]
            for a in range(modes):
                coarse = coarse_ref[a, :, at : at + lanes]
                row = a * variables + v
                for k in range(donors):
                    pair_ref[row : row + 1, k * fine + at : k * fine + at + lanes] = jnp.sum(
                        coarse * masked[k], axis=0, keepdims=True
                    )

    both = jnp.concatenate(split(pair_ref[...]), axis=0)
    lane = rows_of((total, lanes), 1).astype(jnp.int16)
    one, zero = jnp.ones((total, lanes), BF16), jnp.zeros((total, lanes), BF16)
    for c in range(chunks):
        chooser = jnp.concatenate(
            [
                jnp.where(slot == lane + jnp.int16(c * width + j), one, zero)
                for j in range(0, width, lanes)
            ],
            axis=1,
        )
        placed = mm(both, chooser)
        placed = placed[:depth] + placed[depth:]
        rows = out_ref.shape[1] // 2
        for j in range(2):
            out_ref[c, j * rows : (j + 1) * rows] = placed[:rows, j * width // 2 : (j + 1) * width // 2]


def seat_kernel(columns_ref, *refs, capacity):
    out_refs, scratch = refs[:-1], refs[-1]
    sources, rows, _ = columns_ref.shape
    rows = rows // 2
    count, full, block = scratch.shape
    for h in range(count):
        j, at = divmod(h * capacity, columns_ref.shape[2])
        got = jnp.concatenate(
            [
                columns_ref[s, j * rows : j * rows + full + 1, at : at + capacity]
                for s in range(sources)
            ],
            axis=1,
        )
        seat = got[full : full + 1, :]
        chooser = (rows_of((block, got.shape[1]), 0).astype(F32) == seat).astype(F32).astype(BF16)
        high, low = split(got)
        scratch[h] = (mm(high, chooser, 1, 1) + mm(low, chooser, 1, 1))[:full]
    if len(out_refs) == 1:
        out_refs[0][...] = scratch[...]
    else:
        here = lax.axis_index("high")
        for d in range(count):
            out_refs[d][...] = scratch[here ^ d]


def renumber_kernel(place_ref, *refs):
    block_refs, out_ref = refs[:-1], refs[-1]
    block = place_ref.shape[1]
    if len(block_refs) == 1:
        total = block_refs[0][0]
        for h in range(1, block_refs[0].shape[0]):
            total += block_refs[0][h]
    else:
        total = block_refs[0][...]
        for ref in block_refs[1:]:
            total += ref[...]
    full = total.shape[0]
    place = place_ref[...]
    chooser = (rows_of((block, block), 0) == place % block).astype(F32).astype(BF16)
    high, low = split(total)
    out_ref[:full, :] = mm(high, chooser, 1, 1) + mm(low, chooser, 1, 1)
    out_ref[full:, :] = (place // block).astype(F32)


def prepare_kernel(offset_ref, lift_ref, chooser_ref, lift_out_ref, *, variables, slab):
    faces, block = offset_ref.shape
    modes = lift_ref.shape[0]
    full = modes * variables
    lane = rows_of((1, block), 1)
    row = rows_of((2 * block, block), 0)
    for f in range(faces):
        offset = offset_ref[f : f + 1, :]
        source = jnp.where(offset != 0, (lane + offset) & (2 * block - 1), -1)
        chooser_ref[:, f * block : (f + 1) * block] = (row == source).astype(F32).astype(BF16)
    width = variables * faces * slab
    column = rows_of((modes, width), 1)
    mode = rows_of((modes, width), 0)
    spread = jnp.zeros((modes, width), F32)
    for f in range(faces):
        put = (column % slab == mode) & ((column // slab) % faces == f)
        spread += mm(lift_ref[:, f, :], put.astype(F32), 1, 0, lax.Precision.HIGHEST)
    expand = (rows_of((full, modes), 0) // variables == rows_of((full, modes), 1)).astype(F32)
    lifted = mm(expand, spread, 1, 0, lax.Precision.HIGHEST)
    keep = rows_of((full, width), 1) // (slab * faces) == rows_of((full, width), 0) % variables
    lift_out_ref[...] = jnp.where(keep, lifted, 0.0)


def apply_inverse(inverse_ref, field, adder_ref, parts):
    full = inverse_ref.shape[0]
    for i in range(full):
        product = inverse_ref[i] * field
        partial = product[0:8]
        for j in range(8, full - 7, 8):
            partial += product[j : j + 8]
        rest = full % 8
        if rest:
            partial = jnp.concatenate([partial[:rest] + product[full - rest :], partial[rest:]], axis=0)
        parts[i * 8 : i * 8 + 8, :] = partial
    high, low = split(parts[...])
    adder = adder_ref[...]
    return mm(adder, high) + mm(adder, low)


def inner_is_left():
    return lax.axis_index("sub") % 2 == 1


def put_edges(x, inner_ref, outer_ref):
    rows, block = x.shape
    reach, group = block // 4, rows // 4
    lane = rows_of((group, block), 1) // reach

    def packed(start):
        result = jnp.zeros((group, block), F32)
        for g in range(4):
            turned = x[g * group : (g + 1) * group]
            if (g * reach - start) % block:
                turned = pltpu.roll(turned, (g * reach - start) % block, 1)
            result = jnp.where(lane == g, turned, result)
        return result

    first, final = packed(0), packed(block - reach)
    inner_ref[...] = jnp.where(inner_is_left(), first, final)
    outer_ref[...] = jnp.where(inner_is_left(), final, first)


def take_edges(inner, outer):
    group, block = inner.shape
    reach = block // 4
    right = jnp.where(inner_is_left(), outer, inner)
    left = jnp.where(inner_is_left(), inner, outer)
    lower = rows_of((group, block), 1) < block // 2
    rows = []
    for g in range(4):
        after = pltpu.roll(right, block - g * reach, 1) if g else right
        before = pltpu.roll(left, (3 - g) * reach, 1) if g < 3 else left
        rows.append(jnp.where(lower, after, before))
    return jnp.concatenate(rows, axis=0)


def first_kernel(inverse_ref, adder_ref, *refs, subs):
    block_refs, (total_ref, out_ref, inner_ref, outer_ref, parts) = refs[:-5], refs[-5:]
    full = total_ref.shape[0]
    owner = lax.axis_index("high") * lax.axis_size("low") + lax.axis_index("low")
    owner = (owner * subs + lax.axis_index("sub")).astype(F32)
    residual = jnp.zeros(total_ref.shape, F32)
    for ref in block_refs:
        residual += jnp.where(ref[full:, :] == owner, ref[:full, :], 0.0)
    total_ref[...] = residual
    x = apply_inverse(inverse_ref, residual, adder_ref, parts)
    out_ref[...] = x
    put_edges(x, inner_ref, outer_ref)


def sweep_kernel(
    inverse_ref, adder_ref, residual_ref, x_ref, outer_ref, inner_ref, chooser_ref, lift_ref, jacobian_ref, *refs,
    variables, slab
):
    *out_refs, picked_ref, z_high, z_low, parts = refs
    rows, block = x_ref.shape
    modes = inverse_ref.shape[0] // variables
    faces = jacobian_ref.shape[2]
    beside = take_edges(inner_ref[...], outer_ref[...])
    x = jnp.concatenate(split(jnp.concatenate([x_ref[...], beside], axis=1)), axis=0)
    picked = mm(x, chooser_ref[...])
    picked_ref[...] = picked[:rows] + picked[rows:]
    for f in range(faces):
        at = f * block
        part = [
            picked_ref[v * modes : v * modes + slab, at : at + block] for v in range(variables)
        ]
        for w in range(variables):
            z = part[0] * jacobian_ref[w, 0, f : f + 1, :]
            for v in range(1, variables):
                z += part[v] * jacobian_ref[w, v, f : f + 1, :]
            line = (w * faces + f) * slab
            z_high[line : line + slab, :], z_low[line : line + slab, :] = split(z)
    lift_high, lift_low = split(lift_ref[...])
    high, low = z_high[...], z_low[...]
    coupled = mm(lift_high, high) + mm(lift_high, low) + mm(lift_low, high)
    field = residual_ref[...] - coupled
    if len(out_refs) == 2:
        total_ref, out_ref = out_refs
        total_ref[...] = residual_ref[...]
        out_ref[...] = apply_inverse(inverse_ref, field, adder_ref, parts)
    else:
        x = apply_inverse(inverse_ref, field, adder_ref, parts)
        out_refs[0][...] = x
        put_edges(x, *out_refs[1:])


def per_device(
    fine_residual,
    fine_basis,
    coarse_basis,
    donor_cells,
    point_counts,
    solver_pos,
    block_inverse,
    face_jacobian,
    face_lift,
    face_offset,
):
    high_count = lax.axis_size("high")
    passing = lax.axis_size("low") * lax.axis_size("sub")
    owners = high_count * passing
    _, variables, fine = fine_residual.shape
    modes = coarse_basis.shape[1]
    donors = donor_cells.shape[1]
    block = solver_pos.shape[0]
    faces = face_offset.shape[0]
    full = modes * variables
    slab = -(-modes // 16) * 16
    depth = -(-full // 16) * 16

    capacity = max(2, 2 * fine * donors // owners)
    subs = lax.axis_size("sub")
    counter, sweep_adder, adder = call(
        functools.partial(constants_kernel, variables=variables),
        "constants",
        [((128, 256), BF16), ((depth, 8 * full), BF16), ((full, 8 * full), BF16)],
        (),
        cost=pl.CostEstimate(flops=2 * 10**9, bytes_accessed=8 * 10**6, transcendentals=0),
    )
    rows = -(-(full + 1) // 4) * 4
    columns = call(
        functools.partial(
            restrict_kernel, owners=owners, block=block, passing=passing, capacity=capacity
        ),
        "restrict",
        ((passing, 2 * rows, high_count * capacity // 2), F32),
        (
            counter,
            fine_residual.transpose(1, 0, 2),
            fine_basis.T,
            coarse_basis.transpose(1, 0, 2),
            point_counts.T,
            donor_cells.T,
        ),
        [pltpu.VMEM((depth, donors * fine), F32)],
        megabytes=16,
    )
    columns = lax.all_to_all(columns, PLANE, 0, 0, tiled=True)
    few = high_count <= 8
    blocks = call(
        functools.partial(seat_kernel, capacity=capacity),
        "seat_columns",
        [((full, block), F32)] * high_count if few else [((high_count, full, block), F32)],
        (columns,),
        [pltpu.VMEM((high_count, full, block), F32)],
        megabytes=24,
    )
    if few:
        blocks = swap_all(blocks, "high")
    else:
        blocks = [lax.all_to_all(blocks[0], "high", 0, 0, tiled=True)]
    whole = call(
        renumber_kernel, "renumber", ((full + 1, block), F32), (solver_pos[None, :], *blocks)
    )
    blocks = swap_all([whole] * subs, "sub")

    jacobian = face_jacobian.transpose(1, 2, 0, 3)
    chooser, lift = call(
        functools.partial(prepare_kernel, variables=variables, slab=slab),
        "prepare",
        [((2 * block, faces * block), BF16), ((full, variables * faces * slab), F32)],
        (face_offset, face_lift.transpose(1, 0, 2)),
    )
    outer_pairs = [(i, i + 1) for i in range(1, owners - 1, 2)]
    outer_pairs += [(j, i) for i, j in outer_pairs]
    inner_pairs = [(i, i ^ 1) for i in range(owners)]
    parts = pltpu.VMEM((8 * full, block), F32)
    plain, edge = ((full, block), F32), ((depth // 4, block), F32)
    sweep = [((depth, block), F32), edge, edge]
    residual, *x = call(
        functools.partial(first_kernel, subs=subs),
        "first",
        [plain] + sweep,
        (block_inverse, sweep_adder, *blocks),
        [parts],
    )
    for last in (False, True):
        own, inner, outer = x
        outer = lax.ppermute(outer, WHOLE, outer_pairs)
        inner = lax.ppermute(inner, WHOLE, inner_pairs)
        x = call(
            functools.partial(sweep_kernel, variables=variables, slab=slab),
            "correction" if last else "second",
            [plain, plain] if last else sweep,
            (block_inverse, adder if last else sweep_adder, residual, own, outer, inner, chooser, lift, jacobian),
            [pltpu.VMEM((depth, faces * block), F32)]
            + [pltpu.VMEM((variables * faces * slab, block), BF16)] * 2
            + [parts],
        )
    return tuple(x)


def solution(mesh):
    dom, sub = mesh.devices.shape
    low = 2 if dom % 2 == 0 else 1
    split_mesh = jax.sharding.Mesh(mesh.devices.reshape(dom // low, low, sub), WHOLE)
    in_specs = (
        P(None, None, WHOLE),
        P(),
        P(None, None, WHOLE),
        P(WHOLE, None),
        P(WHOLE, None),
        P(WHOLE),
        P(None, None, WHOLE),
        P(None, None, None, WHOLE),
        P(),
        P(None, WHOLE),
    )
    return jax.shard_map(
        per_device,
        mesh=split_mesh,
        in_specs=in_specs,
        out_specs=(P(None, WHOLE), P(None, WHOLE)),
        check_vma=False,
    )
```

```python
import functools
import jax
import jax.numpy as jnp
from jax import lax
from jax.experimental import pallas as pl
from jax.experimental.pallas import tpu as pltpu
from jax.sharding import PartitionSpec as P

F32 = jnp.float32
BF16 = jnp.bfloat16
PLANE = ("low", "sub")
WHOLE = ("high", "low", "sub")
VMEM = pl.BlockSpec(memory_space=pltpu.VMEM)


def split(x):
    high = x.astype(BF16)
    return high, (x - high.astype(F32)).astype(BF16)


def mm(a, b, ca=1, cb=0, precision=None):
    return lax.dot_general(
        a, b, (((ca,), (cb,)), ((), ())), precision=precision, preferred_element_type=F32
    )


def rows_of(iota_shape, dim):
    return lax.broadcasted_iota(jnp.int32, iota_shape, dim)


def call(kernel, name, shapes, args, scratch=(), megabytes=8, cost=None):
    single = not isinstance(shapes, list)
    out = [jax.ShapeDtypeStruct(*shape) for shape in ([shapes] if single else shapes)]
    result = pl.pallas_call(
        kernel,
        out_shape=out,
        in_specs=[VMEM] * len(args),
        out_specs=[VMEM] * len(out),
        scratch_shapes=list(scratch),
        compiler_params=pltpu.CompilerParams(vmem_limit_bytes=megabytes * 2**20),
        cost_estimate=cost,
        name=name,
    )(*args)
    return result[0] if single else result


def swap_all(blocks, axis):
    count = len(blocks)
    return [blocks[0]] + [
        lax.ppermute(blocks[d], axis, [(i, i ^ d) for i in range(count)])
        for d in range(count - 1, 0, -1)
    ]


def constants_kernel(counter_ref, sweep_adder_ref, adder_ref, *, variables):
    lanes = counter_ref.shape[0]
    earlier = (rows_of((lanes, lanes), 0) < rows_of((lanes, lanes), 1)).astype(F32)
    counter = jnp.concatenate([earlier, jnp.ones((lanes, lanes), F32)], axis=1)
    counter_ref[...] = counter.astype(BF16)
    full = adder_ref.shape[0]
    for ref in (sweep_adder_ref, adder_ref):
        row, source = rows_of(ref.shape, 0), rows_of(ref.shape, 1) // 8
        if ref is sweep_adder_ref:
            source = (source % variables) * (full // variables) + source // variables
        ref[...] = (row == source).astype(F32).astype(BF16)


def free_columns(owner, counter, owners, passing, capacity, width):
    lanes = 128
    total = owner.shape[1]
    parts = total // lanes
    mine = (rows_of((owners, total), 0) == owner).astype(F32)
    stacked = jnp.concatenate([mine[:, j * lanes : (j + 1) * lanes] for j in range(parts)], axis=0)
    counted = mm(stacked.astype(BF16), counter)
    before = jnp.zeros((owners, lanes), F32)
    ranks = []
    for j in range(parts):
        own = mine[:, j * lanes : (j + 1) * lanes]
        part = counted[j * owners : (j + 1) * owners]
        ranks.append(jnp.sum(own * (before + part[:, :lanes]), axis=0, keepdims=True))
        before += part[:, lanes:]
    rank = jnp.concatenate(ranks, axis=1).astype(jnp.int32)
    return (owner % passing) * width + (owner // passing) * capacity + rank


def restrict_kernel(
    counter_ref, res_ref, basis_ref, coarse_ref, counts_ref, donors_ref, out_ref, pair_ref,
    *, owners, block, passing, capacity
):
    variables, _, fine = res_ref.shape
    modes, points, _ = coarse_ref.shape
    donors = counts_ref.shape[0]
    chunks = out_ref.shape[0]
    full = modes * variables
    depth = pair_ref.shape[0]
    total = donors * fine
    lanes = 128
    width = owners // passing * capacity

    cell = jnp.concatenate([donors_ref[k : k + 1, :] for k in range(donors)], axis=1)
    pair_ref[full:, :] = jnp.zeros((depth - full, total), F32)
    pair_ref[full : full + 1, :] = (cell % block).astype(F32)
    slot = free_columns(cell // block, counter_ref[...], owners, passing, capacity, width)
    slot = jnp.broadcast_to(slot.astype(F32), (lanes, total)).T.astype(jnp.int32).astype(jnp.int16)

    basis_high, basis_low = split(basis_ref[...])
    res_high, res_low = split(jnp.concatenate([res_ref[v] for v in range(variables)], axis=1))
    values = mm(basis_high, res_high, 0, 0)
    values += mm(basis_high, res_low, 0, 0) + mm(basis_low, res_high, 0, 0)

    point = rows_of((points, lanes), 0)
    for at in range(0, fine, lanes):
        upper = jnp.zeros((1, lanes), jnp.int32)
        inside = []
        for k in range(donors):
            lower = upper
            upper = lower + counts_ref[k : k + 1, at : at + lanes]
            inside.append((point >= lower) & (point < upper))
        for v in range(variables):
            column = v * fine + at
            value = values[:, column : column + lanes]
            masked = [jnp.where(inside[k], value, 0.0) for k in range(donors)]
            for a in range(modes):
                coarse = coarse_ref[a, :, at : at + lanes]
                row = a * variables + v
                for k in range(donors):
                    pair_ref[row : row + 1, k * fine + at : k * fine + at + lanes] = jnp.sum(
                        coarse * masked[k], axis=0, keepdims=True
                    )

    both = jnp.concatenate(split(pair_ref[...]), axis=0)
    lane = rows_of((total, lanes), 1).astype(jnp.int16)
    one, zero = jnp.ones((total, lanes), BF16), jnp.zeros((total, lanes), BF16)
    for c in range(chunks):
        chooser = jnp.concatenate(
            [
                jnp.where(slot == lane + jnp.int16(c * width + j), one, zero)
                for j in range(0, width, lanes)
            ],
            axis=1,
        )
        placed = mm(both, chooser)
        placed = placed[:depth] + placed[depth:]
        rows = out_ref.shape[1] // 2
        for j in range(2):
            out_ref[c, j * rows : (j + 1) * rows] = placed[:rows, j * width // 2 : (j + 1) * width // 2]


def seat_kernel(columns_ref, *refs, capacity):
    out_refs, scratch = refs[:-1], refs[-1]
    sources, rows, _ = columns_ref.shape
    rows = rows // 2
    count, full, block = scratch.shape
    for h in range(count):
        j, at = divmod(h * capacity, columns_ref.shape[2])
        got = jnp.concatenate(
            [
                columns_ref[s, j * rows : j * rows + full + 1, at : at + capacity]
                for s in range(sources)
            ],
            axis=1,
        )
        seat = got[full : full + 1, :]
        chooser = (rows_of((block, got.shape[1]), 0).astype(F32) == seat).astype(F32).astype(BF16)
        high, low = split(got)
        scratch[h] = (mm(high, chooser, 1, 1) + mm(low, chooser, 1, 1))[:full]
    if len(out_refs) == 1:
        out_refs[0][...] = scratch[...]
    else:
        here = lax.axis_index("high")
        for d in range(count):
            out_refs[d][...] = scratch[here ^ d]


def renumber_kernel(place_ref, *refs):
    block_refs, out_ref = refs[:-1], refs[-1]
    block = place_ref.shape[1]
    if len(block_refs) == 1:
        total = block_refs[0][0]
        for h in range(1, block_refs[0].shape[0]):
            total += block_refs[0][h]
    else:
        total = block_refs[0][...]
        for ref in block_refs[1:]:
            total += ref[...]
    full = total.shape[0]
    place = place_ref[...]
    chooser = (rows_of((block, block), 0) == place % block).astype(F32).astype(BF16)
    high, low = split(total)
    out_ref[:full, :] = mm(high, chooser, 1, 1) + mm(low, chooser, 1, 1)
    out_ref[full:, :] = (place // block).astype(F32)


def prepare_kernel(offset_ref, lift_ref, chooser_ref, lift_out_ref, *, variables, slab):
    faces, block = offset_ref.shape
    modes = lift_ref.shape[0]
    full = modes * variables
    choose(offset_ref[...], chooser_ref, 0)
    width = variables * faces * slab
    column = rows_of((modes, width), 1)
    mode = rows_of((modes, width), 0)
    spread = jnp.zeros((modes, width), F32)
    for f in range(faces):
        put = (column % slab == mode) & ((column // slab) % faces == f)
        spread += mm(lift_ref[:, f, :], put.astype(F32), 1, 0, lax.Precision.HIGHEST)
    expand = (rows_of((full, modes), 0) // variables == rows_of((full, modes), 1)).astype(F32)
    lifted = mm(expand, spread, 1, 0, lax.Precision.HIGHEST)
    keep = rows_of((full, width), 1) // (slab * faces) == rows_of((full, width), 0) % variables
    lift_out_ref[...] = jnp.where(keep, lifted, 0.0)


def inner_is_left():
    return lax.axis_index("sub") % 2 == 1


def pack_quarters(pieces):
    reach = pieces[0].shape[1] // 4
    turned = [pieces[0]] + [pltpu.roll(pieces[g], g * reach, 1) for g in range(1, 4)]
    quarter = rows_of(pieces[0].shape, 1) // reach
    to_left, to_right = turned[0], turned[0]
    for g in range(1, 4):
        to_left = jnp.where(quarter == g, turned[g], to_left)
        to_right = jnp.where(quarter == g - 1, turned[g], to_right)
    left = inner_is_left()
    return jnp.where(left, to_left, to_right), jnp.where(left, to_right, to_left)


def take_quarters(inner, outer):
    reach = inner.shape[1] // 4
    quarter = rows_of(inner.shape, 1) // reach
    pieces = []
    for g in range(4):
        piece = jnp.where((quarter == g) != inner_is_left(), inner, outer)
        pieces.append(pltpu.roll(piece, (4 - g) * reach, 1) if g else piece)
    return pieces


def pack_halves(one, two):
    block = one.shape[1]
    turned = pltpu.roll(two, block // 2, 1)
    kept = (rows_of(one.shape, 1) < block // 2) == inner_is_left()
    return jnp.where(kept, one, turned), jnp.where(kept, turned, one)


def take_halves(inner, outer):
    block = inner.shape[1]
    from_inner = (rows_of(inner.shape, 1) >= block // 2) == inner_is_left()
    two = jnp.where(from_inner, outer, inner)
    return jnp.where(from_inner, inner, outer), pltpu.roll(two, block // 2, 1)


def pack_kernel(after_ref, inverse_ref, jacobian_ref, offset_ref, inner_ref, outer_ref, lines):
    del after_ref
    full, _, block = inverse_ref.shape
    variables, _, faces, _ = jacobian_ref.shape
    slabs = inner_ref.shape[0] - 1
    for j in range(slabs):
        index = [j + g * slabs for g in range(4)]
        pieces = [inverse_ref[i] if i < full else jnp.zeros((full, block), F32) for i in index]
        inner_ref[j], outer_ref[j] = pack_quarters(pieces)
    for w in range(variables):
        for v in range(variables):
            at = (w * variables + v) * faces
            lines[at : at + faces, :] = jacobian_ref[w, v]
    count = lines.shape[0] // 4
    packed = pack_quarters([lines[g * count : (g + 1) * count, :] for g in range(4)])
    offset = offset_ref[...].astype(F32)
    for ref, rows in zip((inner_ref, outer_ref), packed):
        ref[slabs] = jnp.zeros((full, block), F32)
        ref[slabs, :count, :] = rows
        ref[slabs, full - faces :, :] = offset


def beside_kernel(inner_ref, outer_ref, inverse_ref, jacobian_ref, chooser_ref, *, faces):
    full, _, block = inverse_ref.shape
    slabs = inner_ref.shape[0] - 1
    for j in range(slabs):
        for g, piece in enumerate(take_quarters(inner_ref[j], outer_ref[j])):
            if j + g * slabs < full:
                inverse_ref[j + g * slabs] = piece
    count = jacobian_ref.shape[0] // 4
    pieces = take_quarters(inner_ref[slabs, :count, :], outer_ref[slabs, :count, :])
    for g, piece in enumerate(pieces):
        jacobian_ref[g * count : (g + 1) * count, :] = piece
    inner, outer = inner_ref[slabs, full - faces :, :], outer_ref[slabs, full - faces :, :]
    from_inner = (rows_of(inner.shape, 1) >= block // 2) == inner_is_left()
    choose(jnp.where(from_inner, inner, outer).astype(jnp.int32), chooser_ref, block)


def choose(offsets, chooser_ref, first):
    faces, block = offsets.shape
    lane = rows_of((1, block), 1) + first
    row = rows_of((2 * block, block), 0)
    for f in range(faces):
        offset = offsets[f : f + 1, :]
        source = jnp.where(offset != 0, (lane + offset) & (2 * block - 1), -1)
        chooser_ref[:, f * block : (f + 1) * block] = (row == source).astype(F32).astype(BF16)


def apply_inverse(inverse_refs, fields, adder_ref, parts):
    full, _, block = inverse_refs[0].shape
    width = len(fields) * block
    for t, (inverse_ref, field) in enumerate(zip(inverse_refs, fields)):
        for i in range(full):
            product = inverse_ref[i] * field
            partial = product[0:8]
            for j in range(8, full - 7, 8):
                partial += product[j : j + 8]
            rest = full % 8
            if rest:
                partial = jnp.concatenate(
                    [partial[:rest] + product[full - rest :], partial[rest:]], axis=0
                )
            parts[i * 8 : i * 8 + 8, t * block : (t + 1) * block] = partial
    high, low = split(parts[:, :width])
    adder = adder_ref[...]
    return mm(adder, high) + mm(adder, low)


def first_kernel(inverse_ref, adder_ref, *refs, subs):
    block_refs, (total_ref, out_ref, inner_ref, outer_ref, padded, parts) = refs[:-6], refs[-6:]
    full = total_ref.shape[0]
    owner = lax.axis_index("high") * lax.axis_size("low") + lax.axis_index("low")
    owner = (owner * subs + lax.axis_index("sub")).astype(F32)
    residual = jnp.zeros(total_ref.shape, F32)
    for ref in block_refs:
        residual += jnp.where(ref[full:, :] == owner, ref[:full, :], 0.0)
    total_ref[...] = residual
    depth = padded.shape[0]
    padded[full:, :] = jnp.zeros((depth - full, padded.shape[1]), F32)
    padded[:full, :] = residual
    x = apply_inverse([inverse_ref], [residual], adder_ref, parts)
    out_ref[...] = x
    half, quarter = depth // 2, depth // 4
    inner_ref[:half, :], outer_ref[:half, :] = pack_halves(x[:half], x[half:])
    inner_ref[half:, :], outer_ref[half:, :] = pack_quarters(
        [padded[g * quarter : (g + 1) * quarter, :] for g in range(4)]
    )


def sweep_kernel(
    inverse_ref, inverse_beside_ref, sweep_adder_ref, adder_ref, residual_ref, x_ref, outer_ref, inner_ref,
    chooser_ref, chooser_beside_ref, lift_ref, jacobian_ref, jacobian_beside_ref, total_ref, out_ref,
    picked_ref, z_high, z_low, parts, *, variables, slab
):
    depth, block = x_ref.shape
    full = residual_ref.shape[0]
    modes = full // variables
    faces = jacobian_ref.shape[2]
    residual = residual_ref[...]
    total_ref[...] = residual
    lift_high, lift_low = split(lift_ref[...])

    def coupled(x, tiles):
        x = jnp.concatenate(split(x), axis=0)
        for t, ref in enumerate((chooser_ref, chooser_beside_ref)[:tiles]):
            picked = mm(x, ref[...])
            picked_ref[...] = picked[:depth] + picked[depth:]
            for f in range(faces):
                at = f * block
                part = [
                    picked_ref[v * modes : v * modes + slab, at : at + block]
                    for v in range(variables)
                ]
                for w in range(variables):
                    z = jnp.zeros((slab, block), F32)
                    for v in range(variables):
                        if t:
                            line = (w * variables + v) * faces + f
                            z += part[v] * jacobian_beside_ref[line : line + 1, :]
                        else:
                            z += part[v] * jacobian_ref[w, v, f : f + 1, :]
                    line, column = (w * faces + f) * slab, t * block
                    high, low = split(z)
                    z_high[line : line + slab, column : column + block] = high
                    z_low[line : line + slab, column : column + block] = low
        high, low = z_high[:, : tiles * block], z_low[:, : tiles * block]
        return mm(lift_high, high) + mm(lift_high, low) + mm(lift_low, high)

    half = depth // 2
    first_beside = jnp.concatenate(take_halves(inner_ref[:half, :], outer_ref[:half, :]), axis=0)
    beside = take_quarters(inner_ref[half:, :], outer_ref[half:, :])
    beside = jnp.concatenate(beside, axis=0)[:full]
    taken = coupled(jnp.concatenate([x_ref[...], first_beside], axis=1), 2)
    second = apply_inverse(
        [inverse_ref, inverse_beside_ref],
        [residual - taken[:, :block], beside - taken[:, block:]],
        sweep_adder_ref,
        parts,
    )
    out_ref[...] = apply_inverse([inverse_ref], [residual - coupled(second, 1)], adder_ref, parts)


def per_device(
    fine_residual,
    fine_basis,
    coarse_basis,
    donor_cells,
    point_counts,
    solver_pos,
    block_inverse,
    face_jacobian,
    face_lift,
    face_offset,
):
    high_count = lax.axis_size("high")
    passing = lax.axis_size("low") * lax.axis_size("sub")
    owners = high_count * passing
    _, variables, fine = fine_residual.shape
    modes = coarse_basis.shape[1]
    donors = donor_cells.shape[1]
    block = solver_pos.shape[0]
    faces = face_offset.shape[0]
    full = modes * variables
    slab = -(-modes // 16) * 16
    depth = -(-full // 16) * 16

    capacity = max(2, 2 * fine * donors // owners)
    subs = lax.axis_size("sub")
    counter, sweep_adder, adder = call(
        functools.partial(constants_kernel, variables=variables),
        "constants",
        [((128, 256), BF16), ((depth, 8 * full), BF16), ((full, 8 * full), BF16)],
        (),
        cost=pl.CostEstimate(flops=2 * 10**9, bytes_accessed=8 * 10**6, transcendentals=0),
    )
    rows = -(-(full + 1) // 4) * 4
    columns = call(
        functools.partial(
            restrict_kernel, owners=owners, block=block, passing=passing, capacity=capacity
        ),
        "restrict",
        ((passing, 2 * rows, high_count * capacity // 2), F32),
        (
            counter,
            fine_residual.transpose(1, 0, 2),
            fine_basis.T,
            coarse_basis.transpose(1, 0, 2),
            point_counts.T,
            donor_cells.T,
        ),
        [pltpu.VMEM((depth, donors * fine), F32)],
        megabytes=16,
    )
    columns = lax.all_to_all(columns, PLANE, 0, 0, tiled=True)
    few = high_count <= 8
    blocks = call(
        functools.partial(seat_kernel, capacity=capacity),
        "seat_columns",
        [((full, block), F32)] * high_count if few else [((high_count, full, block), F32)],
        (columns,),
        [pltpu.VMEM((high_count, full, block), F32)],
        megabytes=24,
    )
    if few:
        blocks = swap_all(blocks, "high")
    else:
        blocks = [lax.all_to_all(blocks[0], "high", 0, 0, tiled=True)]
    whole = call(
        renumber_kernel, "renumber", ((full + 1, block), F32), (solver_pos[None, :], *blocks)
    )
    blocks = swap_all([whole] * subs, "sub")

    jacobian = face_jacobian.transpose(1, 2, 0, 3)
    chooser, lift = call(
        functools.partial(prepare_kernel, variables=variables, slab=slab),
        "prepare",
        [((2 * block, faces * block), BF16), ((full, variables * faces * slab), F32)],
        (face_offset, face_lift.transpose(1, 0, 2)),
    )
    outer_pairs = [(i, i + 1) for i in range(1, owners - 1, 2)]
    outer_pairs += [(j, i) for i, j in outer_pairs]
    inner_pairs = [(i, i ^ 1) for i in range(owners)]
    packed = ((-(-full // 4) + 1, full, block), F32)
    lines = variables * variables * faces
    to_inner, to_outer = call(
        pack_kernel,
        "pack",
        [packed, packed],
        (counter, block_inverse, jacobian, face_offset),
        [pltpu.VMEM((lines, block), F32)],
    )
    outer = lax.ppermute(to_outer, WHOLE, outer_pairs)
    inner = lax.ppermute(to_inner, WHOLE, inner_pairs)
    inverse_beside, jacobian_beside, chooser_beside = call(
        functools.partial(beside_kernel, faces=faces),
        "beside",
        [((full, full, block), F32), ((lines, block), F32), ((2 * block, faces * block), BF16)],
        (inner, outer),
    )
    plain, edge = ((full, block), F32), ((depth // 4 * 3, block), F32)
    residual, x, to_inner, to_outer = call(
        functools.partial(first_kernel, subs=subs),
        "first",
        [plain, ((depth, block), F32), edge, edge],
        (block_inverse, sweep_adder, *blocks),
        [pltpu.VMEM((depth, block), F32), pltpu.VMEM((8 * full, block), F32)],
    )
    outer = lax.ppermute(to_outer, WHOLE, outer_pairs)
    inner = lax.ppermute(to_inner, WHOLE, inner_pairs)
    return tuple(
        call(
            functools.partial(sweep_kernel, variables=variables, slab=slab),
            "sweeps",
            [plain, plain],
            (
                block_inverse,
                inverse_beside,
                sweep_adder,
                adder,
                residual,
                x,
                outer,
                inner,
                chooser,
                chooser_beside,
                lift,
                jacobian,
                jacobian_beside,
            ),
            [pltpu.VMEM((depth, faces * block), F32)]
            + [pltpu.VMEM((variables * faces * slab, 2 * block), BF16)] * 2
            + [pltpu.VMEM((8 * full, 2 * block), F32)],
        )
    )


def solution(mesh):
    dom, sub = mesh.devices.shape
    low = 2 if dom % 2 == 0 else 1
    split_mesh = jax.sharding.Mesh(mesh.devices.reshape(dom // low, low, sub), WHOLE)
    in_specs = (
        P(None, None, WHOLE),
        P(),
        P(None, None, WHOLE),
        P(WHOLE, None),
        P(WHOLE, None),
        P(WHOLE),
        P(None, None, WHOLE),
        P(None, None, None, WHOLE),
        P(),
        P(None, WHOLE),
    )
    return jax.shard_map(
        per_device,
        mesh=split_mesh,
        in_specs=in_specs,
        out_specs=(P(None, WHOLE), P(None, WHOLE)),
        check_vma=False,
    )
```

```python
import functools
import jax
import jax.numpy as jnp
from jax import lax
from jax.experimental import pallas as pl
from jax.experimental.pallas import tpu as pltpu
from jax.sharding import PartitionSpec as P

F32 = jnp.float32
BF16 = jnp.bfloat16
PLANE = ("low", "sub")
WHOLE = ("high", "low", "sub")
VMEM = pl.BlockSpec(memory_space=pltpu.VMEM)


def split(x):
    high = x.astype(BF16)
    return high, (x - high.astype(F32)).astype(BF16)


def mm(a, b, ca=1, cb=0, precision=None):
    return lax.dot_general(
        a, b, (((ca,), (cb,)), ((), ())), precision=precision, preferred_element_type=F32
    )


def rows_of(iota_shape, dim):
    return lax.broadcasted_iota(jnp.int32, iota_shape, dim)


def call(kernel, name, shapes, args, scratch=(), megabytes=8, cost=None):
    single = not isinstance(shapes, list)
    out = [jax.ShapeDtypeStruct(*shape) for shape in ([shapes] if single else shapes)]
    result = pl.pallas_call(
        kernel,
        out_shape=out,
        in_specs=[VMEM] * len(args),
        out_specs=[VMEM] * len(out),
        scratch_shapes=list(scratch),
        compiler_params=pltpu.CompilerParams(vmem_limit_bytes=megabytes * 2**20),
        cost_estimate=cost,
        name=name,
    )(*args)
    return result[0] if single else result


def swap_all(blocks, axis):
    count = len(blocks)
    return [blocks[0]] + [
        lax.ppermute(blocks[d], axis, [(i, i ^ d) for i in range(count)])
        for d in range(count - 1, 0, -1)
    ]


def constants_kernel(counter_ref, sweep_adder_ref, adder_ref, *, variables):
    lanes = counter_ref.shape[0]
    earlier = (rows_of((lanes, lanes), 0) < rows_of((lanes, lanes), 1)).astype(F32)
    counter = jnp.concatenate([earlier, jnp.ones((lanes, lanes), F32)], axis=1)
    counter_ref[...] = counter.astype(BF16)
    full = adder_ref.shape[0]
    for ref in (sweep_adder_ref, adder_ref):
        row, source = rows_of(ref.shape, 0), rows_of(ref.shape, 1) // 8
        if ref is sweep_adder_ref:
            source = (source % variables) * (full // variables) + source // variables
        ref[...] = (row == source).astype(F32).astype(BF16)


def free_columns(owner, counter, owners, passing, capacity, width, high):
    lanes = 128
    total = owner.shape[1]
    parts = total // lanes
    mine = (rows_of((owners, total), 0) == owner).astype(F32)
    stacked = jnp.concatenate([mine[:, j * lanes : (j + 1) * lanes] for j in range(parts)], axis=0)
    counted = mm(stacked.astype(BF16), counter)
    before = jnp.zeros((owners, lanes), F32)
    ranks = []
    for j in range(parts):
        own = mine[:, j * lanes : (j + 1) * lanes]
        part = counted[j * owners : (j + 1) * owners]
        ranks.append(jnp.sum(own * (before + part[:, :lanes]), axis=0, keepdims=True))
        before += part[:, lanes:]
    rank = jnp.concatenate(ranks, axis=1).astype(jnp.int32)
    return (owner % passing) * width + (owner // passing ^ high) * capacity + rank


def restrict_kernel(
    counter_ref, res_ref, basis_ref, coarse_ref, counts_ref, donors_ref, out_ref, pair_ref,
    *, owners, block, passing, capacity, few
):
    variables, _, fine = res_ref.shape
    modes, points, _ = coarse_ref.shape
    donors = counts_ref.shape[0]
    chunks = out_ref.shape[0]
    full = modes * variables
    depth = pair_ref.shape[0]
    total = donors * fine
    lanes = 128
    width = owners // passing * capacity

    cell = jnp.concatenate([donors_ref[k : k + 1, :] for k in range(donors)], axis=1)
    pair_ref[full:, :] = jnp.zeros((depth - full, total), F32)
    pair_ref[full : full + 1, :] = (cell % block).astype(F32)
    high = lax.axis_index("high") if few else 0
    slot = free_columns(cell // block, counter_ref[...], owners, passing, capacity, width, high)
    slot = jnp.broadcast_to(slot.astype(F32), (lanes, total)).T.astype(jnp.int32).astype(jnp.int16)

    basis_high, basis_low = split(basis_ref[...])
    res_high, res_low = split(jnp.concatenate([res_ref[v] for v in range(variables)], axis=1))
    values = mm(basis_high, res_high, 0, 0)
    values += mm(basis_high, res_low, 0, 0) + mm(basis_low, res_high, 0, 0)

    point = rows_of((points, lanes), 0)
    for at in range(0, fine, lanes):
        upper = jnp.zeros((1, lanes), jnp.int32)
        inside = []
        for k in range(donors):
            lower = upper
            upper = lower + counts_ref[k : k + 1, at : at + lanes]
            inside.append((point >= lower) & (point < upper))
        for v in range(variables):
            column = v * fine + at
            value = values[:, column : column + lanes]
            masked = [jnp.where(inside[k], value, 0.0) for k in range(donors)]
            for a in range(modes):
                coarse = coarse_ref[a, :, at : at + lanes]
                row = a * variables + v
                for k in range(donors):
                    pair_ref[row : row + 1, k * fine + at : k * fine + at + lanes] = jnp.sum(
                        coarse * masked[k], axis=0, keepdims=True
                    )

    both = jnp.concatenate(split(pair_ref[...]), axis=0)
    lane = rows_of((total, lanes), 1).astype(jnp.int16)
    one, zero = jnp.ones((total, lanes), BF16), jnp.zeros((total, lanes), BF16)
    for c in range(chunks):
        chooser = jnp.concatenate(
            [
                jnp.where(slot == lane + jnp.int16(c * width + j), one, zero)
                for j in range(0, width, lanes)
            ],
            axis=1,
        )
        placed = mm(both, chooser)
        placed = placed[:depth] + placed[depth:]
        rows = out_ref.shape[1] // 2
        for j in range(2):
            out_ref[c, j * rows : (j + 1) * rows] = placed[:rows, j * width // 2 : (j + 1) * width // 2]


def seat_kernel(columns_ref, *out_refs, groups, capacity):
    sources, rows, _ = columns_ref.shape
    rows = rows // 2
    full, block = out_refs[0].shape[-2:]
    for n, group in enumerate(groups):
        j, at = divmod(group * capacity, columns_ref.shape[2])
        got = jnp.concatenate(
            [
                columns_ref[s, j * rows : j * rows + full + 1, at : at + capacity]
                for s in range(sources)
            ],
            axis=1,
        )
        seat = got[full : full + 1, :]
        chooser = (rows_of((block, got.shape[1]), 0).astype(F32) == seat).astype(F32).astype(BF16)
        high, low = split(got)
        dense = (mm(high, chooser, 1, 1) + mm(low, chooser, 1, 1))[:full]
        if len(out_refs) == len(groups):
            out_refs[n][...] = dense
        else:
            out_refs[0][n] = dense


def renumber_kernel(place_ref, *refs):
    block_refs, out_ref = refs[:-1], refs[-1]
    block = place_ref.shape[1]
    if len(block_refs) == 1:
        total = block_refs[0][0]
        for h in range(1, block_refs[0].shape[0]):
            total += block_refs[0][h]
    else:
        total = block_refs[0][...]
        for ref in block_refs[1:]:
            total += ref[...]
    full = total.shape[0]
    place = place_ref[...]
    chooser = (rows_of((block, block), 0) == place % block).astype(F32).astype(BF16)
    high, low = split(total)
    out_ref[:full, :] = mm(high, chooser, 1, 1) + mm(low, chooser, 1, 1)
    out_ref[full:, :] = (place // block).astype(F32)


def prepare_kernel(after_ref, offset_ref, lift_ref, chooser_ref, lift_out_ref, *, variables, slab):
    del after_ref
    faces, block = offset_ref.shape
    modes = lift_ref.shape[0]
    full = modes * variables
    choose(offset_ref[...], chooser_ref, 0)
    width = variables * faces * slab
    column = rows_of((modes, width), 1)
    mode = rows_of((modes, width), 0)
    spread = jnp.zeros((modes, width), F32)
    for f in range(faces):
        put = (column % slab == mode) & ((column // slab) % faces == f)
        spread += mm(lift_ref[:, f, :], put.astype(F32), 1, 0, lax.Precision.HIGHEST)
    expand = (rows_of((full, modes), 0) // variables == rows_of((full, modes), 1)).astype(F32)
    lifted = mm(expand, spread, 1, 0, lax.Precision.HIGHEST)
    keep = rows_of((full, width), 1) // (slab * faces) == rows_of((full, width), 0) % variables
    lift_out_ref[...] = jnp.where(keep, lifted, 0.0)


def inner_is_left():
    return lax.axis_index("sub") % 2 == 1


def pack_quarters(pieces):
    reach = pieces[0].shape[1] // 4
    turned = [pieces[0]] + [pltpu.roll(pieces[g], g * reach, 1) for g in range(1, 4)]
    quarter = rows_of(pieces[0].shape, 1) // reach
    to_left, to_right = turned[0], turned[0]
    for g in range(1, 4):
        to_left = jnp.where(quarter == g, turned[g], to_left)
        to_right = jnp.where(quarter == g - 1, turned[g], to_right)
    left = inner_is_left()
    return jnp.where(left, to_left, to_right), jnp.where(left, to_right, to_left)


def take_quarters(inner, outer):
    reach = inner.shape[1] // 4
    quarter = rows_of(inner.shape, 1) // reach
    pieces = []
    for g in range(4):
        piece = jnp.where((quarter == g) != inner_is_left(), inner, outer)
        pieces.append(pltpu.roll(piece, (4 - g) * reach, 1) if g else piece)
    return pieces


def pack_halves(one, two):
    block = one.shape[1]
    turned = pltpu.roll(two, block // 2, 1)
    kept = (rows_of(one.shape, 1) < block // 2) == inner_is_left()
    return jnp.where(kept, one, turned), jnp.where(kept, turned, one)


def take_halves(inner, outer):
    block = inner.shape[1]
    from_inner = (rows_of(inner.shape, 1) >= block // 2) == inner_is_left()
    two = jnp.where(from_inner, outer, inner)
    return jnp.where(from_inner, inner, outer), pltpu.roll(two, block // 2, 1)


def pack_kernel(after_ref, inverse_ref, jacobian_ref, offset_ref, inner_ref, outer_ref, lines):
    del after_ref
    full, _, block = inverse_ref.shape
    variables, _, faces, _ = jacobian_ref.shape
    slabs = inner_ref.shape[0] - 1
    for j in range(slabs):
        index = [j + g * slabs for g in range(4)]
        pieces = [inverse_ref[i] if i < full else jnp.zeros((full, block), F32) for i in index]
        inner_ref[j], outer_ref[j] = pack_quarters(pieces)
    for w in range(variables):
        for v in range(variables):
            at = (w * variables + v) * faces
            lines[at : at + faces, :] = jacobian_ref[w, v]
    count = lines.shape[0] // 4
    packed = pack_quarters([lines[g * count : (g + 1) * count, :] for g in range(4)])
    offset = offset_ref[...].astype(F32)
    for ref, rows in zip((inner_ref, outer_ref), packed):
        ref[slabs] = jnp.zeros((full, block), F32)
        ref[slabs, :count, :] = rows
        ref[slabs, full - faces :, :] = offset


def beside_kernel(inner_ref, outer_ref, inverse_ref, jacobian_ref, chooser_ref, *, faces):
    full, _, block = inverse_ref.shape
    slabs = inner_ref.shape[0] - 1
    for j in range(slabs):
        for g, piece in enumerate(take_quarters(inner_ref[j], outer_ref[j])):
            if j + g * slabs < full:
                inverse_ref[j + g * slabs] = piece
    count = jacobian_ref.shape[0] // 4
    pieces = take_quarters(inner_ref[slabs, :count, :], outer_ref[slabs, :count, :])
    for g, piece in enumerate(pieces):
        jacobian_ref[g * count : (g + 1) * count, :] = piece
    inner, outer = inner_ref[slabs, full - faces :, :], outer_ref[slabs, full - faces :, :]
    from_inner = (rows_of(inner.shape, 1) >= block // 2) == inner_is_left()
    choose(jnp.where(from_inner, inner, outer).astype(jnp.int32), chooser_ref, block)


def choose(offsets, chooser_ref, first):
    faces, block = offsets.shape
    lane = rows_of((1, block), 1) + first
    row = rows_of((2 * block, block), 0)
    for f in range(faces):
        offset = offsets[f : f + 1, :]
        source = jnp.where(offset != 0, (lane + offset) & (2 * block - 1), -1)
        chooser_ref[:, f * block : (f + 1) * block] = (row == source).astype(F32).astype(BF16)


def apply_inverse(inverse_refs, fields, adder_ref, parts):
    full, _, block = inverse_refs[0].shape
    width = len(fields) * block
    for t, (inverse_ref, field) in enumerate(zip(inverse_refs, fields)):
        for i in range(full):
            product = inverse_ref[i] * field
            partial = product[0:8]
            for j in range(8, full - 7, 8):
                partial += product[j : j + 8]
            rest = full % 8
            if rest:
                partial = jnp.concatenate(
                    [partial[:rest] + product[full - rest :], partial[rest:]], axis=0
                )
            parts[i * 8 : i * 8 + 8, t * block : (t + 1) * block] = partial
    high, low = split(parts[:, :width])
    adder = adder_ref[...]
    return mm(adder, high) + mm(adder, low)


def first_kernel(inverse_ref, adder_ref, *refs, subs):
    block_refs, (total_ref, out_ref, inner_ref, outer_ref, padded, parts) = refs[:-6], refs[-6:]
    full = total_ref.shape[0]
    owner = lax.axis_index("high") * lax.axis_size("low") + lax.axis_index("low")
    owner = (owner * subs + lax.axis_index("sub")).astype(F32)
    residual = jnp.zeros(total_ref.shape, F32)
    for ref in block_refs:
        residual += jnp.where(ref[full:, :] == owner, ref[:full, :], 0.0)
    total_ref[...] = residual
    depth = padded.shape[0]
    padded[full:, :] = jnp.zeros((depth - full, padded.shape[1]), F32)
    padded[:full, :] = residual
    x = apply_inverse([inverse_ref], [residual], adder_ref, parts)
    out_ref[...] = x
    half, quarter = depth // 2, depth // 4
    inner_ref[:half, :], outer_ref[:half, :] = pack_halves(x[:half], x[half:])
    inner_ref[half:, :], outer_ref[half:, :] = pack_quarters(
        [padded[g * quarter : (g + 1) * quarter, :] for g in range(4)]
    )


def sweep_kernel(
    inverse_ref, inverse_beside_ref, sweep_adder_ref, adder_ref, residual_ref, x_ref, outer_ref, inner_ref,
    chooser_ref, chooser_beside_ref, lift_ref, jacobian_ref, jacobian_beside_ref, total_ref, out_ref,
    picked_ref, z_high, z_low, parts, *, variables, slab
):
    depth, block = x_ref.shape
    full = residual_ref.shape[0]
    modes = full // variables
    faces = jacobian_ref.shape[2]
    residual = residual_ref[...]
    total_ref[...] = residual
    lift_high, lift_low = split(lift_ref[...])

    def coupled(x, tiles):
        x = jnp.concatenate(split(x), axis=0)
        for t, ref in enumerate((chooser_ref, chooser_beside_ref)[:tiles]):
            picked = mm(x, ref[...])
            picked_ref[...] = picked[:depth] + picked[depth:]
            for f in range(faces):
                at = f * block
                part = [
                    picked_ref[v * modes : v * modes + slab, at : at + block]
                    for v in range(variables)
                ]
                for w in range(variables):
                    z = jnp.zeros((slab, block), F32)
                    for v in range(variables):
                        if t:
                            line = (w * variables + v) * faces + f
                            z += part[v] * jacobian_beside_ref[line : line + 1, :]
                        else:
                            z += part[v] * jacobian_ref[w, v, f : f + 1, :]
                    line, column = (w * faces + f) * slab, t * block
                    high, low = split(z)
                    z_high[line : line + slab, column : column + block] = high
                    z_low[line : line + slab, column : column + block] = low
        high, low = z_high[:, : tiles * block], z_low[:, : tiles * block]
        return mm(lift_high, high) + mm(lift_high, low) + mm(lift_low, high)

    half = depth // 2
    first_beside = jnp.concatenate(take_halves(inner_ref[:half, :], outer_ref[:half, :]), axis=0)
    beside = take_quarters(inner_ref[half:, :], outer_ref[half:, :])
    beside = jnp.concatenate(beside, axis=0)[:full]
    taken = coupled(jnp.concatenate([x_ref[...], first_beside], axis=1), 2)
    second = apply_inverse(
        [inverse_ref, inverse_beside_ref],
        [residual - taken[:, :block], beside - taken[:, block:]],
        sweep_adder_ref,
        parts,
    )
    out_ref[...] = apply_inverse([inverse_ref], [residual - coupled(second, 1)], adder_ref, parts)


def per_device(
    fine_residual,
    fine_basis,
    coarse_basis,
    donor_cells,
    point_counts,
    solver_pos,
    block_inverse,
    face_jacobian,
    face_lift,
    face_offset,
):
    high_count = lax.axis_size("high")
    passing = lax.axis_size("low") * lax.axis_size("sub")
    owners = high_count * passing
    _, variables, fine = fine_residual.shape
    modes = coarse_basis.shape[1]
    donors = donor_cells.shape[1]
    block = solver_pos.shape[0]
    faces = face_offset.shape[0]
    full = modes * variables
    slab = -(-modes // 16) * 16
    depth = -(-full // 16) * 16

    capacity = max(2, 2 * fine * donors // owners)
    few = 1 < high_count <= 8 and high_count & (high_count - 1) == 0
    subs = lax.axis_size("sub")
    counter, sweep_adder, adder = call(
        functools.partial(constants_kernel, variables=variables),
        "constants",
        [((128, 256), BF16), ((depth, 8 * full), BF16), ((full, 8 * full), BF16)],
        (),
        cost=pl.CostEstimate(flops=2 * 10**9, bytes_accessed=8 * 10**6, transcendentals=0),
    )
    rows = -(-(full + 1) // 4) * 4
    columns = call(
        functools.partial(
            restrict_kernel,
            owners=owners,
            block=block,
            passing=passing,
            capacity=capacity,
            few=few,
        ),
        "restrict",
        ((passing, 2 * rows, high_count * capacity // 2), F32),
        (
            counter,
            fine_residual.transpose(1, 0, 2),
            fine_basis.T,
            coarse_basis.transpose(1, 0, 2),
            point_counts.T,
            donor_cells.T,
        ),
        [pltpu.VMEM((depth, donors * fine), F32)],
        megabytes=16,
    )
    columns = lax.all_to_all(columns, PLANE, 0, 0, tiled=True)
    def seat(name, groups, shapes):
        return call(
            functools.partial(seat_kernel, groups=groups, capacity=capacity),
            name,
            shapes,
            (columns,),
            megabytes=24,
        )

    dense = ((full, block), F32)
    if few:
        far = high_count - 1
        last = seat("seat_far", [far], [dense])
        blocks = swap_all(seat("seat_near", range(far), [dense] * far) + last, "high")
    else:
        blocks = seat("seat_all", range(high_count), ((high_count, full, block), F32))
        blocks = [lax.all_to_all(blocks, "high", 0, 0, tiled=True)]
    whole = call(
        renumber_kernel, "renumber", ((full + 1, block), F32), (solver_pos[None, :], *blocks)
    )
    blocks = swap_all([whole] * subs, "sub")

    jacobian = face_jacobian.transpose(1, 2, 0, 3)
    chooser, lift = call(
        functools.partial(prepare_kernel, variables=variables, slab=slab),
        "prepare",
        [((2 * block, faces * block), BF16), ((full, variables * faces * slab), F32)],
        (counter, face_offset, face_lift.transpose(1, 0, 2)),
    )
    outer_pairs = [(i, i + 1) for i in range(1, owners - 1, 2)]
    outer_pairs += [(j, i) for i, j in outer_pairs]
    inner_pairs = [(i, i ^ 1) for i in range(owners)]
    packed = ((-(-full // 4) + 1, full, block), F32)
    lines = variables * variables * faces
    to_inner, to_outer = call(
        pack_kernel,
        "pack",
        [packed, packed],
        (lift, block_inverse, jacobian, face_offset),
        [pltpu.VMEM((lines, block), F32)],
    )
    outer = lax.ppermute(to_outer, WHOLE, outer_pairs)
    inner = lax.ppermute(to_inner, WHOLE, inner_pairs)
    inverse_beside, jacobian_beside, chooser_beside = call(
        functools.partial(beside_kernel, faces=faces),
        "beside",
        [((full, full, block), F32), ((lines, block), F32), ((2 * block, faces * block), BF16)],
        (inner, outer),
    )
    plain, edge = ((full, block), F32), ((depth // 4 * 3, block), F32)
    residual, x, to_inner, to_outer = call(
        functools.partial(first_kernel, subs=subs),
        "first",
        [plain, ((depth, block), F32), edge, edge],
        (block_inverse, sweep_adder, *blocks),
        [pltpu.VMEM((depth, block), F32), pltpu.VMEM((8 * full, block), F32)],
    )
    outer = lax.ppermute(to_outer, WHOLE, outer_pairs)
    inner = lax.ppermute(to_inner, WHOLE, inner_pairs)
    return tuple(
        call(
            functools.partial(sweep_kernel, variables=variables, slab=slab),
            "sweeps",
            [plain, plain],
            (
                block_inverse,
                inverse_beside,
                sweep_adder,
                adder,
                residual,
                x,
                outer,
                inner,
                chooser,
                chooser_beside,
                lift,
                jacobian,
                jacobian_beside,
            ),
            [pltpu.VMEM((depth, faces * block), F32)]
            + [pltpu.VMEM((variables * faces * slab, 2 * block), BF16)] * 2
            + [pltpu.VMEM((8 * full, 2 * block), F32)],
        )
    )


def solution(mesh):
    dom, sub = mesh.devices.shape
    low = 2 if dom % 2 == 0 else 1
    split_mesh = jax.sharding.Mesh(mesh.devices.reshape(dom // low, low, sub), WHOLE)
    in_specs = (
        P(None, None, WHOLE),
        P(),
        P(None, None, WHOLE),
        P(WHOLE, None),
        P(WHOLE, None),
        P(WHOLE),
        P(None, None, WHOLE),
        P(None, None, None, WHOLE),
        P(),
        P(None, WHOLE),
    )
    return jax.shard_map(
        per_device,
        mesh=split_mesh,
        in_specs=in_specs,
        out_specs=(P(None, WHOLE), P(None, WHOLE)),
        check_vma=False,
    )
```

```python
import functools
import jax
import jax.numpy as jnp
from jax import lax
from jax.experimental import pallas as pl
from jax.experimental.pallas import tpu as pltpu
from jax.sharding import PartitionSpec as P

F32 = jnp.float32
BF16 = jnp.bfloat16
PLANE = ("low", "sub")
WHOLE = ("high", "low", "sub")
VMEM = pl.BlockSpec(memory_space=pltpu.VMEM)


def split(x):
    high = x.astype(BF16)
    return high, (x - high.astype(F32)).astype(BF16)


def mm(a, b, ca=1, cb=0, precision=None):
    return lax.dot_general(
        a, b, (((ca,), (cb,)), ((), ())), precision=precision, preferred_element_type=F32
    )


def rows_of(iota_shape, dim):
    return lax.broadcasted_iota(jnp.int32, iota_shape, dim)


def call(kernel, name, shapes, args, scratch=(), megabytes=8, cost=None, out_spec=VMEM):
    single = not isinstance(shapes, list)
    out = [jax.ShapeDtypeStruct(*shape) for shape in ([shapes] if single else shapes)]
    result = pl.pallas_call(
        kernel,
        out_shape=out,
        in_specs=[VMEM] * len(args),
        out_specs=[out_spec] * len(out),
        scratch_shapes=list(scratch),
        compiler_params=pltpu.CompilerParams(vmem_limit_bytes=megabytes * 2**20),
        cost_estimate=cost,
        name=name,
    )(*args)
    return result[0] if single else result


def swap_all(blocks, axis):
    count = len(blocks)
    return [blocks[0]] + [
        lax.ppermute(blocks[d], axis, [(i, i ^ d) for i in range(count)])
        for d in range(count - 1, 0, -1)
    ]


def constants_kernel(counter_ref):
    lanes = counter_ref.shape[0]
    earlier = (rows_of((lanes, lanes), 0) < rows_of((lanes, lanes), 1)).astype(F32)
    counter = jnp.concatenate([earlier, jnp.ones((lanes, lanes), F32)], axis=1)
    counter_ref[...] = counter.astype(BF16)


def free_columns(owner, counter, owners, passing, capacity, width, high):
    lanes = 128
    total = owner.shape[1]
    parts = total // lanes
    mine = (rows_of((owners, total), 0) == owner).astype(F32)
    stacked = jnp.concatenate([mine[:, j * lanes : (j + 1) * lanes] for j in range(parts)], axis=0)
    counted = mm(stacked.astype(BF16), counter)
    before = jnp.zeros((owners, lanes), F32)
    ranks = []
    for j in range(parts):
        own = mine[:, j * lanes : (j + 1) * lanes]
        part = counted[j * owners : (j + 1) * owners]
        ranks.append(jnp.sum(own * (before + part[:, :lanes]), axis=0, keepdims=True))
        before += part[:, lanes:]
    rank = jnp.concatenate(ranks, axis=1).astype(jnp.int32)
    return (owner % passing) * width + (owner // passing ^ high) * capacity + rank


def restrict_kernel(
    counter_ref, res_ref, basis_ref, coarse_ref, counts_ref, donors_ref, out_hbm, pair_ref, out_ref, sems,
    *, owners, block, passing, capacity, few
):
    variables, _, fine = res_ref.shape
    modes, points, _ = coarse_ref.shape
    donors = counts_ref.shape[0]
    chunks = out_ref.shape[0]
    full = modes * variables
    depth = pair_ref.shape[0]
    total = donors * fine
    lanes = 128
    width = owners // passing * capacity

    cell = jnp.concatenate([donors_ref[k : k + 1, :] for k in range(donors)], axis=1)
    pair_ref[full:, :] = jnp.zeros((depth - full, total), F32)
    pair_ref[full : full + 1, :] = (cell % block).astype(F32)
    high = lax.axis_index("high") if few else 0
    slot = free_columns(cell // block, counter_ref[...], owners, passing, capacity, width, high)
    slot = jnp.broadcast_to(slot.astype(F32), (lanes, total)).T.astype(jnp.int32).astype(jnp.int16)

    basis_high, basis_low = split(basis_ref[...])
    res_high, res_low = split(jnp.concatenate([res_ref[v] for v in range(variables)], axis=1))
    values = mm(basis_high, res_high, 0, 0)
    values += mm(basis_high, res_low, 0, 0) + mm(basis_low, res_high, 0, 0)

    point = rows_of((points, lanes), 0)
    for at in range(0, fine, lanes):
        upper = jnp.zeros((1, lanes), jnp.int32)
        inside = []
        for k in range(donors):
            lower = upper
            upper = lower + counts_ref[k : k + 1, at : at + lanes]
            inside.append((point >= lower) & (point < upper))
        for v in range(variables):
            column = v * fine + at
            value = values[:, column : column + lanes]
            masked = [jnp.where(inside[k], value, 0.0) for k in range(donors)]
            for a in range(modes):
                coarse = coarse_ref[a, :, at : at + lanes]
                row = a * variables + v
                for k in range(donors):
                    pair_ref[row : row + 1, k * fine + at : k * fine + at + lanes] = jnp.sum(
                        coarse * masked[k], axis=0, keepdims=True
                    )

    both = jnp.concatenate(split(pair_ref[...]), axis=0)
    lane = rows_of((total, lanes), 1).astype(jnp.int16)
    one, zero = jnp.ones((total, lanes), BF16), jnp.zeros((total, lanes), BF16)
    for c in range(chunks):
        chooser = jnp.concatenate(
            [
                jnp.where(slot == lane + jnp.int16(c * width + j), one, zero)
                for j in range(0, width, lanes)
            ],
            axis=1,
        )
        placed = mm(both, chooser)
        placed = placed[:depth] + placed[depth:]
        rows = out_ref.shape[1] // 2
        for j in range(2):
            out_ref[c, j * rows : (j + 1) * rows] = placed[:rows, j * width // 2 : (j + 1) * width // 2]
        pltpu.make_async_copy(out_ref.at[c], out_hbm.at[c], sems.at[c]).start()
    for c in range(chunks):
        pltpu.make_async_copy(out_ref.at[c], out_hbm.at[c], sems.at[c]).wait()


def seat_kernel(columns_ref, *out_refs, groups, capacity):
    sources, rows, _ = columns_ref.shape
    rows = rows // 2
    full, block = out_refs[0].shape[-2:]
    for n, group in enumerate(groups):
        j, at = divmod(group * capacity, columns_ref.shape[2])
        got = jnp.concatenate(
            [
                columns_ref[s, j * rows : j * rows + full + 1, at : at + capacity]
                for s in range(sources)
            ],
            axis=1,
        )
        seat = got[full : full + 1, :]
        chooser = (rows_of((block, got.shape[1]), 0).astype(F32) == seat).astype(F32).astype(BF16)
        high, low = split(got)
        dense = (mm(high, chooser, 1, 1) + mm(low, chooser, 1, 1))[:full]
        if len(out_refs) == len(groups):
            out_refs[n][...] = dense
        else:
            out_refs[0][n] = dense


def renumber_kernel(place_ref, *refs):
    block_refs, out_ref = refs[:-1], refs[-1]
    block = place_ref.shape[1]
    if len(block_refs) == 1:
        total = block_refs[0][0]
        for h in range(1, block_refs[0].shape[0]):
            total += block_refs[0][h]
    else:
        total = block_refs[0][...]
        for ref in block_refs[1:]:
            total += ref[...]
    full = total.shape[0]
    place = place_ref[...]
    chooser = (rows_of((block, block), 0) == place % block).astype(F32).astype(BF16)
    high, low = split(total)
    out_ref[:full, :] = mm(high, chooser, 1, 1) + mm(low, chooser, 1, 1)
    out_ref[full:, :] = (place // block).astype(F32)


def prepare_kernel(after_ref, offset_ref, lift_ref, chooser_ref, lift_out_ref, *, variables, slab):
    del after_ref
    faces, block = offset_ref.shape
    modes = lift_ref.shape[0]
    full = modes * variables
    choose(offset_ref[...], chooser_ref, 0)
    width = variables * faces * slab
    column = rows_of((modes, width), 1)
    mode = rows_of((modes, width), 0)
    spread = jnp.zeros((modes, width), F32)
    for f in range(faces):
        put = (column % slab == mode) & ((column // slab) % faces == f)
        spread += mm(lift_ref[:, f, :], put.astype(F32), 1, 0, lax.Precision.HIGHEST)
    expand = (rows_of((full, modes), 0) // variables == rows_of((full, modes), 1)).astype(F32)
    lifted = mm(expand, spread, 1, 0, lax.Precision.HIGHEST)
    keep = rows_of((full, width), 1) // (slab * faces) == rows_of((full, width), 0) % variables
    lift_out_ref[...] = jnp.where(keep, lifted, 0.0)


def inner_is_left():
    return lax.axis_index("sub") % 2 == 1


def pack_quarters(pieces):
    reach = pieces[0].shape[1] // 4
    turned = [pieces[0]] + [pltpu.roll(pieces[g], g * reach, 1) for g in range(1, 4)]
    quarter = rows_of(pieces[0].shape, 1) // reach
    to_left, to_right = turned[0], turned[0]
    for g in range(1, 4):
        to_left = jnp.where(quarter == g, turned[g], to_left)
        to_right = jnp.where(quarter == g - 1, turned[g], to_right)
    left = inner_is_left()
    return jnp.where(left, to_left, to_right), jnp.where(left, to_right, to_left)


def take_quarters(inner, outer):
    reach = inner.shape[1] // 4
    quarter = rows_of(inner.shape, 1) // reach
    pieces = []
    for g in range(4):
        piece = jnp.where((quarter == g) != inner_is_left(), inner, outer)
        pieces.append(pltpu.roll(piece, (4 - g) * reach, 1) if g else piece)
    return pieces


def pack_halves(one, two):
    block = one.shape[1]
    turned = pltpu.roll(two, block // 2, 1)
    kept = (rows_of(one.shape, 1) < block // 2) == inner_is_left()
    return jnp.where(kept, one, turned), jnp.where(kept, turned, one)


def take_halves(inner, outer):
    block = inner.shape[1]
    from_inner = (rows_of(inner.shape, 1) >= block // 2) == inner_is_left()
    two = jnp.where(from_inner, outer, inner)
    return jnp.where(from_inner, inner, outer), pltpu.roll(two, block // 2, 1)


def pack_kernel(after_ref, inverse_ref, jacobian_ref, offset_ref, inner_ref, outer_ref, lines):
    del after_ref
    full, _, block = inverse_ref.shape
    variables, _, faces, _ = jacobian_ref.shape
    slabs = inner_ref.shape[0] - 1
    for j in range(slabs):
        index = [j + g * slabs for g in range(4)]
        pieces = [inverse_ref[i] if i < full else jnp.zeros((full, block), F32) for i in index]
        inner_ref[j], outer_ref[j] = pack_quarters(pieces)
    for w in range(variables):
        for v in range(variables):
            at = (w * variables + v) * faces
            lines[at : at + faces, :] = jacobian_ref[w, v]
    count = lines.shape[0] // 4
    packed = pack_quarters([lines[g * count : (g + 1) * count, :] for g in range(4)])
    offset = offset_ref[...].astype(F32)
    for ref, rows in zip((inner_ref, outer_ref), packed):
        ref[slabs] = jnp.zeros((full, block), F32)
        ref[slabs, :count, :] = rows
        ref[slabs, full - faces :, :] = offset


def beside_kernel(inner_ref, outer_ref, inverse_ref, jacobian_ref, chooser_ref, *, faces):
    full, _, block = inverse_ref.shape
    slabs = inner_ref.shape[0] - 1
    for j in range(slabs):
        for g, piece in enumerate(take_quarters(inner_ref[j], outer_ref[j])):
            if j + g * slabs < full:
                inverse_ref[j + g * slabs] = piece
    count = jacobian_ref.shape[0] // 4
    pieces = take_quarters(inner_ref[slabs, :count, :], outer_ref[slabs, :count, :])
    for g, piece in enumerate(pieces):
        jacobian_ref[g * count : (g + 1) * count, :] = piece
    inner, outer = inner_ref[slabs, full - faces :, :], outer_ref[slabs, full - faces :, :]
    from_inner = (rows_of(inner.shape, 1) >= block // 2) == inner_is_left()
    choose(jnp.where(from_inner, inner, outer).astype(jnp.int32), chooser_ref, block)


def choose(offsets, chooser_ref, first):
    faces, block = offsets.shape
    lane = rows_of((1, block), 1) + first
    row = rows_of((2 * block, block), 0)
    for f in range(faces):
        offset = offsets[f : f + 1, :]
        source = jnp.where(offset != 0, (lane + offset) & (2 * block - 1), -1)
        chooser_ref[:, f * block : (f + 1) * block] = (row == source).astype(F32).astype(BF16)


def sum_rows(pieces):
    row = rows_of(pieces[0].shape, 0)
    pieces = [pieces[k] for k in (3, 2, 1, 0, 7, 6, 5, 4)]
    upper = row < 4
    halves = []
    for one, two in zip(pieces[:4], pieces[4:]):
        kept, moved = jnp.where(upper, one, two), jnp.where(upper, two, one)
        halves.append(kept + pltpu.roll(moved, 4, 0))
    for shift in (2, 1):
        pairs = list(zip(halves[:shift], halves[shift:]))
        halves = [
            jnp.where(
                row & shift != 0, one + pltpu.roll(one, shift, 0), two + pltpu.roll(two, 8 - shift, 0)
            )
            for one, two in pairs
        ]
    return halves[0]


def apply_inverse(inverse_ref, field, variables, depth=None):
    full, _, block = inverse_ref.shape
    modes = full // variables
    zero = jnp.zeros((8, block), F32)

    def piece(row):
        if row >= full:
            return zero
        product = inverse_ref[row % modes * variables + row // modes if depth else row] * field
        partial = product[0:8]
        for j in range(8, full - 7, 8):
            partial += product[j : j + 8]
        rest = full % 8
        if rest:
            partial += jnp.concatenate([product[full - rest :], zero[rest:]], axis=0)
        return partial

    rows = []
    for at in range(0, depth or full, 8):
        rows.append(sum_rows([piece(at + r) for r in range(8)]) if at < full else zero)
    return jnp.concatenate(rows, axis=0)[: depth or full]


def first_kernel(inverse_ref, *refs, subs, variables):
    block_refs, (total_ref, out_ref, inner_ref, outer_ref, padded) = refs[:-5], refs[-5:]
    full = total_ref.shape[0]
    owner = lax.axis_index("high") * lax.axis_size("low") + lax.axis_index("low")
    owner = (owner * subs + lax.axis_index("sub")).astype(F32)
    residual = jnp.zeros(total_ref.shape, F32)
    for ref in block_refs:
        residual += jnp.where(ref[full:, :] == owner, ref[:full, :], 0.0)
    total_ref[...] = residual
    depth = padded.shape[0]
    padded[full:, :] = jnp.zeros((depth - full, padded.shape[1]), F32)
    padded[:full, :] = residual
    x = apply_inverse(inverse_ref, residual, variables, depth)
    out_ref[...] = x
    half, quarter = depth // 2, depth // 4
    inner_ref[:half, :], outer_ref[:half, :] = pack_halves(x[:half], x[half:])
    inner_ref[half:, :], outer_ref[half:, :] = pack_quarters(
        [padded[g * quarter : (g + 1) * quarter, :] for g in range(4)]
    )


def sweep_kernel(
    inverse_ref, inverse_beside_ref, residual_ref, x_ref, outer_ref, inner_ref, chooser_ref,
    chooser_beside_ref, lift_ref, jacobian_ref, jacobian_beside_ref, total_ref, out_ref,
    picked_ref, z_high, z_low, *, variables, slab
):
    depth, block = x_ref.shape
    full = residual_ref.shape[0]
    modes = full // variables
    faces = jacobian_ref.shape[2]
    residual = residual_ref[...]
    total_ref[...] = residual
    lift_high, lift_low = split(lift_ref[...])

    def coupled(x, tiles):
        x = jnp.concatenate(split(x), axis=0)
        for t, ref in enumerate((chooser_ref, chooser_beside_ref)[:tiles]):
            picked = mm(x, ref[...])
            picked_ref[t] = picked[:depth] + picked[depth:]
        for t in range(tiles):
            for f in range(faces):
                at = f * block
                part = [
                    picked_ref[t, v * modes : v * modes + slab, at : at + block]
                    for v in range(variables)
                ]
                for w in range(variables):
                    z = None
                    for v in range(variables):
                        if t:
                            line = (w * variables + v) * faces + f
                            term = part[v] * jacobian_beside_ref[line : line + 1, :]
                        else:
                            term = part[v] * jacobian_ref[w, v, f : f + 1, :]
                        z = z + term if v else term
                    line, column = (w * faces + f) * slab, t * block
                    high, low = split(z)
                    z_high[line : line + slab, column : column + block] = high
                    z_low[line : line + slab, column : column + block] = low
        high, low = z_high[:, : tiles * block], z_low[:, : tiles * block]
        return mm(lift_high, high) + mm(lift_high, low) + mm(lift_low, high)

    half = depth // 2
    first_beside = jnp.concatenate(take_halves(inner_ref[:half, :], outer_ref[:half, :]), axis=0)
    beside = take_quarters(inner_ref[half:, :], outer_ref[half:, :])
    beside = jnp.concatenate(beside, axis=0)[:full]
    taken = coupled(jnp.concatenate([x_ref[...], first_beside], axis=1), 2)
    second = jnp.concatenate(
        [
            apply_inverse(inverse_ref, residual - taken[:, :block], variables, depth),
            apply_inverse(inverse_beside_ref, beside - taken[:, block:], variables, depth),
        ],
        axis=1,
    )
    out_ref[...] = apply_inverse(inverse_ref, residual - coupled(second, 1), variables)


def per_device(
    fine_residual,
    fine_basis,
    coarse_basis,
    donor_cells,
    point_counts,
    solver_pos,
    block_inverse,
    face_jacobian,
    face_lift,
    face_offset,
):
    high_count = lax.axis_size("high")
    passing = lax.axis_size("low") * lax.axis_size("sub")
    owners = high_count * passing
    _, variables, fine = fine_residual.shape
    modes = coarse_basis.shape[1]
    donors = donor_cells.shape[1]
    block = solver_pos.shape[0]
    faces = face_offset.shape[0]
    full = modes * variables
    slab = -(-modes // 16) * 16
    depth = -(-full // 16) * 16

    capacity = max(2, 2 * fine * donors // owners)
    few = 1 < high_count <= 8 and high_count & (high_count - 1) == 0
    subs = lax.axis_size("sub")
    counter = call(
        constants_kernel,
        "constants",
        ((128, 256), BF16),
        (),
        cost=pl.CostEstimate(flops=2 * 10**9, bytes_accessed=8 * 10**6, transcendentals=0),
    )
    rows = -(-(full + 1) // 4) * 4
    chunk_shape = (passing, 2 * rows, high_count * capacity // 2)
    columns = call(
        functools.partial(
            restrict_kernel,
            owners=owners,
            block=block,
            passing=passing,
            capacity=capacity,
            few=few,
        ),
        "restrict",
        (chunk_shape, F32),
        (
            counter,
            fine_residual.transpose(1, 0, 2),
            fine_basis.T,
            coarse_basis.transpose(1, 0, 2),
            point_counts.T,
            donor_cells.T,
        ),
        [
            pltpu.VMEM((depth, donors * fine), F32),
            pltpu.VMEM(chunk_shape, F32),
            pltpu.SemaphoreType.DMA((passing,)),
        ],
        megabytes=16,
        out_spec=pl.BlockSpec(memory_space=pl.ANY),
    )
    columns = lax.all_to_all(columns, PLANE, 0, 0, tiled=True)
    def seat(name, groups, shapes):
        return call(
            functools.partial(seat_kernel, groups=groups, capacity=capacity),
            name,
            shapes,
            (columns,),
            megabytes=24,
        )

    dense = ((full, block), F32)
    if few:
        far = high_count - 1
        last = seat("seat_far", [far], [dense])
        blocks = swap_all(seat("seat_near", range(far), [dense] * far) + last, "high")
    else:
        blocks = seat("seat_all", range(high_count), ((high_count, full, block), F32))
        blocks = [lax.all_to_all(blocks, "high", 0, 0, tiled=True)]
    whole = call(
        renumber_kernel, "renumber", ((full + 1, block), F32), (solver_pos[None, :], *blocks)
    )
    blocks = swap_all([whole] * subs, "sub")

    jacobian = face_jacobian.transpose(1, 2, 0, 3)
    chooser, lift = call(
        functools.partial(prepare_kernel, variables=variables, slab=slab),
        "prepare",
        [((2 * block, faces * block), BF16), ((full, variables * faces * slab), F32)],
        (counter, face_offset, face_lift.transpose(1, 0, 2)),
    )
    outer_pairs = [(i, i + 1) for i in range(1, owners - 1, 2)]
    outer_pairs += [(j, i) for i, j in outer_pairs]
    inner_pairs = [(i, i ^ 1) for i in range(owners)]
    packed = ((-(-full // 4) + 1, full, block), F32)
    lines = variables * variables * faces
    to_inner, to_outer = call(
        pack_kernel,
        "pack",
        [packed, packed],
        (lift, block_inverse, jacobian, face_offset),
        [pltpu.VMEM((lines, block), F32)],
    )
    outer = lax.ppermute(to_outer, WHOLE, outer_pairs)
    inner = lax.ppermute(to_inner, WHOLE, inner_pairs)
    inverse_beside, jacobian_beside, chooser_beside = call(
        functools.partial(beside_kernel, faces=faces),
        "beside",
        [((full, full, block), F32), ((lines, block), F32), ((2 * block, faces * block), BF16)],
        (inner, outer),
    )
    plain, edge = ((full, block), F32), ((depth // 4 * 3, block), F32)
    residual, x, to_inner, to_outer = call(
        functools.partial(first_kernel, subs=subs, variables=variables),
        "first",
        [plain, ((depth, block), F32), edge, edge],
        (block_inverse, *blocks),
        [pltpu.VMEM((depth, block), F32)],
    )
    outer = lax.ppermute(to_outer, WHOLE, outer_pairs)
    inner = lax.ppermute(to_inner, WHOLE, inner_pairs)
    return tuple(
        call(
            functools.partial(sweep_kernel, variables=variables, slab=slab),
            "sweeps",
            [plain, plain],
            (
                block_inverse,
                inverse_beside,
                residual,
                x,
                outer,
                inner,
                chooser,
                chooser_beside,
                lift,
                jacobian,
                jacobian_beside,
            ),
            [pltpu.VMEM((2, depth, faces * block), F32)]
            + [pltpu.VMEM((variables * faces * slab, 2 * block), BF16)] * 2,
        )
    )


def solution(mesh):
    dom, sub = mesh.devices.shape
    low = 2 if dom % 2 == 0 else 1
    split_mesh = jax.sharding.Mesh(mesh.devices.reshape(dom // low, low, sub), WHOLE)
    in_specs = (
        P(None, None, WHOLE),
        P(),
        P(None, None, WHOLE),
        P(WHOLE, None),
        P(WHOLE, None),
        P(WHOLE),
        P(None, None, WHOLE),
        P(None, None, None, WHOLE),
        P(),
        P(None, WHOLE),
    )
    return jax.shard_map(
        per_device,
        mesh=split_mesh,
        in_specs=in_specs,
        out_specs=(P(None, WHOLE), P(None, WHOLE)),
        check_vma=False,
    )
```

```python
import functools
import jax
import jax.numpy as jnp
from jax import lax
from jax.experimental import pallas as pl
from jax.experimental.pallas import tpu as pltpu
from jax.sharding import PartitionSpec as P

F32 = jnp.float32
BF16 = jnp.bfloat16
PLANE = ("low", "sub")
WHOLE = ("high", "low", "sub")
VMEM = pl.BlockSpec(memory_space=pltpu.VMEM)


def split(x):
    high = x.astype(BF16)
    return high, (x - high.astype(F32)).astype(BF16)


def mm(a, b, ca=1, cb=0, precision=None):
    return lax.dot_general(
        a, b, (((ca,), (cb,)), ((), ())), precision=precision, preferred_element_type=F32
    )


def rows_of(iota_shape, dim):
    return lax.broadcasted_iota(jnp.int32, iota_shape, dim)


def call(kernel, name, shapes, args, scratch=(), megabytes=8, cost=None, out_spec=VMEM):
    single = not isinstance(shapes, list)
    out = [jax.ShapeDtypeStruct(*shape) for shape in ([shapes] if single else shapes)]
    result = pl.pallas_call(
        kernel,
        out_shape=out,
        in_specs=[VMEM] * len(args),
        out_specs=[out_spec] * len(out),
        scratch_shapes=list(scratch),
        compiler_params=pltpu.CompilerParams(vmem_limit_bytes=megabytes * 2**20),
        cost_estimate=cost,
        name=name,
    )(*args)
    return result[0] if single else result


def swap_all(blocks, axis):
    count = len(blocks)
    return [blocks[0]] + [
        lax.ppermute(blocks[d], axis, [(i, i ^ d) for i in range(count)])
        for d in range(count - 1, 0, -1)
    ]


def constants_kernel(counter_ref):
    lanes = counter_ref.shape[0]
    earlier = (rows_of((lanes, lanes), 0) < rows_of((lanes, lanes), 1)).astype(F32)
    counter = jnp.concatenate([earlier, jnp.ones((lanes, lanes), F32)], axis=1)
    counter_ref[...] = counter.astype(BF16)


def free_columns(owner, counter, owners, passing, capacity, width, high):
    lanes = 128
    total = owner.shape[1]
    parts = total // lanes
    mine = (rows_of((owners, total), 0) == owner).astype(F32)
    stacked = jnp.concatenate([mine[:, j * lanes : (j + 1) * lanes] for j in range(parts)], axis=0)
    counted = mm(stacked.astype(BF16), counter)
    before = jnp.zeros((owners, lanes), F32)
    ranks = []
    for j in range(parts):
        own = mine[:, j * lanes : (j + 1) * lanes]
        part = counted[j * owners : (j + 1) * owners]
        ranks.append(jnp.sum(own * (before + part[:, :lanes]), axis=0, keepdims=True))
        before += part[:, lanes:]
    rank = jnp.concatenate(ranks, axis=1).astype(jnp.int32)
    return (owner % passing) * width + (owner // passing ^ high) * capacity + rank


def add_eights(x):
    total = x[0:8]
    for j in range(8, x.shape[0], 8):
        total += x[j : j + 8]
    return total


def sum_rows(pieces):
    row = rows_of(pieces[0].shape, 0)
    pieces = [pieces[k] for k in (3, 2, 1, 0, 7, 6, 5, 4)]
    upper = row < 4
    halves = []
    for one, two in zip(pieces[:4], pieces[4:]):
        kept, moved = jnp.where(upper, one, two), jnp.where(upper, two, one)
        halves.append(kept + pltpu.roll(moved, 4, 0))
    for shift in (2, 1):
        pairs = list(zip(halves[:shift], halves[shift:]))
        halves = [
            jnp.where(
                row & shift != 0, one + pltpu.roll(one, shift, 0), two + pltpu.roll(two, 8 - shift, 0)
            )
            for one, two in pairs
        ]
    return halves[0]


def restrict_kernel(
    counter_ref, res_ref, basis_ref, coarse_ref, counts_ref, donors_ref, out_hbm, pair_ref, out_ref, sems,
    *, owners, block, passing, capacity, few
):
    variables, _, fine = res_ref.shape
    modes, points, _ = coarse_ref.shape
    donors = counts_ref.shape[0]
    chunks = out_ref.shape[0]
    full = modes * variables
    depth = pair_ref.shape[1]
    total = donors * fine
    lanes = 128
    width = owners // passing * capacity

    cell = jnp.concatenate([donors_ref[k : k + 1, :] for k in range(donors)], axis=1)
    seat = (cell % block).astype(F32)
    for j in range(total // lanes):
        pair_ref[j, full:, :] = jnp.zeros((depth - full, lanes), F32)
        pair_ref[j, full : full + 1, :] = seat[:, j * lanes : (j + 1) * lanes]
    high = lax.axis_index("high") if few else 0
    slot = free_columns(cell // block, counter_ref[...], owners, passing, capacity, width, high)
    slot = jnp.broadcast_to(slot.astype(F32), (lanes, total)).T.astype(jnp.int32).astype(jnp.int16)

    basis_high, basis_low = split(basis_ref[...])
    res_high, res_low = split(jnp.concatenate([res_ref[v] for v in range(variables)], axis=1))
    values = mm(basis_high, res_high, 0, 0)
    values += mm(basis_high, res_low, 0, 0) + mm(basis_low, res_high, 0, 0)

    point = rows_of((points, lanes), 0)
    for at in range(0, fine, lanes):
        upper = jnp.zeros((1, lanes), jnp.int32)
        inside = []
        for k in range(donors):
            lower = upper
            upper = lower + counts_ref[k : k + 1, at : at + lanes]
            inside.append((point >= lower) & (point < upper))
        for v in range(variables):
            column = v * fine + at
            value = values[:, column : column + lanes]
            masked = [jnp.where(inside[k], value, 0.0) for k in range(donors)]
            pieces = []
            for a in range(modes):
                coarse = coarse_ref[a, :, at : at + lanes]
                terms = [coarse * masked[k] for k in range(donors)]
                pieces.append([add_eights(term) for term in terms])
            whole = modes - modes % 8
            for k in range(donors):
                left = k * fine + at
                for a in range(0, whole, 8):
                    rows = pl.ds(a * variables + v, 8, stride=variables)
                    pair_ref[left // lanes, rows, :] = sum_rows(
                        [pieces[a + r][k] for r in range(8)]
                    )
            rest = [(k, a) for k in range(donors) for a in range(whole, modes)]
            for first in range(0, len(rest), 8):
                group = rest[first : first + 8]
                filled = group + [group[0]] * (8 - len(group))
                sums = sum_rows([pieces[a][k] for k, a in filled])
                for r, (k, a) in enumerate(group):
                    row, left = a * variables + v, k * fine + at
                    pair_ref[left // lanes, row : row + 1, :] = sums[r : r + 1]

    pair = jnp.concatenate([pair_ref[j] for j in range(total // lanes)], axis=1)
    both = jnp.concatenate(split(pair), axis=0)
    lane = rows_of((total, lanes), 1).astype(jnp.int16)
    one, zero = jnp.ones((total, lanes), BF16), jnp.zeros((total, lanes), BF16)
    for c in range(chunks):
        chooser = jnp.concatenate(
            [
                jnp.where(slot == lane + jnp.int16(c * width + j), one, zero)
                for j in range(0, width, lanes)
            ],
            axis=1,
        )
        placed = mm(both, chooser)
        placed = placed[:depth] + placed[depth:]
        rows = out_ref.shape[1] // 2
        for j in range(2):
            out_ref[c, j * rows : (j + 1) * rows] = placed[:rows, j * width // 2 : (j + 1) * width // 2]
        pltpu.make_async_copy(out_ref.at[c], out_hbm.at[c], sems.at[c]).start()
    for c in range(chunks):
        pltpu.make_async_copy(out_ref.at[c], out_hbm.at[c], sems.at[c]).wait()


def seat_kernel(columns_ref, *out_refs, groups, capacity):
    sources, rows, _ = columns_ref.shape
    rows = rows // 2
    full, block = out_refs[0].shape[-2:]
    for n, group in enumerate(groups):
        j, at = divmod(group * capacity, columns_ref.shape[2])
        got = jnp.concatenate(
            [
                columns_ref[s, j * rows : j * rows + full + 1, at : at + capacity]
                for s in range(sources)
            ],
            axis=1,
        )
        seat = got[full : full + 1, :]
        chooser = (rows_of((block, got.shape[1]), 0).astype(F32) == seat).astype(F32).astype(BF16)
        high, low = split(got)
        dense = (mm(high, chooser, 1, 1) + mm(low, chooser, 1, 1))[:full]
        if len(out_refs) == len(groups):
            out_refs[n][...] = dense
        else:
            out_refs[0][n] = dense


def renumber_kernel(place_ref, *refs):
    block_refs, out_ref = refs[:-1], refs[-1]
    block = place_ref.shape[1]
    if len(block_refs) == 1:
        total = block_refs[0][0]
        for h in range(1, block_refs[0].shape[0]):
            total += block_refs[0][h]
    else:
        total = block_refs[0][...]
        for ref in block_refs[1:]:
            total += ref[...]
    full = total.shape[0]
    place = place_ref[...]
    chooser = (rows_of((block, block), 0) == place % block).astype(F32).astype(BF16)
    high, low = split(total)
    out_ref[:full, :] = mm(high, chooser, 1, 1) + mm(low, chooser, 1, 1)
    out_ref[full:, :] = (place // block).astype(F32)


def prepare_kernel(after_ref, offset_ref, lift_ref, chooser_ref, lift_out_ref, *, variables, slab):
    del after_ref
    faces, block = offset_ref.shape
    modes = lift_ref.shape[0]
    full = modes * variables
    choose(offset_ref[...], chooser_ref, 0)
    width = variables * faces * slab
    column = rows_of((modes, width), 1)
    mode = rows_of((modes, width), 0)
    spread = jnp.zeros((modes, width), F32)
    for f in range(faces):
        put = (column % slab == mode) & ((column // slab) % faces == f)
        spread += mm(lift_ref[:, f, :], put.astype(F32), 1, 0, lax.Precision.HIGHEST)
    expand = (rows_of((full, modes), 0) // variables == rows_of((full, modes), 1)).astype(F32)
    lifted = mm(expand, spread, 1, 0, lax.Precision.HIGHEST)
    keep = rows_of((full, width), 1) // (slab * faces) == rows_of((full, width), 0) % variables
    high, low = split(jnp.where(keep, lifted, 0.0))
    lift_out_ref[...] = jnp.concatenate([high, high, low], axis=1)


def inner_is_left():
    return lax.axis_index("sub") % 2 == 1


def pack_quarters(pieces):
    reach = pieces[0].shape[1] // 4
    turned = [pieces[0]] + [pltpu.roll(pieces[g], g * reach, 1) for g in range(1, 4)]
    quarter = rows_of(pieces[0].shape, 1) // reach
    to_left, to_right = turned[0], turned[0]
    for g in range(1, 4):
        to_left = jnp.where(quarter == g, turned[g], to_left)
        to_right = jnp.where(quarter == g - 1, turned[g], to_right)
    left = inner_is_left()
    return jnp.where(left, to_left, to_right), jnp.where(left, to_right, to_left)


def take_quarters(inner, outer):
    reach = inner.shape[1] // 4
    quarter = rows_of(inner.shape, 1) // reach
    pieces = []
    for g in range(4):
        piece = jnp.where((quarter == g) != inner_is_left(), inner, outer)
        pieces.append(pltpu.roll(piece, (4 - g) * reach, 1) if g else piece)
    return pieces


def pack_halves(one, two):
    block = one.shape[1]
    turned = pltpu.roll(two, block // 2, 1)
    kept = (rows_of(one.shape, 1) < block // 2) == inner_is_left()
    return jnp.where(kept, one, turned), jnp.where(kept, turned, one)


def take_halves(inner, outer):
    block = inner.shape[1]
    from_inner = (rows_of(inner.shape, 1) >= block // 2) == inner_is_left()
    two = jnp.where(from_inner, outer, inner)
    return jnp.where(from_inner, inner, outer), pltpu.roll(two, block // 2, 1)


def pack_kernel(after_ref, inverse_ref, jacobian_ref, offset_ref, inner_ref, outer_ref, lines):
    del after_ref
    full, _, block = inverse_ref.shape
    variables, _, faces, _ = jacobian_ref.shape
    slabs = inner_ref.shape[0] - 1
    for j in range(slabs):
        index = [j + g * slabs for g in range(4)]
        pieces = [inverse_ref[i] if i < full else jnp.zeros((full, block), F32) for i in index]
        inner_ref[j], outer_ref[j] = pack_quarters(pieces)
    for w in range(variables):
        for v in range(variables):
            at = (w * variables + v) * faces
            lines[at : at + faces, :] = jacobian_ref[w, v]
    count = lines.shape[0] // 4
    packed = pack_quarters([lines[g * count : (g + 1) * count, :] for g in range(4)])
    offset = offset_ref[...].astype(F32)
    for ref, rows in zip((inner_ref, outer_ref), packed):
        ref[slabs] = jnp.zeros((full, block), F32)
        ref[slabs, :count, :] = rows
        ref[slabs, full - faces :, :] = offset


def beside_kernel(inner_ref, outer_ref, inverse_ref, jacobian_ref, chooser_ref, *, faces):
    full, _, block = inverse_ref.shape
    slabs = inner_ref.shape[0] - 1
    for j in range(slabs):
        for g, piece in enumerate(take_quarters(inner_ref[j], outer_ref[j])):
            if j + g * slabs < full:
                inverse_ref[j + g * slabs] = piece
    count = jacobian_ref.shape[0] // 4
    pieces = take_quarters(inner_ref[slabs, :count, :], outer_ref[slabs, :count, :])
    for g, piece in enumerate(pieces):
        jacobian_ref[g * count : (g + 1) * count, :] = piece
    inner, outer = inner_ref[slabs, full - faces :, :], outer_ref[slabs, full - faces :, :]
    from_inner = (rows_of(inner.shape, 1) >= block // 2) == inner_is_left()
    choose(jnp.where(from_inner, inner, outer).astype(jnp.int32), chooser_ref, block)


def choose(offsets, chooser_ref, first):
    faces, block = offsets.shape
    lane = rows_of((1, block), 1) + first
    row = rows_of((2 * block, block), 0)
    for f in range(faces):
        offset = offsets[f : f + 1, :]
        source = jnp.where(offset != 0, (lane + offset) & (2 * block - 1), -1)
        chooser_ref[:, f * block : (f + 1) * block] = (row == source).astype(F32).astype(BF16)


def apply_inverse(inverse_ref, field, variables, depth=None):
    full, _, block = inverse_ref.shape
    modes = full // variables
    zero = jnp.zeros((8, block), F32)

    def piece(row):
        if row >= full:
            return zero
        product = inverse_ref[row % modes * variables + row // modes if depth else row] * field
        partial = product[0:8]
        for j in range(8, full - 7, 8):
            partial += product[j : j + 8]
        rest = full % 8
        if rest:
            partial += jnp.concatenate([product[full - rest :], zero[rest:]], axis=0)
        return partial

    rows = []
    for at in range(0, depth or full, 8):
        rows.append(sum_rows([piece(at + r) for r in range(8)]) if at < full else zero)
    return jnp.concatenate(rows, axis=0)[: depth or full]


def first_kernel(inverse_ref, *refs, subs, variables):
    block_refs, (total_ref, out_ref, inner_ref, outer_ref, padded) = refs[:-5], refs[-5:]
    full = total_ref.shape[0]
    owner = lax.axis_index("high") * lax.axis_size("low") + lax.axis_index("low")
    owner = (owner * subs + lax.axis_index("sub")).astype(F32)
    residual = jnp.zeros(total_ref.shape, F32)
    for ref in block_refs:
        residual += jnp.where(ref[full:, :] == owner, ref[:full, :], 0.0)
    total_ref[...] = residual
    depth = padded.shape[0]
    padded[full:, :] = jnp.zeros((depth - full, padded.shape[1]), F32)
    padded[:full, :] = residual
    x = apply_inverse(inverse_ref, residual, variables, depth)
    out_ref[...] = x
    half, quarter = depth // 2, depth // 4
    inner_ref[:half, :], outer_ref[:half, :] = pack_halves(x[:half], x[half:])
    inner_ref[half:, :], outer_ref[half:, :] = pack_quarters(
        [padded[g * quarter : (g + 1) * quarter, :] for g in range(4)]
    )


def sweep_kernel(
    inverse_ref, inverse_beside_ref, residual_ref, x_ref, outer_ref, inner_ref, chooser_ref,
    chooser_beside_ref, lift_ref, jacobian_ref, jacobian_beside_ref, total_ref, out_ref,
    picked_ref, z_ref, *, variables, slab
):
    depth, block = x_ref.shape
    full = residual_ref.shape[0]
    modes = full // variables
    faces = jacobian_ref.shape[2]
    residual = residual_ref[...]
    total_ref[...] = residual
    third = z_ref.shape[0] // 3

    def coupled(x, tiles):
        x = jnp.concatenate(split(x), axis=0)
        for t, ref in enumerate((chooser_ref, chooser_beside_ref)[:tiles]):
            picked = mm(x, ref[...])
            picked_ref[t] = picked[:depth] + picked[depth:]
        for t in range(tiles):
            for f in range(faces):
                at = f * block
                part = [
                    picked_ref[t, v * modes : v * modes + slab, at : at + block]
                    for v in range(variables)
                ]
                for w in range(variables):
                    z = None
                    for v in range(variables):
                        if t:
                            line = (w * variables + v) * faces + f
                            term = part[v] * jacobian_beside_ref[line : line + 1, :]
                        else:
                            term = part[v] * jacobian_ref[w, v, f : f + 1, :]
                        z = z + term if v else term
                    line, column = (w * faces + f) * slab, t * block
                    high, low = split(z)
                    for n, value in enumerate((high, low, high)):
                        at_row = n * third + line
                        z_ref[at_row : at_row + slab, column : column + block] = value
        return mm(lift_ref[...], z_ref[:, : tiles * block])

    half = depth // 2
    first_beside = jnp.concatenate(take_halves(inner_ref[:half, :], outer_ref[:half, :]), axis=0)
    beside = take_quarters(inner_ref[half:, :], outer_ref[half:, :])
    beside = jnp.concatenate(beside, axis=0)[:full]
    taken = coupled(jnp.concatenate([x_ref[...], first_beside], axis=1), 2)
    second = jnp.concatenate(
        [
            apply_inverse(inverse_ref, residual - taken[:, :block], variables, depth),
            apply_inverse(inverse_beside_ref, beside - taken[:, block:], variables, depth),
        ],
        axis=1,
    )
    out_ref[...] = apply_inverse(inverse_ref, residual - coupled(second, 1), variables)


def per_device(
    fine_residual,
    fine_basis,
    coarse_basis,
    donor_cells,
    point_counts,
    solver_pos,
    block_inverse,
    face_jacobian,
    face_lift,
    face_offset,
):
    high_count = lax.axis_size("high")
    passing = lax.axis_size("low") * lax.axis_size("sub")
    owners = high_count * passing
    _, variables, fine = fine_residual.shape
    modes = coarse_basis.shape[1]
    donors = donor_cells.shape[1]
    block = solver_pos.shape[0]
    faces = face_offset.shape[0]
    full = modes * variables
    slab = -(-modes // 16) * 16
    depth = -(-full // 16) * 16

    capacity = max(2, 2 * fine * donors // owners)
    few = 1 < high_count <= 8 and high_count & (high_count - 1) == 0
    subs = lax.axis_size("sub")
    counter = call(
        constants_kernel,
        "constants",
        ((128, 256), BF16),
        (),
        cost=pl.CostEstimate(flops=2 * 10**9, bytes_accessed=8 * 10**6, transcendentals=0),
    )
    rows = -(-(full + 1) // 4) * 4
    chunk_shape = (passing, 2 * rows, high_count * capacity // 2)
    columns = call(
        functools.partial(
            restrict_kernel,
            owners=owners,
            block=block,
            passing=passing,
            capacity=capacity,
            few=few,
        ),
        "restrict",
        (chunk_shape, F32),
        (
            counter,
            fine_residual.transpose(1, 0, 2),
            fine_basis.T,
            coarse_basis.transpose(1, 0, 2),
            point_counts.T,
            donor_cells.T,
        ),
        [
            pltpu.VMEM((donors * fine // 128, depth, 128), F32),
            pltpu.VMEM(chunk_shape, F32),
            pltpu.SemaphoreType.DMA((passing,)),
        ],
        megabytes=16,
        out_spec=pl.BlockSpec(memory_space=pl.ANY),
    )
    columns = lax.all_to_all(columns, PLANE, 0, 0, tiled=True)
    def seat(name, groups, shapes):
        return call(
            functools.partial(seat_kernel, groups=groups, capacity=capacity),
            name,
            shapes,
            (columns,),
            megabytes=24,
        )

    dense = ((full, block), F32)
    if few:
        near = seat("seat_near", range(min(2, high_count)), [dense] * min(2, high_count))
        rest = [seat("seat_far", [d], [dense])[0] for d in range(2, high_count)]
        blocks = swap_all([*near, *rest], "high")
    else:
        blocks = seat("seat_all", range(high_count), ((high_count, full, block), F32))
        blocks = [lax.all_to_all(blocks, "high", 0, 0, tiled=True)]
    whole = call(
        renumber_kernel, "renumber", ((full + 1, block), F32), (solver_pos[None, :], *blocks)
    )
    blocks = swap_all([whole] * subs, "sub")

    jacobian = face_jacobian.transpose(1, 2, 0, 3)
    chooser, lift = call(
        functools.partial(prepare_kernel, variables=variables, slab=slab),
        "prepare",
        [((2 * block, faces * block), BF16), ((full, 3 * variables * faces * slab), BF16)],
        (counter, face_offset, face_lift.transpose(1, 0, 2)),
    )
    outer_pairs = [(i, i + 1) for i in range(1, owners - 1, 2)]
    outer_pairs += [(j, i) for i, j in outer_pairs]
    inner_pairs = [(i, i ^ 1) for i in range(owners)]
    packed = ((-(-full // 4) + 1, full, block), F32)
    lines = variables * variables * faces
    to_inner, to_outer = call(
        pack_kernel,
        "pack",
        [packed, packed],
        (lift, block_inverse, jacobian, face_offset),
        [pltpu.VMEM((lines, block), F32)],
    )
    outer = lax.ppermute(to_outer, WHOLE, outer_pairs)
    inner = lax.ppermute(to_inner, WHOLE, inner_pairs)
    inverse_beside, jacobian_beside, chooser_beside = call(
        functools.partial(beside_kernel, faces=faces),
        "beside",
        [((full, full, block), F32), ((lines, block), F32), ((2 * block, faces * block), BF16)],
        (inner, outer),
    )
    plain, edge = ((full, block), F32), ((depth // 4 * 3, block), F32)
    residual, x, to_inner, to_outer = call(
        functools.partial(first_kernel, subs=subs, variables=variables),
        "first",
        [plain, ((depth, block), F32), edge, edge],
        (block_inverse, *blocks),
        [pltpu.VMEM((depth, block), F32)],
    )
    outer = lax.ppermute(to_outer, WHOLE, outer_pairs)
    inner = lax.ppermute(to_inner, WHOLE, inner_pairs)
    return tuple(
        call(
            functools.partial(sweep_kernel, variables=variables, slab=slab),
            "sweeps",
            [plain, plain],
            (
                block_inverse,
                inverse_beside,
                residual,
                x,
                outer,
                inner,
                chooser,
                chooser_beside,
                lift,
                jacobian,
                jacobian_beside,
            ),
            [pltpu.VMEM((2, depth, faces * block), F32)]
            + [pltpu.VMEM((3 * variables * faces * slab, 2 * block), BF16)],
        )
    )


def solution(mesh):
    dom, sub = mesh.devices.shape
    low = 2 if dom % 2 == 0 else 1
    split_mesh = jax.sharding.Mesh(mesh.devices.reshape(dom // low, low, sub), WHOLE)
    in_specs = (
        P(None, None, WHOLE),
        P(),
        P(None, None, WHOLE),
        P(WHOLE, None),
        P(WHOLE, None),
        P(WHOLE),
        P(None, None, WHOLE),
        P(None, None, None, WHOLE),
        P(),
        P(None, WHOLE),
    )
    return jax.shard_map(
        per_device,
        mesh=split_mesh,
        in_specs=in_specs,
        out_specs=(P(None, WHOLE), P(None, WHOLE)),
        check_vma=False,
    )
```

```python
import functools
import jax
import jax.numpy as jnp
from jax import lax
from jax.experimental import pallas as pl
from jax.experimental.pallas import tpu as pltpu
from jax.sharding import PartitionSpec as P

F32 = jnp.float32
BF16 = jnp.bfloat16
PLANE = ("low", "sub")
WHOLE = ("high", "low", "sub")
VMEM = pl.BlockSpec(memory_space=pltpu.VMEM)


def split(x):
    high = x.astype(BF16)
    return high, (x - high.astype(F32)).astype(BF16)


def mm(a, b, ca=1, cb=0, precision=None):
    return lax.dot_general(
        a, b, (((ca,), (cb,)), ((), ())), precision=precision, preferred_element_type=F32
    )


def rows_of(iota_shape, dim):
    return lax.broadcasted_iota(jnp.int32, iota_shape, dim)


def call(kernel, name, shapes, args, scratch=(), megabytes=8, cost=None, out_spec=VMEM):
    single = not isinstance(shapes, list)
    out = [jax.ShapeDtypeStruct(*shape) for shape in ([shapes] if single else shapes)]
    result = pl.pallas_call(
        kernel,
        out_shape=out,
        in_specs=[VMEM] * len(args),
        out_specs=[out_spec] * len(out),
        scratch_shapes=list(scratch),
        compiler_params=pltpu.CompilerParams(vmem_limit_bytes=megabytes * 2**20),
        cost_estimate=cost,
        name=name,
    )(*args)
    return result[0] if single else result


def swap_all(blocks, axis):
    count = len(blocks)
    return [blocks[0]] + [
        lax.ppermute(blocks[d], axis, [(i, i ^ d) for i in range(count)])
        for d in range(count - 1, 0, -1)
    ]


def constants_kernel(counter_ref):
    lanes = counter_ref.shape[0]
    earlier = (rows_of((lanes, lanes), 0) < rows_of((lanes, lanes), 1)).astype(F32)
    counter = jnp.concatenate([earlier, jnp.ones((lanes, lanes), F32)], axis=1)
    counter_ref[...] = counter.astype(BF16)


def free_columns(owner, counter, owners, passing, capacity, width, high):
    lanes = 128
    total = owner.shape[1]
    parts = total // lanes
    mine = (rows_of((owners, total), 0) == owner).astype(F32)
    stacked = jnp.concatenate([mine[:, j * lanes : (j + 1) * lanes] for j in range(parts)], axis=0)
    counted = mm(stacked.astype(BF16), counter)
    before = jnp.zeros((owners, lanes), F32)
    ranks = []
    for j in range(parts):
        own = mine[:, j * lanes : (j + 1) * lanes]
        part = counted[j * owners : (j + 1) * owners]
        ranks.append(jnp.sum(own * (before + part[:, :lanes]), axis=0, keepdims=True))
        before += part[:, lanes:]
    rank = jnp.concatenate(ranks, axis=1).astype(jnp.int32)
    return (owner % passing) * width + (owner // passing ^ high) * capacity + rank


def add_eights(x):
    total = x[0:8]
    for j in range(8, x.shape[0], 8):
        total += x[j : j + 8]
    return total


def sum_rows(pieces):
    row = rows_of(pieces[0].shape, 0)
    pieces = [pieces[k] for k in (3, 2, 1, 0, 7, 6, 5, 4)]
    upper = row < 4
    halves = []
    for one, two in zip(pieces[:4], pieces[4:]):
        kept, moved = jnp.where(upper, one, two), jnp.where(upper, two, one)
        halves.append(kept + pltpu.roll(moved, 4, 0))
    for shift in (2, 1):
        pairs = list(zip(halves[:shift], halves[shift:]))
        halves = [
            jnp.where(
                row & shift != 0, one + pltpu.roll(one, shift, 0), two + pltpu.roll(two, 8 - shift, 0)
            )
            for one, two in pairs
        ]
    return halves[0]


def restrict_kernel(
    counter_ref, res_ref, basis_ref, coarse_ref, counts_ref, donors_ref, out_hbm, pair_ref, out_ref, sems,
    *, owners, block, passing, capacity, few
):
    variables, _, fine = res_ref.shape
    modes, points, _ = coarse_ref.shape
    donors = counts_ref.shape[0]
    chunks = out_ref.shape[0]
    full = modes * variables
    depth = pair_ref.shape[1]
    total = donors * fine
    lanes = 128
    width = owners // passing * capacity

    cell = jnp.concatenate([donors_ref[k : k + 1, :] for k in range(donors)], axis=1)
    seat = (cell % block).astype(F32)
    for j in range(total // lanes):
        pair_ref[j, full:, :] = jnp.zeros((depth - full, lanes), F32)
        pair_ref[j, full : full + 1, :] = seat[:, j * lanes : (j + 1) * lanes]
    high = lax.axis_index("high") if few else 0
    slot = free_columns(cell // block, counter_ref[...], owners, passing, capacity, width, high)
    slot = jnp.broadcast_to(slot.astype(F32), (lanes, total)).T.astype(jnp.int32).astype(jnp.int16)

    basis_high, basis_low = split(basis_ref[...])
    res_high, res_low = split(jnp.concatenate([res_ref[v] for v in range(variables)], axis=1))
    values = mm(basis_high, res_high, 0, 0)
    values += mm(basis_high, res_low, 0, 0) + mm(basis_low, res_high, 0, 0)

    point = rows_of((points, lanes), 0)
    for at in range(0, fine, lanes):
        upper = jnp.zeros((1, lanes), jnp.int32)
        inside = []
        for k in range(donors):
            lower = upper
            upper = lower + counts_ref[k : k + 1, at : at + lanes]
            inside.append((point >= lower) & (point < upper))
        for v in range(variables):
            column = v * fine + at
            value = values[:, column : column + lanes]
            masked = [jnp.where(inside[k], value, 0.0) for k in range(donors)]
            pieces = []
            for a in range(modes):
                coarse = coarse_ref[a, :, at : at + lanes]
                terms = [coarse * masked[k] for k in range(donors)]
                pieces.append([add_eights(term) for term in terms])
            whole = modes - modes % 8
            for k in range(donors):
                left = k * fine + at
                for a in range(0, whole, 8):
                    rows = pl.ds(a * variables + v, 8, stride=variables)
                    pair_ref[left // lanes, rows, :] = sum_rows(
                        [pieces[a + r][k] for r in range(8)]
                    )
            rest = [(k, a) for k in range(donors) for a in range(whole, modes)]
            for first in range(0, len(rest), 8):
                group = rest[first : first + 8]
                filled = group + [group[0]] * (8 - len(group))
                sums = sum_rows([pieces[a][k] for k, a in filled])
                for r, (k, a) in enumerate(group):
                    row, left = a * variables + v, k * fine + at
                    pair_ref[left // lanes, row : row + 1, :] = sums[r : r + 1]

    pair = jnp.concatenate([pair_ref[j] for j in range(total // lanes)], axis=1)
    both = jnp.concatenate(split(pair), axis=0)
    lane = rows_of((total, lanes), 1).astype(jnp.int16)
    one, zero = jnp.ones((total, lanes), BF16), jnp.zeros((total, lanes), BF16)
    part = out_ref.shape[2]
    rows = out_ref.shape[1] * part // width
    together = max(1, 256 // width)
    for first in range(0, chunks, together):
        chooser = jnp.concatenate(
            [
                jnp.where(slot == lane + jnp.int16(first * width + j), one, zero)
                for j in range(0, together * width, lanes)
            ],
            axis=1,
        )
        placed = mm(both, chooser)
        placed = placed[:depth] + placed[depth:]
        for c in range(first, first + together):
            for j in range(width // part):
                at = (c - first) * width + j * part
                out_ref[c, j * rows : (j + 1) * rows] = placed[:rows, at : at + part]
            pltpu.make_async_copy(out_ref.at[c], out_hbm.at[c], sems.at[c]).start()
    for c in range(chunks):
        pltpu.make_async_copy(out_ref.at[c], out_hbm.at[c], sems.at[c]).wait()


def seat_kernel(columns_ref, *out_refs, groups, capacity, rows):
    sources = columns_ref.shape[0]
    full, block = out_refs[0].shape[-2:]
    for n, group in enumerate(groups):
        j, at = divmod(group * capacity, columns_ref.shape[2])
        got = jnp.concatenate(
            [
                columns_ref[s, j * rows : j * rows + full + 1, at : at + capacity]
                for s in range(sources)
            ],
            axis=1,
        )
        seat = got[full : full + 1, :]
        chooser = (rows_of((block, got.shape[1]), 0).astype(F32) == seat).astype(F32).astype(BF16)
        high, low = split(got)
        dense = (mm(high, chooser, 1, 1) + mm(low, chooser, 1, 1))[:full]
        if len(out_refs) == len(groups):
            out_refs[n][...] = dense
        else:
            out_refs[0][n] = dense


def renumber_kernel(place_ref, *refs):
    block_refs, out_ref = refs[:-1], refs[-1]
    block = place_ref.shape[1]
    if len(block_refs) == 1:
        total = block_refs[0][0]
        for h in range(1, block_refs[0].shape[0]):
            total += block_refs[0][h]
    else:
        total = block_refs[0][...]
        for ref in block_refs[1:]:
            total += ref[...]
    full = total.shape[0]
    place = place_ref[...]
    chooser = (rows_of((block, block), 0) == place % block).astype(F32).astype(BF16)
    high, low = split(total)
    out_ref[:full, :] = mm(high, chooser, 1, 1) + mm(low, chooser, 1, 1)
    out_ref[full:, :] = (place // block).astype(F32)


def prepare_kernel(after_ref, offset_ref, lift_ref, chooser_ref, lift_out_ref, *, variables, slab):
    del after_ref
    faces, block = offset_ref.shape
    modes = lift_ref.shape[0]
    full = modes * variables
    choose(offset_ref[...], chooser_ref, 0)
    width = variables * faces * slab
    column = rows_of((modes, width), 1)
    mode = rows_of((modes, width), 0)
    spread = jnp.zeros((modes, width), F32)
    for f in range(faces):
        put = (column % slab == mode) & ((column // slab) % faces == f)
        spread += mm(lift_ref[:, f, :], put.astype(F32), 1, 0, lax.Precision.HIGHEST)
    expand = (rows_of((full, modes), 0) // variables == rows_of((full, modes), 1)).astype(F32)
    lifted = mm(expand, spread, 1, 0, lax.Precision.HIGHEST)
    keep = rows_of((full, width), 1) // (slab * faces) == rows_of((full, width), 0) % variables
    high, low = split(jnp.where(keep, lifted, 0.0))
    lift_out_ref[...] = jnp.concatenate([high, high, low], axis=1)


def inner_is_left():
    return lax.axis_index("sub") % 2 == 1


def pack_quarters(pieces):
    reach = pieces[0].shape[1] // 4
    turned = [pieces[0]] + [pltpu.roll(pieces[g], g * reach, 1) for g in range(1, 4)]
    quarter = rows_of(pieces[0].shape, 1) // reach
    to_left, to_right = turned[0], turned[0]
    for g in range(1, 4):
        to_left = jnp.where(quarter == g, turned[g], to_left)
        to_right = jnp.where(quarter == g - 1, turned[g], to_right)
    left = inner_is_left()
    return jnp.where(left, to_left, to_right), jnp.where(left, to_right, to_left)


def take_quarters(inner, outer):
    reach = inner.shape[1] // 4
    quarter = rows_of(inner.shape, 1) // reach
    pieces = []
    for g in range(4):
        piece = jnp.where((quarter == g) != inner_is_left(), inner, outer)
        pieces.append(pltpu.roll(piece, (4 - g) * reach, 1) if g else piece)
    return pieces


def pack_halves(one, two):
    block = one.shape[1]
    turned = pltpu.roll(two, block // 2, 1)
    kept = (rows_of(one.shape, 1) < block // 2) == inner_is_left()
    return jnp.where(kept, one, turned), jnp.where(kept, turned, one)


def take_halves(inner, outer):
    block = inner.shape[1]
    from_inner = (rows_of(inner.shape, 1) >= block // 2) == inner_is_left()
    two = jnp.where(from_inner, outer, inner)
    return jnp.where(from_inner, inner, outer), pltpu.roll(two, block // 2, 1)


def pack_kernel(after_ref, inverse_ref, jacobian_ref, offset_ref, inner_ref, outer_ref, lines):
    del after_ref
    full, _, block = inverse_ref.shape
    variables, _, faces, _ = jacobian_ref.shape
    slabs = inner_ref.shape[0] - 1
    for j in range(slabs):
        index = [j + g * slabs for g in range(4)]
        pieces = [inverse_ref[i] if i < full else jnp.zeros((full, block), F32) for i in index]
        inner_ref[j], outer_ref[j] = pack_quarters(pieces)
    for w in range(variables):
        for v in range(variables):
            at = (w * variables + v) * faces
            lines[at : at + faces, :] = jacobian_ref[w, v]
    count = lines.shape[0] // 4
    packed = pack_quarters([lines[g * count : (g + 1) * count, :] for g in range(4)])
    offset = offset_ref[...].astype(F32)
    for ref, rows in zip((inner_ref, outer_ref), packed):
        ref[slabs] = jnp.zeros((full, block), F32)
        ref[slabs, :count, :] = rows
        ref[slabs, full - faces :, :] = offset


def beside_kernel(inner_ref, outer_ref, inverse_ref, jacobian_ref, chooser_ref, *, faces):
    full, _, block = inverse_ref.shape
    slabs = inner_ref.shape[0] - 1
    for j in range(slabs):
        for g, piece in enumerate(take_quarters(inner_ref[j], outer_ref[j])):
            if j + g * slabs < full:
                inverse_ref[j + g * slabs] = piece
    count = jacobian_ref.shape[0] // 4
    pieces = take_quarters(inner_ref[slabs, :count, :], outer_ref[slabs, :count, :])
    for g, piece in enumerate(pieces):
        jacobian_ref[g * count : (g + 1) * count, :] = piece
    inner, outer = inner_ref[slabs, full - faces :, :], outer_ref[slabs, full - faces :, :]
    from_inner = (rows_of(inner.shape, 1) >= block // 2) == inner_is_left()
    choose(jnp.where(from_inner, inner, outer).astype(jnp.int32), chooser_ref, block)


def choose(offsets, chooser_ref, first):
    faces, block = offsets.shape
    lane = rows_of((1, block), 1) + first
    row = rows_of((2 * block, block), 0)
    for f in range(faces):
        offset = offsets[f : f + 1, :]
        source = jnp.where(offset != 0, (lane + offset) & (2 * block - 1), -1)
        chooser_ref[:, f * block : (f + 1) * block] = (row == source).astype(F32).astype(BF16)


def apply_inverse(inverse_ref, field, variables, depth=None):
    full, _, block = inverse_ref.shape
    modes = full // variables
    zero = jnp.zeros((8, block), F32)

    def piece(row):
        if row >= full:
            return zero
        product = inverse_ref[row % modes * variables + row // modes if depth else row] * field
        partial = product[0:8]
        for j in range(8, full - 7, 8):
            partial += product[j : j + 8]
        rest = full % 8
        if rest:
            partial += jnp.concatenate([product[full - rest :], zero[rest:]], axis=0)
        return partial

    rows = []
    for at in range(0, depth or full, 8):
        rows.append(sum_rows([piece(at + r) for r in range(8)]) if at < full else zero)
    return jnp.concatenate(rows, axis=0)[: depth or full]


def first_kernel(inverse_ref, *refs, subs, variables):
    block_refs, (total_ref, out_ref, inner_ref, outer_ref, padded) = refs[:-5], refs[-5:]
    full = total_ref.shape[0]
    owner = lax.axis_index("high") * lax.axis_size("low") + lax.axis_index("low")
    owner = (owner * subs + lax.axis_index("sub")).astype(F32)
    residual = jnp.zeros(total_ref.shape, F32)
    for ref in block_refs:
        residual += jnp.where(ref[full:, :] == owner, ref[:full, :], 0.0)
    total_ref[...] = residual
    depth = padded.shape[0]
    padded[full:, :] = jnp.zeros((depth - full, padded.shape[1]), F32)
    padded[:full, :] = residual
    x = apply_inverse(inverse_ref, residual, variables, depth)
    out_ref[...] = x
    half, quarter = depth // 2, depth // 4
    inner_ref[:half, :], outer_ref[:half, :] = pack_halves(x[:half], x[half:])
    inner_ref[half:, :], outer_ref[half:, :] = pack_quarters(
        [padded[g * quarter : (g + 1) * quarter, :] for g in range(4)]
    )


def sweep_kernel(
    inverse_ref, inverse_beside_ref, residual_ref, x_ref, outer_ref, inner_ref, chooser_ref,
    chooser_beside_ref, lift_ref, jacobian_ref, jacobian_beside_ref, total_ref, out_ref,
    picked_ref, z_ref, *, variables, slab
):
    depth, block = x_ref.shape
    full = residual_ref.shape[0]
    modes = full // variables
    faces = jacobian_ref.shape[2]
    residual = residual_ref[...]
    total_ref[...] = residual
    third = z_ref.shape[0] // 3

    def coupled(x, tiles):
        x = jnp.concatenate(split(x), axis=0)
        for t, ref in enumerate((chooser_ref, chooser_beside_ref)[:tiles]):
            picked = mm(x, ref[...])
            picked_ref[t] = picked[:depth] + picked[depth:]
        for t in range(tiles):
            for f in range(faces):
                at = f * block
                part = [
                    picked_ref[t, v * modes : v * modes + slab, at : at + block]
                    for v in range(variables)
                ]
                for w in range(variables):
                    z = None
                    for v in range(variables):
                        if t:
                            line = (w * variables + v) * faces + f
                            term = part[v] * jacobian_beside_ref[line : line + 1, :]
                        else:
                            term = part[v] * jacobian_ref[w, v, f : f + 1, :]
                        z = z + term if v else term
                    line, column = (w * faces + f) * slab, t * block
                    high, low = split(z)
                    for n, value in enumerate((high, low, high)):
                        at_row = n * third + line
                        z_ref[at_row : at_row + slab, column : column + block] = value
        return mm(lift_ref[...], z_ref[:, : tiles * block])

    half = depth // 2
    first_beside = jnp.concatenate(take_halves(inner_ref[:half, :], outer_ref[:half, :]), axis=0)
    beside = take_quarters(inner_ref[half:, :], outer_ref[half:, :])
    beside = jnp.concatenate(beside, axis=0)[:full]
    taken = coupled(jnp.concatenate([x_ref[...], first_beside], axis=1), 2)
    second = jnp.concatenate(
        [
            apply_inverse(inverse_ref, residual - taken[:, :block], variables, depth),
            apply_inverse(inverse_beside_ref, beside - taken[:, block:], variables, depth),
        ],
        axis=1,
    )
    out_ref[...] = apply_inverse(inverse_ref, residual - coupled(second, 1), variables)


def per_device(
    fine_residual,
    fine_basis,
    coarse_basis,
    donor_cells,
    point_counts,
    solver_pos,
    block_inverse,
    face_jacobian,
    face_lift,
    face_offset,
):
    high_count = lax.axis_size("high")
    passing = lax.axis_size("low") * lax.axis_size("sub")
    owners = high_count * passing
    _, variables, fine = fine_residual.shape
    modes = coarse_basis.shape[1]
    donors = donor_cells.shape[1]
    block = solver_pos.shape[0]
    faces = face_offset.shape[0]
    full = modes * variables
    slab = -(-modes // 16) * 16
    depth = -(-full // 16) * 16

    capacity = max(2, 2 * fine * donors // owners)
    few = 1 < high_count <= 8 and high_count & (high_count - 1) == 0
    subs = lax.axis_size("sub")
    counter = call(
        constants_kernel,
        "constants",
        ((128, 256), BF16),
        (),
        cost=pl.CostEstimate(flops=2 * 10**9, bytes_accessed=8 * 10**6, transcendentals=0),
    )
    width = high_count * capacity
    halves = 2 if width > 128 else 1
    rows = -(-(full + 1) // 4) * 4 if halves > 1 else -(-(full + 1) // 8) * 8
    chunk_shape = (passing, halves * rows, width // halves)
    columns = call(
        functools.partial(
            restrict_kernel,
            owners=owners,
            block=block,
            passing=passing,
            capacity=capacity,
            few=few,
        ),
        "restrict",
        (chunk_shape, F32),
        (
            counter,
            fine_residual.transpose(1, 0, 2),
            fine_basis.T,
            coarse_basis.transpose(1, 0, 2),
            point_counts.T,
            donor_cells.T,
        ),
        [
            pltpu.VMEM((donors * fine // 128, depth, 128), F32),
            pltpu.VMEM(chunk_shape, F32),
            pltpu.SemaphoreType.DMA((passing,)),
        ],
        megabytes=16,
        out_spec=pl.BlockSpec(memory_space=pl.ANY),
    )
    columns = lax.all_to_all(columns, PLANE, 0, 0, tiled=True)
    def seat(name, groups, shapes):
        return call(
            functools.partial(seat_kernel, groups=groups, capacity=capacity, rows=rows),
            name,
            shapes,
            (columns,),
            megabytes=24,
        )

    dense = ((full, block), F32)
    if few:
        count = high_count // 2
        near = seat("seat_near", range(count), [dense] * count)
        rest = [seat("seat_far", [d], [dense])[0] for d in range(count, high_count)]
        blocks = swap_all([*near, *rest], "high")
    else:
        blocks = seat("seat_all", range(high_count), ((high_count, full, block), F32))
        blocks = [lax.all_to_all(blocks, "high", 0, 0, tiled=True)]
    whole = call(
        renumber_kernel, "renumber", ((full + 1, block), F32), (solver_pos[None, :], *blocks)
    )
    blocks = swap_all([whole] * subs, "sub")

    jacobian = face_jacobian.transpose(1, 2, 0, 3)
    chooser, lift = call(
        functools.partial(prepare_kernel, variables=variables, slab=slab),
        "prepare",
        [((2 * block, faces * block), BF16), ((full, 3 * variables * faces * slab), BF16)],
        (counter, face_offset, face_lift.transpose(1, 0, 2)),
    )
    outer_pairs = [(i, i + 1) for i in range(1, owners - 1, 2)]
    outer_pairs += [(j, i) for i, j in outer_pairs]
    inner_pairs = [(i, i ^ 1) for i in range(owners)]
    packed = ((-(-full // 4) + 1, full, block), F32)
    lines = variables * variables * faces
    to_inner, to_outer = call(
        pack_kernel,
        "pack",
        [packed, packed],
        (lift, block_inverse, jacobian, face_offset),
        [pltpu.VMEM((lines, block), F32)],
    )
    outer = lax.ppermute(to_outer, WHOLE, outer_pairs)
    inner = lax.ppermute(to_inner, WHOLE, inner_pairs)
    inverse_beside, jacobian_beside, chooser_beside = call(
        functools.partial(beside_kernel, faces=faces),
        "beside",
        [((full, full, block), F32), ((lines, block), F32), ((2 * block, faces * block), BF16)],
        (inner, outer),
    )
    plain, edge = ((full, block), F32), ((depth // 4 * 3, block), F32)
    residual, x, to_inner, to_outer = call(
        functools.partial(first_kernel, subs=subs, variables=variables),
        "first",
        [plain, ((depth, block), F32), edge, edge],
        (block_inverse, *blocks),
        [pltpu.VMEM((depth, block), F32)],
    )
    outer = lax.ppermute(to_outer, WHOLE, outer_pairs)
    inner = lax.ppermute(to_inner, WHOLE, inner_pairs)
    return tuple(
        call(
            functools.partial(sweep_kernel, variables=variables, slab=slab),
            "sweeps",
            [plain, plain],
            (
                block_inverse,
                inverse_beside,
                residual,
                x,
                outer,
                inner,
                chooser,
                chooser_beside,
                lift,
                jacobian,
                jacobian_beside,
            ),
            [pltpu.VMEM((2, depth, faces * block), F32)]
            + [pltpu.VMEM((3 * variables * faces * slab, 2 * block), BF16)],
        )
    )


def solution(mesh):
    dom, sub = mesh.devices.shape
    low = next(count for count in (4, 2, 1) if dom % count == 0)
    split_mesh = jax.sharding.Mesh(mesh.devices.reshape(dom // low, low, sub), WHOLE)
    in_specs = (
        P(None, None, WHOLE),
        P(),
        P(None, None, WHOLE),
        P(WHOLE, None),
        P(WHOLE, None),
        P(WHOLE),
        P(None, None, WHOLE),
        P(None, None, None, WHOLE),
        P(),
        P(None, WHOLE),
    )
    return jax.shard_map(
        per_device,
        mesh=split_mesh,
        in_specs=in_specs,
        out_specs=(P(None, WHOLE), P(None, WHOLE)),
        check_vma=False,
    )
```

```python
import functools
import jax
import jax.numpy as jnp
from jax import lax
from jax.experimental import pallas as pl
from jax.experimental.pallas import tpu as pltpu
from jax.sharding import PartitionSpec as P

F32 = jnp.float32
BF16 = jnp.bfloat16
PLANE = ("low", "sub")
WHOLE = ("high", "low", "sub")
VMEM = pl.BlockSpec(memory_space=pltpu.VMEM)


def split(x):
    high = x.astype(BF16)
    return high, (x - high.astype(F32)).astype(BF16)


def mm(a, b, ca=1, cb=0, precision=None):
    return lax.dot_general(
        a, b, (((ca,), (cb,)), ((), ())), precision=precision, preferred_element_type=F32
    )


def rows_of(iota_shape, dim):
    return lax.broadcasted_iota(jnp.int32, iota_shape, dim)


def call(kernel, name, shapes, args, scratch=(), megabytes=8, cost=None, out_spec=VMEM):
    single = not isinstance(shapes, list)
    out = [jax.ShapeDtypeStruct(*shape) for shape in ([shapes] if single else shapes)]
    result = pl.pallas_call(
        kernel,
        out_shape=out,
        in_specs=[VMEM] * len(args),
        out_specs=[out_spec] * len(out),
        scratch_shapes=list(scratch),
        compiler_params=pltpu.CompilerParams(vmem_limit_bytes=megabytes * 2**20),
        cost_estimate=cost,
        name=name,
    )(*args)
    return result[0] if single else result


def swap_all(blocks, axis):
    count = len(blocks)
    return [blocks[0]] + [
        lax.ppermute(blocks[d], axis, [(i, i ^ d) for i in range(count)])
        for d in range(count - 1, 0, -1)
    ]


def constants_kernel(counter_ref):
    lanes = counter_ref.shape[0]
    earlier = (rows_of((lanes, lanes), 0) < rows_of((lanes, lanes), 1)).astype(F32)
    counter = jnp.concatenate([earlier, jnp.ones((lanes, lanes), F32)], axis=1)
    counter_ref[...] = counter.astype(BF16)


def free_columns(owner, counter, owners, passing, capacity, width, high):
    lanes = 128
    total = owner.shape[1]
    parts = total // lanes
    mine = (rows_of((owners, total), 0) == owner).astype(F32)
    stacked = jnp.concatenate([mine[:, j * lanes : (j + 1) * lanes] for j in range(parts)], axis=0)
    counted = mm(stacked.astype(BF16), counter)
    before = jnp.zeros((owners, lanes), F32)
    ranks = []
    for j in range(parts):
        own = mine[:, j * lanes : (j + 1) * lanes]
        part = counted[j * owners : (j + 1) * owners]
        ranks.append(jnp.sum(own * (before + part[:, :lanes]), axis=0, keepdims=True))
        before += part[:, lanes:]
    rank = jnp.concatenate(ranks, axis=1).astype(jnp.int32)
    return (owner % passing) * width + (owner // passing ^ high) * capacity + rank


def add_eights(x):
    total = x[0:8]
    for j in range(8, x.shape[0], 8):
        total += x[j : j + 8]
    return total


def sum_rows(pieces):
    row = rows_of(pieces[0].shape, 0)
    pieces = [pieces[k] for k in (3, 2, 1, 0, 7, 6, 5, 4)]
    upper = row < 4
    halves = []
    for one, two in zip(pieces[:4], pieces[4:]):
        kept, moved = jnp.where(upper, one, two), jnp.where(upper, two, one)
        halves.append(kept + pltpu.roll(moved, 4, 0))
    for shift in (2, 1):
        pairs = list(zip(halves[:shift], halves[shift:]))
        halves = [
            jnp.where(
                row & shift != 0, one + pltpu.roll(one, shift, 0), two + pltpu.roll(two, 8 - shift, 0)
            )
            for one, two in pairs
        ]
    return halves[0]


def restrict_kernel(
    counter_ref, res_ref, basis_ref, coarse_ref, counts_ref, donors_ref, out_hbm, pair_ref, out_ref, sems,
    *, owners, block, passing, capacity, few
):
    variables, _, fine = res_ref.shape
    modes, points, _ = coarse_ref.shape
    donors = counts_ref.shape[0]
    chunks = out_ref.shape[0]
    full = modes * variables
    depth = pair_ref.shape[1]
    total = donors * fine
    lanes = 128
    width = owners // passing * capacity

    cell = jnp.concatenate([donors_ref[k : k + 1, :] for k in range(donors)], axis=1)
    seat = (cell % block).astype(F32)
    for j in range(total // lanes):
        pair_ref[j, full:, :] = jnp.zeros((depth - full, lanes), F32)
        pair_ref[j, full : full + 1, :] = seat[:, j * lanes : (j + 1) * lanes]
    high = lax.axis_index("high") if few else 0
    slot = free_columns(cell // block, counter_ref[...], owners, passing, capacity, width, high)
    slot = jnp.broadcast_to(slot.astype(F32), (lanes, total)).T.astype(jnp.int32).astype(jnp.int16)

    basis_high, basis_low = split(basis_ref[...])
    res_high, res_low = split(jnp.concatenate([res_ref[v] for v in range(variables)], axis=1))
    values = mm(basis_high, res_high, 0, 0)
    values += mm(basis_high, res_low, 0, 0) + mm(basis_low, res_high, 0, 0)

    point = rows_of((points, lanes), 0)
    for at in range(0, fine, lanes):
        upper = jnp.zeros((1, lanes), jnp.int32)
        inside = []
        for k in range(donors):
            lower = upper
            upper = lower + counts_ref[k : k + 1, at : at + lanes]
            inside.append((point >= lower) & (point < upper))
        for v in range(variables):
            column = v * fine + at
            value = values[:, column : column + lanes]
            masked = [jnp.where(inside[k], value, 0.0) for k in range(donors)]
            pieces = []
            for a in range(modes):
                coarse = coarse_ref[a, :, at : at + lanes]
                terms = [coarse * masked[k] for k in range(donors)]
                pieces.append([add_eights(term) for term in terms])
            whole = modes - modes % 8
            for k in range(donors):
                left = k * fine + at
                for a in range(0, whole, 8):
                    rows = pl.ds(a * variables + v, 8, stride=variables)
                    pair_ref[left // lanes, rows, :] = sum_rows(
                        [pieces[a + r][k] for r in range(8)]
                    )
            rest = [(k, a) for k in range(donors) for a in range(whole, modes)]
            for first in range(0, len(rest), 8):
                group = rest[first : first + 8]
                filled = group + [group[0]] * (8 - len(group))
                sums = sum_rows([pieces[a][k] for k, a in filled])
                for r, (k, a) in enumerate(group):
                    row, left = a * variables + v, k * fine + at
                    pair_ref[left // lanes, row : row + 1, :] = sums[r : r + 1]

    pair = jnp.concatenate([pair_ref[j] for j in range(total // lanes)], axis=1)
    both = jnp.concatenate(split(pair), axis=0)
    lane = rows_of((total, lanes), 1).astype(jnp.int16)
    one, zero = jnp.ones((total, lanes), BF16), jnp.zeros((total, lanes), BF16)
    part = out_ref.shape[2]
    rows = out_ref.shape[1] * part // width
    together = max(1, 256 // width)
    for first in range(0, chunks, together):
        chooser = jnp.concatenate(
            [
                jnp.where(slot == lane + jnp.int16(first * width + j), one, zero)
                for j in range(0, together * width, lanes)
            ],
            axis=1,
        )
        placed = mm(both, chooser)
        placed = placed[:depth] + placed[depth:]
        for c in range(first, first + together):
            for j in range(width // part):
                at = (c - first) * width + j * part
                out_ref[c, j * rows : (j + 1) * rows] = placed[:rows, at : at + part]
            pltpu.make_async_copy(out_ref.at[c], out_hbm.at[c], sems.at[c]).start()
    for c in range(chunks):
        pltpu.make_async_copy(out_ref.at[c], out_hbm.at[c], sems.at[c]).wait()


def seat_kernel(columns_ref, *out_refs, groups, capacity, rows):
    sources = columns_ref.shape[0]
    full, block = out_refs[0].shape[-2:]
    for n, group in enumerate(groups):
        j, at = divmod(group * capacity, columns_ref.shape[2])
        got = jnp.concatenate(
            [
                columns_ref[s, j * rows : j * rows + full + 1, at : at + capacity]
                for s in range(sources)
            ],
            axis=1,
        )
        seat = got[full : full + 1, :]
        chooser = (rows_of((block, got.shape[1]), 0).astype(F32) == seat).astype(F32).astype(BF16)
        high, low = split(got)
        dense = (mm(high, chooser, 1, 1) + mm(low, chooser, 1, 1))[:full]
        if len(out_refs) == len(groups):
            out_refs[n][...] = dense
        else:
            out_refs[0][n] = dense


def renumber_kernel(place_ref, *refs):
    block_refs, out_ref = refs[:-1], refs[-1]
    block = place_ref.shape[1]
    if len(block_refs) == 1:
        total = block_refs[0][0]
        for h in range(1, block_refs[0].shape[0]):
            total += block_refs[0][h]
    else:
        total = block_refs[0][...]
        for ref in block_refs[1:]:
            total += ref[...]
    full = total.shape[0]
    place = place_ref[...]
    chooser = (rows_of((block, block), 0) == place % block).astype(F32).astype(BF16)
    high, low = split(total)
    out_ref[:full, :] = mm(high, chooser, 1, 1) + mm(low, chooser, 1, 1)
    out_ref[full:, :] = (place // block).astype(F32)


def prepare_kernel(after_ref, offset_ref, lift_ref, chooser_ref, lift_out_ref, *, variables, slab):
    del after_ref
    faces, block = offset_ref.shape
    modes = lift_ref.shape[0]
    full = modes * variables
    choose(offset_ref[...], chooser_ref, 0)
    width = variables * faces * slab
    column = rows_of((modes, width), 1)
    mode = rows_of((modes, width), 0)
    spread = jnp.zeros((modes, width), F32)
    for f in range(faces):
        put = (column % slab == mode) & ((column // slab) % faces == f)
        spread += mm(lift_ref[:, f, :], put.astype(F32), 1, 0, lax.Precision.HIGHEST)
    expand = (rows_of((full, modes), 0) // variables == rows_of((full, modes), 1)).astype(F32)
    lifted = mm(expand, spread, 1, 0, lax.Precision.HIGHEST)
    keep = rows_of((full, width), 1) // (slab * faces) == rows_of((full, width), 0) % variables
    high, low = split(jnp.where(keep, lifted, 0.0))
    lift_out_ref[...] = jnp.concatenate([high, high, low], axis=1)


def inner_is_left():
    return lax.axis_index("sub") % 2 == 1


def pack_quarters(pieces):
    reach = pieces[0].shape[1] // 4
    turned = [pieces[0]] + [pltpu.roll(pieces[g], g * reach, 1) for g in range(1, 4)]
    quarter = rows_of(pieces[0].shape, 1) // reach
    to_left, to_right = turned[0], turned[0]
    for g in range(1, 4):
        to_left = jnp.where(quarter == g, turned[g], to_left)
        to_right = jnp.where(quarter == g - 1, turned[g], to_right)
    left = inner_is_left()
    return jnp.where(left, to_left, to_right), jnp.where(left, to_right, to_left)


def take_quarters(inner, outer):
    reach = inner.shape[1] // 4
    quarter = rows_of(inner.shape, 1) // reach
    pieces = []
    for g in range(4):
        piece = jnp.where((quarter == g) != inner_is_left(), inner, outer)
        pieces.append(pltpu.roll(piece, (4 - g) * reach, 1) if g else piece)
    return pieces


def pack_halves(one, two):
    block = one.shape[1]
    turned = pltpu.roll(two, block // 2, 1)
    kept = (rows_of(one.shape, 1) < block // 2) == inner_is_left()
    return jnp.where(kept, one, turned), jnp.where(kept, turned, one)


def take_halves(inner, outer):
    block = inner.shape[1]
    from_inner = (rows_of(inner.shape, 1) >= block // 2) == inner_is_left()
    two = jnp.where(from_inner, outer, inner)
    return jnp.where(from_inner, inner, outer), pltpu.roll(two, block // 2, 1)


def pack_kernel(after_ref, inverse_ref, jacobian_ref, offset_ref, inner_ref, outer_ref, lines):
    del after_ref
    full, _, block = inverse_ref.shape
    variables, _, faces, _ = jacobian_ref.shape
    slabs = -(-full // 4)
    for j in range(slabs):
        index = [j + g * slabs for g in range(4)]
        pieces = [inverse_ref[i] if i < full else jnp.zeros((full, block), F32) for i in index]
        at = j * full
        inner_ref[at : at + full, :], outer_ref[at : at + full, :] = pack_quarters(pieces)
    for w in range(variables):
        for v in range(variables):
            at = (w * variables + v) * faces
            lines[at : at + faces, :] = jacobian_ref[w, v]
    count = lines.shape[0] // 4
    packed = pack_quarters([lines[g * count : (g + 1) * count, :] for g in range(4)])
    offset = offset_ref[...].astype(F32)
    at = slabs * full
    for ref, rows in zip((inner_ref, outer_ref), packed):
        ref[at : at + count, :] = rows
        ref[at + count : ref.shape[0] - faces, :] = jnp.zeros((ref.shape[0] - faces - at - count, block), F32)
        ref[ref.shape[0] - faces :, :] = offset


def beside_kernel(inner_ref, outer_ref, inverse_ref, jacobian_ref, chooser_ref, *, faces):
    full, _, block = inverse_ref.shape
    slabs = -(-full // 4)
    for j in range(slabs):
        at = j * full
        pieces = take_quarters(inner_ref[at : at + full, :], outer_ref[at : at + full, :])
        for g, piece in enumerate(pieces):
            if j + g * slabs < full:
                inverse_ref[j + g * slabs] = piece
    count = jacobian_ref.shape[0] // 4
    at = slabs * full
    pieces = take_quarters(inner_ref[at : at + count, :], outer_ref[at : at + count, :])
    for g, piece in enumerate(pieces):
        jacobian_ref[g * count : (g + 1) * count, :] = piece
    last = inner_ref.shape[0] - faces
    inner, outer = inner_ref[last:, :], outer_ref[last:, :]
    from_inner = (rows_of(inner.shape, 1) >= block // 2) == inner_is_left()
    choose(jnp.where(from_inner, inner, outer).astype(jnp.int32), chooser_ref, block)


def choose(offsets, chooser_ref, first):
    faces, block = offsets.shape
    lane = rows_of((1, block), 1) + first
    row = rows_of((2 * block, block), 0)
    for f in range(faces):
        offset = offsets[f : f + 1, :]
        source = jnp.where(offset != 0, (lane + offset) & (2 * block - 1), -1)
        chooser_ref[:, f * block : (f + 1) * block] = (row == source).astype(F32).astype(BF16)


def apply_inverse(inverse_ref, field, variables, depth=None):
    full, _, block = inverse_ref.shape
    modes = full // variables
    zero = jnp.zeros((8, block), F32)

    def piece(row):
        if row >= full:
            return zero
        product = inverse_ref[row % modes * variables + row // modes if depth else row] * field
        partial = product[0:8]
        for j in range(8, full - 7, 8):
            partial += product[j : j + 8]
        rest = full % 8
        if rest:
            partial += jnp.concatenate([product[full - rest :], zero[rest:]], axis=0)
        return partial

    rows = []
    for at in range(0, depth or full, 8):
        rows.append(sum_rows([piece(at + r) for r in range(8)]) if at < full else zero)
    return jnp.concatenate(rows, axis=0)[: depth or full]


def first_kernel(inverse_ref, *refs, subs, variables):
    block_refs, (total_ref, out_ref, inner_ref, outer_ref, padded) = refs[:-5], refs[-5:]
    full = total_ref.shape[0]
    owner = lax.axis_index("high") * lax.axis_size("low") + lax.axis_index("low")
    owner = (owner * subs + lax.axis_index("sub")).astype(F32)
    residual = jnp.zeros(total_ref.shape, F32)
    for ref in block_refs:
        residual += jnp.where(ref[full:, :] == owner, ref[:full, :], 0.0)
    total_ref[...] = residual
    depth = padded.shape[0]
    padded[full:, :] = jnp.zeros((depth - full, padded.shape[1]), F32)
    padded[:full, :] = residual
    x = apply_inverse(inverse_ref, residual, variables, depth)
    out_ref[...] = x
    half, quarter = depth // 2, depth // 4
    inner_ref[:half, :], outer_ref[:half, :] = pack_halves(x[:half], x[half:])
    inner_ref[half:, :], outer_ref[half:, :] = pack_quarters(
        [padded[g * quarter : (g + 1) * quarter, :] for g in range(4)]
    )


def sweep_kernel(
    inverse_ref, inverse_beside_ref, residual_ref, x_ref, outer_ref, inner_ref, chooser_ref,
    chooser_beside_ref, lift_ref, jacobian_ref, jacobian_beside_ref, total_ref, out_ref,
    picked_ref, z_ref, *, variables, slab
):
    depth, block = x_ref.shape
    full = residual_ref.shape[0]
    modes = full // variables
    faces = jacobian_ref.shape[2]
    residual = residual_ref[...]
    total_ref[...] = residual
    third = z_ref.shape[0] // 3

    def coupled(x, tiles):
        x = jnp.concatenate(split(x), axis=0)
        for t, ref in enumerate((chooser_ref, chooser_beside_ref)[:tiles]):
            picked = mm(x, ref[...])
            picked_ref[t] = picked[:depth] + picked[depth:]
        for t in range(tiles):
            for f in range(faces):
                at = f * block
                part = [
                    picked_ref[t, v * modes : v * modes + slab, at : at + block]
                    for v in range(variables)
                ]
                for w in range(variables):
                    z = None
                    for v in range(variables):
                        if t:
                            line = (w * variables + v) * faces + f
                            term = part[v] * jacobian_beside_ref[line : line + 1, :]
                        else:
                            term = part[v] * jacobian_ref[w, v, f : f + 1, :]
                        z = z + term if v else term
                    line, column = (w * faces + f) * slab, t * block
                    high, low = split(z)
                    for n, value in enumerate((high, low, high)):
                        at_row = n * third + line
                        z_ref[at_row : at_row + slab, column : column + block] = value
        return mm(lift_ref[...], z_ref[:, : tiles * block])

    half = depth // 2
    first_beside = jnp.concatenate(take_halves(inner_ref[:half, :], outer_ref[:half, :]), axis=0)
    beside = take_quarters(inner_ref[half:, :], outer_ref[half:, :])
    beside = jnp.concatenate(beside, axis=0)[:full]
    taken = coupled(jnp.concatenate([x_ref[...], first_beside], axis=1), 2)
    second = jnp.concatenate(
        [
            apply_inverse(inverse_ref, residual - taken[:, :block], variables, depth),
            apply_inverse(inverse_beside_ref, beside - taken[:, block:], variables, depth),
        ],
        axis=1,
    )
    out_ref[...] = apply_inverse(inverse_ref, residual - coupled(second, 1), variables)


def per_device(
    fine_residual,
    fine_basis,
    coarse_basis,
    donor_cells,
    point_counts,
    solver_pos,
    block_inverse,
    face_jacobian,
    face_lift,
    face_offset,
):
    high_count = lax.axis_size("high")
    passing = lax.axis_size("low") * lax.axis_size("sub")
    owners = high_count * passing
    _, variables, fine = fine_residual.shape
    modes = coarse_basis.shape[1]
    donors = donor_cells.shape[1]
    block = solver_pos.shape[0]
    faces = face_offset.shape[0]
    full = modes * variables
    slab = -(-modes // 16) * 16
    depth = -(-full // 16) * 16

    capacity = max(2, 2 * fine * donors // owners)
    few = 1 < high_count <= 8 and high_count & (high_count - 1) == 0
    subs = lax.axis_size("sub")
    counter = call(
        constants_kernel,
        "constants",
        ((128, 256), BF16),
        (),
        cost=pl.CostEstimate(flops=2 * 10**9, bytes_accessed=8 * 10**6, transcendentals=0),
    )
    width = high_count * capacity
    halves = 2 if width > 128 else 1
    rows = -(-(full + 1) // 4) * 4 if halves > 1 else -(-(full + 1) // 8) * 8
    chunk_shape = (passing, halves * rows, width // halves)
    columns = call(
        functools.partial(
            restrict_kernel,
            owners=owners,
            block=block,
            passing=passing,
            capacity=capacity,
            few=few,
        ),
        "restrict",
        (chunk_shape, F32),
        (
            counter,
            fine_residual.transpose(1, 0, 2),
            fine_basis.T,
            coarse_basis.transpose(1, 0, 2),
            point_counts.T,
            donor_cells.T,
        ),
        [
            pltpu.VMEM((donors * fine // 128, depth, 128), F32),
            pltpu.VMEM(chunk_shape, F32),
            pltpu.SemaphoreType.DMA((passing,)),
        ],
        megabytes=16,
        out_spec=pl.BlockSpec(memory_space=pl.ANY),
    )
    columns = lax.all_to_all(columns, PLANE, 0, 0, tiled=True)
    def seat(name, groups, shapes):
        return call(
            functools.partial(seat_kernel, groups=groups, capacity=capacity, rows=rows),
            name,
            shapes,
            (columns,),
            megabytes=24,
        )

    dense = ((full, block), F32)
    if few:
        count = high_count // 2
        near = seat("seat_near", range(count), [dense] * count)
        rest = [seat("seat_far", [d], [dense])[0] for d in range(count, high_count)]
        blocks = swap_all([*near, *rest], "high")
    else:
        blocks = seat("seat_all", range(high_count), ((high_count, full, block), F32))
        blocks = [lax.all_to_all(blocks, "high", 0, 0, tiled=True)]
    whole = call(
        renumber_kernel, "renumber", ((full + 1, block), F32), (solver_pos[None, :], *blocks)
    )
    blocks = swap_all([whole] * subs, "sub")

    jacobian = face_jacobian.transpose(1, 2, 0, 3)
    chooser, lift = call(
        functools.partial(prepare_kernel, variables=variables, slab=slab),
        "prepare",
        [((2 * block, faces * block), BF16), ((full, 3 * variables * faces * slab), BF16)],
        (counter, face_offset, face_lift.transpose(1, 0, 2)),
    )
    outer_pairs = [(i, i + 1) for i in range(1, owners - 1, 2)]
    outer_pairs += [(j, i) for i, j in outer_pairs]
    inner_pairs = [(i, i ^ 1) for i in range(owners)]
    lines = variables * variables * faces
    packed = ((-(-(-(-full // 4) * full + lines // 4 + faces + 1) // 8) * 8, block), F32)
    to_inner, to_outer = call(
        pack_kernel,
        "pack",
        [packed, packed],
        (lift, block_inverse, jacobian, face_offset),
        [pltpu.VMEM((lines, block), F32)],
    )
    outer = lax.ppermute(to_outer, WHOLE, outer_pairs)
    inner = lax.ppermute(to_inner, WHOLE, inner_pairs)
    inverse_beside, jacobian_beside, chooser_beside = call(
        functools.partial(beside_kernel, faces=faces),
        "beside",
        [((full, full, block), F32), ((lines, block), F32), ((2 * block, faces * block), BF16)],
        (inner, outer),
    )
    plain, edge = ((full, block), F32), ((depth // 4 * 3, block), F32)
    residual, x, to_inner, to_outer = call(
        functools.partial(first_kernel, subs=subs, variables=variables),
        "first",
        [plain, ((depth, block), F32), edge, edge],
        (block_inverse, *blocks),
        [pltpu.VMEM((depth, block), F32)],
    )
    outer = lax.ppermute(to_outer, WHOLE, outer_pairs)
    inner = lax.ppermute(to_inner, WHOLE, inner_pairs)
    return tuple(
        call(
            functools.partial(sweep_kernel, variables=variables, slab=slab),
            "sweeps",
            [plain, plain],
            (
                block_inverse,
                inverse_beside,
                residual,
                x,
                outer,
                inner,
                chooser,
                chooser_beside,
                lift,
                jacobian,
                jacobian_beside,
            ),
            [pltpu.VMEM((2, depth, faces * block), F32)]
            + [pltpu.VMEM((3 * variables * faces * slab, 2 * block), BF16)],
        )
    )


def solution(mesh):
    dom, sub = mesh.devices.shape
    low = next(count for count in (4, 2, 1) if dom % count == 0)
    split_mesh = jax.sharding.Mesh(mesh.devices.reshape(dom // low, low, sub), WHOLE)
    in_specs = (
        P(None, None, WHOLE),
        P(),
        P(None, None, WHOLE),
        P(WHOLE, None),
        P(WHOLE, None),
        P(WHOLE),
        P(None, None, WHOLE),
        P(None, None, None, WHOLE),
        P(),
        P(None, WHOLE),
    )
    return jax.shard_map(
        per_device,
        mesh=split_mesh,
        in_specs=in_specs,
        out_specs=(P(None, WHOLE), P(None, WHOLE)),
        check_vma=False,
    )
```

```python
import functools
import jax
import jax.numpy as jnp
from jax import lax
from jax.experimental import pallas as pl
from jax.experimental.pallas import tpu as pltpu
from jax.sharding import PartitionSpec as P

F32 = jnp.float32
BF16 = jnp.bfloat16
PLANE = ("low", "sub")
WHOLE = ("high", "low", "sub")
VMEM = pl.BlockSpec(memory_space=pltpu.VMEM)


def split(x):
    high = x.astype(BF16)
    return high, (x - high.astype(F32)).astype(BF16)


def mm(a, b, ca=1, cb=0, precision=None):
    return lax.dot_general(
        a, b, (((ca,), (cb,)), ((), ())), precision=precision, preferred_element_type=F32
    )


def rows_of(iota_shape, dim):
    return lax.broadcasted_iota(jnp.int32, iota_shape, dim)


def call(kernel, name, shapes, args, scratch=(), megabytes=8, cost=None, out_spec=VMEM):
    single = not isinstance(shapes, list)
    out = [jax.ShapeDtypeStruct(*shape) for shape in ([shapes] if single else shapes)]
    result = pl.pallas_call(
        kernel,
        out_shape=out,
        in_specs=[VMEM] * len(args),
        out_specs=[out_spec] * len(out),
        scratch_shapes=list(scratch),
        compiler_params=pltpu.CompilerParams(vmem_limit_bytes=megabytes * 2**20),
        cost_estimate=cost,
        name=name,
    )(*args)
    return result[0] if single else result


def swap_all(blocks, axis):
    count = len(blocks)
    return [blocks[0]] + [
        lax.ppermute(blocks[d], axis, [(i, i ^ d) for i in range(count)])
        for d in range(count - 1, 0, -1)
    ]


def constants_kernel(counter_ref):
    lanes = counter_ref.shape[0]
    earlier = (rows_of((lanes, lanes), 0) < rows_of((lanes, lanes), 1)).astype(F32)
    counter = jnp.concatenate([earlier, jnp.ones((lanes, lanes), F32)], axis=1)
    counter_ref[...] = counter.astype(BF16)


def free_columns(owner, counter, owners, passing, capacity, width, high):
    lanes = 128
    total = owner.shape[1]
    parts = total // lanes
    mine = (rows_of((owners, total), 0) == owner).astype(F32)
    stacked = jnp.concatenate([mine[:, j * lanes : (j + 1) * lanes] for j in range(parts)], axis=0)
    counted = mm(stacked.astype(BF16), counter)
    before = jnp.zeros((owners, lanes), F32)
    ranks = []
    for j in range(parts):
        own = mine[:, j * lanes : (j + 1) * lanes]
        part = counted[j * owners : (j + 1) * owners]
        ranks.append(jnp.sum(own * (before + part[:, :lanes]), axis=0, keepdims=True))
        before += part[:, lanes:]
    rank = jnp.concatenate(ranks, axis=1).astype(jnp.int32)
    return (owner % passing) * width + (owner // passing ^ high) * capacity + rank


def add_eights(x):
    total = x[0:8]
    for j in range(8, x.shape[0], 8):
        total += x[j : j + 8]
    return total


def sum_rows(pieces):
    row = rows_of(pieces[0].shape, 0)
    pieces = [pieces[k] for k in (3, 2, 1, 0, 7, 6, 5, 4)]
    upper = row < 4
    halves = []
    for one, two in zip(pieces[:4], pieces[4:]):
        kept, moved = jnp.where(upper, one, two), jnp.where(upper, two, one)
        halves.append(kept + pltpu.roll(moved, 4, 0))
    for shift in (2, 1):
        pairs = list(zip(halves[:shift], halves[shift:]))
        halves = [
            jnp.where(
                row & shift != 0, one + pltpu.roll(one, shift, 0), two + pltpu.roll(two, 8 - shift, 0)
            )
            for one, two in pairs
        ]
    return halves[0]


def restrict_kernel(
    counter_ref, res_ref, basis_ref, coarse_ref, counts_ref, donors_ref, out_hbm, pair_ref, out_ref, sems,
    *, owners, block, passing, capacity, few
):
    variables, _, fine = res_ref.shape
    modes, points, _ = coarse_ref.shape
    donors = counts_ref.shape[0]
    chunks = out_ref.shape[0]
    full = modes * variables
    depth = pair_ref.shape[1]
    total = donors * fine
    lanes = 128
    width = owners // passing * capacity

    cell = jnp.concatenate([donors_ref[k : k + 1, :] for k in range(donors)], axis=1)
    seat = (cell % block).astype(F32)
    for j in range(total // lanes):
        pair_ref[j, full:, :] = jnp.zeros((depth - full, lanes), F32)
        pair_ref[j, full : full + 1, :] = seat[:, j * lanes : (j + 1) * lanes]
    high = lax.axis_index("high") if few else 0
    slot = free_columns(cell // block, counter_ref[...], owners, passing, capacity, width, high)
    slot = jnp.broadcast_to(slot.astype(F32), (lanes, total)).T.astype(jnp.int32).astype(jnp.int16)

    basis_high, basis_low = split(basis_ref[...])
    res_high, res_low = split(jnp.concatenate([res_ref[v] for v in range(variables)], axis=1))
    values = mm(basis_high, res_high, 0, 0)
    values += mm(basis_high, res_low, 0, 0) + mm(basis_low, res_high, 0, 0)

    point = rows_of((points, lanes), 0)
    for at in range(0, fine, lanes):
        upper = jnp.zeros((1, lanes), jnp.int32)
        inside = []
        for k in range(donors):
            lower = upper
            upper = lower + counts_ref[k : k + 1, at : at + lanes]
            inside.append((point >= lower) & (point < upper))
        for v in range(variables):
            column = v * fine + at
            value = values[:, column : column + lanes]
            masked = [jnp.where(inside[k], value, 0.0) for k in range(donors)]
            pieces = []
            for a in range(modes):
                coarse = coarse_ref[a, :, at : at + lanes]
                terms = [coarse * masked[k] for k in range(donors)]
                pieces.append([add_eights(term) for term in terms])
            whole = modes - modes % 8
            for k in range(donors):
                left = k * fine + at
                for a in range(0, whole, 8):
                    rows = pl.ds(a * variables + v, 8, stride=variables)
                    pair_ref[left // lanes, rows, :] = sum_rows(
                        [pieces[a + r][k] for r in range(8)]
                    )
            rest = [(k, a) for k in range(donors) for a in range(whole, modes)]
            for first in range(0, len(rest), 8):
                group = rest[first : first + 8]
                filled = group + [group[0]] * (8 - len(group))
                sums = sum_rows([pieces[a][k] for k, a in filled])
                for r, (k, a) in enumerate(group):
                    row, left = a * variables + v, k * fine + at
                    pair_ref[left // lanes, row : row + 1, :] = sums[r : r + 1]

    pair = jnp.concatenate([pair_ref[j] for j in range(total // lanes)], axis=1)
    both = jnp.concatenate(split(pair), axis=0)
    lane = rows_of((total, lanes), 1).astype(jnp.int16)
    one, zero = jnp.ones((total, lanes), BF16), jnp.zeros((total, lanes), BF16)
    part = out_ref.shape[2]
    rows = out_ref.shape[1] * part // width
    together = max(1, 256 // width)
    for first in range(0, chunks, together):
        chooser = jnp.concatenate(
            [
                jnp.where(slot == lane + jnp.int16(first * width + j), one, zero)
                for j in range(0, together * width, lanes)
            ],
            axis=1,
        )
        placed = mm(both, chooser)
        placed = placed[:depth] + placed[depth:]
        for c in range(first, first + together):
            for j in range(width // part):
                at = (c - first) * width + j * part
                out_ref[c, j * rows : (j + 1) * rows] = placed[:rows, at : at + part]
            pltpu.make_async_copy(out_ref.at[c], out_hbm.at[c], sems.at[c]).start()
    for c in range(chunks):
        pltpu.make_async_copy(out_ref.at[c], out_hbm.at[c], sems.at[c]).wait()


def seat_kernel(columns_ref, *out_refs, groups, capacity, rows):
    sources = columns_ref.shape[0]
    full, block = out_refs[0].shape[-2:]
    for n, group in enumerate(groups):
        j, at = divmod(group * capacity, columns_ref.shape[2])
        got = jnp.concatenate(
            [
                columns_ref[s, j * rows : j * rows + full + 1, at : at + capacity]
                for s in range(sources)
            ],
            axis=1,
        )
        seat = got[full : full + 1, :]
        chooser = (rows_of((block, got.shape[1]), 0).astype(F32) == seat).astype(F32).astype(BF16)
        high, low = split(got)
        dense = (mm(high, chooser, 1, 1) + mm(low, chooser, 1, 1))[:full]
        if len(out_refs) == len(groups):
            out_refs[n][...] = dense
        else:
            out_refs[0][n] = dense


def renumber_kernel(place_ref, *refs):
    block_refs, out_ref = refs[:-1], refs[-1]
    block = place_ref.shape[1]
    if len(block_refs) == 1:
        total = block_refs[0][0]
        for h in range(1, block_refs[0].shape[0]):
            total += block_refs[0][h]
    else:
        total = block_refs[0][...]
        for ref in block_refs[1:]:
            total += ref[...]
    full = total.shape[0]
    place = place_ref[...]
    chooser = (rows_of((block, block), 0) == place % block).astype(F32).astype(BF16)
    high, low = split(total)
    out_ref[:full, :] = mm(high, chooser, 1, 1) + mm(low, chooser, 1, 1)
    out_ref[full:, :] = (place // block).astype(F32)


def prepare_kernel(after_ref, offset_ref, lift_ref, chooser_ref, lift_out_ref, *, variables, slab):
    del after_ref
    faces, block = offset_ref.shape
    modes = lift_ref.shape[0]
    full = modes * variables
    choose(offset_ref[...], chooser_ref, 0)
    width = variables * faces * slab
    column = rows_of((modes, width), 1)
    mode = rows_of((modes, width), 0)
    spread = jnp.zeros((modes, width), F32)
    for f in range(faces):
        put = (column % slab == mode) & ((column // slab) % faces == f)
        spread += mm(lift_ref[:, f, :], put.astype(F32), 1, 0, lax.Precision.HIGHEST)
    expand = (rows_of((full, modes), 0) // variables == rows_of((full, modes), 1)).astype(F32)
    lifted = mm(expand, spread, 1, 0, lax.Precision.HIGHEST)
    keep = rows_of((full, width), 1) // (slab * faces) == rows_of((full, width), 0) % variables
    high, low = split(jnp.where(keep, lifted, 0.0))
    lift_out_ref[...] = jnp.concatenate([high, high, low], axis=1)


def inner_is_left():
    return lax.axis_index("sub") % 2 == 1


def pack_quarters(pieces, for_left):
    reach = pieces[0].shape[1] // 4
    turned = [pieces[0]] + [pltpu.roll(pieces[g], g * reach, 1) for g in range(1, 4)]
    quarter = rows_of(pieces[0].shape, 1) // reach
    to_left, to_right = turned[0], turned[0]
    for g in range(1, 4):
        to_left = jnp.where(quarter == g, turned[g], to_left)
        to_right = jnp.where(quarter == g - 1, turned[g], to_right)
    return jnp.where(for_left, to_left, to_right)


def take_quarters(inner, outer):
    reach = inner.shape[1] // 4
    quarter = rows_of(inner.shape, 1) // reach
    pieces = []
    for g in range(4):
        piece = jnp.where((quarter == g) != inner_is_left(), inner, outer)
        pieces.append(pltpu.roll(piece, (4 - g) * reach, 1) if g else piece)
    return pieces


def pack_halves(one, two):
    block = one.shape[1]
    turned = pltpu.roll(two, block // 2, 1)
    kept = (rows_of(one.shape, 1) < block // 2) == inner_is_left()
    return jnp.where(kept, one, turned), jnp.where(kept, turned, one)


def take_halves(inner, outer):
    block = inner.shape[1]
    from_inner = (rows_of(inner.shape, 1) >= block // 2) == inner_is_left()
    two = jnp.where(from_inner, outer, inner)
    return jnp.where(from_inner, inner, outer), pltpu.roll(two, block // 2, 1)


def pack_kernel(after_ref, inverse_ref, jacobian_ref, offset_ref, out_ref, lines, *, outer):
    del after_ref
    full, _, block = inverse_ref.shape
    variables, _, faces, _ = jacobian_ref.shape
    for_left = inner_is_left() != outer
    slabs = -(-full // 4)
    for j in range(slabs):
        index = [j + g * slabs for g in range(4)]
        pieces = [inverse_ref[i] if i < full else jnp.zeros((full, block), F32) for i in index]
        out_ref[j * full : (j + 1) * full, :] = pack_quarters(pieces, for_left)
    for w in range(variables):
        for v in range(variables):
            at = (w * variables + v) * faces
            lines[at : at + faces, :] = jacobian_ref[w, v]
    count = lines.shape[0] // 4
    at, last = slabs * full, out_ref.shape[0] - faces
    pieces = [lines[g * count : (g + 1) * count, :] for g in range(4)]
    out_ref[at : at + count, :] = pack_quarters(pieces, for_left)
    out_ref[at + count : last, :] = jnp.zeros((last - at - count, block), F32)
    out_ref[last:, :] = offset_ref[...].astype(F32)


def beside_kernel(inner_ref, outer_ref, inverse_ref, jacobian_ref, chooser_ref, *, faces):
    full, _, block = inverse_ref.shape
    slabs = -(-full // 4)
    for j in range(slabs):
        at = j * full
        pieces = take_quarters(inner_ref[at : at + full, :], outer_ref[at : at + full, :])
        for g, piece in enumerate(pieces):
            if j + g * slabs < full:
                inverse_ref[j + g * slabs] = piece
    count = jacobian_ref.shape[0] // 4
    at = slabs * full
    pieces = take_quarters(inner_ref[at : at + count, :], outer_ref[at : at + count, :])
    for g, piece in enumerate(pieces):
        jacobian_ref[g * count : (g + 1) * count, :] = piece
    last = inner_ref.shape[0] - faces
    inner, outer = inner_ref[last:, :], outer_ref[last:, :]
    from_inner = (rows_of(inner.shape, 1) >= block // 2) == inner_is_left()
    choose(jnp.where(from_inner, inner, outer).astype(jnp.int32), chooser_ref, block)


def choose(offsets, chooser_ref, first):
    faces, block = offsets.shape
    lane = rows_of((1, block), 1) + first
    row = rows_of((2 * block, block), 0)
    for f in range(faces):
        offset = offsets[f : f + 1, :]
        source = jnp.where(offset != 0, (lane + offset) & (2 * block - 1), -1)
        chooser_ref[:, f * block : (f + 1) * block] = (row == source).astype(F32).astype(BF16)


def apply_inverse(inverse_ref, field, variables, depth=None):
    full, _, block = inverse_ref.shape
    modes = full // variables
    zero = jnp.zeros((8, block), F32)

    def piece(row):
        if row >= full:
            return zero
        product = inverse_ref[row % modes * variables + row // modes if depth else row] * field
        partial = product[0:8]
        for j in range(8, full - 7, 8):
            partial += product[j : j + 8]
        rest = full % 8
        if rest:
            partial += jnp.concatenate([product[full - rest :], zero[rest:]], axis=0)
        return partial

    rows = []
    for at in range(0, depth or full, 8):
        rows.append(sum_rows([piece(at + r) for r in range(8)]) if at < full else zero)
    return jnp.concatenate(rows, axis=0)[: depth or full]


def first_kernel(inverse_ref, *refs, subs, variables):
    block_refs, (total_ref, out_ref, inner_ref, outer_ref) = refs[:-4], refs[-4:]
    full = total_ref.shape[0]
    owner = lax.axis_index("high") * lax.axis_size("low") + lax.axis_index("low")
    owner = (owner * subs + lax.axis_index("sub")).astype(F32)
    residual = jnp.zeros(total_ref.shape, F32)
    for ref in block_refs:
        residual += jnp.where(ref[full:, :] == owner, ref[:full, :], 0.0)
    total_ref[...] = residual
    x = apply_inverse(inverse_ref, residual, variables, out_ref.shape[0])
    out_ref[...] = x
    half = inner_ref.shape[0]
    inner_ref[...], outer_ref[...] = pack_halves(x[:half], x[half:])


def sweep_kernel(
    inverse_ref, inverse_beside_ref, residual_ref, x_ref, outer_ref, inner_ref, chooser_ref,
    chooser_beside_ref, lift_ref, jacobian_ref, jacobian_beside_ref, total_ref, out_ref,
    picked_ref, z_ref, *, variables, slab
):
    depth, block = x_ref.shape
    full = residual_ref.shape[0]
    modes = full // variables
    faces = jacobian_ref.shape[2]
    residual = residual_ref[...]
    total_ref[...] = residual
    third = z_ref.shape[0] // 3

    def coupled(x, tiles):
        x = jnp.concatenate(split(x), axis=0)
        for t, ref in enumerate((chooser_ref, chooser_beside_ref)[:tiles]):
            picked = mm(x, ref[...])
            picked_ref[t] = picked[:depth] + picked[depth:]
        for t in range(tiles):
            for f in range(faces):
                at = f * block
                part = [
                    picked_ref[t, v * modes : v * modes + slab, at : at + block]
                    for v in range(variables)
                ]
                for w in range(variables):
                    z = None
                    for v in range(variables):
                        if t:
                            line = (w * variables + v) * faces + f
                            term = part[v] * jacobian_beside_ref[line : line + 1, :]
                        else:
                            term = part[v] * jacobian_ref[w, v, f : f + 1, :]
                        z = z + term if v else term
                    line, column = (w * faces + f) * slab, t * block
                    high, low = split(z)
                    for n, value in enumerate((high, low, high)):
                        at_row = n * third + line
                        z_ref[at_row : at_row + slab, column : column + block] = value
        return mm(lift_ref[...], z_ref[:, : tiles * block])

    first = x_ref[...]
    first_beside = jnp.concatenate(take_halves(inner_ref[...], outer_ref[...]), axis=0)
    taken = coupled(jnp.concatenate([first, first_beside], axis=1), 2)
    second = jnp.concatenate(
        [
            first - apply_inverse(inverse_ref, taken[:, :block], variables, depth),
            first_beside - apply_inverse(inverse_beside_ref, taken[:, block:], variables, depth),
        ],
        axis=1,
    )
    out_ref[...] = apply_inverse(inverse_ref, residual - coupled(second, 1), variables)


def per_device(
    fine_residual,
    fine_basis,
    coarse_basis,
    donor_cells,
    point_counts,
    solver_pos,
    block_inverse,
    face_jacobian,
    face_lift,
    face_offset,
):
    high_count = lax.axis_size("high")
    passing = lax.axis_size("low") * lax.axis_size("sub")
    owners = high_count * passing
    _, variables, fine = fine_residual.shape
    modes = coarse_basis.shape[1]
    donors = donor_cells.shape[1]
    block = solver_pos.shape[0]
    faces = face_offset.shape[0]
    full = modes * variables
    slab = -(-modes // 16) * 16
    depth = -(-full // 16) * 16

    capacity = max(2, 2 * fine * donors // owners)
    few = 1 < high_count <= 8 and high_count & (high_count - 1) == 0
    subs = lax.axis_size("sub")
    counter = call(
        constants_kernel,
        "constants",
        ((128, 256), BF16),
        (),
        cost=pl.CostEstimate(flops=2 * 10**9, bytes_accessed=8 * 10**6, transcendentals=0),
    )
    width = high_count * capacity
    halves = 2 if width > 128 else 1
    rows = -(-(full + 1) // 4) * 4 if halves > 1 else -(-(full + 1) // 8) * 8
    chunk_shape = (passing, halves * rows, width // halves)
    columns = call(
        functools.partial(
            restrict_kernel,
            owners=owners,
            block=block,
            passing=passing,
            capacity=capacity,
            few=few,
        ),
        "restrict",
        (chunk_shape, F32),
        (
            counter,
            fine_residual.transpose(1, 0, 2),
            fine_basis.T,
            coarse_basis.transpose(1, 0, 2),
            point_counts.T,
            donor_cells.T,
        ),
        [
            pltpu.VMEM((donors * fine // 128, depth, 128), F32),
            pltpu.VMEM(chunk_shape, F32),
            pltpu.SemaphoreType.DMA((passing,)),
        ],
        megabytes=16,
        out_spec=pl.BlockSpec(memory_space=pl.ANY),
    )
    columns = lax.all_to_all(columns, PLANE, 0, 0, tiled=True)
    def seat(name, groups, shapes):
        return call(
            functools.partial(seat_kernel, groups=groups, capacity=capacity, rows=rows),
            name,
            shapes,
            (columns,),
            megabytes=24,
        )

    dense = ((full, block), F32)
    if few:
        count = high_count // 2
        near = seat("seat_near", range(count), [dense] * count)
        rest = [seat("seat_far", [d], [dense])[0] for d in range(count, high_count)]
        blocks = swap_all([*near, *rest], "high")
    else:
        blocks = seat("seat_all", range(high_count), ((high_count, full, block), F32))
        blocks = [lax.all_to_all(blocks, "high", 0, 0, tiled=True)]
    whole = call(
        renumber_kernel, "renumber", ((full + 1, block), F32), (solver_pos[None, :], *blocks)
    )
    blocks = swap_all([whole] * subs, "sub")

    jacobian = face_jacobian.transpose(1, 2, 0, 3)
    chooser, lift = call(
        functools.partial(prepare_kernel, variables=variables, slab=slab),
        "prepare",
        [((2 * block, faces * block), BF16), ((full, 3 * variables * faces * slab), BF16)],
        (counter, face_offset, face_lift.transpose(1, 0, 2)),
    )
    outer_pairs = [(i, i + 1) for i in range(1, owners - 1, 2)]
    outer_pairs += [(j, i) for i, j in outer_pairs]
    inner_pairs = [(i, i ^ 1) for i in range(owners)]
    lines = variables * variables * faces
    packed = ((-(-(-(-full // 4) * full + lines // 4 + faces + 1) // 8) * 8, block), F32)
    packs = []
    for outer in (False, True):
        packs.append(
            call(
                functools.partial(pack_kernel, outer=outer),
                "pack_outer" if outer else "pack_inner",
                packed,
                (packs[0] if outer else lift, block_inverse, jacobian, face_offset),
                [pltpu.VMEM((lines, block), F32)],
            )
        )
    inner = lax.ppermute(packs[0], WHOLE, inner_pairs)
    outer = lax.ppermute(packs[1], WHOLE, outer_pairs)
    inverse_beside, jacobian_beside, chooser_beside = call(
        functools.partial(beside_kernel, faces=faces),
        "beside",
        [((full, full, block), F32), ((lines, block), F32), ((2 * block, faces * block), BF16)],
        (inner, outer),
    )
    plain, edge = ((full, block), F32), ((depth // 2, block), F32)
    residual, x, to_inner, to_outer = call(
        functools.partial(first_kernel, subs=subs, variables=variables),
        "first",
        [plain, ((depth, block), F32), edge, edge],
        (block_inverse, *blocks),
    )
    outer = lax.ppermute(to_outer, WHOLE, outer_pairs)
    inner = lax.ppermute(to_inner, WHOLE, inner_pairs)
    return tuple(
        call(
            functools.partial(sweep_kernel, variables=variables, slab=slab),
            "sweeps",
            [plain, plain],
            (
                block_inverse,
                inverse_beside,
                residual,
                x,
                outer,
                inner,
                chooser,
                chooser_beside,
                lift,
                jacobian,
                jacobian_beside,
            ),
            [pltpu.VMEM((2, depth, faces * block), F32)]
            + [pltpu.VMEM((3 * variables * faces * slab, 2 * block), BF16)],
        )
    )


def solution(mesh):
    dom, sub = mesh.devices.shape
    low = next(count for count in (4, 2, 1) if dom % count == 0)
    split_mesh = jax.sharding.Mesh(mesh.devices.reshape(dom // low, low, sub), WHOLE)
    in_specs = (
        P(None, None, WHOLE),
        P(),
        P(None, None, WHOLE),
        P(WHOLE, None),
        P(WHOLE, None),
        P(WHOLE),
        P(None, None, WHOLE),
        P(None, None, None, WHOLE),
        P(),
        P(None, WHOLE),
    )
    return jax.shard_map(
        per_device,
        mesh=split_mesh,
        in_specs=in_specs,
        out_specs=(P(None, WHOLE), P(None, WHOLE)),
        check_vma=False,
    )
```

```python
import functools
import jax
import jax.numpy as jnp
from jax import lax
from jax.experimental import pallas as pl
from jax.experimental.pallas import tpu as pltpu
from jax.sharding import PartitionSpec as P

F32 = jnp.float32
BF16 = jnp.bfloat16
PLANE = ("sub", "low")
WHOLE = ("high", "low", "sub")
VMEM = pl.BlockSpec(memory_space=pltpu.VMEM)


def split(x):
    high = x.astype(BF16)
    return high, (x - high.astype(F32)).astype(BF16)


def mm(a, b, ca=1, cb=0, precision=None):
    return lax.dot_general(
        a, b, (((ca,), (cb,)), ((), ())), precision=precision, preferred_element_type=F32
    )


def rows_of(iota_shape, dim):
    return lax.broadcasted_iota(jnp.int32, iota_shape, dim)


def call(kernel, name, shapes, args, scratch=(), megabytes=8, cost=None, out_spec=VMEM):
    single = not isinstance(shapes, list)
    out = [jax.ShapeDtypeStruct(*shape) for shape in ([shapes] if single else shapes)]
    result = pl.pallas_call(
        kernel,
        out_shape=out,
        in_specs=[VMEM] * len(args),
        out_specs=[out_spec] * len(out),
        scratch_shapes=list(scratch),
        compiler_params=pltpu.CompilerParams(vmem_limit_bytes=megabytes * 2**20),
        cost_estimate=cost,
        name=name,
    )(*args)
    return result[0] if single else result


def swap_all(blocks, axis):
    count = len(blocks)
    return [blocks[0]] + [
        lax.ppermute(blocks[d], axis, [(i, i ^ d) for i in range(count)])
        for d in range(count - 1, 0, -1)
    ]


def constants_kernel(counter_ref):
    lanes = counter_ref.shape[0]
    earlier = (rows_of((lanes, lanes), 0) < rows_of((lanes, lanes), 1)).astype(F32)
    counter = jnp.concatenate([earlier, jnp.ones((lanes, lanes), F32)], axis=1)
    counter_ref[...] = counter.astype(BF16)


def free_columns(owner, counter, owners, passing, subs, capacity, width, high):
    lanes = 128
    total = owner.shape[1]
    parts = total // lanes
    mine = (rows_of((owners, total), 0) == owner).astype(F32)
    stacked = jnp.concatenate([mine[:, j * lanes : (j + 1) * lanes] for j in range(parts)], axis=0)
    counted = mm(stacked.astype(BF16), counter)
    before = jnp.zeros((owners, lanes), F32)
    ranks = []
    for j in range(parts):
        own = mine[:, j * lanes : (j + 1) * lanes]
        part = counted[j * owners : (j + 1) * owners]
        ranks.append(jnp.sum(own * (before + part[:, :lanes]), axis=0, keepdims=True))
        before += part[:, lanes:]
    rank = jnp.concatenate(ranks, axis=1).astype(jnp.int32)
    lows = passing // subs
    chunk = owner % subs * lows + owner // subs % lows
    return chunk * width + (owner // passing ^ high) * capacity + rank


def add_eights(x):
    total = x[0:8]
    for j in range(8, x.shape[0], 8):
        total += x[j : j + 8]
    return total


def sum_rows(pieces):
    row = rows_of(pieces[0].shape, 0)
    pieces = [pieces[k] for k in (3, 2, 1, 0, 7, 6, 5, 4)]
    upper = row < 4
    halves = []
    for one, two in zip(pieces[:4], pieces[4:]):
        kept, moved = jnp.where(upper, one, two), jnp.where(upper, two, one)
        halves.append(kept + pltpu.roll(moved, 4, 0))
    for shift in (2, 1):
        pairs = list(zip(halves[:shift], halves[shift:]))
        halves = [
            jnp.where(
                row & shift != 0, one + pltpu.roll(one, shift, 0), two + pltpu.roll(two, 8 - shift, 0)
            )
            for one, two in pairs
        ]
    return halves[0]


def restrict_kernel(
    counter_ref, res_ref, basis_ref, coarse_ref, counts_ref, donors_ref, out_hbm, pair_ref, out_ref, sems,
    *, owners, block, passing, subs, capacity, few
):
    variables, _, fine = res_ref.shape
    modes, points, _ = coarse_ref.shape
    donors = counts_ref.shape[0]
    chunks = out_ref.shape[0]
    full = modes * variables
    depth = pair_ref.shape[1]
    total = donors * fine
    lanes = 128
    width = owners // passing * capacity

    cell = jnp.concatenate([donors_ref[k : k + 1, :] for k in range(donors)], axis=1)
    seat = (cell % block).astype(F32)
    for j in range(total // lanes):
        pair_ref[j, full:, :] = jnp.zeros((depth - full, lanes), F32)
        pair_ref[j, full : full + 1, :] = seat[:, j * lanes : (j + 1) * lanes]
    high = lax.axis_index("high") if few else 0
    owner = cell // block
    slot = free_columns(owner, counter_ref[...], owners, passing, subs, capacity, width, high)
    slot = jnp.broadcast_to(slot.astype(F32), (lanes, total)).T.astype(jnp.int32).astype(jnp.int16)

    basis_high, basis_low = split(basis_ref[...])
    res_high, res_low = split(jnp.concatenate([res_ref[v] for v in range(variables)], axis=1))
    values = mm(basis_high, res_high, 0, 0)
    values += mm(basis_high, res_low, 0, 0) + mm(basis_low, res_high, 0, 0)

    point = rows_of((points, lanes), 0)
    for at in range(0, fine, lanes):
        upper = jnp.zeros((1, lanes), jnp.int32)
        inside = []
        for k in range(donors):
            lower = upper
            upper = lower + counts_ref[k : k + 1, at : at + lanes]
            inside.append((point >= lower) & (point < upper))
        for v in range(variables):
            column = v * fine + at
            value = values[:, column : column + lanes]
            masked = [jnp.where(inside[k], value, 0.0) for k in range(donors)]
            pieces = []
            for a in range(modes):
                coarse = coarse_ref[a, :, at : at + lanes]
                terms = [coarse * masked[k] for k in range(donors)]
                pieces.append([add_eights(term) for term in terms])
            whole = modes - modes % 8
            for k in range(donors):
                left = k * fine + at
                for a in range(0, whole, 8):
                    rows = pl.ds(a * variables + v, 8, stride=variables)
                    pair_ref[left // lanes, rows, :] = sum_rows(
                        [pieces[a + r][k] for r in range(8)]
                    )
            rest = [(k, a) for k in range(donors) for a in range(whole, modes)]
            for first in range(0, len(rest), 8):
                group = rest[first : first + 8]
                filled = group + [group[0]] * (8 - len(group))
                sums = sum_rows([pieces[a][k] for k, a in filled])
                for r, (k, a) in enumerate(group):
                    row, left = a * variables + v, k * fine + at
                    pair_ref[left // lanes, row : row + 1, :] = sums[r : r + 1]

    pair = jnp.concatenate([pair_ref[j] for j in range(total // lanes)], axis=1)
    both = jnp.concatenate(split(pair), axis=0)
    lane = rows_of((total, lanes), 1).astype(jnp.int16)
    one, zero = jnp.ones((total, lanes), BF16), jnp.zeros((total, lanes), BF16)
    part = out_ref.shape[2]
    rows = out_ref.shape[1] * part // width
    together = max(1, 256 // width)
    for first in range(0, chunks, together):
        chooser = jnp.concatenate(
            [
                jnp.where(slot == lane + jnp.int16(first * width + j), one, zero)
                for j in range(0, together * width, lanes)
            ],
            axis=1,
        )
        placed = mm(both, chooser)
        placed = placed[:depth] + placed[depth:]
        for c in range(first, first + together):
            for j in range(width // part):
                at = (c - first) * width + j * part
                out_ref[c, j * rows : (j + 1) * rows] = placed[:rows, at : at + part]
            pltpu.make_async_copy(out_ref.at[c], out_hbm.at[c], sems.at[c]).start()
    for c in range(chunks):
        pltpu.make_async_copy(out_ref.at[c], out_hbm.at[c], sems.at[c]).wait()


def seat_kernel(columns_ref, *out_refs, groups, capacity, rows):
    sources = columns_ref.shape[0]
    full, block = out_refs[0].shape[-2:]
    for n, group in enumerate(groups):
        j, at = divmod(group * capacity, columns_ref.shape[2])
        got = jnp.concatenate(
            [
                columns_ref[s, j * rows : j * rows + full + 1, at : at + capacity]
                for s in range(sources)
            ],
            axis=1,
        )
        seat = got[full : full + 1, :]
        chooser = (rows_of((block, got.shape[1]), 0).astype(F32) == seat).astype(F32).astype(BF16)
        high, low = split(got)
        dense = (mm(high, chooser, 1, 1) + mm(low, chooser, 1, 1))[:full]
        if len(out_refs) == len(groups):
            out_refs[n][...] = dense
        else:
            out_refs[0][n] = dense


def renumber_kernel(place_ref, *refs):
    block_refs, out_ref = refs[:-1], refs[-1]
    block = place_ref.shape[1]
    if len(block_refs) == 1:
        total = block_refs[0][0]
        for h in range(1, block_refs[0].shape[0]):
            total += block_refs[0][h]
    else:
        total = block_refs[0][...]
        for ref in block_refs[1:]:
            total += ref[...]
    full = total.shape[0]
    place = place_ref[...]
    chooser = (rows_of((block, block), 0) == place % block).astype(F32).astype(BF16)
    high, low = split(total)
    out_ref[:full, :] = mm(high, chooser, 1, 1) + mm(low, chooser, 1, 1)
    out_ref[full:, :] = (place // block).astype(F32)


def prepare_kernel(after_ref, offset_ref, lift_ref, chooser_ref, lift_out_ref, *, variables, slab):
    del after_ref
    faces, block = offset_ref.shape
    modes = lift_ref.shape[0]
    full = modes * variables
    choose(offset_ref[...], chooser_ref, 0)
    width = variables * faces * slab
    column = rows_of((modes, width), 1)
    mode = rows_of((modes, width), 0)
    spread = jnp.zeros((modes, width), F32)
    for f in range(faces):
        put = (column % slab == mode) & ((column // slab) % faces == f)
        spread += mm(lift_ref[:, f, :], put.astype(F32), 1, 0, lax.Precision.HIGHEST)
    expand = (rows_of((full, modes), 0) // variables == rows_of((full, modes), 1)).astype(F32)
    lifted = mm(expand, spread, 1, 0, lax.Precision.HIGHEST)
    keep = rows_of((full, width), 1) // (slab * faces) == rows_of((full, width), 0) % variables
    high, low = split(jnp.where(keep, lifted, 0.0))
    lift_out_ref[...] = jnp.concatenate([high, high, low], axis=1)


def inner_is_left():
    return lax.axis_index("sub") % 2 == 1


def pack_quarters(pieces, for_left):
    reach = pieces[0].shape[1] // 4
    turned = [pieces[0]] + [pltpu.roll(pieces[g], g * reach, 1) for g in range(1, 4)]
    quarter = rows_of(pieces[0].shape, 1) // reach
    to_left, to_right = turned[0], turned[0]
    for g in range(1, 4):
        to_left = jnp.where(quarter == g, turned[g], to_left)
        to_right = jnp.where(quarter == g - 1, turned[g], to_right)
    return jnp.where(for_left, to_left, to_right)


def take_quarters(inner, outer):
    reach = inner.shape[1] // 4
    quarter = rows_of(inner.shape, 1) // reach
    pieces = []
    for g in range(4):
        piece = jnp.where((quarter == g) != inner_is_left(), inner, outer)
        pieces.append(pltpu.roll(piece, (4 - g) * reach, 1) if g else piece)
    return pieces


def pack_halves(one, two):
    block = one.shape[1]
    turned = pltpu.roll(two, block // 2, 1)
    kept = (rows_of(one.shape, 1) < block // 2) == inner_is_left()
    return jnp.where(kept, one, turned), jnp.where(kept, turned, one)


def take_halves(inner, outer):
    block = inner.shape[1]
    from_inner = (rows_of(inner.shape, 1) >= block // 2) == inner_is_left()
    two = jnp.where(from_inner, outer, inner)
    return jnp.where(from_inner, inner, outer), pltpu.roll(two, block // 2, 1)


def pack_kernel(after_ref, inverse_ref, jacobian_ref, offset_ref, out_ref, lines, *, outer):
    del after_ref
    full, _, block = inverse_ref.shape
    variables, _, faces, _ = jacobian_ref.shape
    for_left = inner_is_left() != outer
    slabs = -(-full // 4)
    for j in range(slabs):
        index = [j + g * slabs for g in range(4)]
        pieces = [inverse_ref[i] if i < full else jnp.zeros((full, block), F32) for i in index]
        out_ref[j * full : (j + 1) * full, :] = pack_quarters(pieces, for_left)
    for w in range(variables):
        for v in range(variables):
            at = (w * variables + v) * faces
            lines[at : at + faces, :] = jacobian_ref[w, v]
    count = lines.shape[0] // 4
    at, last = slabs * full, out_ref.shape[0] - faces
    pieces = [lines[g * count : (g + 1) * count, :] for g in range(4)]
    out_ref[at : at + count, :] = pack_quarters(pieces, for_left)
    out_ref[at + count : last, :] = jnp.zeros((last - at - count, block), F32)
    out_ref[last:, :] = offset_ref[...].astype(F32)


def beside_kernel(inner_ref, outer_ref, inverse_ref, jacobian_ref, chooser_ref, *, faces):
    full, _, block = inverse_ref.shape
    slabs = -(-full // 4)
    for j in range(slabs):
        at = j * full
        pieces = take_quarters(inner_ref[at : at + full, :], outer_ref[at : at + full, :])
        for g, piece in enumerate(pieces):
            if j + g * slabs < full:
                inverse_ref[j + g * slabs] = piece
    count = jacobian_ref.shape[0] // 4
    at = slabs * full
    pieces = take_quarters(inner_ref[at : at + count, :], outer_ref[at : at + count, :])
    for g, piece in enumerate(pieces):
        jacobian_ref[g * count : (g + 1) * count, :] = piece
    last = inner_ref.shape[0] - faces
    inner, outer = inner_ref[last:, :], outer_ref[last:, :]
    from_inner = (rows_of(inner.shape, 1) >= block // 2) == inner_is_left()
    choose(jnp.where(from_inner, inner, outer).astype(jnp.int32), chooser_ref, block)


def choose(offsets, chooser_ref, first):
    faces, block = offsets.shape
    lane = rows_of((1, block), 1) + first
    row = rows_of((2 * block, block), 0)
    for f in range(faces):
        offset = offsets[f : f + 1, :]
        source = jnp.where(offset != 0, (lane + offset) & (2 * block - 1), -1)
        chooser_ref[:, f * block : (f + 1) * block] = (row == source).astype(F32).astype(BF16)


def apply_inverse(inverse_ref, field, variables, depth=None):
    full, _, block = inverse_ref.shape
    modes = full // variables
    zero = jnp.zeros((8, block), F32)

    def piece(row):
        if row >= full:
            return zero
        product = inverse_ref[row % modes * variables + row // modes if depth else row] * field
        partial = product[0:8]
        for j in range(8, full - 7, 8):
            partial += product[j : j + 8]
        rest = full % 8
        if rest:
            partial += jnp.concatenate([product[full - rest :], zero[rest:]], axis=0)
        return partial

    rows = []
    for at in range(0, depth or full, 8):
        rows.append(sum_rows([piece(at + r) for r in range(8)]) if at < full else zero)
    return jnp.concatenate(rows, axis=0)[: depth or full]


def first_kernel(inverse_ref, *refs, subs, variables):
    block_refs, (total_ref, out_ref, inner_ref, outer_ref) = refs[:-4], refs[-4:]
    full = total_ref.shape[0]
    owner = lax.axis_index("high") * lax.axis_size("low") + lax.axis_index("low")
    owner = (owner * subs + lax.axis_index("sub")).astype(F32)
    residual = jnp.zeros(total_ref.shape, F32)
    for ref in block_refs:
        residual += jnp.where(ref[full:, :] == owner, ref[:full, :], 0.0)
    total_ref[...] = residual
    x = apply_inverse(inverse_ref, residual, variables, out_ref.shape[0])
    out_ref[...] = x
    half = inner_ref.shape[0]
    inner_ref[...], outer_ref[...] = pack_halves(x[:half], x[half:])


def sweep_kernel(
    inverse_ref, inverse_beside_ref, residual_ref, x_ref, outer_ref, inner_ref, chooser_ref,
    chooser_beside_ref, lift_ref, jacobian_ref, jacobian_beside_ref, total_ref, out_ref,
    picked_ref, z_ref, *, variables, slab
):
    depth, block = x_ref.shape
    full = residual_ref.shape[0]
    modes = full // variables
    faces = jacobian_ref.shape[2]
    residual = residual_ref[...]
    total_ref[...] = residual
    third = z_ref.shape[0] // 3

    def coupled(x, tiles):
        x = jnp.concatenate(split(x), axis=0)
        for t, ref in enumerate((chooser_ref, chooser_beside_ref)[:tiles]):
            picked = mm(x, ref[...])
            picked_ref[t] = picked[:depth] + picked[depth:]
        for t in range(tiles):
            for f in range(faces):
                at = f * block
                part = [
                    picked_ref[t, v * modes : v * modes + slab, at : at + block]
                    for v in range(variables)
                ]
                for w in range(variables):
                    z = None
                    for v in range(variables):
                        if t:
                            line = (w * variables + v) * faces + f
                            term = part[v] * jacobian_beside_ref[line : line + 1, :]
                        else:
                            term = part[v] * jacobian_ref[w, v, f : f + 1, :]
                        z = z + term if v else term
                    line, column = (w * faces + f) * slab, t * block
                    high, low = split(z)
                    for n, value in enumerate((high, low, high)):
                        at_row = n * third + line
                        z_ref[at_row : at_row + slab, column : column + block] = value
        return mm(lift_ref[...], z_ref[:, : tiles * block])

    first = x_ref[...]
    first_beside = jnp.concatenate(take_halves(inner_ref[...], outer_ref[...]), axis=0)
    taken = coupled(jnp.concatenate([first, first_beside], axis=1), 2)
    second = jnp.concatenate(
        [
            first - apply_inverse(inverse_ref, taken[:, :block], variables, depth),
            first_beside - apply_inverse(inverse_beside_ref, taken[:, block:], variables, depth),
        ],
        axis=1,
    )
    out_ref[...] = apply_inverse(inverse_ref, residual - coupled(second, 1), variables)


def per_device(
    fine_residual,
    fine_basis,
    coarse_basis,
    donor_cells,
    point_counts,
    solver_pos,
    block_inverse,
    face_jacobian,
    face_lift,
    face_offset,
):
    high_count = lax.axis_size("high")
    passing = lax.axis_size("low") * lax.axis_size("sub")
    owners = high_count * passing
    _, variables, fine = fine_residual.shape
    modes = coarse_basis.shape[1]
    donors = donor_cells.shape[1]
    block = solver_pos.shape[0]
    faces = face_offset.shape[0]
    full = modes * variables
    slab = -(-modes // 16) * 16
    depth = -(-full // 16) * 16

    capacity = max(2, 2 * fine * donors // owners)
    few = 1 < high_count <= 8 and high_count & (high_count - 1) == 0
    subs = lax.axis_size("sub")
    counter = call(
        constants_kernel,
        "constants",
        ((128, 256), BF16),
        (),
        cost=pl.CostEstimate(flops=2 * 10**9, bytes_accessed=8 * 10**6, transcendentals=0),
    )
    width = high_count * capacity
    halves = 2 if width > 128 else 1
    rows = -(-(full + 1) // 4) * 4 if halves > 1 else -(-(full + 1) // 8) * 8
    chunk_shape = (passing, halves * rows, width // halves)
    columns = call(
        functools.partial(
            restrict_kernel,
            owners=owners,
            block=block,
            passing=passing,
            subs=subs,
            capacity=capacity,
            few=few,
        ),
        "restrict",
        (chunk_shape, F32),
        (
            counter,
            fine_residual.transpose(1, 0, 2),
            fine_basis.T,
            coarse_basis.transpose(1, 0, 2),
            point_counts.T,
            donor_cells.T,
        ),
        [
            pltpu.VMEM((donors * fine // 128, depth, 128), F32),
            pltpu.VMEM(chunk_shape, F32),
            pltpu.SemaphoreType.DMA((passing,)),
        ],
        megabytes=16,
        out_spec=pl.BlockSpec(memory_space=pl.ANY),
    )
    columns = lax.all_to_all(columns, PLANE, 0, 0, tiled=True)
    def seat(name, groups, shapes):
        return call(
            functools.partial(seat_kernel, groups=groups, capacity=capacity, rows=rows),
            name,
            shapes,
            (columns,),
            megabytes=24,
        )

    dense = ((full, block), F32)
    if few:
        count = high_count // 2
        near = seat("seat_near", range(count), [dense] * count)
        rest = [seat("seat_far", [d], [dense])[0] for d in range(count, high_count)]
        blocks = swap_all([*near, *rest], "high")
    else:
        blocks = seat("seat_all", range(high_count), ((high_count, full, block), F32))
        blocks = [lax.all_to_all(blocks, "high", 0, 0, tiled=True)]
    whole = call(
        renumber_kernel, "renumber", ((full + 1, block), F32), (solver_pos[None, :], *blocks)
    )
    blocks = swap_all([whole] * subs, "sub")

    jacobian = face_jacobian.transpose(1, 2, 0, 3)
    chooser, lift = call(
        functools.partial(prepare_kernel, variables=variables, slab=slab),
        "prepare",
        [((2 * block, faces * block), BF16), ((full, 3 * variables * faces * slab), BF16)],
        (counter, face_offset, face_lift.transpose(1, 0, 2)),
    )
    outer_pairs = [(i, i + 1) for i in range(1, owners - 1, 2)]
    outer_pairs += [(j, i) for i, j in outer_pairs]
    inner_pairs = [(i, i ^ 1) for i in range(owners)]
    lines = variables * variables * faces
    packed = ((-(-(-(-full // 4) * full + lines // 4 + faces + 1) // 8) * 8, block), F32)
    packs = []
    for outer in (False, True):
        packs.append(
            call(
                functools.partial(pack_kernel, outer=outer),
                "pack_outer" if outer else "pack_inner",
                packed,
                (packs[0] if outer else lift, block_inverse, jacobian, face_offset),
                [pltpu.VMEM((lines, block), F32)],
            )
        )
    inner = lax.ppermute(packs[0], WHOLE, inner_pairs)
    outer = lax.ppermute(packs[1], WHOLE, outer_pairs)
    inverse_beside, jacobian_beside, chooser_beside = call(
        functools.partial(beside_kernel, faces=faces),
        "beside",
        [((full, full, block), F32), ((lines, block), F32), ((2 * block, faces * block), BF16)],
        (inner, outer),
    )
    plain, edge = ((full, block), F32), ((depth // 2, block), F32)
    residual, x, to_inner, to_outer = call(
        functools.partial(first_kernel, subs=subs, variables=variables),
        "first",
        [plain, ((depth, block), F32), edge, edge],
        (block_inverse, *blocks),
    )
    outer = lax.ppermute(to_outer, WHOLE, outer_pairs)
    inner = lax.ppermute(to_inner, WHOLE, inner_pairs)
    return tuple(
        call(
            functools.partial(sweep_kernel, variables=variables, slab=slab),
            "sweeps",
            [plain, plain],
            (
                block_inverse,
                inverse_beside,
                residual,
                x,
                outer,
                inner,
                chooser,
                chooser_beside,
                lift,
                jacobian,
                jacobian_beside,
            ),
            [pltpu.VMEM((2, depth, faces * block), F32)]
            + [pltpu.VMEM((3 * variables * faces * slab, 2 * block), BF16)],
        )
    )


def solution(mesh):
    dom, sub = mesh.devices.shape
    low = next(count for count in (4, 2, 1) if dom % count == 0)
    split_mesh = jax.sharding.Mesh(mesh.devices.reshape(dom // low, low, sub), WHOLE)
    in_specs = (
        P(None, None, WHOLE),
        P(),
        P(None, None, WHOLE),
        P(WHOLE, None),
        P(WHOLE, None),
        P(WHOLE),
        P(None, None, WHOLE),
        P(None, None, None, WHOLE),
        P(),
        P(None, WHOLE),
    )
    return jax.shard_map(
        per_device,
        mesh=split_mesh,
        in_specs=in_specs,
        out_specs=(P(None, WHOLE), P(None, WHOLE)),
        check_vma=False,
    )
```

```python
import functools
import jax
import jax.numpy as jnp
from jax import lax
from jax.experimental import pallas as pl
from jax.experimental.pallas import tpu as pltpu
from jax.sharding import PartitionSpec as P

F32 = jnp.float32
BF16 = jnp.bfloat16
PLANE = ("sub", "low")
WHOLE = ("high", "low", "sub")
VMEM = pl.BlockSpec(memory_space=pltpu.VMEM)


def split(x):
    high = x.astype(BF16)
    return high, (x - high.astype(F32)).astype(BF16)


def stack(x):
    high = x.astype(BF16).astype(F32)
    return jnp.concatenate([high, x - high], axis=0).astype(BF16)


def unstack(x):
    return x[: x.shape[0] // 2] + x[x.shape[0] // 2 :]


def mm(a, b, ca=1, cb=0, precision=None):
    return lax.dot_general(
        a, b, (((ca,), (cb,)), ((), ())), precision=precision, preferred_element_type=F32
    )


def rows_of(iota_shape, dim):
    return lax.broadcasted_iota(jnp.int32, iota_shape, dim)


def call(kernel, name, shapes, args, scratch=(), megabytes=8, cost=None, out_spec=VMEM):
    single = not isinstance(shapes, list)
    out = [jax.ShapeDtypeStruct(*shape) for shape in ([shapes] if single else shapes)]
    result = pl.pallas_call(
        kernel,
        out_shape=out,
        in_specs=[VMEM] * len(args),
        out_specs=[out_spec] * len(out),
        scratch_shapes=list(scratch),
        compiler_params=pltpu.CompilerParams(vmem_limit_bytes=megabytes * 2**20),
        cost_estimate=cost,
        name=name,
    )(*args)
    return result[0] if single else result


def swap_all(blocks, axis):
    count = len(blocks)
    return [blocks[0]] + [
        lax.ppermute(blocks[d], axis, [(i, i ^ d) for i in range(count)])
        for d in range(count - 1, 0, -1)
    ]


def constants_kernel(counter_ref):
    lanes = counter_ref.shape[0]
    earlier = (rows_of((lanes, lanes), 0) < rows_of((lanes, lanes), 1)).astype(F32)
    counter = jnp.concatenate([earlier, jnp.ones((lanes, lanes), F32)], axis=1)
    counter_ref[...] = counter.astype(BF16)


def free_columns(owner, counter, owners, passing, subs, capacity, width, high):
    lanes = 128
    total = owner.shape[1]
    parts = total // lanes
    mine = (rows_of((owners, total), 0) == owner).astype(F32)
    stacked = jnp.concatenate([mine[:, j * lanes : (j + 1) * lanes] for j in range(parts)], axis=0)
    counted = mm(stacked.astype(BF16), counter)
    before = jnp.zeros((owners, lanes), F32)
    ranks = []
    for j in range(parts):
        own = mine[:, j * lanes : (j + 1) * lanes]
        part = counted[j * owners : (j + 1) * owners]
        ranks.append(jnp.sum(own * (before + part[:, :lanes]), axis=0, keepdims=True))
        before += part[:, lanes:]
    rank = jnp.concatenate(ranks, axis=1).astype(jnp.int32)
    lows = passing // subs
    chunk = owner % subs * lows + owner // subs % lows
    return chunk * width + (owner // passing ^ high) * capacity + rank


def add_eights(x):
    total = x[0:8]
    for j in range(8, x.shape[0], 8):
        total += x[j : j + 8]
    return total


def sum_rows(pieces):
    row = rows_of(pieces[0].shape, 0)
    pieces = [pieces[k] for k in (3, 2, 1, 0, 7, 6, 5, 4)]
    upper = row < 4
    halves = []
    for one, two in zip(pieces[:4], pieces[4:]):
        kept, moved = jnp.where(upper, one, two), jnp.where(upper, two, one)
        halves.append(kept + pltpu.roll(moved, 4, 0))
    for shift in (2, 1):
        pairs = list(zip(halves[:shift], halves[shift:]))
        halves = [
            jnp.where(
                row & shift != 0, one + pltpu.roll(one, shift, 0), two + pltpu.roll(two, 8 - shift, 0)
            )
            for one, two in pairs
        ]
    return halves[0]


def restrict_kernel(
    counter_ref, res_ref, basis_ref, coarse_ref, counts_ref, donors_ref, out_hbm, pair_ref, out_ref, sems,
    *, owners, block, passing, subs, capacity, few
):
    variables, _, fine = res_ref.shape
    modes, points, _ = coarse_ref.shape
    donors = counts_ref.shape[0]
    chunks = out_ref.shape[0]
    full = modes * variables
    depth = pair_ref.shape[1]
    total = donors * fine
    lanes = 128
    width = owners // passing * capacity

    cell = jnp.concatenate([donors_ref[k : k + 1, :] for k in range(donors)], axis=1)
    seat = (cell % block).astype(F32)
    for j in range(total // lanes):
        pair_ref[j, full:, :] = jnp.zeros((depth - full, lanes), F32)
        pair_ref[j, full : full + 1, :] = seat[:, j * lanes : (j + 1) * lanes]
    high = lax.axis_index("high") if few else 0
    owner = cell // block
    slot = free_columns(owner, counter_ref[...], owners, passing, subs, capacity, width, high)
    slot = jnp.broadcast_to(slot.astype(F32), (lanes, total)).T.astype(jnp.int32).astype(jnp.int16)

    basis_high, basis_low = split(basis_ref[...])
    res_high, res_low = split(jnp.concatenate([res_ref[v] for v in range(variables)], axis=1))
    values = mm(basis_high, res_high, 0, 0)
    values += mm(basis_high, res_low, 0, 0) + mm(basis_low, res_high, 0, 0)

    point = rows_of((points, lanes), 0)
    for at in range(0, fine, lanes):
        upper = jnp.zeros((1, lanes), jnp.int32)
        inside = []
        for k in range(donors):
            lower = upper
            upper = lower + counts_ref[k : k + 1, at : at + lanes]
            inside.append((point >= lower) & (point < upper))
        for v in range(variables):
            column = v * fine + at
            value = values[:, column : column + lanes]
            masked = [jnp.where(inside[k], value, 0.0) for k in range(donors)]
            pieces = []
            for a in range(modes):
                coarse = coarse_ref[a, :, at : at + lanes]
                terms = [coarse * masked[k] for k in range(donors)]
                pieces.append([add_eights(term) for term in terms])
            whole = modes - modes % 8
            for k in range(donors):
                left = k * fine + at
                for a in range(0, whole, 8):
                    rows = pl.ds(a * variables + v, 8, stride=variables)
                    pair_ref[left // lanes, rows, :] = sum_rows(
                        [pieces[a + r][k] for r in range(8)]
                    )
            rest = [(k, a) for k in range(donors) for a in range(whole, modes)]
            for first in range(0, len(rest), 8):
                group = rest[first : first + 8]
                filled = group + [group[0]] * (8 - len(group))
                sums = sum_rows([pieces[a][k] for k, a in filled])
                for r, (k, a) in enumerate(group):
                    row, left = a * variables + v, k * fine + at
                    pair_ref[left // lanes, row : row + 1, :] = sums[r : r + 1]

    pair = jnp.concatenate([pair_ref[j] for j in range(total // lanes)], axis=1)
    both = stack(pair)
    lane = rows_of((total, lanes), 1).astype(jnp.int16)
    one, zero = jnp.ones((total, lanes), BF16), jnp.zeros((total, lanes), BF16)
    part = out_ref.shape[2]
    rows = out_ref.shape[1] * part // width
    together = max(1, 256 // width)
    for first in range(0, chunks, together):
        chooser = jnp.concatenate(
            [
                jnp.where(slot == lane + jnp.int16(first * width + j), one, zero)
                for j in range(0, together * width, lanes)
            ],
            axis=1,
        )
        placed = unstack(mm(both, chooser))
        for c in range(first, first + together):
            for j in range(width // part):
                at = (c - first) * width + j * part
                out_ref[c, j * rows : (j + 1) * rows] = placed[:rows, at : at + part]
            pltpu.make_async_copy(out_ref.at[c], out_hbm.at[c], sems.at[c]).start()
    for c in range(chunks):
        pltpu.make_async_copy(out_ref.at[c], out_hbm.at[c], sems.at[c]).wait()


def seat_kernel(columns_ref, *out_refs, groups, capacity, rows, full):
    sources = columns_ref.shape[0]
    block = out_refs[0].shape[-1]
    for n, group in enumerate(groups):
        j, at = divmod(group * capacity, columns_ref.shape[2])
        got = jnp.concatenate(
            [
                columns_ref[s, j * rows : (j + 1) * rows, at : at + capacity]
                for s in range(sources)
            ],
            axis=1,
        )
        seat = got[full : full + 1, :]
        chooser = (rows_of((block, got.shape[1]), 0).astype(F32) == seat).astype(F32).astype(BF16)
        dense = unstack(mm(stack(got), chooser, 1, 1))
        if len(out_refs) == len(groups):
            out_refs[n][...] = dense
        else:
            out_refs[0][n] = dense


def renumber_kernel(place_ref, *refs):
    block_refs, out_ref = refs[:-1], refs[-1]
    block = place_ref.shape[1]
    if len(block_refs) == 1:
        total = block_refs[0][0]
        for h in range(1, block_refs[0].shape[0]):
            total += block_refs[0][h]
    else:
        total = block_refs[0][...]
        for ref in block_refs[1:]:
            total += ref[...]
    full = out_ref.shape[0] - 1
    place = place_ref[...]
    chooser = (rows_of((block, block), 0) == place % block).astype(F32).astype(BF16)
    out_ref[:full, :] = unstack(mm(stack(total), chooser, 1, 1))[:full]
    out_ref[full:, :] = (place // block).astype(F32)


def prepare_kernel(after_ref, offset_ref, lift_ref, chooser_ref, lift_out_ref, *, variables, slab):
    del after_ref
    faces, block = offset_ref.shape
    modes = lift_ref.shape[0]
    full = modes * variables
    choose(offset_ref[...], chooser_ref, 0)
    width = variables * faces * slab
    column = rows_of((modes, width), 1)
    mode = rows_of((modes, width), 0)
    spread = jnp.zeros((modes, width), F32)
    for f in range(faces):
        put = (column % slab == mode) & ((column // slab) % faces == f)
        spread += mm(lift_ref[:, f, :], put.astype(F32), 1, 0, lax.Precision.HIGHEST)
    expand = (rows_of((full, modes), 0) // variables == rows_of((full, modes), 1)).astype(F32)
    lifted = mm(expand, spread, 1, 0, lax.Precision.HIGHEST)
    keep = rows_of((full, width), 1) // (slab * faces) == rows_of((full, width), 0) % variables
    high, low = split(jnp.where(keep, lifted, 0.0))
    lift_out_ref[...] = jnp.concatenate([high, high, low], axis=1)


def inner_is_left():
    return lax.axis_index("sub") % 2 == 1


def pack_quarters(pieces, for_left):
    reach = pieces[0].shape[1] // 4
    turned = [pieces[0]] + [pltpu.roll(pieces[g], g * reach, 1) for g in range(1, 4)]
    quarter = rows_of(pieces[0].shape, 1) // reach
    to_left, to_right = turned[0], turned[0]
    for g in range(1, 4):
        to_left = jnp.where(quarter == g, turned[g], to_left)
        to_right = jnp.where(quarter == g - 1, turned[g], to_right)
    return jnp.where(for_left, to_left, to_right)


def take_quarters(inner, outer):
    reach = inner.shape[1] // 4
    quarter = rows_of(inner.shape, 1) // reach
    pieces = []
    for g in range(4):
        piece = jnp.where((quarter == g) != inner_is_left(), inner, outer)
        pieces.append(pltpu.roll(piece, (4 - g) * reach, 1) if g else piece)
    return pieces


def pack_halves(one, two):
    block = one.shape[1]
    turned = pltpu.roll(two, block // 2, 1)
    kept = (rows_of(one.shape, 1) < block // 2) == inner_is_left()
    return jnp.where(kept, one, turned), jnp.where(kept, turned, one)


def take_halves(inner, outer):
    block = inner.shape[1]
    from_inner = (rows_of(inner.shape, 1) >= block // 2) == inner_is_left()
    two = jnp.where(from_inner, outer, inner)
    return jnp.where(from_inner, inner, outer), pltpu.roll(two, block // 2, 1)


def pack_kernel(after_ref, inverse_ref, jacobian_ref, offset_ref, out_ref, lines, *, outer):
    del after_ref
    full, _, block = inverse_ref.shape
    variables, _, faces, _ = jacobian_ref.shape
    for_left = inner_is_left() != outer
    slabs = -(-full // 4)
    for j in range(slabs):
        index = [j + g * slabs for g in range(4)]
        pieces = [inverse_ref[i] if i < full else jnp.zeros((full, block), F32) for i in index]
        out_ref[j * full : (j + 1) * full, :] = pack_quarters(pieces, for_left)
    for w in range(variables):
        for v in range(variables):
            at = (w * variables + v) * faces
            lines[at : at + faces, :] = jacobian_ref[w, v]
    count = lines.shape[0] // 4
    at, last = slabs * full, out_ref.shape[0] - faces
    pieces = [lines[g * count : (g + 1) * count, :] for g in range(4)]
    out_ref[at : at + count, :] = pack_quarters(pieces, for_left)
    out_ref[at + count : last, :] = jnp.zeros((last - at - count, block), F32)
    out_ref[last:, :] = offset_ref[...].astype(F32)


def beside_kernel(inner_ref, outer_ref, inverse_ref, jacobian_ref, chooser_ref, *, faces):
    full, _, block = inverse_ref.shape
    slabs = -(-full // 4)
    for j in range(slabs):
        at = j * full
        pieces = take_quarters(inner_ref[at : at + full, :], outer_ref[at : at + full, :])
        for g, piece in enumerate(pieces):
            if j + g * slabs < full:
                inverse_ref[j + g * slabs] = piece
    count = jacobian_ref.shape[0] // 4
    at = slabs * full
    pieces = take_quarters(inner_ref[at : at + count, :], outer_ref[at : at + count, :])
    for g, piece in enumerate(pieces):
        jacobian_ref[g * count : (g + 1) * count, :] = piece
    last = inner_ref.shape[0] - faces
    inner, outer = inner_ref[last:, :], outer_ref[last:, :]
    from_inner = (rows_of(inner.shape, 1) >= block // 2) == inner_is_left()
    choose(jnp.where(from_inner, inner, outer).astype(jnp.int32), chooser_ref, block)


def choose(offsets, chooser_ref, first):
    faces, block = offsets.shape
    lane = rows_of((1, block), 1) + first
    row = rows_of((2 * block, block), 0)
    for f in range(faces):
        offset = offsets[f : f + 1, :]
        source = jnp.where(offset != 0, (lane + offset) & (2 * block - 1), -1)
        chooser_ref[:, f * block : (f + 1) * block] = (row == source).astype(F32).astype(BF16)


def apply_inverse(inverse_ref, field, variables, depth=None):
    full, _, block = inverse_ref.shape
    modes = full // variables
    zero = jnp.zeros((8, block), F32)

    def piece(row):
        if row >= full:
            return zero
        product = inverse_ref[row % modes * variables + row // modes if depth else row] * field
        partial = product[0:8]
        for j in range(8, full - 7, 8):
            partial += product[j : j + 8]
        rest = full % 8
        if rest:
            partial += jnp.concatenate([product[full - rest :], zero[rest:]], axis=0)
        return partial

    rows = []
    for at in range(0, depth or full, 8):
        rows.append(sum_rows([piece(at + r) for r in range(8)]) if at < full else zero)
    return jnp.concatenate(rows, axis=0)[: depth or full]


def first_kernel(inverse_ref, *refs, subs, variables):
    block_refs, (total_ref, out_ref, inner_ref, outer_ref) = refs[:-4], refs[-4:]
    full = total_ref.shape[0]
    owner = lax.axis_index("high") * lax.axis_size("low") + lax.axis_index("low")
    owner = (owner * subs + lax.axis_index("sub")).astype(F32)
    residual = jnp.zeros(total_ref.shape, F32)
    for ref in block_refs:
        residual += jnp.where(ref[full:, :] == owner, ref[:full, :], 0.0)
    total_ref[...] = residual
    x = apply_inverse(inverse_ref, residual, variables, out_ref.shape[0])
    out_ref[...] = x
    half = inner_ref.shape[0]
    inner_ref[...], outer_ref[...] = pack_halves(x[:half], x[half:])


def sweep_kernel(
    inverse_ref, inverse_beside_ref, residual_ref, x_ref, outer_ref, inner_ref, chooser_ref,
    chooser_beside_ref, lift_ref, jacobian_ref, jacobian_beside_ref, total_ref, out_ref,
    picked_ref, z_ref, *, variables, slab
):
    depth, block = x_ref.shape
    full = residual_ref.shape[0]
    modes = full // variables
    faces = jacobian_ref.shape[2]
    residual = residual_ref[...]
    total_ref[...] = residual
    third = z_ref.shape[0] // 3

    def coupled(x, tiles):
        x = jnp.concatenate(split(x), axis=0)
        for t, ref in enumerate((chooser_ref, chooser_beside_ref)[:tiles]):
            picked = mm(x, ref[...])
            picked_ref[t] = picked[:depth] + picked[depth:]
        for t in range(tiles):
            for f in range(faces):
                at = f * block
                part = [
                    picked_ref[t, v * modes : v * modes + slab, at : at + block]
                    for v in range(variables)
                ]
                for w in range(variables):
                    z = None
                    for v in range(variables):
                        if t:
                            line = (w * variables + v) * faces + f
                            term = part[v] * jacobian_beside_ref[line : line + 1, :]
                        else:
                            term = part[v] * jacobian_ref[w, v, f : f + 1, :]
                        z = z + term if v else term
                    line, column = (w * faces + f) * slab, t * block
                    high, low = split(z)
                    for n, value in enumerate((high, low, high)):
                        at_row = n * third + line
                        z_ref[at_row : at_row + slab, column : column + block] = value
        return mm(lift_ref[...], z_ref[:, : tiles * block])

    first = x_ref[...]
    first_beside = jnp.concatenate(take_halves(inner_ref[...], outer_ref[...]), axis=0)
    taken = coupled(jnp.concatenate([first, first_beside], axis=1), 2)
    second = jnp.concatenate(
        [
            first - apply_inverse(inverse_ref, taken[:, :block], variables, depth),
            first_beside - apply_inverse(inverse_beside_ref, taken[:, block:], variables, depth),
        ],
        axis=1,
    )
    out_ref[...] = apply_inverse(inverse_ref, residual - coupled(second, 1), variables)


def per_device(
    fine_residual,
    fine_basis,
    coarse_basis,
    donor_cells,
    point_counts,
    solver_pos,
    block_inverse,
    face_jacobian,
    face_lift,
    face_offset,
):
    high_count = lax.axis_size("high")
    passing = lax.axis_size("low") * lax.axis_size("sub")
    owners = high_count * passing
    _, variables, fine = fine_residual.shape
    modes = coarse_basis.shape[1]
    donors = donor_cells.shape[1]
    block = solver_pos.shape[0]
    faces = face_offset.shape[0]
    full = modes * variables
    slab = -(-modes // 16) * 16
    depth = -(-full // 16) * 16

    capacity = max(2, 2 * fine * donors // owners)
    few = 1 < high_count <= 8 and high_count & (high_count - 1) == 0
    subs = lax.axis_size("sub")
    counter = call(
        constants_kernel,
        "constants",
        ((128, 256), BF16),
        (),
        cost=pl.CostEstimate(flops=2 * 10**9, bytes_accessed=8 * 10**6, transcendentals=0),
    )
    width = high_count * capacity
    halves = 2 if width > 128 else 1
    rows = -(-(full + 1) // 4) * 4 if halves > 1 else -(-(full + 1) // 8) * 8
    chunk_shape = (passing, halves * rows, width // halves)
    columns = call(
        functools.partial(
            restrict_kernel,
            owners=owners,
            block=block,
            passing=passing,
            subs=subs,
            capacity=capacity,
            few=few,
        ),
        "restrict",
        (chunk_shape, F32),
        (
            counter,
            fine_residual.transpose(1, 0, 2),
            fine_basis.T,
            coarse_basis.transpose(1, 0, 2),
            point_counts.T,
            donor_cells.T,
        ),
        [
            pltpu.VMEM((donors * fine // 128, -(-(full + 1) // 8) * 8, 128), F32),
            pltpu.VMEM(chunk_shape, F32),
            pltpu.SemaphoreType.DMA((passing,)),
        ],
        megabytes=16,
        out_spec=pl.BlockSpec(memory_space=pl.ANY),
    )
    columns = lax.all_to_all(columns, PLANE, 0, 0, tiled=True)
    def seat(name, groups, shapes):
        return call(
            functools.partial(
                seat_kernel, groups=groups, capacity=capacity, rows=rows, full=full
            ),
            name,
            shapes,
            (columns,),
            megabytes=24,
        )

    dense = ((rows, block), F32)
    if few:
        count = high_count // 2
        near = seat("seat_near", range(count), [dense] * count)
        rest = [seat("seat_far", [d], [dense])[0] for d in range(count, high_count)]
        blocks = swap_all([*near, *rest], "high")
    else:
        blocks = seat("seat_all", range(high_count), ((high_count, rows, block), F32))
        blocks = [lax.all_to_all(blocks, "high", 0, 0, tiled=True)]
    whole = call(
        renumber_kernel, "renumber", ((full + 1, block), F32), (solver_pos[None, :], *blocks)
    )
    blocks = swap_all([whole] * subs, "sub")

    jacobian = face_jacobian.transpose(1, 2, 0, 3)
    chooser, lift = call(
        functools.partial(prepare_kernel, variables=variables, slab=slab),
        "prepare",
        [((2 * block, faces * block), BF16), ((full, 3 * variables * faces * slab), BF16)],
        (counter, face_offset, face_lift.transpose(1, 0, 2)),
    )
    outer_pairs = [(i, i + 1) for i in range(1, owners - 1, 2)]
    outer_pairs += [(j, i) for i, j in outer_pairs]
    inner_pairs = [(i, i ^ 1) for i in range(owners)]
    lines = variables * variables * faces
    packed = ((-(-(-(-full // 4) * full + lines // 4 + faces + 1) // 8) * 8, block), F32)
    packs = []
    for outer in (False, True):
        packs.append(
            call(
                functools.partial(pack_kernel, outer=outer),
                "pack_outer" if outer else "pack_inner",
                packed,
                (packs[0] if outer else lift, block_inverse, jacobian, face_offset),
                [pltpu.VMEM((lines, block), F32)],
            )
        )
    inner = lax.ppermute(packs[0], WHOLE, inner_pairs)
    outer = lax.ppermute(packs[1], WHOLE, outer_pairs)
    inverse_beside, jacobian_beside, chooser_beside = call(
        functools.partial(beside_kernel, faces=faces),
        "beside",
        [((full, full, block), F32), ((lines, block), F32), ((2 * block, faces * block), BF16)],
        (inner, outer),
    )
    plain, edge = ((full, block), F32), ((depth // 2, block), F32)
    residual, x, to_inner, to_outer = call(
        functools.partial(first_kernel, subs=subs, variables=variables),
        "first",
        [plain, ((depth, block), F32), edge, edge],
        (block_inverse, *blocks),
    )
    outer = lax.ppermute(to_outer, WHOLE, outer_pairs)
    inner = lax.ppermute(to_inner, WHOLE, inner_pairs)
    return tuple(
        call(
            functools.partial(sweep_kernel, variables=variables, slab=slab),
            "sweeps",
            [plain, plain],
            (
                block_inverse,
                inverse_beside,
                residual,
                x,
                outer,
                inner,
                chooser,
                chooser_beside,
                lift,
                jacobian,
                jacobian_beside,
            ),
            [pltpu.VMEM((2, depth, faces * block), F32)]
            + [pltpu.VMEM((3 * variables * faces * slab, 2 * block), BF16)],
        )
    )


def solution(mesh):
    dom, sub = mesh.devices.shape
    low = next(count for count in (4, 2, 1) if dom % count == 0)
    split_mesh = jax.sharding.Mesh(mesh.devices.reshape(dom // low, low, sub), WHOLE)
    in_specs = (
        P(None, None, WHOLE),
        P(),
        P(None, None, WHOLE),
        P(WHOLE, None),
        P(WHOLE, None),
        P(WHOLE),
        P(None, None, WHOLE),
        P(None, None, None, WHOLE),
        P(),
        P(None, WHOLE),
    )
    return jax.shard_map(
        per_device,
        mesh=split_mesh,
        in_specs=in_specs,
        out_specs=(P(None, WHOLE), P(None, WHOLE)),
        check_vma=False,
    )
```

```python
import functools
import jax
import jax.numpy as jnp
from jax import lax
from jax.experimental import pallas as pl
from jax.experimental.pallas import tpu as pltpu
from jax.sharding import PartitionSpec as P

F32 = jnp.float32
BF16 = jnp.bfloat16
PLANE = ("sub", "low")
WHOLE = ("high", "low", "sub")
VMEM = pl.BlockSpec(memory_space=pltpu.VMEM)


def split(x):
    high = x.astype(BF16)
    return high, (x - high.astype(F32)).astype(BF16)


def stack(x):
    high = x.astype(BF16).astype(F32)
    return jnp.concatenate([high, x - high], axis=0).astype(BF16)


def unstack(x):
    return x[: x.shape[0] // 2] + x[x.shape[0] // 2 :]


def mm(a, b, ca=1, cb=0, precision=None):
    return lax.dot_general(
        a, b, (((ca,), (cb,)), ((), ())), precision=precision, preferred_element_type=F32
    )


def rows_of(iota_shape, dim):
    return lax.broadcasted_iota(jnp.int32, iota_shape, dim)


def call(kernel, name, shapes, args, scratch=(), megabytes=8, cost=None, out_spec=VMEM):
    single = not isinstance(shapes, list)
    out = [jax.ShapeDtypeStruct(*shape) for shape in ([shapes] if single else shapes)]
    result = pl.pallas_call(
        kernel,
        out_shape=out,
        in_specs=[VMEM] * len(args),
        out_specs=[out_spec] * len(out),
        scratch_shapes=list(scratch),
        compiler_params=pltpu.CompilerParams(vmem_limit_bytes=megabytes * 2**20),
        cost_estimate=cost,
        name=name,
    )(*args)
    return result[0] if single else result


def swap_all(blocks, axis):
    count = len(blocks)
    return [blocks[0]] + [
        lax.ppermute(blocks[d], axis, [(i, i ^ d) for i in range(count)])
        for d in range(count - 1, 0, -1)
    ]


def constants_kernel(counter_ref):
    lanes = counter_ref.shape[0]
    earlier = (rows_of((lanes, lanes), 0) < rows_of((lanes, lanes), 1)).astype(F32)
    counter = jnp.concatenate([earlier, jnp.ones((lanes, lanes), F32)], axis=1)
    counter_ref[...] = counter.astype(BF16)


def free_columns(owner, counter, owners, passing, subs, capacity, width, high):
    lanes = 128
    total = owner.shape[1]
    parts = total // lanes
    mine = (rows_of((owners, total), 0) == owner).astype(F32)
    stacked = jnp.concatenate([mine[:, j * lanes : (j + 1) * lanes] for j in range(parts)], axis=0)
    counted = mm(stacked.astype(BF16), counter)
    before = jnp.zeros((owners, lanes), F32)
    ranks = []
    for j in range(parts):
        own = mine[:, j * lanes : (j + 1) * lanes]
        part = counted[j * owners : (j + 1) * owners]
        ranks.append(jnp.sum(own * (before + part[:, :lanes]), axis=0, keepdims=True))
        before += part[:, lanes:]
    rank = jnp.concatenate(ranks, axis=1).astype(jnp.int32)
    lows = passing // subs
    chunk = owner % subs * lows + owner // subs % lows
    return chunk * width + (owner // passing ^ high) * capacity + rank


def add_eights(x):
    total = x[0:8]
    for j in range(8, x.shape[0], 8):
        total += x[j : j + 8]
    return total


def sum_rows(pieces):
    row = rows_of(pieces[0].shape, 0)
    pieces = [pieces[k] for k in (3, 2, 1, 0, 7, 6, 5, 4)]
    upper = row < 4
    halves = []
    for one, two in zip(pieces[:4], pieces[4:]):
        kept, moved = jnp.where(upper, one, two), jnp.where(upper, two, one)
        halves.append(kept + pltpu.roll(moved, 4, 0))
    for shift in (2, 1):
        pairs = list(zip(halves[:shift], halves[shift:]))
        halves = [
            jnp.where(
                row & shift != 0, one + pltpu.roll(one, shift, 0), two + pltpu.roll(two, 8 - shift, 0)
            )
            for one, two in pairs
        ]
    return halves[0]


def restrict_kernel(
    counter_ref, res_ref, basis_ref, coarse_ref, counts_ref, donors_ref, out_hbm, pair_ref, out_ref, sems,
    *, owners, block, passing, subs, capacity, few
):
    variables, _, fine = res_ref.shape
    modes, points, _ = coarse_ref.shape
    donors = counts_ref.shape[0]
    chunks = out_ref.shape[0]
    full = modes * variables
    depth = pair_ref.shape[1]
    total = donors * fine
    lanes = 128
    width = owners // passing * capacity

    cell = jnp.concatenate([donors_ref[k : k + 1, :] for k in range(donors)], axis=1)
    seat = (cell % block).astype(F32)
    for j in range(total // lanes):
        pair_ref[j, full:, :] = jnp.zeros((depth - full, lanes), F32)
        pair_ref[j, full : full + 1, :] = seat[:, j * lanes : (j + 1) * lanes]
    high = lax.axis_index("high") if few else 0
    owner = cell // block
    slot = free_columns(owner, counter_ref[...], owners, passing, subs, capacity, width, high)
    slot = jnp.broadcast_to(slot.astype(F32), (lanes, total)).T.astype(jnp.int32).astype(jnp.int16)

    basis_high, basis_low = split(basis_ref[...])
    res_high, res_low = split(jnp.concatenate([res_ref[v] for v in range(variables)], axis=1))
    values = mm(basis_high, res_high, 0, 0)
    values += mm(basis_high, res_low, 0, 0) + mm(basis_low, res_high, 0, 0)

    point = rows_of((points, lanes), 0)
    for at in range(0, fine, lanes):
        upper = jnp.zeros((1, lanes), jnp.int32)
        inside = []
        for k in range(donors):
            lower = upper
            upper = lower + counts_ref[k : k + 1, at : at + lanes]
            inside.append((point >= lower) & (point < upper))
        for v in range(variables):
            column = v * fine + at
            value = values[:, column : column + lanes]
            masked = [jnp.where(inside[k], value, 0.0) for k in range(donors)]
            pieces = []
            for a in range(modes):
                coarse = coarse_ref[a, :, at : at + lanes]
                terms = [coarse * masked[k] for k in range(donors)]
                pieces.append([add_eights(term) for term in terms])
            whole = modes - modes % 8
            for k in range(donors):
                left = k * fine + at
                for a in range(0, whole, 8):
                    rows = pl.ds(a * variables + v, 8, stride=variables)
                    pair_ref[left // lanes, rows, :] = sum_rows(
                        [pieces[a + r][k] for r in range(8)]
                    )
            rest = [(k, a) for k in range(donors) for a in range(whole, modes)]
            for first in range(0, len(rest), 8):
                group = rest[first : first + 8]
                filled = group + [group[0]] * (8 - len(group))
                sums = sum_rows([pieces[a][k] for k, a in filled])
                for r, (k, a) in enumerate(group):
                    row, left = a * variables + v, k * fine + at
                    pair_ref[left // lanes, row : row + 1, :] = sums[r : r + 1]

    pair = jnp.concatenate([pair_ref[j] for j in range(total // lanes)], axis=1)
    both = stack(pair)
    lane = rows_of((total, lanes), 1).astype(jnp.int16)
    one, zero = jnp.ones((total, lanes), BF16), jnp.zeros((total, lanes), BF16)
    part = out_ref.shape[2]
    rows = out_ref.shape[1] * part // width
    together = max(1, 256 // width)
    for first in range(0, chunks, together):
        chooser = jnp.concatenate(
            [
                jnp.where(slot == lane + jnp.int16(first * width + j), one, zero)
                for j in range(0, together * width, lanes)
            ],
            axis=1,
        )
        placed = unstack(mm(both, chooser))
        for c in range(first, first + together):
            for j in range(width // part):
                at = (c - first) * width + j * part
                out_ref[c, j * rows : (j + 1) * rows] = placed[:rows, at : at + part]
            pltpu.make_async_copy(out_ref.at[c], out_hbm.at[c], sems.at[c]).start()
    for c in range(chunks):
        pltpu.make_async_copy(out_ref.at[c], out_hbm.at[c], sems.at[c]).wait()


def seat_kernel(columns_ref, *out_refs, groups, capacity, rows, full):
    sources = columns_ref.shape[0]
    block = out_refs[0].shape[-1]
    for n, group in enumerate(groups):
        j, at = divmod(group * capacity, columns_ref.shape[2])
        got = jnp.concatenate(
            [
                columns_ref[s, j * rows : (j + 1) * rows, at : at + capacity]
                for s in range(sources)
            ],
            axis=1,
        )
        seat = got[full : full + 1, :]
        chooser = (rows_of((block, got.shape[1]), 0).astype(F32) == seat).astype(F32).astype(BF16)
        dense = unstack(mm(stack(got), chooser, 1, 1))
        if len(out_refs) == len(groups):
            out_refs[n][...] = dense
        else:
            out_refs[0][n] = dense


def renumber_kernel(place_ref, *refs):
    block_refs, out_ref = refs[:-1], refs[-1]
    block = place_ref.shape[1]
    if len(block_refs) == 1:
        total = block_refs[0][0]
        for h in range(1, block_refs[0].shape[0]):
            total += block_refs[0][h]
    else:
        total = block_refs[0][...]
        for ref in block_refs[1:]:
            total += ref[...]
    full = out_ref.shape[0] - 1
    place = place_ref[...]
    chooser = (rows_of((block, block), 0) == place % block).astype(F32).astype(BF16)
    out_ref[:full, :] = unstack(mm(stack(total), chooser, 1, 1))[:full]
    out_ref[full:, :] = (place // block).astype(F32)


def prepare_kernel(
    after_ref, offset_ref, lift_ref, jacobian_ref, chooser_ref, lift_out_ref, lines_ref, *, variables, slab
):
    del after_ref
    faces, block = offset_ref.shape
    modes = lift_ref.shape[0]
    full = modes * variables
    choose(offset_ref[...], chooser_ref, 0)
    for w in range(variables):
        for v in range(variables):
            at = (w * variables + v) * faces
            lines_ref[at : at + faces, :] = jacobian_ref[w, v]
    width = variables * faces * slab
    column = rows_of((modes, width), 1)
    mode = rows_of((modes, width), 0)
    spread = jnp.zeros((modes, width), F32)
    for f in range(faces):
        put = (column % slab == mode) & ((column // slab) % faces == f)
        spread += mm(lift_ref[:, f, :], put.astype(F32), 1, 0, lax.Precision.HIGHEST)
    expand = (rows_of((full, modes), 0) // variables == rows_of((full, modes), 1)).astype(F32)
    lifted = mm(expand, spread, 1, 0, lax.Precision.HIGHEST)
    keep = rows_of((full, width), 1) // (slab * faces) == rows_of((full, width), 0) % variables
    high, low = split(jnp.where(keep, lifted, 0.0))
    lift_out_ref[...] = jnp.concatenate([high, high, low], axis=1)


def inner_is_left():
    return lax.axis_index("sub") % 2 == 1


def pack_quarters(pieces, for_left):
    reach = pieces[0].shape[1] // 4
    turned = [pieces[0]] + [pltpu.roll(pieces[g], g * reach, 1) for g in range(1, 4)]
    quarter = rows_of(pieces[0].shape, 1) // reach
    to_left, to_right = turned[0], turned[0]
    for g in range(1, 4):
        to_left = jnp.where(quarter == g, turned[g], to_left)
        to_right = jnp.where(quarter == g - 1, turned[g], to_right)
    return jnp.where(for_left, to_left, to_right)


def take_quarters(inner, outer):
    reach = inner.shape[1] // 4
    quarter = rows_of(inner.shape, 1) // reach
    pieces = []
    for g in range(4):
        piece = jnp.where((quarter == g) != inner_is_left(), inner, outer)
        pieces.append(pltpu.roll(piece, (4 - g) * reach, 1) if g else piece)
    return pieces


def pack_halves(one, two):
    block = one.shape[1]
    turned = pltpu.roll(two, block // 2, 1)
    kept = (rows_of(one.shape, 1) < block // 2) == inner_is_left()
    return jnp.where(kept, one, turned), jnp.where(kept, turned, one)


def take_halves(inner, outer):
    block = inner.shape[1]
    from_inner = (rows_of(inner.shape, 1) >= block // 2) == inner_is_left()
    two = jnp.where(from_inner, outer, inner)
    return jnp.where(from_inner, inner, outer), pltpu.roll(two, block // 2, 1)


def pack_kernel(after_ref, inverse_ref, lines_ref, offset_ref, out_ref, *, outer):
    del after_ref
    full, _, block = inverse_ref.shape
    faces = offset_ref.shape[0]
    for_left = inner_is_left() != outer
    slabs = -(-full // 4)
    for j in range(slabs):
        index = [j + g * slabs for g in range(4)]
        pieces = [inverse_ref[i] if i < full else jnp.zeros((full, block), F32) for i in index]
        out_ref[j * full : (j + 1) * full, :] = pack_quarters(pieces, for_left)
    count = lines_ref.shape[0] // 4
    at, last = slabs * full, out_ref.shape[0] - faces
    pieces = [lines_ref[g * count : (g + 1) * count, :] for g in range(4)]
    out_ref[at : at + count, :] = pack_quarters(pieces, for_left)
    out_ref[at + count : last, :] = jnp.zeros((last - at - count, block), F32)
    out_ref[last:, :] = offset_ref[...].astype(F32)


def beside_kernel(inner_ref, outer_ref, inverse_ref, jacobian_ref, chooser_ref, *, faces):
    full, _, block = inverse_ref.shape
    slabs = -(-full // 4)
    for j in range(slabs):
        at = j * full
        pieces = take_quarters(inner_ref[at : at + full, :], outer_ref[at : at + full, :])
        for g, piece in enumerate(pieces):
            if j + g * slabs < full:
                inverse_ref[j + g * slabs] = piece
    count = jacobian_ref.shape[0] // 4
    at = slabs * full
    pieces = take_quarters(inner_ref[at : at + count, :], outer_ref[at : at + count, :])
    for g, piece in enumerate(pieces):
        jacobian_ref[g * count : (g + 1) * count, :] = piece
    last = inner_ref.shape[0] - faces
    inner, outer = inner_ref[last:, :], outer_ref[last:, :]
    from_inner = (rows_of(inner.shape, 1) >= block // 2) == inner_is_left()
    choose(jnp.where(from_inner, inner, outer).astype(jnp.int32), chooser_ref, block)


def choose(offsets, chooser_ref, first):
    faces, block = offsets.shape
    lane = rows_of((1, block), 1) + first
    row = rows_of((2 * block, block), 0)
    for f in range(faces):
        offset = offsets[f : f + 1, :]
        source = jnp.where(offset != 0, (lane + offset) & (2 * block - 1), -1)
        chooser_ref[:, f * block : (f + 1) * block] = (row == source).astype(F32).astype(BF16)


def apply_inverse(inverse_ref, field, variables, depth=None):
    full, _, block = inverse_ref.shape
    modes = full // variables
    zero = jnp.zeros((8, block), F32)

    def piece(row):
        if row >= full:
            return zero
        product = inverse_ref[row % modes * variables + row // modes if depth else row] * field
        partial = product[0:8]
        for j in range(8, full - 7, 8):
            partial += product[j : j + 8]
        rest = full % 8
        if rest:
            partial += jnp.concatenate([product[full - rest :], zero[rest:]], axis=0)
        return partial

    rows = []
    for at in range(0, depth or full, 8):
        rows.append(sum_rows([piece(at + r) for r in range(8)]) if at < full else zero)
    return jnp.concatenate(rows, axis=0)[: depth or full]


def first_kernel(inverse_ref, *refs, subs, variables):
    block_refs, (total_ref, out_ref, inner_ref, outer_ref) = refs[:-4], refs[-4:]
    full = total_ref.shape[0]
    owner = lax.axis_index("high") * lax.axis_size("low") + lax.axis_index("low")
    owner = (owner * subs + lax.axis_index("sub")).astype(F32)
    residual = jnp.zeros(total_ref.shape, F32)
    for ref in block_refs:
        residual += jnp.where(ref[full:, :] == owner, ref[:full, :], 0.0)
    total_ref[...] = residual
    x = apply_inverse(inverse_ref, residual, variables, out_ref.shape[0])
    out_ref[...] = x
    half = inner_ref.shape[0]
    inner_ref[...], outer_ref[...] = pack_halves(x[:half], x[half:])


def sweep_kernel(
    inverse_ref, inverse_beside_ref, residual_ref, x_ref, outer_ref, inner_ref, chooser_ref,
    chooser_beside_ref, lift_ref, jacobian_ref, jacobian_beside_ref, total_ref, out_ref,
    picked_ref, z_ref, *, variables, slab
):
    depth, block = x_ref.shape
    full = residual_ref.shape[0]
    modes = full // variables
    faces = jacobian_ref.shape[0] // variables**2
    residual = residual_ref[...]
    total_ref[...] = residual
    third = z_ref.shape[0] // 3

    def coupled(x, tiles):
        x = jnp.concatenate(split(x), axis=0)
        for t, ref in enumerate((chooser_ref, chooser_beside_ref)[:tiles]):
            picked = mm(x, ref[...])
            picked_ref[t] = picked[:depth] + picked[depth:]
        for t in range(tiles):
            for f in range(faces):
                at = f * block
                part = [
                    picked_ref[t, v * modes : v * modes + slab, at : at + block]
                    for v in range(variables)
                ]
                for w in range(variables):
                    z = None
                    for v in range(variables):
                        line = (w * variables + v) * faces + f
                        term = part[v] * (jacobian_beside_ref if t else jacobian_ref)[line : line + 1, :]
                        z = z + term if v else term
                    line, column = (w * faces + f) * slab, t * block
                    high, low = split(z)
                    for n, value in enumerate((high, low, high)):
                        at_row = n * third + line
                        z_ref[at_row : at_row + slab, column : column + block] = value
        return mm(lift_ref[...], z_ref[:, : tiles * block])

    first = x_ref[...]
    first_beside = jnp.concatenate(take_halves(inner_ref[...], outer_ref[...]), axis=0)
    taken = coupled(jnp.concatenate([first, first_beside], axis=1), 2)
    second = jnp.concatenate(
        [
            first - apply_inverse(inverse_ref, taken[:, :block], variables, depth),
            first_beside - apply_inverse(inverse_beside_ref, taken[:, block:], variables, depth),
        ],
        axis=1,
    )
    out_ref[...] = apply_inverse(inverse_ref, residual - coupled(second, 1), variables)


def per_device(
    fine_residual,
    fine_basis,
    coarse_basis,
    donor_cells,
    point_counts,
    solver_pos,
    block_inverse,
    face_jacobian,
    face_lift,
    face_offset,
):
    high_count = lax.axis_size("high")
    passing = lax.axis_size("low") * lax.axis_size("sub")
    owners = high_count * passing
    _, variables, fine = fine_residual.shape
    modes = coarse_basis.shape[1]
    donors = donor_cells.shape[1]
    block = solver_pos.shape[0]
    faces = face_offset.shape[0]
    full = modes * variables
    slab = -(-modes // 16) * 16
    depth = -(-full // 16) * 16

    capacity = max(2, 2 * fine * donors // owners)
    few = 1 < high_count <= 8 and high_count & (high_count - 1) == 0
    subs = lax.axis_size("sub")
    counter = call(
        constants_kernel,
        "constants",
        ((128, 256), BF16),
        (),
        cost=pl.CostEstimate(flops=2 * 10**9, bytes_accessed=8 * 10**6, transcendentals=0),
    )
    width = high_count * capacity
    halves = 2 if width > 128 else 1
    rows = -(-(full + 1) // 4) * 4 if halves > 1 else -(-(full + 1) // 8) * 8
    chunk_shape = (passing, halves * rows, width // halves)
    columns = call(
        functools.partial(
            restrict_kernel,
            owners=owners,
            block=block,
            passing=passing,
            subs=subs,
            capacity=capacity,
            few=few,
        ),
        "restrict",
        (chunk_shape, F32),
        (
            counter,
            fine_residual.transpose(1, 0, 2),
            fine_basis.T,
            coarse_basis.transpose(1, 0, 2),
            point_counts.T,
            donor_cells.T,
        ),
        [
            pltpu.VMEM((donors * fine // 128, -(-(full + 1) // 8) * 8, 128), F32),
            pltpu.VMEM(chunk_shape, F32),
            pltpu.SemaphoreType.DMA((passing,)),
        ],
        megabytes=16,
        out_spec=pl.BlockSpec(memory_space=pl.ANY),
    )
    columns = lax.all_to_all(columns, PLANE, 0, 0, tiled=True)
    def seat(name, groups, shapes):
        return call(
            functools.partial(
                seat_kernel, groups=groups, capacity=capacity, rows=rows, full=full
            ),
            name,
            shapes,
            (columns,),
            megabytes=24,
        )

    dense = ((rows, block), F32)
    if few:
        count = high_count // 2
        near = seat("seat_near", range(count), [dense] * count)
        rest = [seat("seat_far", [d], [dense])[0] for d in range(count, high_count)]
        blocks = swap_all([*near, *rest], "high")
    else:
        blocks = seat("seat_all", range(high_count), ((high_count, rows, block), F32))
        blocks = [lax.all_to_all(blocks, "high", 0, 0, tiled=True)]
    whole = call(
        renumber_kernel, "renumber", ((full + 1, block), F32), (solver_pos[None, :], *blocks)
    )
    blocks = swap_all([whole] * subs, "sub")

    lines = variables * variables * faces
    chooser, lift, jacobian = call(
        functools.partial(prepare_kernel, variables=variables, slab=slab),
        "prepare",
        [
            ((2 * block, faces * block), BF16),
            ((full, 3 * variables * faces * slab), BF16),
            ((lines, block), F32),
        ],
        (counter, face_offset, face_lift.transpose(1, 0, 2), face_jacobian.transpose(1, 2, 0, 3)),
    )
    outer_pairs = [(i, i + 1) for i in range(1, owners - 1, 2)]
    outer_pairs += [(j, i) for i, j in outer_pairs]
    inner_pairs = [(i, i ^ 1) for i in range(owners)]
    packed = ((-(-(-(-full // 4) * full + lines // 4 + faces + 1) // 8) * 8, block), F32)
    packs = []
    for outer in (False, True):
        packs.append(
            call(
                functools.partial(pack_kernel, outer=outer),
                "pack_outer" if outer else "pack_inner",
                packed,
                (packs[0] if outer else lift, block_inverse, jacobian, face_offset),
            )
        )
    inner = lax.ppermute(packs[0], WHOLE, inner_pairs)
    outer = lax.ppermute(packs[1], WHOLE, outer_pairs)
    inverse_beside, jacobian_beside, chooser_beside = call(
        functools.partial(beside_kernel, faces=faces),
        "beside",
        [((full, full, block), F32), ((lines, block), F32), ((2 * block, faces * block), BF16)],
        (inner, outer),
    )
    plain, edge = ((full, block), F32), ((depth // 2, block), F32)
    residual, x, to_inner, to_outer = call(
        functools.partial(first_kernel, subs=subs, variables=variables),
        "first",
        [plain, ((depth, block), F32), edge, edge],
        (block_inverse, *blocks),
    )
    outer = lax.ppermute(to_outer, WHOLE, outer_pairs)
    inner = lax.ppermute(to_inner, WHOLE, inner_pairs)
    return tuple(
        call(
            functools.partial(sweep_kernel, variables=variables, slab=slab),
            "sweeps",
            [plain, plain],
            (
                block_inverse,
                inverse_beside,
                residual,
                x,
                outer,
                inner,
                chooser,
                chooser_beside,
                lift,
                jacobian,
                jacobian_beside,
            ),
            [pltpu.VMEM((2, depth, faces * block), F32)]
            + [pltpu.VMEM((3 * variables * faces * slab, 2 * block), BF16)],
        )
    )


def solution(mesh):
    dom, sub = mesh.devices.shape
    low = next(count for count in (4, 2, 1) if dom % count == 0)
    split_mesh = jax.sharding.Mesh(mesh.devices.reshape(dom // low, low, sub), WHOLE)
    in_specs = (
        P(None, None, WHOLE),
        P(),
        P(None, None, WHOLE),
        P(WHOLE, None),
        P(WHOLE, None),
        P(WHOLE),
        P(None, None, WHOLE),
        P(None, None, None, WHOLE),
        P(),
        P(None, WHOLE),
    )
    return jax.shard_map(
        per_device,
        mesh=split_mesh,
        in_specs=in_specs,
        out_specs=(P(None, WHOLE), P(None, WHOLE)),
        check_vma=False,
    )
```

```python
import functools
import jax
import jax.numpy as jnp
from jax import lax
from jax.experimental import pallas as pl
from jax.experimental.pallas import tpu as pltpu
from jax.sharding import PartitionSpec as P

F32 = jnp.float32
BF16 = jnp.bfloat16
PLANE = ("sub", "low")
WHOLE = ("high", "low", "sub")
VMEM = pl.BlockSpec(memory_space=pltpu.VMEM)


def split(x):
    high = x.astype(BF16)
    return high, (x - high.astype(F32)).astype(BF16)


def stack(x):
    high = x.astype(BF16).astype(F32)
    return jnp.concatenate([high, x - high], axis=0).astype(BF16)


def unstack(x):
    return x[: x.shape[0] // 2] + x[x.shape[0] // 2 :]


def mm(a, b, ca=1, cb=0, precision=None):
    return lax.dot_general(
        a, b, (((ca,), (cb,)), ((), ())), precision=precision, preferred_element_type=F32
    )


def rows_of(iota_shape, dim):
    return lax.broadcasted_iota(jnp.int32, iota_shape, dim)


def call(kernel, name, shapes, args, scratch=(), megabytes=8, cost=None, out_spec=VMEM):
    single = not isinstance(shapes, list)
    out = [jax.ShapeDtypeStruct(*shape) for shape in ([shapes] if single else shapes)]
    result = pl.pallas_call(
        kernel,
        out_shape=out,
        in_specs=[VMEM] * len(args),
        out_specs=[out_spec] * len(out),
        scratch_shapes=list(scratch),
        compiler_params=pltpu.CompilerParams(vmem_limit_bytes=megabytes * 2**20),
        cost_estimate=cost,
        name=name,
    )(*args)
    return result[0] if single else result


def swap_all(blocks, axis):
    count = len(blocks)
    return [blocks[0]] + [
        lax.ppermute(blocks[d], axis, [(i, i ^ d) for i in range(count)])
        for d in range(count - 1, 0, -1)
    ]


def constants_kernel(counter_ref):
    lanes = counter_ref.shape[0]
    earlier = (rows_of((lanes, lanes), 0) < rows_of((lanes, lanes), 1)).astype(F32)
    counter = jnp.concatenate([earlier, jnp.ones((lanes, lanes), F32)], axis=1)
    counter_ref[...] = counter.astype(BF16)


def free_columns(owner, counter, owners, passing, subs, capacity, width, high):
    lanes = 128
    total = owner.shape[1]
    parts = total // lanes
    mine = (rows_of((owners, total), 0) == owner).astype(F32)
    stacked = jnp.concatenate([mine[:, j * lanes : (j + 1) * lanes] for j in range(parts)], axis=0)
    counted = mm(stacked.astype(BF16), counter)
    before = jnp.zeros((owners, lanes), F32)
    ranks = []
    for j in range(parts):
        own = mine[:, j * lanes : (j + 1) * lanes]
        part = counted[j * owners : (j + 1) * owners]
        ranks.append(jnp.sum(own * (before + part[:, :lanes]), axis=0, keepdims=True))
        before += part[:, lanes:]
    rank = jnp.concatenate(ranks, axis=1).astype(jnp.int32)
    lows = passing // subs
    chunk = owner % subs * lows + owner // subs % lows
    return chunk * width + (owner // passing ^ high) * capacity + rank


def add_eights(x):
    total = x[0:8]
    for j in range(8, x.shape[0], 8):
        total += x[j : j + 8]
    return total


def sum_rows(pieces):
    row = rows_of(pieces[0].shape, 0)
    pieces = [pieces[k] for k in (3, 2, 1, 0, 7, 6, 5, 4)]
    upper = row < 4
    halves = []
    for one, two in zip(pieces[:4], pieces[4:]):
        kept, moved = jnp.where(upper, one, two), jnp.where(upper, two, one)
        halves.append(kept + pltpu.roll(moved, 4, 0))
    for shift in (2, 1):
        pairs = list(zip(halves[:shift], halves[shift:]))
        halves = [
            jnp.where(
                row & shift != 0, one + pltpu.roll(one, shift, 0), two + pltpu.roll(two, 8 - shift, 0)
            )
            for one, two in pairs
        ]
    return halves[0]


def restrict_kernel(
    counter_ref, res_ref, basis_ref, coarse_ref, counts_ref, donors_ref, out_hbm, pair_ref, out_ref, sems,
    *, owners, block, passing, subs, capacity, few
):
    variables, _, fine = res_ref.shape
    modes, points, _ = coarse_ref.shape
    donors = counts_ref.shape[0]
    chunks = out_ref.shape[0]
    full = modes * variables
    depth = pair_ref.shape[1]
    total = donors * fine
    lanes = 128
    width = owners // passing * capacity

    cell = jnp.concatenate([donors_ref[k : k + 1, :] for k in range(donors)], axis=1)
    seat = (cell % block).astype(F32)
    for j in range(total // lanes):
        pair_ref[j, full:, :] = jnp.zeros((depth - full, lanes), F32)
        pair_ref[j, full : full + 1, :] = seat[:, j * lanes : (j + 1) * lanes]
    high = lax.axis_index("high") if few else 0
    owner = cell // block
    slot = free_columns(owner, counter_ref[...], owners, passing, subs, capacity, width, high)
    slot = jnp.broadcast_to(slot.astype(F32), (lanes, total)).T.astype(jnp.int32).astype(jnp.int16)

    basis_high, basis_low = split(basis_ref[...])
    res_high, res_low = split(jnp.concatenate([res_ref[v] for v in range(variables)], axis=1))
    values = mm(basis_high, res_high, 0, 0)
    values += mm(basis_high, res_low, 0, 0) + mm(basis_low, res_high, 0, 0)

    point = rows_of((points, lanes), 0)
    for at in range(0, fine, lanes):
        upper = jnp.zeros((1, lanes), jnp.int32)
        inside = []
        for k in range(donors):
            lower = upper
            upper = lower + counts_ref[k : k + 1, at : at + lanes]
            inside.append((point >= lower) & (point < upper))
        for v in range(variables):
            column = v * fine + at
            value = values[:, column : column + lanes]
            masked = [jnp.where(inside[k], value, 0.0) for k in range(donors)]
            pieces = []
            for a in range(modes):
                coarse = coarse_ref[a, :, at : at + lanes]
                terms = [coarse * masked[k] for k in range(donors)]
                pieces.append([add_eights(term) for term in terms])
            whole = modes - modes % 8
            for k in range(donors):
                left = k * fine + at
                for a in range(0, whole, 8):
                    rows = pl.ds(a * variables + v, 8, stride=variables)
                    pair_ref[left // lanes, rows, :] = sum_rows(
                        [pieces[a + r][k] for r in range(8)]
                    )
            rest = [(k, a) for k in range(donors) for a in range(whole, modes)]
            for first in range(0, len(rest), 8):
                group = rest[first : first + 8]
                filled = group + [group[0]] * (8 - len(group))
                sums = sum_rows([pieces[a][k] for k, a in filled])
                for r, (k, a) in enumerate(group):
                    row, left = a * variables + v, k * fine + at
                    pair_ref[left // lanes, row : row + 1, :] = sums[r : r + 1]

    pair = jnp.concatenate([pair_ref[j] for j in range(total // lanes)], axis=1)
    both = stack(pair)
    lane = rows_of((total, lanes), 1).astype(jnp.int16)
    one, zero = jnp.ones((total, lanes), BF16), jnp.zeros((total, lanes), BF16)
    part = out_ref.shape[2]
    rows = out_ref.shape[1] * part // width
    together = max(1, 256 // width)
    for first in range(0, chunks, together):
        chooser = jnp.concatenate(
            [
                jnp.where(slot == lane + jnp.int16(first * width + j), one, zero)
                for j in range(0, together * width, lanes)
            ],
            axis=1,
        )
        placed = unstack(mm(both, chooser))
        for c in range(first, first + together):
            for j in range(width // part):
                at = (c - first) * width + j * part
                out_ref[c, j * rows : (j + 1) * rows] = placed[:rows, at : at + part]
            pltpu.make_async_copy(out_ref.at[c], out_hbm.at[c], sems.at[c]).start()
    for c in range(chunks):
        pltpu.make_async_copy(out_ref.at[c], out_hbm.at[c], sems.at[c]).wait()


def seat_kernel(columns_ref, *out_refs, groups, capacity, rows, full):
    sources = columns_ref.shape[0]
    block = out_refs[0].shape[-1]
    for n, group in enumerate(groups):
        j, at = divmod(group * capacity, columns_ref.shape[2])
        got = jnp.concatenate(
            [
                columns_ref[s, j * rows : (j + 1) * rows, at : at + capacity]
                for s in range(sources)
            ],
            axis=1,
        )
        seat = got[full : full + 1, :]
        chooser = (rows_of((block, got.shape[1]), 0).astype(F32) == seat).astype(F32).astype(BF16)
        dense = unstack(mm(stack(got), chooser, 1, 1))
        if len(out_refs) == len(groups):
            out_refs[n][...] = dense
        else:
            out_refs[0][n] = dense


def renumber_kernel(place_ref, *refs):
    block_refs, out_ref = refs[:-1], refs[-1]
    block = place_ref.shape[1]
    if len(block_refs) == 1:
        total = block_refs[0][0]
        for h in range(1, block_refs[0].shape[0]):
            total += block_refs[0][h]
    else:
        total = block_refs[0][...]
        for ref in block_refs[1:]:
            total += ref[...]
    full = out_ref.shape[0] - 1
    place = place_ref[...]
    chooser = (rows_of((block, block), 0) == place % block).astype(F32).astype(BF16)
    out_ref[:full, :] = unstack(mm(stack(total), chooser, 1, 1))[:full]
    out_ref[full:, :] = (place // block).astype(F32)


def prepare_kernel(
    after_ref, offset_ref, lift_ref, jacobian_ref, chooser_ref, lift_out_ref, lines_ref, *, variables, slab
):
    del after_ref
    faces, block = offset_ref.shape
    modes = lift_ref.shape[0]
    full = modes * variables
    choose(offset_ref[...], chooser_ref, 0)
    for w in range(variables):
        for v in range(variables):
            at = (w * variables + v) * faces
            lines_ref[at : at + faces, :] = jacobian_ref[w, v]
    lines_ref[lines_ref.shape[0] - faces :, :] = offset_ref[...].astype(F32)
    width = variables * faces * slab
    column = rows_of((modes, width), 1)
    mode = rows_of((modes, width), 0)
    spread = jnp.zeros((modes, width), F32)
    for f in range(faces):
        put = (column % slab == mode) & ((column // slab) % faces == f)
        spread += mm(lift_ref[:, f, :], put.astype(F32), 1, 0, lax.Precision.HIGHEST)
    expand = (rows_of((full, modes), 0) // variables == rows_of((full, modes), 1)).astype(F32)
    lifted = mm(expand, spread, 1, 0, lax.Precision.HIGHEST)
    keep = rows_of((full, width), 1) // (slab * faces) == rows_of((full, width), 0) % variables
    high, low = split(jnp.where(keep, lifted, 0.0))
    lift_out_ref[...] = jnp.concatenate([high, high, low], axis=1)


def inner_is_left():
    return lax.axis_index("sub") % 2 == 1


def pack_quarters(pieces, for_left):
    reach = pieces[0].shape[1] // 4
    turned = [pieces[0]] + [pltpu.roll(pieces[g], g * reach, 1) for g in range(1, 4)]
    quarter = rows_of(pieces[0].shape, 1) // reach
    to_left, to_right = turned[0], turned[0]
    for g in range(1, 4):
        to_left = jnp.where(quarter == g, turned[g], to_left)
        to_right = jnp.where(quarter == g - 1, turned[g], to_right)
    return jnp.where(for_left, to_left, to_right)


def take_quarters(inner, outer):
    reach = inner.shape[1] // 4
    quarter = rows_of(inner.shape, 1) // reach
    pieces = []
    for g in range(4):
        piece = jnp.where((quarter == g) != inner_is_left(), inner, outer)
        pieces.append(pltpu.roll(piece, (4 - g) * reach, 1) if g else piece)
    return pieces


def pack_halves(one, two):
    block = one.shape[1]
    turned = pltpu.roll(two, block // 2, 1)
    kept = (rows_of(one.shape, 1) < block // 2) == inner_is_left()
    return jnp.where(kept, one, turned), jnp.where(kept, turned, one)


def take_halves(inner, outer):
    block = inner.shape[1]
    from_inner = (rows_of(inner.shape, 1) >= block // 2) == inner_is_left()
    two = jnp.where(from_inner, outer, inner)
    return jnp.where(from_inner, inner, outer), pltpu.roll(two, block // 2, 1)


def pack_kernel(after_ref, inverse_ref, lines_ref, out_ref, *, outer, faces):
    del after_ref
    full, _, block = inverse_ref.shape
    for_left = inner_is_left() != outer
    slabs = -(-full // 4)
    for j in range(slabs):
        index = [j + g * slabs for g in range(4)]
        pieces = [inverse_ref[i] if i < full else jnp.zeros((full, block), F32) for i in index]
        out_ref[j * full : (j + 1) * full, :] = pack_quarters(pieces, for_left)
    count = (lines_ref.shape[0] - faces) // 4
    at, last = slabs * full, out_ref.shape[0] - faces
    pieces = [lines_ref[g * count : (g + 1) * count, :] for g in range(4)]
    out_ref[at : at + count, :] = pack_quarters(pieces, for_left)
    out_ref[at + count : last, :] = jnp.zeros((last - at - count, block), F32)
    out_ref[last:, :] = lines_ref[lines_ref.shape[0] - faces :, :]


def beside_kernel(inner_ref, outer_ref, inverse_ref, jacobian_ref, chooser_ref, *, faces):
    full, _, block = inverse_ref.shape
    slabs = -(-full // 4)
    for j in range(slabs):
        at = j * full
        pieces = take_quarters(inner_ref[at : at + full, :], outer_ref[at : at + full, :])
        for g, piece in enumerate(pieces):
            if j + g * slabs < full:
                inverse_ref[j + g * slabs] = piece
    count = jacobian_ref.shape[0] // 4
    at = slabs * full
    pieces = take_quarters(inner_ref[at : at + count, :], outer_ref[at : at + count, :])
    for g, piece in enumerate(pieces):
        jacobian_ref[g * count : (g + 1) * count, :] = piece
    last = inner_ref.shape[0] - faces
    inner, outer = inner_ref[last:, :], outer_ref[last:, :]
    from_inner = (rows_of(inner.shape, 1) >= block // 2) == inner_is_left()
    choose(jnp.where(from_inner, inner, outer).astype(jnp.int32), chooser_ref, block)


def choose(offsets, chooser_ref, first):
    faces, block = offsets.shape
    lane = rows_of((1, block), 1) + first
    row = rows_of((2 * block, block), 0)
    for f in range(faces):
        offset = offsets[f : f + 1, :]
        source = jnp.where(offset != 0, (lane + offset) & (2 * block - 1), -1)
        chooser_ref[:, f * block : (f + 1) * block] = (row == source).astype(F32).astype(BF16)


def apply_inverse(inverse_ref, field, variables, depth=None):
    full, _, block = inverse_ref.shape
    modes = full // variables
    zero = jnp.zeros((8, block), F32)

    def piece(row):
        if row >= full:
            return zero
        product = inverse_ref[row % modes * variables + row // modes if depth else row] * field
        partial = product[0:8]
        for j in range(8, full - 7, 8):
            partial += product[j : j + 8]
        rest = full % 8
        if rest:
            partial += jnp.concatenate([product[full - rest :], zero[rest:]], axis=0)
        return partial

    rows = []
    for at in range(0, depth or full, 8):
        rows.append(sum_rows([piece(at + r) for r in range(8)]) if at < full else zero)
    return jnp.concatenate(rows, axis=0)[: depth or full]


def first_kernel(inverse_ref, *refs, subs, variables):
    block_refs, (total_ref, out_ref, inner_ref, outer_ref) = refs[:-4], refs[-4:]
    full = total_ref.shape[0]
    owner = lax.axis_index("high") * lax.axis_size("low") + lax.axis_index("low")
    owner = (owner * subs + lax.axis_index("sub")).astype(F32)
    residual = jnp.zeros(total_ref.shape, F32)
    for ref in block_refs:
        residual += jnp.where(ref[full:, :] == owner, ref[:full, :], 0.0)
    total_ref[...] = residual
    x = apply_inverse(inverse_ref, residual, variables, out_ref.shape[0])
    out_ref[...] = x
    half = inner_ref.shape[0]
    inner_ref[...], outer_ref[...] = pack_halves(x[:half], x[half:])


def sweep_kernel(
    inverse_ref, inverse_beside_ref, residual_ref, x_ref, outer_ref, inner_ref, chooser_ref,
    chooser_beside_ref, lift_ref, jacobian_ref, jacobian_beside_ref, total_ref, out_ref,
    picked_ref, z_ref, *, variables, slab
):
    depth, block = x_ref.shape
    full = residual_ref.shape[0]
    modes = full // variables
    faces = jacobian_ref.shape[0] // variables**2
    residual = residual_ref[...]
    total_ref[...] = residual
    third = z_ref.shape[0] // 3

    def coupled(x, tiles):
        x = jnp.concatenate(split(x), axis=0)
        for t, ref in enumerate((chooser_ref, chooser_beside_ref)[:tiles]):
            picked = mm(x, ref[...])
            picked_ref[t] = picked[:depth] + picked[depth:]
        for t in range(tiles):
            for f in range(faces):
                at = f * block
                part = [
                    picked_ref[t, v * modes : v * modes + slab, at : at + block]
                    for v in range(variables)
                ]
                for w in range(variables):
                    z = None
                    for v in range(variables):
                        line = (w * variables + v) * faces + f
                        term = part[v] * (jacobian_beside_ref if t else jacobian_ref)[line : line + 1, :]
                        z = z + term if v else term
                    line, column = (w * faces + f) * slab, t * block
                    high, low = split(z)
                    for n, value in enumerate((high, low, high)):
                        at_row = n * third + line
                        z_ref[at_row : at_row + slab, column : column + block] = value
        return mm(lift_ref[...], z_ref[:, : tiles * block])

    first = x_ref[...]
    first_beside = jnp.concatenate(take_halves(inner_ref[...], outer_ref[...]), axis=0)
    taken = coupled(jnp.concatenate([first, first_beside], axis=1), 2)
    second = jnp.concatenate(
        [
            first - apply_inverse(inverse_ref, taken[:, :block], variables, depth),
            first_beside - apply_inverse(inverse_beside_ref, taken[:, block:], variables, depth),
        ],
        axis=1,
    )
    out_ref[...] = apply_inverse(inverse_ref, residual - coupled(second, 1), variables)


def per_device(
    fine_residual,
    fine_basis,
    coarse_basis,
    donor_cells,
    point_counts,
    solver_pos,
    block_inverse,
    face_jacobian,
    face_lift,
    face_offset,
):
    high_count = lax.axis_size("high")
    passing = lax.axis_size("low") * lax.axis_size("sub")
    owners = high_count * passing
    _, variables, fine = fine_residual.shape
    modes = coarse_basis.shape[1]
    donors = donor_cells.shape[1]
    block = solver_pos.shape[0]
    faces = face_offset.shape[0]
    full = modes * variables
    slab = -(-modes // 16) * 16
    depth = -(-full // 16) * 16

    capacity = max(2, 2 * fine * donors // owners)
    few = 1 < high_count <= 8 and high_count & (high_count - 1) == 0
    subs = lax.axis_size("sub")
    counter = call(
        constants_kernel,
        "constants",
        ((128, 256), BF16),
        (),
        cost=pl.CostEstimate(flops=2 * 10**9, bytes_accessed=8 * 10**6, transcendentals=0),
    )
    width = high_count * capacity
    halves = 2 if width > 128 else 1
    rows = -(-(full + 1) // 4) * 4 if halves > 1 else -(-(full + 1) // 8) * 8
    chunk_shape = (passing, halves * rows, width // halves)
    columns = call(
        functools.partial(
            restrict_kernel,
            owners=owners,
            block=block,
            passing=passing,
            subs=subs,
            capacity=capacity,
            few=few,
        ),
        "restrict",
        (chunk_shape, F32),
        (
            counter,
            fine_residual.transpose(1, 0, 2),
            fine_basis.T,
            coarse_basis.transpose(1, 0, 2),
            point_counts.T,
            donor_cells.T,
        ),
        [
            pltpu.VMEM((donors * fine // 128, -(-(full + 1) // 8) * 8, 128), F32),
            pltpu.VMEM(chunk_shape, F32),
            pltpu.SemaphoreType.DMA((passing,)),
        ],
        megabytes=16,
        out_spec=pl.BlockSpec(memory_space=pl.ANY),
    )
    columns = lax.all_to_all(columns, PLANE, 0, 0, tiled=True)
    def seat(name, groups, shapes):
        return call(
            functools.partial(
                seat_kernel, groups=groups, capacity=capacity, rows=rows, full=full
            ),
            name,
            shapes,
            (columns,),
            megabytes=24,
        )

    dense = ((rows, block), F32)
    if few:
        count = high_count // 2
        near = seat("seat_near", range(count), [dense] * count)
        rest = [seat("seat_far", [d], [dense])[0] for d in range(count, high_count)]
        blocks = swap_all([*near, *rest], "high")
    else:
        blocks = seat("seat_all", range(high_count), ((high_count, rows, block), F32))
        blocks = [lax.all_to_all(blocks, "high", 0, 0, tiled=True)]
    whole = call(
        renumber_kernel, "renumber", ((full + 1, block), F32), (solver_pos[None, :], *blocks)
    )
    blocks = swap_all([whole] * subs, "sub")

    lines = variables * variables * faces
    chooser, lift, jacobian = call(
        functools.partial(prepare_kernel, variables=variables, slab=slab),
        "prepare",
        [
            ((2 * block, faces * block), BF16),
            ((full, 3 * variables * faces * slab), BF16),
            ((lines + faces, block), F32),
        ],
        (counter, face_offset, face_lift.transpose(1, 0, 2), face_jacobian.transpose(1, 2, 0, 3)),
    )
    outer_pairs = [(i, i + 1) for i in range(1, owners - 1, 2)]
    outer_pairs += [(j, i) for i, j in outer_pairs]
    inner_pairs = [(i, i ^ 1) for i in range(owners)]
    packed = ((-(-(-(-full // 4) * full + lines // 4 + faces + 1) // 8) * 8, block), F32)
    packs = []
    for outer in (False, True):
        packs.append(
            call(
                functools.partial(pack_kernel, outer=outer, faces=faces),
                "pack_outer" if outer else "pack_inner",
                packed,
                (packs[0] if outer else lift, block_inverse, jacobian),
            )
        )
    inner = lax.ppermute(packs[0], WHOLE, inner_pairs)
    outer = lax.ppermute(packs[1], WHOLE, outer_pairs)
    inverse_beside, jacobian_beside, chooser_beside = call(
        functools.partial(beside_kernel, faces=faces),
        "beside",
        [((full, full, block), F32), ((lines, block), F32), ((2 * block, faces * block), BF16)],
        (inner, outer),
    )
    plain, edge = ((full, block), F32), ((depth // 2, block), F32)
    residual, x, to_inner, to_outer = call(
        functools.partial(first_kernel, subs=subs, variables=variables),
        "first",
        [plain, ((depth, block), F32), edge, edge],
        (block_inverse, *blocks),
    )
    outer = lax.ppermute(to_outer, WHOLE, outer_pairs)
    inner = lax.ppermute(to_inner, WHOLE, inner_pairs)
    return tuple(
        call(
            functools.partial(sweep_kernel, variables=variables, slab=slab),
            "sweeps",
            [plain, plain],
            (
                block_inverse,
                inverse_beside,
                residual,
                x,
                outer,
                inner,
                chooser,
                chooser_beside,
                lift,
                jacobian,
                jacobian_beside,
            ),
            [pltpu.VMEM((2, depth, faces * block), F32)]
            + [pltpu.VMEM((3 * variables * faces * slab, 2 * block), BF16)],
        )
    )


def solution(mesh):
    dom, sub = mesh.devices.shape
    low = next(count for count in (4, 2, 1) if dom % count == 0)
    split_mesh = jax.sharding.Mesh(mesh.devices.reshape(dom // low, low, sub), WHOLE)
    in_specs = (
        P(None, None, WHOLE),
        P(),
        P(None, None, WHOLE),
        P(WHOLE, None),
        P(WHOLE, None),
        P(WHOLE),
        P(None, None, WHOLE),
        P(None, None, None, WHOLE),
        P(),
        P(None, WHOLE),
    )
    return jax.shard_map(
        per_device,
        mesh=split_mesh,
        in_specs=in_specs,
        out_specs=(P(None, WHOLE), P(None, WHOLE)),
        check_vma=False,
    )
```

```python
import functools
import jax
import jax.numpy as jnp
from jax import lax
from jax.experimental import pallas as pl
from jax.experimental.pallas import tpu as pltpu
from jax.sharding import PartitionSpec as P

F32 = jnp.float32
BF16 = jnp.bfloat16
PLANE = ("sub", "low")
WHOLE = ("high", "low", "sub")
VMEM = pl.BlockSpec(memory_space=pltpu.VMEM)


def split(x):
    high = x.astype(BF16)
    return high, (x - high.astype(F32)).astype(BF16)


def mm(a, b, ca=1, cb=0, precision=None):
    return lax.dot_general(
        a, b, (((ca,), (cb,)), ((), ())), precision=precision, preferred_element_type=F32
    )


def rows_of(iota_shape, dim):
    return lax.broadcasted_iota(jnp.int32, iota_shape, dim)


def call(kernel, name, shapes, args, scratch=(), megabytes=8, cost=None, out_spec=VMEM):
    single = not isinstance(shapes, list)
    out = [jax.ShapeDtypeStruct(*shape) for shape in ([shapes] if single else shapes)]
    result = pl.pallas_call(
        kernel,
        out_shape=out,
        in_specs=[VMEM] * len(args),
        out_specs=[out_spec] * len(out),
        scratch_shapes=list(scratch),
        compiler_params=pltpu.CompilerParams(vmem_limit_bytes=megabytes * 2**20),
        cost_estimate=cost,
        name=name,
    )(*args)
    return result[0] if single else result


def swap_all(blocks, axis):
    count = len(blocks)
    return [blocks[0]] + [
        lax.ppermute(blocks[d], axis, [(i, i ^ d) for i in range(count)])
        for d in range(count - 1, 0, -1)
    ]


def constants_kernel(counter_ref):
    lanes = counter_ref.shape[0]
    earlier = (rows_of((lanes, lanes), 0) < rows_of((lanes, lanes), 1)).astype(F32)
    counter = jnp.concatenate([earlier, jnp.ones((lanes, lanes), F32)], axis=1)
    counter_ref[...] = counter.astype(BF16)


def free_columns(owner, counter, owners, passing, subs, capacity, width, high):
    lanes = 128
    total = owner.shape[1]
    parts = total // lanes
    mine = (rows_of((owners, total), 0) == owner).astype(F32)
    stacked = jnp.concatenate([mine[:, j * lanes : (j + 1) * lanes] for j in range(parts)], axis=0)
    counted = mm(stacked.astype(BF16), counter)
    before = jnp.zeros((owners, lanes), F32)
    ranks = []
    for j in range(parts):
        own = mine[:, j * lanes : (j + 1) * lanes]
        part = counted[j * owners : (j + 1) * owners]
        ranks.append(jnp.sum(own * (before + part[:, :lanes]), axis=0, keepdims=True))
        before += part[:, lanes:]
    rank = jnp.concatenate(ranks, axis=1).astype(jnp.int32)
    lows = passing // subs
    chunk = owner % subs * lows + owner // subs % lows
    return chunk * width + (owner // passing ^ high) * capacity + rank


def add_eights(x):
    total = x[0:8]
    for j in range(8, x.shape[0], 8):
        total += x[j : j + 8]
    return total


def sum_rows(pieces):
    row = rows_of(pieces[0].shape, 0)
    pieces = [pieces[k] for k in (3, 2, 1, 0, 7, 6, 5, 4)]
    upper = row < 4
    halves = []
    for one, two in zip(pieces[:4], pieces[4:]):
        kept, moved = jnp.where(upper, one, two), jnp.where(upper, two, one)
        halves.append(kept + pltpu.roll(moved, 4, 0))
    for shift in (2, 1):
        pairs = list(zip(halves[:shift], halves[shift:]))
        halves = [
            jnp.where(
                row & shift != 0, one + pltpu.roll(one, shift, 0), two + pltpu.roll(two, 8 - shift, 0)
            )
            for one, two in pairs
        ]
    return halves[0]


def restrict_kernel(
    counter_ref, res_ref, basis_ref, coarse_ref, counts_ref, donors_ref, out_hbm, pair_ref, out_ref, sems,
    *, owners, block, passing, subs, capacity, few
):
    variables, _, fine = res_ref.shape
    modes, points, _ = coarse_ref.shape
    donors = counts_ref.shape[0]
    chunks = out_ref.shape[0]
    full = modes * variables
    depth = pair_ref.shape[1]
    total = donors * fine
    lanes = 128
    width = owners // passing * capacity

    cell = jnp.concatenate([donors_ref[k : k + 1, :] for k in range(donors)], axis=1)
    seat = (cell % block).astype(F32)
    for j in range(total // lanes):
        pair_ref[j, full:, :] = jnp.zeros((depth - full, lanes), F32)
        pair_ref[j, full : full + 1, :] = seat[:, j * lanes : (j + 1) * lanes]
    high = lax.axis_index("high") if few else 0
    owner = cell // block
    slot = free_columns(owner, counter_ref[...], owners, passing, subs, capacity, width, high)
    slot = jnp.broadcast_to(slot.astype(F32), (lanes, total)).T.astype(jnp.int32).astype(jnp.int16)

    basis_high, basis_low = split(basis_ref[...])
    res_high, res_low = split(jnp.concatenate([res_ref[v] for v in range(variables)], axis=1))
    values = mm(basis_high, res_high, 0, 0)
    values += mm(basis_high, res_low, 0, 0) + mm(basis_low, res_high, 0, 0)

    point = rows_of((points, lanes), 0)
    for at in range(0, fine, lanes):
        upper = jnp.zeros((1, lanes), jnp.int32)
        inside = []
        for k in range(donors):
            lower = upper
            upper = lower + counts_ref[k : k + 1, at : at + lanes]
            inside.append((point >= lower) & (point < upper))
        for v in range(variables):
            column = v * fine + at
            value = values[:, column : column + lanes]
            masked = [jnp.where(inside[k], value, 0.0) for k in range(donors)]
            pieces = []
            for a in range(modes):
                coarse = coarse_ref[a, :, at : at + lanes]
                terms = [coarse * masked[k] for k in range(donors)]
                pieces.append([add_eights(term) for term in terms])
            whole = modes - modes % 8
            for k in range(donors):
                left = k * fine + at
                for a in range(0, whole, 8):
                    rows = pl.ds(a * variables + v, 8, stride=variables)
                    pair_ref[left // lanes, rows, :] = sum_rows(
                        [pieces[a + r][k] for r in range(8)]
                    )
            rest = [(k, a) for k in range(donors) for a in range(whole, modes)]
            for first in range(0, len(rest), 8):
                group = rest[first : first + 8]
                filled = group + [group[0]] * (8 - len(group))
                sums = sum_rows([pieces[a][k] for k, a in filled])
                for r, (k, a) in enumerate(group):
                    row, left = a * variables + v, k * fine + at
                    pair_ref[left // lanes, row : row + 1, :] = sums[r : r + 1]

    pair = jnp.concatenate([pair_ref[j] for j in range(total // lanes)], axis=1)
    both = jnp.concatenate(split(pair), axis=0)
    lane = rows_of((total, lanes), 1).astype(jnp.int16)
    one, zero = jnp.ones((total, lanes), BF16), jnp.zeros((total, lanes), BF16)
    part = out_ref.shape[2]
    rows = out_ref.shape[1] * part // width
    together = max(1, 256 // width)
    for first in range(0, chunks, together):
        chooser = jnp.concatenate(
            [
                jnp.where(slot == lane + jnp.int16(first * width + j), one, zero)
                for j in range(0, together * width, lanes)
            ],
            axis=1,
        )
        placed = mm(both, chooser)
        placed = placed[:depth] + placed[depth:]
        for c in range(first, first + together):
            for j in range(width // part):
                at = (c - first) * width + j * part
                out_ref[c, j * rows : (j + 1) * rows] = placed[:rows, at : at + part]
            pltpu.make_async_copy(out_ref.at[c], out_hbm.at[c], sems.at[c]).start()
    for c in range(chunks):
        pltpu.make_async_copy(out_ref.at[c], out_hbm.at[c], sems.at[c]).wait()


def seat_kernel(columns_ref, *out_refs, groups, capacity, rows):
    sources = columns_ref.shape[0]
    full, block = out_refs[0].shape[-2:]
    for n, group in enumerate(groups):
        j, at = divmod(group * capacity, columns_ref.shape[2])
        got = jnp.concatenate(
            [
                columns_ref[s, j * rows : j * rows + full + 1, at : at + capacity]
                for s in range(sources)
            ],
            axis=1,
        )
        seat = got[full : full + 1, :]
        chooser = (rows_of((block, got.shape[1]), 0).astype(F32) == seat).astype(F32).astype(BF16)
        high, low = split(got)
        dense = (mm(high, chooser, 1, 1) + mm(low, chooser, 1, 1))[:full]
        if len(out_refs) == len(groups):
            out_refs[n][...] = dense
        else:
            out_refs[0][n] = dense


def renumber_kernel(place_ref, *refs):
    block_refs, out_ref = refs[:-1], refs[-1]
    block = place_ref.shape[1]
    if len(block_refs) == 1:
        total = block_refs[0][0]
        for h in range(1, block_refs[0].shape[0]):
            total += block_refs[0][h]
    else:
        total = block_refs[0][...]
        for ref in block_refs[1:]:
            total += ref[...]
    full = total.shape[0]
    place = place_ref[...]
    chooser = (rows_of((block, block), 0) == place % block).astype(F32).astype(BF16)
    high, low = split(total)
    out_ref[:full, :] = mm(high, chooser, 1, 1) + mm(low, chooser, 1, 1)
    out_ref[full:, :] = (place // block).astype(F32)


def prepare_kernel(after_ref, offset_ref, lift_ref, chooser_ref, lift_out_ref, *, variables, slab):
    del after_ref
    faces, block = offset_ref.shape
    modes = lift_ref.shape[0]
    full = modes * variables
    choose(offset_ref[...], chooser_ref, 0)
    width = variables * faces * slab
    column = rows_of((modes, width), 1)
    mode = rows_of((modes, width), 0)
    spread = jnp.zeros((modes, width), F32)
    for f in range(faces):
        put = (column % slab == mode) & ((column // slab) % faces == f)
        spread += mm(lift_ref[:, f, :], put.astype(F32), 1, 0, lax.Precision.HIGHEST)
    expand = (rows_of((full, modes), 0) // variables == rows_of((full, modes), 1)).astype(F32)
    lifted = mm(expand, spread, 1, 0, lax.Precision.HIGHEST)
    keep = rows_of((full, width), 1) // (slab * faces) == rows_of((full, width), 0) % variables
    high, low = split(jnp.where(keep, lifted, 0.0))
    lift_out_ref[...] = jnp.concatenate([high, high, low], axis=1)


def inner_is_left():
    return lax.axis_index("sub") % 2 == 1


def pack_quarters(pieces, for_left):
    reach = pieces[0].shape[1] // 4
    turned = [pieces[0]] + [pltpu.roll(pieces[g], g * reach, 1) for g in range(1, 4)]
    quarter = rows_of(pieces[0].shape, 1) // reach
    to_left, to_right = turned[0], turned[0]
    for g in range(1, 4):
        to_left = jnp.where(quarter == g, turned[g], to_left)
        to_right = jnp.where(quarter == g - 1, turned[g], to_right)
    return jnp.where(for_left, to_left, to_right)


def take_quarters(inner, outer):
    reach = inner.shape[1] // 4
    quarter = rows_of(inner.shape, 1) // reach
    pieces = []
    for g in range(4):
        piece = jnp.where((quarter == g) != inner_is_left(), inner, outer)
        pieces.append(pltpu.roll(piece, (4 - g) * reach, 1) if g else piece)
    return pieces


def pack_halves(one, two):
    block = one.shape[1]
    turned = pltpu.roll(two, block // 2, 1)
    kept = (rows_of(one.shape, 1) < block // 2) == inner_is_left()
    return jnp.where(kept, one, turned), jnp.where(kept, turned, one)


def take_halves(inner, outer):
    block = inner.shape[1]
    from_inner = (rows_of(inner.shape, 1) >= block // 2) == inner_is_left()
    two = jnp.where(from_inner, outer, inner)
    return jnp.where(from_inner, inner, outer), pltpu.roll(two, block // 2, 1)


def pack_kernel(after_ref, inverse_ref, jacobian_ref, offset_ref, out_ref, lines, *, outer):
    del after_ref
    full, _, block = inverse_ref.shape
    variables, _, faces, _ = jacobian_ref.shape
    for_left = inner_is_left() != outer
    slabs = -(-full // 4)
    for j in range(slabs):
        index = [j + g * slabs for g in range(4)]
        pieces = [inverse_ref[i] if i < full else jnp.zeros((full, block), F32) for i in index]
        out_ref[j * full : (j + 1) * full, :] = pack_quarters(pieces, for_left)
    for w in range(variables):
        for v in range(variables):
            at = (w * variables + v) * faces
            lines[at : at + faces, :] = jacobian_ref[w, v]
    count = lines.shape[0] // 4
    at, last = slabs * full, out_ref.shape[0] - faces
    pieces = [lines[g * count : (g + 1) * count, :] for g in range(4)]
    out_ref[at : at + count, :] = pack_quarters(pieces, for_left)
    out_ref[at + count : last, :] = jnp.zeros((last - at - count, block), F32)
    out_ref[last:, :] = offset_ref[...].astype(F32)


def beside_kernel(inner_ref, outer_ref, inverse_ref, jacobian_ref, chooser_ref, *, faces):
    full, _, block = inverse_ref.shape
    slabs = -(-full // 4)
    for j in range(slabs):
        at = j * full
        pieces = take_quarters(inner_ref[at : at + full, :], outer_ref[at : at + full, :])
        for g, piece in enumerate(pieces):
            if j + g * slabs < full:
                inverse_ref[j + g * slabs] = piece
    count = jacobian_ref.shape[0] // 4
    at = slabs * full
    pieces = take_quarters(inner_ref[at : at + count, :], outer_ref[at : at + count, :])
    for g, piece in enumerate(pieces):
        jacobian_ref[g * count : (g + 1) * count, :] = piece
    last = inner_ref.shape[0] - faces
    inner, outer = inner_ref[last:, :], outer_ref[last:, :]
    from_inner = (rows_of(inner.shape, 1) >= block // 2) == inner_is_left()
    choose(jnp.where(from_inner, inner, outer).astype(jnp.int32), chooser_ref, block)


def choose(offsets, chooser_ref, first):
    faces, block = offsets.shape
    lane = rows_of((1, block), 1) + first
    row = rows_of((2 * block, block), 0)
    for f in range(faces):
        offset = offsets[f : f + 1, :]
        source = jnp.where(offset != 0, (lane + offset) & (2 * block - 1), -1)
        chooser_ref[:, f * block : (f + 1) * block] = (row == source).astype(F32).astype(BF16)


def apply_inverse(inverse_ref, field, variables, depth=None):
    full, _, block = inverse_ref.shape
    modes = full // variables
    zero = jnp.zeros((8, block), F32)

    def piece(row):
        if row >= full:
            return zero
        product = inverse_ref[row % modes * variables + row // modes if depth else row] * field
        partial = product[0:8]
        for j in range(8, full - 7, 8):
            partial += product[j : j + 8]
        rest = full % 8
        if rest:
            partial += jnp.concatenate([product[full - rest :], zero[rest:]], axis=0)
        return partial

    rows = []
    for at in range(0, depth or full, 8):
        rows.append(sum_rows([piece(at + r) for r in range(8)]) if at < full else zero)
    return jnp.concatenate(rows, axis=0)[: depth or full]


def first_kernel(inverse_ref, *refs, subs, variables):
    block_refs, (total_ref, out_ref, inner_ref, outer_ref) = refs[:-4], refs[-4:]
    full = total_ref.shape[0]
    owner = lax.axis_index("high") * lax.axis_size("low") + lax.axis_index("low")
    owner = (owner * subs + lax.axis_index("sub")).astype(F32)
    residual = jnp.zeros(total_ref.shape, F32)
    for ref in block_refs:
        residual += jnp.where(ref[full:, :] == owner, ref[:full, :], 0.0)
    total_ref[...] = residual
    x = apply_inverse(inverse_ref, residual, variables, out_ref.shape[0])
    out_ref[...] = x
    half = inner_ref.shape[0]
    inner_ref[...], outer_ref[...] = pack_halves(x[:half], x[half:])


def sweep_kernel(
    inverse_ref, inverse_beside_ref, residual_ref, x_ref, outer_ref, inner_ref, chooser_ref,
    chooser_beside_ref, lift_ref, jacobian_ref, jacobian_beside_ref, total_ref, out_ref,
    picked_ref, z_ref, *, variables, slab
):
    depth, block = x_ref.shape
    full = residual_ref.shape[0]
    modes = full // variables
    faces = jacobian_ref.shape[2]
    residual = residual_ref[...]
    total_ref[...] = residual
    third = z_ref.shape[0] // 3

    def coupled(x, tiles):
        x = jnp.concatenate(split(x), axis=0)
        for t, ref in enumerate((chooser_ref, chooser_beside_ref)[:tiles]):
            picked = mm(x, ref[...])
            picked_ref[t] = picked[:depth] + picked[depth:]
        for t in range(tiles):
            for f in range(faces):
                at = f * block
                part = [
                    picked_ref[t, v * modes : v * modes + slab, at : at + block]
                    for v in range(variables)
                ]
                for w in range(variables):
                    z = None
                    for v in range(variables):
                        if t:
                            line = (w * variables + v) * faces + f
                            term = part[v] * jacobian_beside_ref[line : line + 1, :]
                        else:
                            term = part[v] * jacobian_ref[w, v, f : f + 1, :]
                        z = z + term if v else term
                    line, column = (w * faces + f) * slab, t * block
                    high, low = split(z)
                    for n, value in enumerate((high, low, high)):
                        at_row = n * third + line
                        z_ref[at_row : at_row + slab, column : column + block] = value
        return mm(lift_ref[...], z_ref[:, : tiles * block])

    first = x_ref[...]
    first_beside = jnp.concatenate(take_halves(inner_ref[...], outer_ref[...]), axis=0)
    taken = coupled(jnp.concatenate([first, first_beside], axis=1), 2)
    second = jnp.concatenate(
        [
            first - apply_inverse(inverse_ref, taken[:, :block], variables, depth),
            first_beside - apply_inverse(inverse_beside_ref, taken[:, block:], variables, depth),
        ],
        axis=1,
    )
    out_ref[...] = apply_inverse(inverse_ref, residual - coupled(second, 1), variables)


def per_device(
    fine_residual,
    fine_basis,
    coarse_basis,
    donor_cells,
    point_counts,
    solver_pos,
    block_inverse,
    face_jacobian,
    face_lift,
    face_offset,
):
    high_count = lax.axis_size("high")
    passing = lax.axis_size("low") * lax.axis_size("sub")
    owners = high_count * passing
    _, variables, fine = fine_residual.shape
    modes = coarse_basis.shape[1]
    donors = donor_cells.shape[1]
    block = solver_pos.shape[0]
    faces = face_offset.shape[0]
    full = modes * variables
    slab = -(-modes // 16) * 16
    depth = -(-full // 16) * 16

    capacity = max(2, 2 * fine * donors // owners)
    few = 1 < high_count <= 8 and high_count & (high_count - 1) == 0
    subs = lax.axis_size("sub")
    counter = call(
        constants_kernel,
        "constants",
        ((128, 256), BF16),
        (),
        cost=pl.CostEstimate(flops=2 * 10**9, bytes_accessed=8 * 10**6, transcendentals=0),
    )
    width = high_count * capacity
    halves = 2 if width > 128 else 1
    rows = -(-(full + 1) // 4) * 4 if halves > 1 else -(-(full + 1) // 8) * 8
    chunk_shape = (passing, halves * rows, width // halves)
    columns = call(
        functools.partial(
            restrict_kernel,
            owners=owners,
            block=block,
            passing=passing,
            subs=subs,
            capacity=capacity,
            few=few,
        ),
        "restrict",
        (chunk_shape, F32),
        (
            counter,
            fine_residual.transpose(1, 0, 2),
            fine_basis.T,
            coarse_basis.transpose(1, 0, 2),
            point_counts.T,
            donor_cells.T,
        ),
        [
            pltpu.VMEM((donors * fine // 128, depth, 128), F32),
            pltpu.VMEM(chunk_shape, F32),
            pltpu.SemaphoreType.DMA((passing,)),
        ],
        megabytes=16,
        out_spec=pl.BlockSpec(memory_space=pl.ANY),
    )
    columns = lax.all_to_all(columns, PLANE, 0, 0, tiled=True)
    def seat(name, groups, shapes):
        return call(
            functools.partial(seat_kernel, groups=groups, capacity=capacity, rows=rows),
            name,
            shapes,
            (columns,),
            megabytes=24,
        )

    dense = ((full, block), F32)
    if few:
        count = high_count // 2
        near = seat("seat_near", range(count), [dense] * count)
        rest = [seat("seat_far", [d], [dense])[0] for d in range(count, high_count)]
        blocks = swap_all([*near, *rest], "high")
    else:
        blocks = seat("seat_all", range(high_count), ((high_count, full, block), F32))
        blocks = [lax.all_to_all(blocks, "high", 0, 0, tiled=True)]
    whole = call(
        renumber_kernel, "renumber", ((full + 1, block), F32), (solver_pos[None, :], *blocks)
    )
    blocks = swap_all([whole] * subs, "sub")

    jacobian = face_jacobian.transpose(1, 2, 0, 3)
    chooser, lift = call(
        functools.partial(prepare_kernel, variables=variables, slab=slab),
        "prepare",
        [((2 * block, faces * block), BF16), ((full, 3 * variables * faces * slab), BF16)],
        (counter, face_offset, face_lift.transpose(1, 0, 2)),
    )
    outer_pairs = [(i, i + 1) for i in range(1, owners - 1, 2)]
    outer_pairs += [(j, i) for i, j in outer_pairs]
    inner_pairs = [(i, i ^ 1) for i in range(owners)]
    lines = variables * variables * faces
    packed = ((-(-(-(-full // 4) * full + lines // 4 + faces + 1) // 8) * 8, block), F32)
    packs = []
    for outer in (False, True):
        packs.append(
            call(
                functools.partial(pack_kernel, outer=outer),
                "pack_outer" if outer else "pack_inner",
                packed,
                (packs[0] if outer else counter, block_inverse, jacobian, face_offset),
                [pltpu.VMEM((lines, block), F32)],
            )
        )
    inner = lax.ppermute(packs[0], WHOLE, inner_pairs)
    outer = lax.ppermute(packs[1], WHOLE, outer_pairs)
    inverse_beside, jacobian_beside, chooser_beside = call(
        functools.partial(beside_kernel, faces=faces),
        "beside",
        [((full, full, block), F32), ((lines, block), F32), ((2 * block, faces * block), BF16)],
        (inner, outer),
    )
    plain, edge = ((full, block), F32), ((depth // 2, block), F32)
    residual, x, to_inner, to_outer = call(
        functools.partial(first_kernel, subs=subs, variables=variables),
        "first",
        [plain, ((depth, block), F32), edge, edge],
        (block_inverse, *blocks),
    )
    outer = lax.ppermute(to_outer, WHOLE, outer_pairs)
    inner = lax.ppermute(to_inner, WHOLE, inner_pairs)
    return tuple(
        call(
            functools.partial(sweep_kernel, variables=variables, slab=slab),
            "sweeps",
            [plain, plain],
            (
                block_inverse,
                inverse_beside,
                residual,
                x,
                outer,
                inner,
                chooser,
                chooser_beside,
                lift,
                jacobian,
                jacobian_beside,
            ),
            [pltpu.VMEM((2, depth, faces * block), F32)]
            + [pltpu.VMEM((3 * variables * faces * slab, 2 * block), BF16)],
        )
    )


def solution(mesh):
    dom, sub = mesh.devices.shape
    low = next(count for count in (4, 2, 1) if dom % count == 0)
    split_mesh = jax.sharding.Mesh(mesh.devices.reshape(dom // low, low, sub), WHOLE)
    in_specs = (
        P(None, None, WHOLE),
        P(),
        P(None, None, WHOLE),
        P(WHOLE, None),
        P(WHOLE, None),
        P(WHOLE),
        P(None, None, WHOLE),
        P(None, None, None, WHOLE),
        P(),
        P(None, WHOLE),
    )
    return jax.shard_map(
        per_device,
        mesh=split_mesh,
        in_specs=in_specs,
        out_specs=(P(None, WHOLE), P(None, WHOLE)),
        check_vma=False,
    )
```

```python
import functools
import jax
import jax.numpy as jnp
from jax import lax
from jax.experimental import pallas as pl
from jax.experimental.pallas import tpu as pltpu
from jax.sharding import PartitionSpec as P

F32 = jnp.float32
BF16 = jnp.bfloat16
PLANE = ("sub", "low")
WHOLE = ("high", "low", "sub")
VMEM = pl.BlockSpec(memory_space=pltpu.VMEM)


def split(x):
    high = x.astype(BF16)
    return high, (x - high.astype(F32)).astype(BF16)


def mm(a, b, ca=1, cb=0, precision=None):
    return lax.dot_general(
        a, b, (((ca,), (cb,)), ((), ())), precision=precision, preferred_element_type=F32
    )


def rows_of(iota_shape, dim):
    return lax.broadcasted_iota(jnp.int32, iota_shape, dim)


def call(kernel, name, shapes, args, scratch=(), megabytes=8, cost=None, out_spec=VMEM):
    single = not isinstance(shapes, list)
    out = [jax.ShapeDtypeStruct(*shape) for shape in ([shapes] if single else shapes)]
    result = pl.pallas_call(
        kernel,
        out_shape=out,
        in_specs=[VMEM] * len(args),
        out_specs=[out_spec] * len(out),
        scratch_shapes=list(scratch),
        compiler_params=pltpu.CompilerParams(vmem_limit_bytes=megabytes * 2**20),
        cost_estimate=cost,
        name=name,
    )(*args)
    return result[0] if single else result


def swap_all(blocks, axis):
    count = len(blocks)
    return [blocks[0]] + [
        lax.ppermute(blocks[d], axis, [(i, i ^ d) for i in range(count)])
        for d in range(count - 1, 0, -1)
    ]


def constants_kernel(counter_ref):
    lanes = counter_ref.shape[0]
    earlier = (rows_of((lanes, lanes), 0) < rows_of((lanes, lanes), 1)).astype(F32)
    counter = jnp.concatenate([earlier, jnp.ones((lanes, lanes), F32)], axis=1)
    counter_ref[...] = counter.astype(BF16)


def free_columns(owner, counter, owners, passing, subs, capacity, width, high):
    lanes = 128
    total = owner.shape[1]
    parts = total // lanes
    mine = (rows_of((owners, total), 0) == owner).astype(F32)
    stacked = jnp.concatenate([mine[:, j * lanes : (j + 1) * lanes] for j in range(parts)], axis=0)
    counted = mm(stacked.astype(BF16), counter)
    before = jnp.zeros((owners, lanes), F32)
    ranks = []
    for j in range(parts):
        own = mine[:, j * lanes : (j + 1) * lanes]
        part = counted[j * owners : (j + 1) * owners]
        ranks.append(jnp.sum(own * (before + part[:, :lanes]), axis=0, keepdims=True))
        before += part[:, lanes:]
    rank = jnp.concatenate(ranks, axis=1).astype(jnp.int32)
    lows = passing // subs
    chunk = owner % subs * lows + owner // subs % lows
    return chunk * width + (owner // passing ^ high) * capacity + rank


def add_eights(x):
    total = x[0:8]
    for j in range(8, x.shape[0], 8):
        total += x[j : j + 8]
    return total


def sum_rows(pieces):
    row = rows_of(pieces[0].shape, 0)
    pieces = [pieces[k] for k in (3, 2, 1, 0, 7, 6, 5, 4)]
    upper = row < 4
    halves = []
    for one, two in zip(pieces[:4], pieces[4:]):
        kept, moved = jnp.where(upper, one, two), jnp.where(upper, two, one)
        halves.append(kept + pltpu.roll(moved, 4, 0))
    for shift in (2, 1):
        pairs = list(zip(halves[:shift], halves[shift:]))
        halves = [
            jnp.where(
                row & shift != 0, one + pltpu.roll(one, shift, 0), two + pltpu.roll(two, 8 - shift, 0)
            )
            for one, two in pairs
        ]
    return halves[0]


def restrict_kernel(
    counter_ref, res_ref, basis_ref, coarse_ref, counts_ref, donors_ref, out_hbm, pair_ref, out_ref, sems,
    *, owners, block, passing, subs, capacity, few
):
    variables, _, fine = res_ref.shape
    modes, points, _ = coarse_ref.shape
    donors = counts_ref.shape[0]
    chunks = out_ref.shape[0]
    full = modes * variables
    depth = pair_ref.shape[1]
    total = donors * fine
    lanes = 128
    width = owners // passing * capacity

    cell = jnp.concatenate([donors_ref[k : k + 1, :] for k in range(donors)], axis=1)
    seat = (cell % block).astype(F32)
    for j in range(total // lanes):
        pair_ref[j, full:, :] = jnp.zeros((depth - full, lanes), F32)
        pair_ref[j, full : full + 1, :] = seat[:, j * lanes : (j + 1) * lanes]
    high = lax.axis_index("high") if few else 0
    owner = cell // block
    slot = free_columns(owner, counter_ref[...], owners, passing, subs, capacity, width, high)
    slot = jnp.broadcast_to(slot.astype(F32), (lanes, total)).T.astype(jnp.int32).astype(jnp.int16)

    basis_high, basis_low = split(basis_ref[...])
    res_high, res_low = split(jnp.concatenate([res_ref[v] for v in range(variables)], axis=1))
    values = mm(basis_high, res_high, 0, 0)
    values += mm(basis_high, res_low, 0, 0) + mm(basis_low, res_high, 0, 0)

    point = rows_of((points, lanes), 0)
    for at in range(0, fine, lanes):
        upper = jnp.zeros((1, lanes), jnp.int32)
        inside = []
        for k in range(donors):
            lower = upper
            upper = lower + counts_ref[k : k + 1, at : at + lanes]
            inside.append((point >= lower) & (point < upper))
        for v in range(variables):
            column = v * fine + at
            value = values[:, column : column + lanes]
            masked = [jnp.where(inside[k], value, 0.0) for k in range(donors)]
            pieces = []
            for a in range(modes):
                coarse = coarse_ref[a, :, at : at + lanes]
                terms = [coarse * masked[k] for k in range(donors)]
                pieces.append([add_eights(term) for term in terms])
            whole = modes - modes % 8
            for k in range(donors):
                left = k * fine + at
                for a in range(0, whole, 8):
                    rows = pl.ds(a * variables + v, 8, stride=variables)
                    pair_ref[left // lanes, rows, :] = sum_rows(
                        [pieces[a + r][k] for r in range(8)]
                    )
            rest = [(k, a) for k in range(donors) for a in range(whole, modes)]
            for first in range(0, len(rest), 8):
                group = rest[first : first + 8]
                filled = group + [group[0]] * (8 - len(group))
                sums = sum_rows([pieces[a][k] for k, a in filled])
                for r, (k, a) in enumerate(group):
                    row, left = a * variables + v, k * fine + at
                    pair_ref[left // lanes, row : row + 1, :] = sums[r : r + 1]

    pair = jnp.concatenate([pair_ref[j] for j in range(total // lanes)], axis=1)
    both = jnp.concatenate(split(pair), axis=0)
    lane = rows_of((total, lanes), 1).astype(jnp.int16)
    one, zero = jnp.ones((total, lanes), BF16), jnp.zeros((total, lanes), BF16)
    part = out_ref.shape[2]
    rows = out_ref.shape[1] * part // width
    together = max(1, 256 // width)
    for first in range(0, chunks, together):
        chooser = jnp.concatenate(
            [
                jnp.where(slot == lane + jnp.int16(first * width + j), one, zero)
                for j in range(0, together * width, lanes)
            ],
            axis=1,
        )
        placed = mm(both, chooser)
        placed = placed[:depth] + placed[depth:]
        for c in range(first, first + together):
            for j in range(width // part):
                at = (c - first) * width + j * part
                out_ref[c, j * rows : (j + 1) * rows] = placed[:rows, at : at + part]
            pltpu.make_async_copy(out_ref.at[c], out_hbm.at[c], sems.at[c]).start()
    for c in range(chunks):
        pltpu.make_async_copy(out_ref.at[c], out_hbm.at[c], sems.at[c]).wait()


def seat_kernel(columns_ref, *out_refs, groups, capacity, rows):
    sources = columns_ref.shape[0]
    full, block = out_refs[0].shape[-2:]
    for n, group in enumerate(groups):
        j, at = divmod(group * capacity, columns_ref.shape[2])
        got = jnp.concatenate(
            [
                columns_ref[s, j * rows : (j + 1) * rows, at : at + capacity]
                for s in range(sources)
            ],
            axis=1,
        )
        seat = got[full : full + 1, :]
        chooser = (rows_of((block, got.shape[1]), 0).astype(F32) == seat).astype(F32).astype(BF16)
        high = got.astype(BF16).astype(F32)
        both = jnp.concatenate([high, got - high], axis=0).astype(BF16)
        dense = mm(both, chooser, 1, 1)
        dense = (dense[:rows] + dense[rows:])[:full]
        if len(out_refs) == len(groups):
            out_refs[n][...] = dense
        else:
            out_refs[0][n] = dense


def renumber_kernel(place_ref, *refs):
    block_refs, out_ref = refs[:-1], refs[-1]
    block = place_ref.shape[1]
    if len(block_refs) == 1:
        total = block_refs[0][0]
        for h in range(1, block_refs[0].shape[0]):
            total += block_refs[0][h]
    else:
        total = block_refs[0][...]
        for ref in block_refs[1:]:
            total += ref[...]
    full = total.shape[0]
    place = place_ref[...]
    chooser = (rows_of((block, block), 0) == place % block).astype(F32).astype(BF16)
    high, low = split(total)
    out_ref[:full, :] = mm(high, chooser, 1, 1) + mm(low, chooser, 1, 1)
    out_ref[full:, :] = (place // block).astype(F32)


def prepare_kernel(after_ref, offset_ref, lift_ref, chooser_ref, lift_out_ref, *, variables, slab):
    del after_ref
    faces, block = offset_ref.shape
    modes = lift_ref.shape[0]
    full = modes * variables
    choose(offset_ref[...], chooser_ref, 0)
    width = variables * faces * slab
    column = rows_of((modes, width), 1)
    mode = rows_of((modes, width), 0)
    spread = jnp.zeros((modes, width), F32)
    for f in range(faces):
        put = (column % slab == mode) & ((column // slab) % faces == f)
        spread += mm(lift_ref[:, f, :], put.astype(F32), 1, 0, lax.Precision.HIGHEST)
    expand = (rows_of((full, modes), 0) // variables == rows_of((full, modes), 1)).astype(F32)
    lifted = mm(expand, spread, 1, 0, lax.Precision.HIGHEST)
    keep = rows_of((full, width), 1) // (slab * faces) == rows_of((full, width), 0) % variables
    high, low = split(jnp.where(keep, lifted, 0.0))
    lift_out_ref[...] = jnp.concatenate([high, high, low], axis=1)


def inner_is_left():
    return lax.axis_index("sub") % 2 == 1


def pack_quarters(pieces, for_left):
    reach = pieces[0].shape[1] // 4
    turned = [pieces[0]] + [pltpu.roll(pieces[g], g * reach, 1) for g in range(1, 4)]
    quarter = rows_of(pieces[0].shape, 1) // reach
    to_left, to_right = turned[0], turned[0]
    for g in range(1, 4):
        to_left = jnp.where(quarter == g, turned[g], to_left)
        to_right = jnp.where(quarter == g - 1, turned[g], to_right)
    return jnp.where(for_left, to_left, to_right)


def take_quarters(inner, outer):
    reach = inner.shape[1] // 4
    quarter = rows_of(inner.shape, 1) // reach
    pieces = []
    for g in range(4):
        piece = jnp.where((quarter == g) != inner_is_left(), inner, outer)
        pieces.append(pltpu.roll(piece, (4 - g) * reach, 1) if g else piece)
    return pieces


def pack_halves(one, two):
    block = one.shape[1]
    turned = pltpu.roll(two, block // 2, 1)
    kept = (rows_of(one.shape, 1) < block // 2) == inner_is_left()
    return jnp.where(kept, one, turned), jnp.where(kept, turned, one)


def take_halves(inner, outer):
    block = inner.shape[1]
    from_inner = (rows_of(inner.shape, 1) >= block // 2) == inner_is_left()
    two = jnp.where(from_inner, outer, inner)
    return jnp.where(from_inner, inner, outer), pltpu.roll(two, block // 2, 1)


def pack_kernel(after_ref, inverse_ref, jacobian_ref, offset_ref, out_ref, lines, *, outer):
    del after_ref
    full, _, block = inverse_ref.shape
    variables, _, faces, _ = jacobian_ref.shape
    for_left = inner_is_left() != outer
    slabs = -(-full // 4)
    for j in range(slabs):
        index = [j + g * slabs for g in range(4)]
        pieces = [inverse_ref[i] if i < full else jnp.zeros((full, block), F32) for i in index]
        out_ref[j * full : (j + 1) * full, :] = pack_quarters(pieces, for_left)
    for w in range(variables):
        for v in range(variables):
            at = (w * variables + v) * faces
            lines[at : at + faces, :] = jacobian_ref[w, v]
    count = lines.shape[0] // 4
    at, last = slabs * full, out_ref.shape[0] - faces
    pieces = [lines[g * count : (g + 1) * count, :] for g in range(4)]
    out_ref[at : at + count, :] = pack_quarters(pieces, for_left)
    out_ref[at + count : last, :] = jnp.zeros((last - at - count, block), F32)
    out_ref[last:, :] = offset_ref[...].astype(F32)


def beside_kernel(inner_ref, outer_ref, inverse_ref, jacobian_ref, chooser_ref, *, faces):
    full, _, block = inverse_ref.shape
    slabs = -(-full // 4)
    for j in range(slabs):
        at = j * full
        pieces = take_quarters(inner_ref[at : at + full, :], outer_ref[at : at + full, :])
        for g, piece in enumerate(pieces):
            if j + g * slabs < full:
                inverse_ref[j + g * slabs] = piece
    count = jacobian_ref.shape[0] // 4
    at = slabs * full
    pieces = take_quarters(inner_ref[at : at + count, :], outer_ref[at : at + count, :])
    for g, piece in enumerate(pieces):
        jacobian_ref[g * count : (g + 1) * count, :] = piece
    last = inner_ref.shape[0] - faces
    inner, outer = inner_ref[last:, :], outer_ref[last:, :]
    from_inner = (rows_of(inner.shape, 1) >= block // 2) == inner_is_left()
    choose(jnp.where(from_inner, inner, outer).astype(jnp.int32), chooser_ref, block)


def choose(offsets, chooser_ref, first):
    faces, block = offsets.shape
    lane = rows_of((1, block), 1) + first
    row = rows_of((2 * block, block), 0)
    for f in range(faces):
        offset = offsets[f : f + 1, :]
        source = jnp.where(offset != 0, (lane + offset) & (2 * block - 1), -1)
        chooser_ref[:, f * block : (f + 1) * block] = (row == source).astype(F32).astype(BF16)


def apply_inverse(inverse_ref, field, variables, depth=None):
    full, _, block = inverse_ref.shape
    modes = full // variables
    zero = jnp.zeros((8, block), F32)

    def piece(row):
        if row >= full:
            return zero
        product = inverse_ref[row % modes * variables + row // modes if depth else row] * field
        partial = product[0:8]
        for j in range(8, full - 7, 8):
            partial += product[j : j + 8]
        rest = full % 8
        if rest:
            partial += jnp.concatenate([product[full - rest :], zero[rest:]], axis=0)
        return partial

    rows = []
    for at in range(0, depth or full, 8):
        rows.append(sum_rows([piece(at + r) for r in range(8)]) if at < full else zero)
    return jnp.concatenate(rows, axis=0)[: depth or full]


def first_kernel(inverse_ref, *refs, subs, variables):
    block_refs, (total_ref, out_ref, inner_ref, outer_ref) = refs[:-4], refs[-4:]
    full = total_ref.shape[0]
    owner = lax.axis_index("high") * lax.axis_size("low") + lax.axis_index("low")
    owner = (owner * subs + lax.axis_index("sub")).astype(F32)
    residual = jnp.zeros(total_ref.shape, F32)
    for ref in block_refs:
        residual += jnp.where(ref[full:, :] == owner, ref[:full, :], 0.0)
    total_ref[...] = residual
    x = apply_inverse(inverse_ref, residual, variables, out_ref.shape[0])
    out_ref[...] = x
    half = inner_ref.shape[0]
    inner_ref[...], outer_ref[...] = pack_halves(x[:half], x[half:])


def sweep_kernel(
    inverse_ref, inverse_beside_ref, residual_ref, x_ref, outer_ref, inner_ref, chooser_ref,
    chooser_beside_ref, lift_ref, jacobian_ref, jacobian_beside_ref, total_ref, out_ref,
    picked_ref, z_ref, *, variables, slab
):
    depth, block = x_ref.shape
    full = residual_ref.shape[0]
    modes = full // variables
    faces = jacobian_ref.shape[2]
    residual = residual_ref[...]
    total_ref[...] = residual
    third = z_ref.shape[0] // 3

    def coupled(x, tiles):
        x = jnp.concatenate(split(x), axis=0)
        for t, ref in enumerate((chooser_ref, chooser_beside_ref)[:tiles]):
            picked = mm(x, ref[...])
            picked_ref[t] = picked[:depth] + picked[depth:]
        for t in range(tiles):
            for f in range(faces):
                at = f * block
                part = [
                    picked_ref[t, v * modes : v * modes + slab, at : at + block]
                    for v in range(variables)
                ]
                for w in range(variables):
                    z = None
                    for v in range(variables):
                        if t:
                            line = (w * variables + v) * faces + f
                            term = part[v] * jacobian_beside_ref[line : line + 1, :]
                        else:
                            term = part[v] * jacobian_ref[w, v, f : f + 1, :]
                        z = z + term if v else term
                    line, column = (w * faces + f) * slab, t * block
                    high, low = split(z)
                    for n, value in enumerate((high, low, high)):
                        at_row = n * third + line
                        z_ref[at_row : at_row + slab, column : column + block] = value
        return mm(lift_ref[...], z_ref[:, : tiles * block])

    first = x_ref[...]
    first_beside = jnp.concatenate(take_halves(inner_ref[...], outer_ref[...]), axis=0)
    taken = coupled(jnp.concatenate([first, first_beside], axis=1), 2)
    second = jnp.concatenate(
        [
            first - apply_inverse(inverse_ref, taken[:, :block], variables, depth),
            first_beside - apply_inverse(inverse_beside_ref, taken[:, block:], variables, depth),
        ],
        axis=1,
    )
    out_ref[...] = apply_inverse(inverse_ref, residual - coupled(second, 1), variables)


def per_device(
    fine_residual,
    fine_basis,
    coarse_basis,
    donor_cells,
    point_counts,
    solver_pos,
    block_inverse,
    face_jacobian,
    face_lift,
    face_offset,
):
    high_count = lax.axis_size("high")
    passing = lax.axis_size("low") * lax.axis_size("sub")
    owners = high_count * passing
    _, variables, fine = fine_residual.shape
    modes = coarse_basis.shape[1]
    donors = donor_cells.shape[1]
    block = solver_pos.shape[0]
    faces = face_offset.shape[0]
    full = modes * variables
    slab = -(-modes // 16) * 16
    depth = -(-full // 16) * 16

    capacity = max(2, 2 * fine * donors // owners)
    few = 1 < high_count <= 8 and high_count & (high_count - 1) == 0
    subs = lax.axis_size("sub")
    counter = call(
        constants_kernel,
        "constants",
        ((128, 256), BF16),
        (),
        cost=pl.CostEstimate(flops=2 * 10**9, bytes_accessed=8 * 10**6, transcendentals=0),
    )
    width = high_count * capacity
    halves = 2 if width > 128 else 1
    rows = -(-(full + 1) // 4) * 4 if halves > 1 else -(-(full + 1) // 8) * 8
    chunk_shape = (passing, halves * rows, width // halves)
    columns = call(
        functools.partial(
            restrict_kernel,
            owners=owners,
            block=block,
            passing=passing,
            subs=subs,
            capacity=capacity,
            few=few,
        ),
        "restrict",
        (chunk_shape, F32),
        (
            counter,
            fine_residual.transpose(1, 0, 2),
            fine_basis.T,
            coarse_basis.transpose(1, 0, 2),
            point_counts.T,
            donor_cells.T,
        ),
        [
            pltpu.VMEM((donors * fine // 128, depth, 128), F32),
            pltpu.VMEM(chunk_shape, F32),
            pltpu.SemaphoreType.DMA((passing,)),
        ],
        megabytes=16,
        out_spec=pl.BlockSpec(memory_space=pl.ANY),
    )
    columns = lax.all_to_all(columns, PLANE, 0, 0, tiled=True)
    def seat(name, groups, shapes):
        return call(
            functools.partial(seat_kernel, groups=groups, capacity=capacity, rows=rows),
            name,
            shapes,
            (columns,),
            megabytes=24,
        )

    dense = ((full, block), F32)
    if few:
        count = high_count // 2
        near = seat("seat_near", range(count), [dense] * count)
        rest = [seat("seat_far", [d], [dense])[0] for d in range(count, high_count)]
        blocks = swap_all([*near, *rest], "high")
    else:
        blocks = seat("seat_all", range(high_count), ((high_count, full, block), F32))
        blocks = [lax.all_to_all(blocks, "high", 0, 0, tiled=True)]
    whole = call(
        renumber_kernel, "renumber", ((full + 1, block), F32), (solver_pos[None, :], *blocks)
    )
    blocks = swap_all([whole] * subs, "sub")

    jacobian = face_jacobian.transpose(1, 2, 0, 3)
    chooser, lift = call(
        functools.partial(prepare_kernel, variables=variables, slab=slab),
        "prepare",
        [((2 * block, faces * block), BF16), ((full, 3 * variables * faces * slab), BF16)],
        (counter, face_offset, face_lift.transpose(1, 0, 2)),
    )
    outer_pairs = [(i, i + 1) for i in range(1, owners - 1, 2)]
    outer_pairs += [(j, i) for i, j in outer_pairs]
    inner_pairs = [(i, i ^ 1) for i in range(owners)]
    lines = variables * variables * faces
    packed = ((-(-(-(-full // 4) * full + lines // 4 + faces + 1) // 8) * 8, block), F32)
    packs = []
    for outer in (False, True):
        packs.append(
            call(
                functools.partial(pack_kernel, outer=outer),
                "pack_outer" if outer else "pack_inner",
                packed,
                (packs[0] if outer else counter, block_inverse, jacobian, face_offset),
                [pltpu.VMEM((lines, block), F32)],
            )
        )
    inner = lax.ppermute(packs[0], WHOLE, inner_pairs)
    outer = lax.ppermute(packs[1], WHOLE, outer_pairs)
    inverse_beside, jacobian_beside, chooser_beside = call(
        functools.partial(beside_kernel, faces=faces),
        "beside",
        [((full, full, block), F32), ((lines, block), F32), ((2 * block, faces * block), BF16)],
        (inner, outer),
    )
    plain, edge = ((full, block), F32), ((depth // 2, block), F32)
    residual, x, to_inner, to_outer = call(
        functools.partial(first_kernel, subs=subs, variables=variables),
        "first",
        [plain, ((depth, block), F32), edge, edge],
        (block_inverse, *blocks),
    )
    outer = lax.ppermute(to_outer, WHOLE, outer_pairs)
    inner = lax.ppermute(to_inner, WHOLE, inner_pairs)
    return tuple(
        call(
            functools.partial(sweep_kernel, variables=variables, slab=slab),
            "sweeps",
            [plain, plain],
            (
                block_inverse,
                inverse_beside,
                residual,
                x,
                outer,
                inner,
                chooser,
                chooser_beside,
                lift,
                jacobian,
                jacobian_beside,
            ),
            [pltpu.VMEM((2, depth, faces * block), F32)]
            + [pltpu.VMEM((3 * variables * faces * slab, 2 * block), BF16)],
        )
    )


def solution(mesh):
    dom, sub = mesh.devices.shape
    low = next(count for count in (4, 2, 1) if dom % count == 0)
    split_mesh = jax.sharding.Mesh(mesh.devices.reshape(dom // low, low, sub), WHOLE)
    in_specs = (
        P(None, None, WHOLE),
        P(),
        P(None, None, WHOLE),
        P(WHOLE, None),
        P(WHOLE, None),
        P(WHOLE),
        P(None, None, WHOLE),
        P(None, None, None, WHOLE),
        P(),
        P(None, WHOLE),
    )
    return jax.shard_map(
        per_device,
        mesh=split_mesh,
        in_specs=in_specs,
        out_specs=(P(None, WHOLE), P(None, WHOLE)),
        check_vma=False,
    )
```
